32 devices in a mesh: rep: 2 (over y), tp: 4 (over z), sec: 4 (over x, core).
Axes of the slice: x: 2, y: 2, z: 4, core: 2. Of those that a mesh axis runs over, the one named last changes fastest.
Arguments:
- prompt_key_values: bfloat16 [64, 2, 1024, 512], P(('rep', 'sec'), None, 'tp'), parts along dimension 0, may hold values from -16 to 16
- queries: bfloat16 [8, 8, 4, 4096], P(('rep', 'sec')), parts along dimension 0, may hold values from -8 to 8
- routing: int32 [64, 1], P('rep'), parts along dimension 0, may hold values from 0 to 3; in each aligned block of 8 rows (0 to 7, 8 to 15, ...) at most 2 rows name the same one
- lengths: int32 [64], P('rep'), parts along dimension 0, may hold values from 128 to 1024, as said below
- out_weight: bfloat16 [4096, 8192], P(None, 'tp'), may hold values from -0.375 to 0.375
Outputs:
- layer_out: bfloat16 [64, 4, 8192], P(('rep', 'sec'), None, 'tp'), parts along dimension 0
- decode_group_cache: bfloat16 [8, 8, 2, 1024, 512], P(('rep', 'sec'), None, None, 'tp'), parts along dimension 0
The draws below stay inside these ranges and needn't reach their ends.
There are 2 independent parts, one for each index of `rep`. The reference program is written for one: setup_inputs(seed, part) draws one part's arguments, and reference() takes and returns one part's arrays. A program takes and returns all parts, laid end to end along the dimension named above; an argument that names none is the same for every part. Nothing has to cross between parts.
Inputs may be any that keep to these rules, and one draw needn't show every extreme that they name: `routing`: among the 8 prompts of one prefill group, no decode group is named more than 2 times, and in some groups one is named exactly 2 times. `lengths`: some prompt has exactly 1024 positions.
All inputs are finite; a program needn't handle non-finite values.
Results may differ from the reference program's by a relative error of at most 0.008.
Values may be sent and summed in bfloat16 or wider, within the bound.
No kernel may reach another device: no remote copies, remote signals or barrier semaphores. Data moves between devices by JAX's collectives and lax.ppermute only.
A program may use at most 128 MiB of HBM per device.

```python
import math
import jax
import jax.numpy as jnp
import numpy as np
from jax import lax

D = 8192
HEAD_SIZE = 128
QUERY_HEADS = 32
KEY_VALUE_HEADS = 4
CACHE_LENGTH = 1024
SAMPLE_COUNT = 4
REQ_GRP = 8
CAP = 2
PROMPT_COUNT = 32
SLOT_COUNT = 8
N_SEC = 4


def shared_sign(key):
    sign_flips = jax.random.bernoulli(key, 0.5, (KEY_VALUE_HEADS * HEAD_SIZE,))
    return jnp.where(sign_flips, 1.0, -1.0).astype(jnp.float32)


def draw_prompt_key_values(key, part):
    random_signs = shared_sign(key)
    key = jax.random.fold_in(key, 11)
    first_random_key = jax.random.fold_in(key, 0)
    random_noise = jax.random.normal(first_random_key, (PROMPT_COUNT, 2, CACHE_LENGTH, KEY_VALUE_HEADS * HEAD_SIZE), jnp.float32)
    root_size = math.sqrt(HEAD_SIZE)
    first_level = 32.0 / root_size
    second_level = first_level + 0.35 / root_size
    ordinal = jnp.arange(CACHE_LENGTH)[None, :, None]
    aligned = jnp.where(ordinal == 0, first_level * random_signs, jnp.where(ordinal == 1, second_level * random_signs, random_noise[:, 0]))
    random_noise = jnp.stack([aligned, random_noise[:, 1]], axis=1)
    return jnp.clip(random_noise, -16.0, 16.0).astype(jnp.bfloat16)


def draw_queries(key, part):
    random_signs = shared_sign(key)
    key = jax.random.fold_in(key, 23)
    first_random_key, second_random_key = jax.random.split(key)
    random_noise = jnp.clip(2.0 * jax.random.normal(first_random_key, (N_SEC, SLOT_COUNT, SAMPLE_COUNT, QUERY_HEADS * HEAD_SIZE), jnp.float32), -8.0, 8.0)
    levels = jnp.array([3.5, 5.0, 6.5], jnp.float32)
    strength = levels[jax.random.randint(second_random_key, (N_SEC, SLOT_COUNT), 0, 3)]
    target_matrix = random_signs.reshape(KEY_VALUE_HEADS, HEAD_SIZE)[jnp.arange(QUERY_HEADS) // (QUERY_HEADS // KEY_VALUE_HEADS)]
    selected_prompts = (jnp.arange(SAMPLE_COUNT) == 0)[:, None, None] & (jnp.arange(QUERY_HEADS) % (QUERY_HEADS // KEY_VALUE_HEADS) == 0)[None, :, None]
    shaped = random_noise.reshape(N_SEC, SLOT_COUNT, SAMPLE_COUNT, QUERY_HEADS, HEAD_SIZE)
    shaped = jnp.where(selected_prompts, strength[:, :, None, None, None] * target_matrix, shaped)
    random_noise = shaped.reshape(N_SEC, SLOT_COUNT, SAMPLE_COUNT, QUERY_HEADS * HEAD_SIZE)
    return random_noise.astype(jnp.bfloat16)


def draw_lengths(key, part):
    key = jax.random.fold_in(key, 31)
    first_random_key, second_random_key = jax.random.split(key)
    drawn = jax.random.randint(first_random_key, (PROMPT_COUNT,), CACHE_LENGTH // 8, CACHE_LENGTH + 1)
    picked = jax.random.randint(second_random_key, (), 0, PROMPT_COUNT)
    return jnp.where(jnp.arange(PROMPT_COUNT) == picked, CACHE_LENGTH, drawn).astype(jnp.int32)


def block_levels(own_key, extent, cuts, least, largest):
    def one(dim, shards_of):
        heights = jax.random.uniform(jax.random.fold_in(jax.random.fold_in(own_key, 6), dim), (shards_of,), jnp.float32, least / len(cuts), largest / len(cuts))
        return jnp.repeat(jnp.exp(heights), extent[dim] // shards_of).reshape((-1,) + (1,) * (len(extent) - dim - 1))

    level = one(*cuts[0])
    for cut in cuts[1:]:
        level = level * one(*cut)
    return level


def assign_block(key, own, number, rows, number_of, top, most, skew):
    order = jax.random.permutation(key, number_of)
    heavy_load, usual = shares(number_of, rows * top, most, skew, True), shares(number_of, rows * top, most, skew, False)
    places = jnp.arange(number_of)

    def named(tallies, turn):
        used = int((tallies > 0).sum())
        fixed = max(1, used // 4)
        moved = fixed + (places - fixed + turn * (used - fixed)) % max(1, number_of - fixed)
        return jnp.zeros((number_of,), jnp.int32).at[order[jnp.where(places < fixed, places, moved)]].set(jnp.asarray(tallies, jnp.int32))

    tallies = jnp.where(number % 4 == 0, named(heavy_load, number // 4), named(usual, number - number // 4 - 1))
    mixed = jax.random.permutation(jax.random.fold_in(own, 3), number_of)
    source_of, receiver = mixed[0:number_of // 2 * 2:2], mixed[1:number_of // 2 * 2:2]
    room = jnp.minimum(tallies[source_of] - 1, most - tallies[receiver]) // 2
    room = jnp.where((source_of == order[0]) | (receiver == order[0]) | (tallies[receiver] == 0), 0, jnp.maximum(room, 0))
    moved = jax.random.randint(jax.random.fold_in(own, 4), (number_of // 2,), 0, 1 << 20) % (room + 1)
    tallies = tallies.at[source_of].add(-moved).at[receiver].add(moved)
    items = jnp.searchsorted(jnp.cumsum(tallies), jnp.arange(rows * top), side="right").astype(jnp.int32)
    table = items.reshape(top, rows).T
    table = table[jax.random.permutation(jax.random.fold_in(own, 1), rows)]
    turn = jax.random.randint(jax.random.fold_in(own, 2), (rows, 1), 0, top)
    return jnp.take_along_axis(table, (jnp.arange(top)[None, :] + turn) % top, axis=1)


def shares(number_of, total, bound, slope, full):
    weights = [(1 << 20) // math.isqrt(rank ** slope) + 1 for rank in range(1, number_of + 1)]
    largest = bound if full else min(bound, max(-(-total // number_of), total * weights[0] // sum(weights)))
    least = 1 if total - largest >= number_of - 1 else 0
    counts, rest = [largest] + [least] * (number_of - 1), total - largest - least * (number_of - 1)
    while rest > 0:
        movable = [i for i in range(1, number_of) if counts[i] < largest] or [i for i in range(1, number_of) if counts[i] < bound]
        pool, remaining = sum([weights[i] for i in movable]), rest
        for i in movable:
            more = min(bound - counts[i], max(1, remaining * weights[i] // pool), rest)
            counts[i] = counts[i] + more
            rest = rest - more
    return np.array(counts)


def normal_values(own_key, shape, width, most, pieces=(), kind=jnp.bfloat16):
    values = jax.random.normal(own_key, shape, jnp.float32) * width
    if len(pieces) > 0:
        values = block_levels(own_key, shape, pieces, -0.22, 0.18) * values
    return jnp.clip(values, min=-most, max=most).astype(kind)


def setup_inputs(seed: int = 0, part: int = 0) -> dict:
    arg_keys = jax.random.split(jax.random.key(seed), 6)
    part_splits = jax.random.split(jax.random.fold_in(arg_keys[5], part), 6)
    prompt_key_values = draw_prompt_key_values(jax.random.fold_in(jax.random.fold_in(arg_keys[5], part), 71), part)
    queries = draw_queries(jax.random.fold_in(jax.random.fold_in(arg_keys[5], part), 71), part)
    routing_keys = jax.random.split(jax.random.fold_in(part_splits[2], 1), PROMPT_COUNT // REQ_GRP)
    routing_turns = jax.random.permutation(jax.random.fold_in(part_splits[2], 3), PROMPT_COUNT // REQ_GRP)
    routing = jax.vmap(lambda own, number: assign_block(jax.random.fold_in(part_splits[2], 2), own, number, REQ_GRP, N_SEC, 1, CAP, 2))(routing_keys, routing_turns).reshape((PROMPT_COUNT, 1))
    lengths = draw_lengths(jax.random.fold_in(jax.random.fold_in(arg_keys[5], part), 71), part)
    out_weight = normal_values(arg_keys[4], (QUERY_HEADS * HEAD_SIZE, D), (QUERY_HEADS * HEAD_SIZE // 16) ** -0.5, 0.375, ((1, 4),))
    return dict(prompt_key_values=prompt_key_values, queries=queries, routing=routing, lengths=lengths, out_weight=out_weight)


def slot_numbers(target_output, group_size, capacity):
    request_count = target_output.shape[0]
    ordinal = jnp.arange(request_count, dtype=jnp.int32)
    source = ordinal // group_size
    earlier = (source[:, None] == source[None, :]) & (target_output[:, None] == target_output[None, :]) & (ordinal[None, :] < ordinal[:, None])
    position = jnp.sum(earlier.astype(jnp.int32), axis=1)
    return (source * capacity + position).astype(jnp.int32), (target_output * capacity + position).astype(jnp.int32)


def reference(prompt_key_values, queries, routing, lengths, out_weight):
    target_output = routing[:, 0]
    arrival_order, depart = slot_numbers(target_output, REQ_GRP, CAP)
    picked = queries[target_output, arrival_order]
    decode_group_cache = jnp.zeros((N_SEC, SLOT_COUNT, 2, CACHE_LENGTH, KEY_VALUE_HEADS * HEAD_SIZE), jnp.bfloat16).at[target_output, arrival_order].set(prompt_key_values)
    decode_groups = QUERY_HEADS // KEY_VALUE_HEADS

    def attend(request):
        query_matrix, key_value_pairs, length = request
        query_head_count = query_matrix.astype(jnp.float32).reshape(SAMPLE_COUNT, KEY_VALUE_HEADS, decode_groups, HEAD_SIZE)
        key_matrix = key_value_pairs[0].astype(jnp.float32).reshape(CACHE_LENGTH, KEY_VALUE_HEADS, HEAD_SIZE)
        value_matrix = key_value_pairs[1].astype(jnp.float32).reshape(CACHE_LENGTH, KEY_VALUE_HEADS, HEAD_SIZE)
        scores = jnp.einsum('sknd,lkd->sknl', query_head_count, key_matrix) * (HEAD_SIZE ** -0.5)
        visible = jnp.arange(CACHE_LENGTH, dtype=jnp.int32) < length
        scores = jnp.where(visible, scores, -1e30)
        peak_score = jnp.max(scores, axis=-1, keepdims=True)
        weights = jnp.where(visible, jnp.exp(scores - peak_score), 0.0)
        weight_sum = jnp.sum(weights, axis=-1)
        mixed_heads = jnp.einsum('sknl,lkd->sknd', weights, value_matrix) / weight_sum[..., None]
        return mixed_heads.reshape(SAMPLE_COUNT, QUERY_HEADS * HEAD_SIZE).astype(jnp.bfloat16)

    attended = lax.map(attend, (picked, prompt_key_values, lengths))
    result = jnp.dot(attended.reshape(PROMPT_COUNT * SAMPLE_COUNT, QUERY_HEADS * HEAD_SIZE), out_weight, preferred_element_type=jnp.float32)
    layer_out = result.astype(jnp.bfloat16).reshape(PROMPT_COUNT, SAMPLE_COUNT, D)
    return layer_out, decode_group_cache
```

```python
import functools

import jax
import jax.numpy as jnp
from jax import lax
from jax.experimental import pallas as pl
from jax.experimental.pallas import tpu as pltpu
from jax.sharding import PartitionSpec as P

HEAD_SIZE = 128
KEY_VALUE_HEADS = 4
REQ_GRP = 8
CAP = 2
HIDDEN = -1e30

ANY = pl.BlockSpec(memory_space=pl.ANY)
VMEM = pl.BlockSpec(memory_space=pltpu.VMEM)
SMEM = pl.BlockSpec(memory_space=pltpu.SMEM)


def swap(value, axis, offset):
    count = lax.axis_size(axis)
    return lax.ppermute(value, axis, [(i, i ^ offset) for i in range(count)])


def own_slots(routing_ref, section, used, visit):
    for t in range(used.shape[0]):
        used[t] = 0
    for i in range(REQ_GRP):
        target = routing_ref[section * REQ_GRP + i]
        order = used[target]
        used[target] = order + 1
        visit(i, target, order)


def pack_kernel(offsets, section_count, routing_ref, cache_ref, *refs):
    out_refs, (source, used, zeros, sem) = refs[:-4], refs[-4:]
    section = lax.axis_index("sec")
    full = section_count * CAP == REQ_GRP

    def note(i, target, order):
        source[target * CAP + order] = i

    own_slots(routing_ref, section, used, note)
    if not full:
        zeros[...] = jnp.zeros_like(zeros)
    copies = []
    for n, offset in enumerate(offsets):
        target = section ^ offset
        for order in range(CAP):
            if offset == 0:
                place = out_refs[n * CAP].at[0, section * CAP + order]
            else:
                place = out_refs[n * CAP + order].at[0]
            row = source[target * CAP + order]
            slot_sem = sem.at[n * CAP + order]
            if full:
                copy = pltpu.make_async_copy(cache_ref.at[row], place, slot_sem)
                copy.start()
                copies.append(copy)
            else:
                filled = order < used[target]

                @pl.when(filled)
                def _():
                    pltpu.make_async_copy(cache_ref.at[row], place, slot_sem).start()

                @pl.when(jnp.logical_not(filled))
                def _():
                    pltpu.make_async_copy(zeros, place, slot_sem).start()

                copies.append(pltpu.make_async_copy(zeros, place, slot_sem))
    for copy in copies:
        copy.wait()


def pack(routing, cache, offsets, section_count):
    row_shape = cache.shape[1:]
    full = section_count * CAP == REQ_GRP
    shapes = []
    for offset in offsets:
        if offset == 0:
            shapes.append(jax.ShapeDtypeStruct((1, section_count * CAP) + row_shape, cache.dtype))
        else:
            shapes.extend([jax.ShapeDtypeStruct((1,) + row_shape, cache.dtype)] * CAP)
    return pl.pallas_call(
        functools.partial(pack_kernel, offsets, section_count),
        out_shape=shapes,
        in_specs=[SMEM, ANY],
        out_specs=[ANY] * len(shapes),
        scratch_shapes=[
            pltpu.SMEM((section_count * CAP,), jnp.int32),
            pltpu.SMEM((section_count,), jnp.int32),
            pltpu.VMEM((8, 128) if full else row_shape, cache.dtype),
            pltpu.SemaphoreType.DMA((len(offsets) * CAP,)),
        ],
        cost_estimate=pl.CostEstimate(
            flops=0, bytes_accessed=2 * len(offsets) * CAP * 2 * row_shape[1] * row_shape[2] * 2, transcendentals=0
        ),
        name="pack_cache",
    )(routing, cache)


def place_kernel(offsets, *refs):
    count = len(offsets)
    part_refs, out_ref, sem = refs[1 : 1 + count], refs[1 + count], refs[2 + count]
    section = lax.axis_index("sec")
    copies = []
    for n, (offset, first) in enumerate(offsets):
        length = part_refs[n].shape[0]
        slots = out_ref.at[0, pl.ds((section ^ offset) * CAP + first, length)]
        copy = pltpu.make_async_copy(part_refs[n], slots, sem.at[n])
        copy.start()
        copies.append(copy)
    for copy in copies:
        copy.wait()


def place(whole, parts, offsets):
    return pl.pallas_call(
        functools.partial(place_kernel, offsets),
        out_shape=jax.ShapeDtypeStruct(whole.shape, whole.dtype),
        in_specs=[ANY] * (1 + len(parts)),
        out_specs=ANY,
        scratch_shapes=[pltpu.SemaphoreType.DMA((len(parts),))],
        input_output_aliases={0: 0},
        cost_estimate=pl.CostEstimate(
            flops=0, bytes_accessed=sum(4 * part.size for part in parts), transcendentals=0
        ),
        name="place_cache",
    )(whole, *parts)


def attend_kernel(section_count, tp_count, routing_ref, lengths_ref, cache_ref, *refs):
    query_refs, message_refs = refs[:section_count], refs[section_count : section_count + tp_count]
    slot_of, used, held, queries, stats, messages, sem = refs[section_count + tp_count :]
    section = lax.axis_index("sec")
    tp_index = lax.axis_index("tp")
    samples, _, heads, _ = query_refs[0].shape[1:]
    rows = samples * heads
    local = cache_ref.shape[2]
    groups = REQ_GRP * KEY_VALUE_HEADS // tp_count

    def fetch(i):
        return pltpu.make_async_copy(cache_ref.at[i], held.at[i], sem.at[i])

    for i in range(REQ_GRP):
        fetch(i).start()

    def note(i, target, order):
        slot_of[i] = (target ^ section) * CAP + order

    own_slots(routing_ref, section, used, note)
    for offset in range(section_count):
        for order in range(CAP):
            for k in range(KEY_VALUE_HEADS):
                block = query_refs[offset][order, :, k].astype(jnp.float32)
                queries[offset * CAP + order, k] = block.reshape(rows, HEAD_SIZE).astype(jnp.bfloat16)
    stats[...] = jnp.zeros_like(stats)
    lane = lax.broadcasted_iota(jnp.int32, (rows, HEAD_SIZE), 1)
    position = lax.broadcasted_iota(jnp.int32, (rows, local), 1) + tp_index * local

    @pl.loop(0, REQ_GRP)
    def _(i):
        fetch(i).wait()
        visible = position < lengths_ref[section * REQ_GRP + i]
        for k in range(KEY_VALUE_HEADS):
            columns = pl.ds(k * HEAD_SIZE, HEAD_SIZE)
            score = lax.dot_general(
                queries[slot_of[i], k],
                held[i, 0, :, columns],
                (((1,), (1,)), ((), ())),
                preferred_element_type=jnp.float32,
            ) * HEAD_SIZE ** (-0.5)
            score = jnp.where(visible, score, HIDDEN)
            peak = jnp.max(score, axis=1, keepdims=True)
            weight = jnp.where(visible, jnp.exp(score - peak), 0.0)
            total = jnp.sum(weight, axis=1, keepdims=True)
            mixed = jnp.dot(
                weight.astype(jnp.bfloat16), held[i, 1, :, columns], preferred_element_type=jnp.float32
            )
            some = total > 0.0
            safe = jnp.where(some, total, 1.0)
            group = i * KEY_VALUE_HEADS + k
            device, inner = group // groups, group % groups
            messages[device, inner] = (mixed / safe).astype(jnp.bfloat16)
            level = jnp.where(some, peak + jnp.log(safe), HIDDEN)
            stats[device] = jnp.where(lane == inner, level, stats[device])

    for offset in range(tp_count):
        device = tp_index ^ offset
        message_refs[offset][0:groups] = messages[device]
        level = stats[device]
        high = level.astype(jnp.bfloat16).astype(jnp.float32)
        rest = level - high
        middle = rest.astype(jnp.bfloat16).astype(jnp.float32)
        low = rest - middle
        packed = high + pltpu.roll(middle, groups, 1) + pltpu.roll(low, 2 * groups, 1)
        message_refs[offset][groups] = packed.astype(jnp.bfloat16)


def attend(routing, lengths, cache, queries, tp_count):
    section_count = len(queries)
    samples, _, heads, _ = queries[0].shape[1:]
    rows = samples * heads
    groups = REQ_GRP * KEY_VALUE_HEADS // tp_count
    message = jax.ShapeDtypeStruct((groups + 1, rows, HEAD_SIZE), jnp.bfloat16)
    multiplies = REQ_GRP * rows * KEY_VALUE_HEADS * HEAD_SIZE * cache.shape[2]
    return pl.pallas_call(
        functools.partial(attend_kernel, section_count, tp_count),
        out_shape=[message] * tp_count,
        in_specs=[SMEM, SMEM, ANY] + [VMEM] * section_count,
        out_specs=[VMEM] * tp_count,
        scratch_shapes=[
            pltpu.SMEM((REQ_GRP,), jnp.int32),
            pltpu.SMEM((section_count,), jnp.int32),
            pltpu.VMEM(cache.shape, cache.dtype),
            pltpu.VMEM((section_count * CAP, KEY_VALUE_HEADS, rows, HEAD_SIZE), jnp.bfloat16),
            pltpu.VMEM((tp_count, rows, HEAD_SIZE), jnp.float32),
            pltpu.VMEM((tp_count, groups, rows, HEAD_SIZE), jnp.bfloat16),
            pltpu.SemaphoreType.DMA((REQ_GRP,)),
        ],
        compiler_params=pltpu.CompilerParams(vmem_limit_bytes=24 << 20),
        cost_estimate=pl.CostEstimate(
            flops=4 * multiplies, bytes_accessed=2 * cache.size, transcendentals=multiplies // HEAD_SIZE
        ),
        name="attend",
    )(routing, lengths, cache, *queries)


def join_kernel(samples, *refs):
    message_refs, out_ref, joined = refs[:-2], refs[-2], refs[-1]
    groups = message_refs[0].shape[0] - 1
    rows = message_refs[0].shape[1]
    heads = rows // samples
    levels = []
    for ref in message_refs:
        packed = ref[groups].astype(jnp.float32)
        span = HEAD_SIZE
        levels.append(
            packed + pltpu.roll(packed, span - groups, 1) + pltpu.roll(packed, span - 2 * groups, 1)
        )
    summit = functools.reduce(jnp.maximum, levels)
    scales = [jnp.exp(level - summit) for level in levels]
    total = functools.reduce(jnp.add, scales)
    scales = [scale / total for scale in scales]
    for inner in range(groups):
        terms = [
            ref[inner].astype(jnp.float32) * scale[:, inner : inner + 1]
            for ref, scale in zip(message_refs, scales)
        ]
        joined[inner] = functools.reduce(jnp.add, terms)
    for inner in range(groups):
        for head in range(heads):
            block = joined[inner, pl.ds(head, samples, stride=heads), :]
            if len(out_ref.shape) == 2:
                row = inner // KEY_VALUE_HEADS * samples
                column = (inner % KEY_VALUE_HEADS * heads + head) * HEAD_SIZE
                out_ref[row : row + samples, column : column + HEAD_SIZE] = block
            else:
                out_ref[inner, :, head * HEAD_SIZE : (head + 1) * HEAD_SIZE] = block


def join(messages, samples):
    groups = messages[0].shape[0] - 1
    rows = messages[0].shape[1]
    width = rows // samples * HEAD_SIZE
    if groups % KEY_VALUE_HEADS == 0:
        shape = (groups // KEY_VALUE_HEADS * samples, KEY_VALUE_HEADS * width)
    else:
        shape = (groups, samples, width)
    return pl.pallas_call(
        functools.partial(join_kernel, samples),
        out_shape=jax.ShapeDtypeStruct(shape, jnp.float32),
        in_specs=[VMEM] * len(messages),
        out_specs=VMEM,
        scratch_shapes=[pltpu.VMEM((groups, rows, HEAD_SIZE), jnp.float32)],
        cost_estimate=pl.CostEstimate(
            flops=4 * len(messages) * messages[0].size,
            bytes_accessed=2 * len(messages) * messages[0].size,
            transcendentals=0,
        ),
        name="join",
    )(*messages).astype(jnp.bfloat16)


def project_kernel(count, *refs):
    part_refs, weight_ref, out_ref = refs[:count], refs[count], refs[count + 1]
    tp_index = lax.axis_index("tp")
    left = jnp.concatenate([ref[...].astype(jnp.float32) for ref in part_refs], axis=0)
    result = jnp.dot(left.astype(jnp.bfloat16), weight_ref[...], preferred_element_type=jnp.float32)
    samples = out_ref.shape[1]
    share = out_ref.shape[0] // count
    for offset in range(count):
        first = (tp_index ^ offset) * share
        for n in range(share):
            row = (offset * share + n) * samples
            out_ref[first + n] = result[row : row + samples].astype(out_ref.dtype)


def project(parts, weight, samples):
    count = len(parts)
    prompts = sum(part.shape[0] for part in parts) // samples
    depth, width = weight.shape
    tile = min(512, width)
    return pl.pallas_call(
        functools.partial(project_kernel, count),
        grid=(width // tile,),
        out_shape=jax.ShapeDtypeStruct((prompts, samples, width), jnp.bfloat16),
        in_specs=[pl.BlockSpec(part.shape, lambda n: (0, 0)) for part in parts]
        + [pl.BlockSpec((depth, tile), lambda n: (0, n))],
        out_specs=pl.BlockSpec((prompts, samples, tile), lambda n: (0, 0, n)),
        compiler_params=pltpu.CompilerParams(vmem_limit_bytes=24 << 20),
        cost_estimate=pl.CostEstimate(
            flops=2 * prompts * samples * depth * width, bytes_accessed=2 * depth * width, transcendentals=0
        ),
        name="project",
    )(*parts, weight)


def body(prompt_key_values, queries, routing, lengths, out_weight):
    section_count = lax.axis_size("sec")
    tp_count = lax.axis_size("tp")
    section = lax.axis_index("sec")
    slot_count, samples, query_width = queries.shape[1:]
    heads = query_width // HEAD_SIZE // KEY_VALUE_HEADS
    routing = routing.reshape(-1)
    blocks = queries.reshape(section_count, CAP, samples, KEY_VALUE_HEADS, heads, HEAD_SIZE)
    own_queries = []
    for offset in range(section_count):
        block = lax.dynamic_index_in_dim(blocks, section ^ offset, 0, keepdims=False)
        own_queries.append(swap(block, "sec", offset) if offset else block)

    far = [offset for offset in range(2, section_count)]
    outgoing = pack(routing, prompt_key_values, far, section_count)
    arrived = [
        (offset, order, swap(outgoing[n * CAP + order], "sec", offset))
        for order in range(CAP)
        for n, offset in enumerate(far)
    ]
    *near, whole = pack(routing, prompt_key_values, [1, 0], section_count)
    whole = place(whole, [swap(part, "sec", 1) for part in near], [(1, order) for order in range(CAP)])

    messages = attend(routing, lengths, prompt_key_values, own_queries, tp_count)
    messages = [swap(part, "tp", offset) if offset else part for offset, part in enumerate(messages)]
    share = join(messages, samples)
    shares = [swap(share, "tp", offset) if offset else share for offset in range(tp_count)]
    if share.ndim == 3:
        tp_index = lax.axis_index("tp")
        stacked = jnp.stack(shares)[jnp.arange(tp_count) ^ tp_index]
        stacked = stacked.reshape(REQ_GRP, KEY_VALUE_HEADS, samples, -1).transpose(0, 2, 1, 3)
        attended = stacked.reshape(REQ_GRP * samples, query_width)
        layer_out = jnp.dot(attended, out_weight, preferred_element_type=jnp.float32)
        layer_out = layer_out.astype(jnp.bfloat16).reshape(REQ_GRP, samples, -1)
    else:
        layer_out = project(shares, out_weight, samples)

    half = len(arrived) // 2
    for some in (arrived[:half], arrived[half:]):
        whole = place(whole, [part for _, _, part in some], [(offset, order) for offset, order, _ in some])
    return (layer_out, whole)


def solution(mesh):
    placed = (
        P(("rep", "sec"), None, "tp", None),
        P(("rep", "sec"), None, None, None),
        P("rep", None),
        P("rep"),
        P(None, "tp"),
    )
    return jax.shard_map(
        body,
        mesh=mesh,
        in_specs=placed,
        out_specs=(P(("rep", "sec"), None, "tp"), P(("rep", "sec"), None, None, "tp", None)),
        check_vma=False,
    )
```

```python
import functools

import jax
import jax.numpy as jnp
from jax import lax
from jax.experimental import pallas as pl
from jax.experimental.pallas import tpu as pltpu
from jax.sharding import PartitionSpec as P

HEAD_SIZE = 128
KEY_VALUE_HEADS = 4
REQ_GRP = 8
CAP = 2
HIDDEN = -1e30

HBM = pl.BlockSpec(memory_space=pltpu.HBM)
VMEM = pl.BlockSpec(memory_space=pltpu.VMEM)
SMEM = pl.BlockSpec(memory_space=pltpu.SMEM)


def limit(mebibytes):
    return pltpu.CompilerParams(vmem_limit_bytes=mebibytes << 20)


def cost(flops, bytes_accessed, transcendentals=0):
    return pl.CostEstimate(flops=flops, bytes_accessed=bytes_accessed, transcendentals=transcendentals)


def swap(value, axis, offset):
    count = lax.axis_size(axis)
    return lax.ppermute(value, axis, [(i, i ^ offset) for i in range(count)])


def scatter(value, axis):
    return lax.all_to_all(value, axis, split_axis=0, concat_axis=0, tiled=True)


def own_slots(routing_ref, section, used, source):
    for t in range(used.shape[0]):
        used[t] = 0
    for i in range(REQ_GRP):
        target = routing_ref[section * REQ_GRP + i]
        order = used[target]
        used[target] = order + 1
        source[target * CAP + order] = i


def pack_kernel(section_count, routing_ref, cache_ref, *refs):
    out_refs, (source, used, sem) = refs[:-3], refs[-3:]
    section = lax.axis_index("sec")
    full = section_count * CAP == REQ_GRP
    own_slots(routing_ref, section, used, source)

    def copy(n, row):
        return pltpu.make_async_copy(cache_ref.at[row], out_refs[n].at[0], sem.at[n])

    for n in reversed(range(section_count * CAP)):
        slot = (section ^ (n // CAP)) * CAP + n % CAP
        if full:
            copy(n, source[slot]).start()
        else:
            filled = n % CAP < used[slot // CAP]

            @pl.when(filled)
            def _():
                copy(n, source[slot]).start()

            @pl.when(jnp.logical_not(filled))
            def _():
                out_refs[n][...] = jnp.zeros_like(out_refs[n])

    for n in reversed(range(section_count * CAP)):
        if full:
            copy(n, 0).wait()
        else:
            slot = (section ^ (n // CAP)) * CAP + n % CAP

            @pl.when(n % CAP < used[slot // CAP])
            def _():
                copy(n, 0).wait()


def pack(routing, cache, section_count):
    slots = section_count * CAP
    return pl.pallas_call(
        functools.partial(pack_kernel, section_count),
        out_shape=[jax.ShapeDtypeStruct((1,) + cache.shape[1:], cache.dtype)] * slots,
        in_specs=[SMEM, HBM],
        out_specs=[VMEM] * slots,
        scratch_shapes=[
            pltpu.SMEM((slots,), jnp.int32),
            pltpu.SMEM((section_count,), jnp.int32),
            pltpu.SemaphoreType.DMA((slots,)),
        ],
        compiler_params=limit(8),
        cost_estimate=cost(0, 4 * cache.size),
        name="pack_cache",
    )(routing, cache)


def place_kernel(slots, *refs):
    count = len(slots)
    part_refs, out_ref, sem = refs[-2 - count : -2], refs[-2], refs[-1]
    section = lax.axis_index("sec")
    copies = []
    for n, (offset, order) in enumerate(slots):
        slot = out_ref.at[0, (section ^ offset) * CAP + order]
        copy = pltpu.make_async_copy(part_refs[n].at[0], slot, sem.at[n])
        copy.start()
        copies.append(copy)
    for copy in copies:
        copy.wait()


def place(whole, parts, slots, slot_count):
    given = [] if whole is None else [whole]
    part = parts[0]
    return pl.pallas_call(
        functools.partial(place_kernel, slots),
        out_shape=jax.ShapeDtypeStruct((1, slot_count) + part.shape[1:], part.dtype),
        in_specs=[HBM] * len(given) + [VMEM] * len(parts),
        out_specs=HBM,
        scratch_shapes=[pltpu.SemaphoreType.DMA((len(parts),))],
        input_output_aliases={0: 0} if given else {},
        compiler_params=limit(8),
        cost_estimate=cost(0, 4 * len(parts) * part.size),
        name="place_cache",
    )(*given, *parts)


def attend_kernel(section_count, routing_ref, lengths_ref, query_ref, *refs):
    slots = section_count * CAP
    cache_refs, message_ref = refs[:slots], refs[slots]
    source, used, stats = refs[slots + 1 :]
    section = lax.axis_index("sec")
    tp_index = lax.axis_index("tp")
    samples, _, heads, _ = query_ref.shape[2:]
    rows = samples * heads
    local = cache_refs[0].shape[2]
    groups = message_ref.shape[1] - 1
    full = slots == REQ_GRP
    own_slots(routing_ref, section, used, source)
    stats[...] = jnp.zeros_like(stats)
    lane = lax.broadcasted_iota(jnp.int32, (rows, HEAD_SIZE), 1)
    position = lax.broadcasted_iota(jnp.int32, (rows, local), 1) + tp_index * local

    def partial(n, k, row):
        columns = pl.ds(pl.multiple_of(k * HEAD_SIZE, HEAD_SIZE), HEAD_SIZE)
        target = section ^ (n // CAP)
        visible = position < lengths_ref[section * REQ_GRP + row]
        query = query_ref[target, n % CAP, :, k].astype(jnp.float32).reshape(rows, HEAD_SIZE)
        score = lax.dot_general(
            query.astype(jnp.bfloat16),
            cache_refs[n][0, 0, :, columns],
            (((1,), (1,)), ((), ())),
            preferred_element_type=jnp.float32,
        ) * HEAD_SIZE ** (-0.5)
        score = jnp.where(visible, score, HIDDEN)
        peak = jnp.max(score, axis=1, keepdims=True)
        weight = jnp.where(visible, jnp.exp(score - peak), 0.0)
        total = jnp.sum(weight, axis=1, keepdims=True)
        mixed = jnp.dot(
            weight.astype(jnp.bfloat16), cache_refs[n][0, 1, :, columns], preferred_element_type=jnp.float32
        )
        some = total > 0.0
        safe = jnp.where(some, total, 1.0)
        return (mixed / safe).astype(jnp.bfloat16), jnp.where(some, peak + jnp.log(safe), HIDDEN)

    def store(k, row, result):
        mixed, level = result
        group = row * KEY_VALUE_HEADS + k
        device, inner = group // groups, group % groups
        message_ref[device, inner] = mixed
        stats[device] = jnp.where(lane == inner, level, stats[device])

    @pl.loop(0, KEY_VALUE_HEADS)
    def _(k):
        if full:
            numbers = [source[(section ^ (n // CAP)) * CAP + n % CAP] for n in range(slots)]
            results = [partial(n, k, row) for n, row in enumerate(numbers)]
            for row, result in zip(numbers, results):
                store(k, row, result)
        else:
            for n in range(slots):
                target = section ^ (n // CAP)

                @pl.when(n % CAP < used[target])
                def _():
                    row = source[target * CAP + n % CAP]
                    store(k, row, partial(n, k, row))

    for device in range(message_ref.shape[0]):
        level = stats[device]
        high = level.astype(jnp.bfloat16).astype(jnp.float32)
        rest = level - high
        middle = rest.astype(jnp.bfloat16).astype(jnp.float32)
        low = rest - middle
        packed = high + pltpu.roll(middle, groups, 1) + pltpu.roll(low, 2 * groups, 1)
        message_ref[device, groups] = packed.astype(jnp.bfloat16)


def attend(routing, lengths, queries, caches, tp_count):
    section_count, _, samples, _, heads, _ = queries.shape
    rows = samples * heads
    groups = REQ_GRP * KEY_VALUE_HEADS // tp_count
    multiplies = REQ_GRP * rows * KEY_VALUE_HEADS * HEAD_SIZE * caches[0].shape[2]
    return pl.pallas_call(
        functools.partial(attend_kernel, section_count),
        out_shape=jax.ShapeDtypeStruct((tp_count, groups + 1, rows, HEAD_SIZE), jnp.bfloat16),
        in_specs=[SMEM, SMEM] + [VMEM] * (1 + len(caches)),
        out_specs=VMEM,
        scratch_shapes=[
            pltpu.SMEM((section_count * CAP,), jnp.int32),
            pltpu.SMEM((section_count,), jnp.int32),
            pltpu.VMEM((tp_count, rows, HEAD_SIZE), jnp.float32),
        ],
        compiler_params=limit(12),
        cost_estimate=cost(4 * multiplies, 2 * len(caches) * caches[0].size, multiplies // HEAD_SIZE),
        name="attend",
    )(routing, lengths, queries, *caches)


def join_kernel(message_ref, out_ref, joined, flat):
    count, groups, rows, span = message_ref.shape
    groups -= 1
    samples = flat.shape[-2] if len(flat.shape) == 3 else flat.shape[0] // (groups // KEY_VALUE_HEADS)
    heads = rows // samples
    levels = []
    for n in range(count):
        packed = message_ref[n, groups].astype(jnp.float32)
        levels.append(packed + pltpu.roll(packed, span - groups, 1) + pltpu.roll(packed, span - 2 * groups, 1))
    summit = functools.reduce(jnp.maximum, levels)
    scales = [jnp.exp(level - summit) for level in levels]
    total = functools.reduce(jnp.add, scales)
    scales = [scale / total for scale in scales]
    for inner in range(groups):
        terms = [message_ref[n, inner].astype(jnp.float32) * scales[n][:, inner : inner + 1] for n in range(count)]
        joined[inner] = functools.reduce(jnp.add, terms)
    for inner in range(groups):
        for head in range(heads):
            block = joined[inner, pl.ds(head, samples, stride=heads), :]
            if len(flat.shape) == 2:
                row = inner // KEY_VALUE_HEADS * samples
                column = (inner % KEY_VALUE_HEADS * heads + head) * HEAD_SIZE
                flat[row : row + samples, column : column + HEAD_SIZE] = block
            else:
                flat[inner, :, head * HEAD_SIZE : (head + 1) * HEAD_SIZE] = block
    rounded = flat[...].astype(jnp.bfloat16)
    for n in range(count):
        out_ref[n] = rounded


def join(messages, samples):
    count, groups, rows, _ = messages.shape
    groups -= 1
    width = rows // samples * HEAD_SIZE
    if groups % KEY_VALUE_HEADS == 0:
        shape = (groups // KEY_VALUE_HEADS * samples, KEY_VALUE_HEADS * width)
    else:
        shape = (groups, samples, width)
    return pl.pallas_call(
        join_kernel,
        out_shape=jax.ShapeDtypeStruct((count,) + shape, jnp.bfloat16),
        in_specs=[VMEM],
        out_specs=VMEM,
        scratch_shapes=[
            pltpu.VMEM((groups, rows, HEAD_SIZE), jnp.float32),
            pltpu.VMEM(shape, jnp.float32),
        ],
        compiler_params=limit(8),
        cost_estimate=cost(4 * messages.size, 2 * messages.size),
        name="join",
    )(messages)


def project_kernel(left_ref, weight_ref, out_ref):
    count, share, depth = left_ref.shape
    left = left_ref[...].astype(jnp.float32).reshape(count * share, depth).astype(jnp.bfloat16)
    result = jnp.dot(left, weight_ref[...], preferred_element_type=jnp.float32)
    prompts, samples, _ = out_ref.shape
    for n in range(prompts):
        out_ref[n] = result[n * samples : (n + 1) * samples].astype(out_ref.dtype)


def project(left, weight, samples):
    count, share, depth = left.shape
    prompts = count * share // samples
    width = weight.shape[1]
    tile = min(256, width)
    return pl.pallas_call(
        project_kernel,
        grid=(width // tile,),
        out_shape=jax.ShapeDtypeStruct((prompts, samples, width), jnp.bfloat16),
        in_specs=[
            pl.BlockSpec(left.shape, lambda n: (0, 0, 0)),
            pl.BlockSpec((depth, tile), lambda n: (0, n)),
        ],
        out_specs=pl.BlockSpec((prompts, samples, tile), lambda n: (0, 0, n)),
        compiler_params=limit(16),
        cost_estimate=cost(2 * left.size * width, 2 * depth * width),
        name="project",
    )(left, weight)


def body(prompt_key_values, queries, routing, lengths, out_weight):
    section_count = lax.axis_size("sec")
    tp_count = lax.axis_size("tp")
    slot_count, samples, query_width = queries.shape[1:]
    heads = query_width // HEAD_SIZE // KEY_VALUE_HEADS
    routing = routing.reshape(-1)
    own_queries = scatter(
        queries.reshape(section_count, CAP, samples, KEY_VALUE_HEADS, heads, HEAD_SIZE), "sec"
    )

    packed = pack(routing, prompt_key_values, section_count)
    slots = [(n // CAP, n % CAP) for n in range(slot_count)]
    arrived = {
        (offset, order): swap(part, "sec", offset) if offset else part
        for (offset, order), part in zip(slots, packed)
    }

    messages = attend(routing, lengths, own_queries, packed, tp_count)
    shares = scatter(join(scatter(messages, "tp"), samples), "tp")
    if shares.ndim == 4:
        attended = shares.reshape(REQ_GRP, KEY_VALUE_HEADS, samples, -1).transpose(0, 2, 1, 3)
        attended = attended.reshape(REQ_GRP * samples, query_width)
        layer_out = jnp.dot(attended, out_weight, preferred_element_type=jnp.float32)
        layer_out = layer_out.astype(jnp.bfloat16).reshape(REQ_GRP, samples, -1)
    else:
        layer_out = project(shares, out_weight, samples)

    whole = None
    for stage in (
        [slot for slot in slots if slot[0] < 2],
        [slot for slot in slots if slot[0] >= 2 and slot[1] == 0],
        [slot for slot in slots if slot[0] >= 2 and slot[1] == 1],
    ):
        whole = place(whole, [arrived[slot] for slot in stage], stage, slot_count)
    return (layer_out, whole)


def solution(mesh):
    placed = (
        P(("rep", "sec"), None, "tp", None),
        P(("rep", "sec"), None, None, None),
        P("rep", None),
        P("rep"),
        P(None, "tp"),
    )
    return jax.shard_map(
        body,
        mesh=mesh,
        in_specs=placed,
        out_specs=(P(("rep", "sec"), None, "tp"), P(("rep", "sec"), None, None, "tp", None)),
        check_vma=False,
    )
```

```python
import functools

import jax
import jax.numpy as jnp
from jax import lax
from jax.experimental import pallas as pl
from jax.experimental.pallas import tpu as pltpu
from jax.sharding import PartitionSpec as P

HEAD_SIZE = 128
KEY_VALUE_HEADS = 4
REQ_GRP = 8
CAP = 2
HIDDEN = -1e30
SPLIT_LIMIT = 8
PACK_LIMIT = 48
FETCH_LIMIT = 36

ANY = pl.BlockSpec(memory_space=pl.ANY)
HBM = pl.BlockSpec(memory_space=pltpu.HBM)
VMEM = pl.BlockSpec(memory_space=pltpu.VMEM)
SMEM = pl.BlockSpec(memory_space=pltpu.SMEM)


def limit(mebibytes):
    return pltpu.CompilerParams(vmem_limit_bytes=mebibytes << 20)


def cost(flops, bytes_accessed, transcendentals=0):
    return pl.CostEstimate(flops=flops, bytes_accessed=bytes_accessed, transcendentals=transcendentals)


def swap(value, axis, offset):
    if offset == 0:
        return value
    count = lax.axis_size(axis)
    return lax.ppermute(value, axis, [(i, i ^ offset) for i in range(count)])


def own_slots(routing_ref, section, used, source):
    for t in range(used.shape[0]):
        used[t] = 0
    for i in range(REQ_GRP):
        target = routing_ref[section * REQ_GRP + i]
        order = used[target]
        used[target] = order + 1
        source[target * CAP + order] = i


def split_kernel(section_count, query_ref, *refs):
    out_refs, sem = refs[:section_count], refs[section_count]
    section = lax.axis_index("sec")
    copies = []
    for offset in range(section_count):
        part = query_ref.at[0, pl.ds((section ^ offset) * CAP, CAP)]
        copies.append(pltpu.make_async_copy(part, out_refs[offset], sem.at[offset]))
        copies[-1].start()
    for copy in copies:
        copy.wait()


def split(queries, section_count):
    part = jax.ShapeDtypeStruct((CAP,) + queries.shape[2:], queries.dtype)
    return pl.pallas_call(
        functools.partial(split_kernel, section_count),
        out_shape=[part] * section_count,
        in_specs=[HBM],
        out_specs=[VMEM] * section_count,
        scratch_shapes=[pltpu.SemaphoreType.DMA((section_count,))],
        compiler_params=limit(SPLIT_LIMIT),
        cost_estimate=cost(0, 4 * queries.size),
        name="split",
    )(queries)


def pack_kernel(section_count, routing_ref, cache_ref, *refs):
    cache_out, (source, used, sem) = refs[-3 - section_count : -3], refs[-3:]
    section = lax.axis_index("sec")
    full = section_count * CAP == REQ_GRP
    own_slots(routing_ref, section, used, source)
    slots = [(offset, order) for offset in reversed(range(section_count)) for order in range(CAP)]

    def copy(offset, order, row):
        return pltpu.make_async_copy(
            cache_ref.at[row], cache_out[offset].at[order], sem.at[offset * CAP + order]
        )

    for offset, order in slots:
        target = section ^ offset
        if full:
            copy(offset, order, source[target * CAP + order]).start()
        else:

            @pl.when(order < used[target])
            def _():
                copy(offset, order, source[target * CAP + order]).start()

            @pl.when(order >= used[target])
            def _():
                cache_out[offset][order] = jnp.zeros_like(cache_out[offset][order])

    for offset, order in slots:
        if full:
            copy(offset, order, 0).wait()
        else:

            @pl.when(order < used[section ^ offset])
            def _():
                copy(offset, order, 0).wait()


def pack(routing, cache, others, section_count):
    slots = section_count * CAP
    cache_part = jax.ShapeDtypeStruct((CAP,) + cache.shape[1:], cache.dtype)
    return pl.pallas_call(
        functools.partial(pack_kernel, section_count),
        out_shape=[cache_part] * section_count,
        in_specs=[SMEM, HBM] + [ANY] * len(others),
        out_specs=[VMEM] * section_count,
        scratch_shapes=[
            pltpu.SMEM((slots,), jnp.int32),
            pltpu.SMEM((section_count,), jnp.int32),
            pltpu.SemaphoreType.DMA((slots,)),
        ],
        compiler_params=limit(PACK_LIMIT),
        cost_estimate=cost(0, 4 * cache.size),
        name="pack",
    )(routing, cache, *others)


def gate_kernel(*refs):
    pass


def gate(values, others):
    count = len(values)
    return pl.pallas_call(
        gate_kernel,
        out_shape=[jax.ShapeDtypeStruct(value.shape, value.dtype) for value in values],
        in_specs=[ANY] * (count + len(others)),
        out_specs=[ANY] * count,
        input_output_aliases={n: n for n in range(count)},
        compiler_params=limit(1),
        cost_estimate=cost(0, 0),
        name="gate",
    )(*values, *others)


def place_kernel(offsets, *refs):
    count = len(offsets)
    part_refs, out_ref, sem = refs[-2 - count : -2], refs[-2], refs[-1]
    section = lax.axis_index("sec")
    copies = []
    for n, offset in enumerate(offsets):
        for order in range(CAP):
            slot = out_ref.at[0, (section ^ offset) * CAP + order]
            copy = pltpu.make_async_copy(part_refs[n].at[order], slot, sem.at[n * CAP + order])
            copy.start()
            copies.append(copy)
    for copy in copies:
        copy.wait()


def place(given, parts, offsets, slot_count):
    part = parts[0]
    return pl.pallas_call(
        functools.partial(place_kernel, offsets),
        out_shape=jax.ShapeDtypeStruct((1, slot_count) + part.shape[1:], part.dtype),
        in_specs=[HBM] * len(given) + [VMEM] * len(parts),
        out_specs=HBM,
        scratch_shapes=[pltpu.SemaphoreType.DMA((len(parts) * CAP,))],
        input_output_aliases={0: 0} if given else {},
        compiler_params=limit(8),
        cost_estimate=cost(0, 4 * len(parts) * part.size),
        name="place",
    )(*given, *parts)


def attend_kernel(section_count, tp_count, routing_ref, lengths_ref, *refs):
    cache_refs, query_refs = refs[:section_count], refs[section_count : 2 * section_count]
    message_refs = refs[-5 - tp_count : -5]
    source, used, messages, stats, stacked = refs[-5:]
    section = lax.axis_index("sec")
    tp_index = lax.axis_index("tp")
    local = cache_refs[0].shape[2]
    groups, rows, _ = messages.shape[1:]
    span = KEY_VALUE_HEADS * rows
    prompts = max(1, groups // KEY_VALUE_HEADS)
    full = section_count * CAP == REQ_GRP
    own_slots(routing_ref, section, used, source)
    position = lax.broadcasted_iota(jnp.int32, (local, span), 0) + tp_index * local
    owner = lax.broadcasted_iota(jnp.int32, (HEAD_SIZE, span), 1) // rows

    def prompt(offset, order):
        row = source[(section ^ offset) * CAP + order]
        visible = position < lengths_ref[section * REQ_GRP + row]
        values = query_refs[offset][order].astype(jnp.float32)
        samples = values.shape[0]
        slot = offset * CAP + order
        for head in range(span // samples):
            stacked[slot, head * samples : (head + 1) * samples] = values[:, head * HEAD_SIZE : (head + 1) * HEAD_SIZE]
        query = stacked[slot].T.astype(jnp.bfloat16)
        query = [jnp.where(owner == k, query, jnp.zeros_like(query)) for k in range(KEY_VALUE_HEADS)]
        score = jnp.dot(
            cache_refs[offset][order, 0], jnp.concatenate(query, axis=0), preferred_element_type=jnp.float32
        ) * HEAD_SIZE ** (-0.5)
        score = jnp.where(visible, score, HIDDEN)
        peak = jnp.max(score, axis=0, keepdims=True)
        weight = jnp.where(visible, jnp.exp(score - peak), 0.0)
        total = jnp.sum(weight, axis=0, keepdims=True)
        some = total > 0.0
        safe = jnp.where(some, total, 1.0)
        stats[pl.ds(row, 1)] = jnp.where(some, peak + jnp.log(safe), HIDDEN)
        weight = (weight * (1.0 / safe)).T.astype(jnp.bfloat16)
        for k in range(KEY_VALUE_HEADS):
            mixed = jnp.dot(
                weight[k * rows : (k + 1) * rows],
                cache_refs[offset][order, 1, :, k * HEAD_SIZE : (k + 1) * HEAD_SIZE],
                preferred_element_type=jnp.float32,
            )
            group = row * KEY_VALUE_HEADS + k
            messages[group // groups, group % groups] = mixed.astype(jnp.bfloat16)

    for offset in range(section_count):
        for order in range(CAP):
            if full:
                prompt(offset, order)
            else:
                pl.when(order < used[section ^ offset])(functools.partial(prompt, offset, order))

    level = stats[...]
    high = level.astype(jnp.bfloat16).astype(jnp.float32)
    rest = level - high
    middle = rest.astype(jnp.bfloat16).astype(jnp.float32)
    stats[...] = high
    stats_middle, stats_low = middle, rest - middle
    for offset in range(tp_count):
        device = tp_index ^ offset
        message_refs[offset][0:groups] = messages[device]
        message_refs[offset][groups] = jnp.zeros((rows, HEAD_SIZE), jnp.bfloat16)
    for part, values in enumerate((high, stats_middle, stats_low)):
        stats[...] = values
        for offset in range(tp_count):
            first = (tp_index ^ offset) * groups // KEY_VALUE_HEADS
            block = jnp.concatenate(
                [stats[pl.ds(first + n, 1)] for n in range(prompts)]
                + [jnp.zeros((16 - prompts, span), jnp.float32)],
                axis=0,
            )
            if part < 2:
                message_refs[offset][groups, part * 16 : part * 16 + 16] = block.astype(jnp.bfloat16)
            else:
                message_refs[offset][groups + 1] = jnp.concatenate([block, jnp.zeros_like(block)], axis=0).astype(
                    jnp.bfloat16
                )


def attend(routing, lengths, caches, queries, others, tp_count):
    section_count = len(caches)
    samples, width = queries[0].shape[1:]
    span = width // HEAD_SIZE * samples
    rows = span // KEY_VALUE_HEADS
    groups = REQ_GRP * KEY_VALUE_HEADS // tp_count
    multiplies = REQ_GRP * span * HEAD_SIZE * caches[0].shape[2]
    return pl.pallas_call(
        functools.partial(attend_kernel, section_count, tp_count),
        out_shape=[jax.ShapeDtypeStruct((groups + 2, rows, HEAD_SIZE), jnp.bfloat16)] * tp_count,
        in_specs=[SMEM, SMEM] + [VMEM] * (2 * section_count) + [ANY] * len(others),
        out_specs=[VMEM] * tp_count,
        scratch_shapes=[
            pltpu.SMEM((section_count * CAP,), jnp.int32),
            pltpu.SMEM((section_count,), jnp.int32),
            pltpu.VMEM((tp_count, groups, rows, HEAD_SIZE), jnp.bfloat16),
            pltpu.VMEM((REQ_GRP, span), jnp.float32),
            pltpu.VMEM((section_count * CAP, span, HEAD_SIZE), jnp.float32),
        ],
        compiler_params=limit(12),
        cost_estimate=cost(4 * multiplies, 2 * section_count * caches[0].size, multiplies // HEAD_SIZE),
        name="attend",
    )(routing, lengths, *caches, *queries, *others)


def join_kernel(count, samples, *refs):
    message_refs, (out_ref, scaling, flat) = refs[:count], refs[-3:]
    groups, rows, _ = message_refs[0].shape
    groups -= 2
    heads = rows // samples
    tp_index = lax.axis_index("tp")
    levels = []
    for ref in message_refs:
        upper = ref[groups].astype(jnp.float32)
        lower = ref[groups + 1].astype(jnp.float32)
        levels.append(upper[0:8] + upper[16:24] + lower[0:8])
    summit = functools.reduce(jnp.maximum, levels)
    scales = [jnp.exp(level - summit) for level in levels]
    total = functools.reduce(jnp.add, scales)
    for n, scale in enumerate(scales):
        scaling[n] = (scale / total).T
    for inner in range(groups):
        if groups % KEY_VALUE_HEADS:
            first = (tp_index * groups + inner) % KEY_VALUE_HEADS * rows
            part = pl.ds(pl.multiple_of(first, rows), rows)
        else:
            part = pl.ds(inner % KEY_VALUE_HEADS * rows, rows)
        prompt = inner // KEY_VALUE_HEADS
        terms = [
            ref[inner].astype(jnp.float32) * scaling[n, part, prompt : prompt + 1]
            for n, ref in enumerate(message_refs)
        ]
        joined = functools.reduce(jnp.add, terms)
        for head in range(heads):
            block = joined[head * samples : (head + 1) * samples]
            if len(flat.shape) == 2:
                row = prompt * samples
                column = (inner % KEY_VALUE_HEADS * heads + head) * HEAD_SIZE
                flat[row : row + samples, column : column + HEAD_SIZE] = block
            else:
                flat[inner, :, head * HEAD_SIZE : (head + 1) * HEAD_SIZE] = block
    out_ref[...] = flat[...].astype(jnp.bfloat16)


def join(messages, others, samples):
    groups, rows, _ = messages[0].shape
    groups -= 2
    width = rows // samples * HEAD_SIZE
    if groups % KEY_VALUE_HEADS == 0:
        shape = (groups // KEY_VALUE_HEADS * samples, KEY_VALUE_HEADS * width)
    else:
        shape = (groups, samples, width)
    count = len(messages)
    return pl.pallas_call(
        functools.partial(join_kernel, count, samples),
        out_shape=jax.ShapeDtypeStruct(shape, jnp.bfloat16),
        in_specs=[VMEM] * count + [ANY] * len(others),
        out_specs=VMEM,
        scratch_shapes=[
            pltpu.VMEM((count, KEY_VALUE_HEADS * rows, 8), jnp.float32),
            pltpu.VMEM(shape, jnp.float32),
        ],
        compiler_params=limit(8),
        cost_estimate=cost(4 * count * messages[0].size, 2 * count * messages[0].size),
        name="join",
    )(*messages, *others)


def fetch_kernel(weight_ref, *refs):
    out_ref, sem = refs[-2:]
    copies = []
    step = weight_ref.shape[0] // sem.shape[0]
    for n in range(sem.shape[0]):
        part = pl.ds(n * step, step)
        copies.append(pltpu.make_async_copy(weight_ref.at[part], out_ref.at[part], sem.at[n]))
        copies[-1].start()
    for copy in copies:
        copy.wait()


def fetch(weight, others):
    return pl.pallas_call(
        fetch_kernel,
        out_shape=jax.ShapeDtypeStruct(weight.shape, weight.dtype),
        in_specs=[HBM] + [ANY] * len(others),
        out_specs=VMEM,
        scratch_shapes=[pltpu.SemaphoreType.DMA((8,))],
        compiler_params=limit(FETCH_LIMIT),
        cost_estimate=cost(0, 4 * weight.size),
        name="fetch",
    )(weight, *others)


def project_kernel(count, tile, *refs):
    part_refs, weight_ref, out_ref = refs[:count], refs[count], refs[count + 1]
    tp_index = lax.axis_index("tp")
    prompts, samples, width = out_ref.shape
    share = prompts // count
    left = jnp.concatenate([ref[...].astype(jnp.float32) for ref in part_refs], axis=0).astype(jnp.bfloat16)
    for first in range(0, width, tile):
        result = jnp.dot(left, weight_ref[:, first : first + tile], preferred_element_type=jnp.float32)
        for offset in range(count):
            for n in range(share):
                row = (offset * share + n) * samples
                block = result[row : row + samples].astype(out_ref.dtype)
                out_ref[(tp_index ^ offset) * share + n, :, first : first + tile] = block


def project(parts, weight, samples):
    count = len(parts)
    depth, width = weight.shape
    total = count * parts[0].shape[0]
    return pl.pallas_call(
        functools.partial(project_kernel, count, min(256, width)),
        out_shape=jax.ShapeDtypeStruct((total // samples, samples, width), jnp.bfloat16),
        in_specs=[VMEM] * (count + 1),
        out_specs=VMEM,
        compiler_params=limit(24),
        cost_estimate=cost(2 * total * depth * width, 2 * depth * width),
        name="project",
    )(*parts, weight)


def body(prompt_key_values, queries, routing, lengths, out_weight):
    section_count = lax.axis_size("sec")
    tp_count = lax.axis_size("tp")
    slot_count, samples, query_width = queries.shape[1:]
    routing = routing.reshape(-1)

    query_parts = split(queries, section_count)
    own_queries = [swap(part, "sec", offset) for offset, part in enumerate(query_parts)]
    caches = pack(routing, prompt_key_values, query_parts[:1], section_count)
    caches = caches[:1] + gate(caches[1:], own_queries[1:])
    arrived = [swap(part, "sec", offset) for offset, part in enumerate(caches)]
    messages = attend(routing, lengths, caches, own_queries, arrived[1:2], tp_count)
    partials = [swap(part, "tp", offset) for offset, part in enumerate(messages)]
    held_weight = fetch(out_weight, messages[:1])
    share = join(partials, [held_weight], samples)
    shares = [swap(share, "tp", offset) for offset in range(tp_count)]
    if share.ndim == 3:
        attended = jnp.stack(shares)[jnp.arange(tp_count) ^ lax.axis_index("tp")]
        attended = attended.reshape(REQ_GRP, KEY_VALUE_HEADS, samples, -1).transpose(0, 2, 1, 3)
        attended = attended.reshape(REQ_GRP * samples, query_width)
        layer_out = jnp.dot(attended, out_weight, preferred_element_type=jnp.float32)
        layer_out = layer_out.astype(jnp.bfloat16).reshape(REQ_GRP, samples, -1)
    else:
        layer_out = project(shares, held_weight, samples)

    whole = place([], arrived[:2], [0, 1], slot_count)
    for offset in range(2, section_count):
        whole = place([whole, layer_out], arrived[offset : offset + 1], [offset], slot_count)
    return (layer_out, whole)


def solution(mesh):
    placed = (
        P(("rep", "sec"), None, "tp", None),
        P(("rep", "sec"), None, None, None),
        P("rep", None),
        P("rep"),
        P(None, "tp"),
    )
    return jax.shard_map(
        body,
        mesh=mesh,
        in_specs=placed,
        out_specs=(P(("rep", "sec"), None, "tp"), P(("rep", "sec"), None, None, "tp", None)),
        check_vma=False,
    )
```

```python
import functools

import jax
import jax.numpy as jnp
from jax import lax
from jax.experimental import pallas as pl
from jax.experimental.pallas import tpu as pltpu
from jax.sharding import PartitionSpec as P

HEAD_SIZE = 128
KEY_VALUE_HEADS = 4
REQ_GRP = 8
CAP = 2
HIDDEN = -1e30

ANY = pl.BlockSpec(memory_space=pl.ANY)
HBM = pl.BlockSpec(memory_space=pltpu.HBM)
VMEM = pl.BlockSpec(memory_space=pltpu.VMEM)
SMEM = pl.BlockSpec(memory_space=pltpu.SMEM)


def limit(mebibytes):
    return pltpu.CompilerParams(vmem_limit_bytes=mebibytes << 20)


def cost(flops, bytes_accessed, transcendentals=0):
    return pl.CostEstimate(flops=flops, bytes_accessed=bytes_accessed, transcendentals=transcendentals)


def swap(value, axis, offset):
    if offset == 0:
        return value
    count = lax.axis_size(axis)
    return lax.ppermute(value, axis, [(i, i ^ offset) for i in range(count)])


def own_slots(routing_ref, section, used, source):
    for t in range(used.shape[0]):
        used[t] = 0
    for i in range(REQ_GRP):
        target = routing_ref[section * REQ_GRP + i]
        order = used[target]
        used[target] = order + 1
        source[target * CAP + order] = i


def pack_kernel(pieces, section_count, routing_ref, cache_ref, *refs):
    refs, (source, used, sem, query_sem) = refs[:-4], refs[-4:]
    query_ref, refs = (refs[0], refs[1:]) if len(refs) > len(pieces) else (None, refs)
    cache_out, query_out = refs[: len(pieces)], refs[len(pieces) :]
    section = lax.axis_index("sec")
    full = section_count * CAP == REQ_GRP
    query_copies = []
    for offset, out_ref in enumerate(query_out):
        part = query_ref.at[0, pl.ds((section ^ offset) * CAP, CAP)]
        query_copies.append(pltpu.make_async_copy(part, out_ref, query_sem.at[offset]))
        query_copies[-1].start()
    own_slots(routing_ref, section, used, source)

    def copy(n, spot, row):
        offset, order, place = spot
        return pltpu.make_async_copy(cache_ref.at[row], cache_out[n].at[place], sem.at[offset * CAP + order])

    spots = [
        (n, (offset, first + place, place))
        for n, (offset, first, count) in enumerate(pieces)
        for place in range(count)
    ]
    for n, spot in spots:
        offset, order, place = spot
        target = section ^ offset
        if full:
            copy(n, spot, source[target * CAP + order]).start()
        else:

            @pl.when(order < used[target])
            def _():
                copy(n, spot, source[target * CAP + order]).start()

            @pl.when(order >= used[target])
            def _():
                cache_out[n][place] = jnp.zeros_like(cache_out[n][place])

    for n, spot in spots:
        if full:
            copy(n, spot, 0).wait()
        else:

            @pl.when(spot[1] < used[section ^ spot[0]])
            def _():
                copy(n, spot, 0).wait()

    for query_copy in query_copies:
        query_copy.wait()


def in_hbm(value):
    return pltpu.with_memory_space_constraint(value, pltpu.HBM)


def pack(routing, cache, queries, pieces, section_count):
    slots = section_count * CAP
    shapes = [jax.ShapeDtypeStruct((count,) + cache.shape[1:], cache.dtype) for _, _, count in pieces]
    moved = sum(shape.size for shape in shapes)
    for query in queries:
        shapes += [jax.ShapeDtypeStruct((CAP,) + query.shape[2:], query.dtype)] * section_count
        moved += query.size
    return pl.pallas_call(
        functools.partial(pack_kernel, pieces, section_count),
        out_shape=shapes,
        in_specs=[SMEM, HBM] + [HBM] * len(queries),
        out_specs=[VMEM] * len(shapes),
        scratch_shapes=[
            pltpu.SMEM((slots,), jnp.int32),
            pltpu.SMEM((section_count,), jnp.int32),
            pltpu.SemaphoreType.DMA((slots,)),
            pltpu.SemaphoreType.DMA((section_count,)),
        ],
        compiler_params=limit(16),
        cost_estimate=cost(0, 4 * moved),
        name="pack",
    )(in_hbm(routing), in_hbm(cache), *[in_hbm(query) for query in queries])


def place_kernel(pieces, *refs):
    count = len(pieces)
    part_refs, out_ref, sem = refs[-2 - count : -2], refs[-2], refs[-1]
    section = lax.axis_index("sec")
    copies = []
    for n, (offset, first, size) in enumerate(pieces):
        slots = out_ref.at[0, pl.ds((section ^ offset) * CAP + first, size)]
        copies.append(pltpu.make_async_copy(part_refs[n], slots, sem.at[n]))
        copies[-1].start()
    for copy in copies:
        copy.wait()


def place(given, parts, pieces, slot_count):
    part = parts[0]
    return pl.pallas_call(
        functools.partial(place_kernel, pieces),
        out_shape=jax.ShapeDtypeStruct((1, slot_count) + part.shape[1:], part.dtype),
        in_specs=[HBM] * len(given) + [VMEM] * len(parts),
        out_specs=HBM,
        scratch_shapes=[pltpu.SemaphoreType.DMA((len(parts),))],
        input_output_aliases={1: 0} if len(given) > 1 else {},
        compiler_params=limit(8),
        cost_estimate=cost(0, 4 * sum(piece.size for piece in parts)),
        name="place",
    )(*[in_hbm(value) for value in given], *parts)


def attend_kernel(pieces, section_count, tp_count, routing_ref, lengths_ref, *refs):
    cache_refs, query_refs = refs[: len(pieces)], refs[len(pieces) : len(pieces) + section_count]
    message_refs = refs[-5 - tp_count : -5]
    source, used, messages, stats, stacked = refs[-5:]
    section = lax.axis_index("sec")
    tp_index = lax.axis_index("tp")
    local = cache_refs[0].shape[2]
    groups, rows, _ = messages.shape[1:]
    span = KEY_VALUE_HEADS * rows
    prompts = max(1, groups // KEY_VALUE_HEADS)
    full = section_count * CAP == REQ_GRP
    own_slots(routing_ref, section, used, source)
    position = lax.broadcasted_iota(jnp.int32, (local, span), 0) + tp_index * local
    owner = lax.broadcasted_iota(jnp.int32, (HEAD_SIZE, span), 1) // rows

    def prompt(cache_ref, place, offset, order):
        row = source[(section ^ offset) * CAP + order]
        visible = position < lengths_ref[section * REQ_GRP + row]
        values = query_refs[offset][order].astype(jnp.float32)
        samples = values.shape[0]
        slot = offset * CAP + order
        for head in range(span // samples):
            stacked[slot, head * samples : (head + 1) * samples] = values[:, head * HEAD_SIZE : (head + 1) * HEAD_SIZE]
        query = stacked[slot].T.astype(jnp.bfloat16)
        query = [jnp.where(owner == k, query, jnp.zeros_like(query)) for k in range(KEY_VALUE_HEADS)]
        score = jnp.dot(
            cache_ref[place, 0], jnp.concatenate(query, axis=0), preferred_element_type=jnp.float32
        ) * HEAD_SIZE ** (-0.5)
        score = jnp.where(visible, score, HIDDEN)
        peak = jnp.max(score, axis=0, keepdims=True)
        weight = jnp.where(visible, jnp.exp(score - peak), 0.0)
        total = jnp.sum(weight, axis=0, keepdims=True)
        some = total > 0.0
        safe = jnp.where(some, total, 1.0)
        stats[pl.ds(row, 1)] = jnp.where(some, peak + jnp.log(safe), HIDDEN)
        weight = (weight * (1.0 / safe)).T.astype(jnp.bfloat16)
        for k in range(KEY_VALUE_HEADS):
            mixed = jnp.dot(
                weight[k * rows : (k + 1) * rows],
                cache_ref[place, 1, :, k * HEAD_SIZE : (k + 1) * HEAD_SIZE],
                preferred_element_type=jnp.float32,
            )
            group = row * KEY_VALUE_HEADS + k
            messages[group // groups, group % groups] = mixed.astype(jnp.bfloat16)

    for cache_ref, (offset, first, size) in zip(cache_refs, pieces):
        for place in range(size):
            one = functools.partial(prompt, cache_ref, place, offset, first + place)
            if full:
                one()
            else:
                pl.when(first + place < used[section ^ offset])(one)

    level = stats[...]
    high = level.astype(jnp.bfloat16).astype(jnp.float32)
    rest = level - high
    middle = rest.astype(jnp.bfloat16).astype(jnp.float32)
    stats[...] = high
    stats_middle, stats_low = middle, rest - middle
    for offset in range(tp_count):
        device = tp_index ^ offset
        message_refs[offset][0:groups] = messages[device]
        message_refs[offset][groups] = jnp.zeros((rows, HEAD_SIZE), jnp.bfloat16)
    for part, values in enumerate((high, stats_middle, stats_low)):
        stats[...] = values
        for offset in range(tp_count):
            first = (tp_index ^ offset) * groups // KEY_VALUE_HEADS
            block = jnp.concatenate(
                [stats[pl.ds(first + n, 1)] for n in range(prompts)]
                + [jnp.zeros((16 - prompts, span), jnp.float32)],
                axis=0,
            )
            if part < 2:
                message_refs[offset][groups, part * 16 : part * 16 + 16] = block.astype(jnp.bfloat16)
            else:
                message_refs[offset][groups + 1] = jnp.concatenate([block, jnp.zeros_like(block)], axis=0).astype(
                    jnp.bfloat16
                )


def attend(routing, lengths, caches, pieces, queries, tp_count):
    section_count = len(queries)
    samples, width = queries[0].shape[1:]
    span = width // HEAD_SIZE * samples
    rows = span // KEY_VALUE_HEADS
    groups = REQ_GRP * KEY_VALUE_HEADS // tp_count
    multiplies = REQ_GRP * span * HEAD_SIZE * caches[0].shape[2]
    return pl.pallas_call(
        functools.partial(attend_kernel, pieces, section_count, tp_count),
        out_shape=[jax.ShapeDtypeStruct((groups + 2, rows, HEAD_SIZE), jnp.bfloat16)] * tp_count,
        in_specs=[SMEM, SMEM] + [VMEM] * (len(caches) + section_count),
        out_specs=[VMEM] * tp_count,
        scratch_shapes=[
            pltpu.SMEM((section_count * CAP,), jnp.int32),
            pltpu.SMEM((section_count,), jnp.int32),
            pltpu.VMEM((tp_count, groups, rows, HEAD_SIZE), jnp.bfloat16),
            pltpu.VMEM((REQ_GRP, span), jnp.float32),
            pltpu.VMEM((section_count * CAP, span, HEAD_SIZE), jnp.float32),
        ],
        compiler_params=limit(12),
        cost_estimate=cost(2 * 10**10, 2 * sum(part.size for part in caches), multiplies // HEAD_SIZE),
        name="attend",
    )(routing, lengths, *caches, *queries)


def join_kernel(count, samples, *refs):
    message_refs, (out_ref, scaling, flat) = refs[:count], refs[-3:]
    groups, rows, _ = message_refs[0].shape
    groups -= 2
    heads = rows // samples
    tp_index = lax.axis_index("tp")
    levels = []
    for ref in message_refs:
        upper = ref[groups].astype(jnp.float32)
        lower = ref[groups + 1].astype(jnp.float32)
        levels.append(upper[0:8] + upper[16:24] + lower[0:8])
    summit = functools.reduce(jnp.maximum, levels)
    scales = [jnp.exp(level - summit) for level in levels]
    total = functools.reduce(jnp.add, scales)
    for n, scale in enumerate(scales):
        scaling[n] = (scale / total).T
    for inner in range(groups):
        if groups % KEY_VALUE_HEADS:
            first = (tp_index * groups + inner) % KEY_VALUE_HEADS * rows
            part = pl.ds(pl.multiple_of(first, rows), rows)
        else:
            part = pl.ds(inner % KEY_VALUE_HEADS * rows, rows)
        prompt = inner // KEY_VALUE_HEADS
        terms = [
            ref[inner].astype(jnp.float32) * scaling[n, part, prompt : prompt + 1]
            for n, ref in enumerate(message_refs)
        ]
        joined = functools.reduce(jnp.add, terms)
        for head in range(heads):
            block = joined[head * samples : (head + 1) * samples]
            if len(flat.shape) == 2:
                row = prompt * samples
                column = (inner % KEY_VALUE_HEADS * heads + head) * HEAD_SIZE
                flat[row : row + samples, column : column + HEAD_SIZE] = block
            else:
                flat[inner, :, head * HEAD_SIZE : (head + 1) * HEAD_SIZE] = block
    out_ref[...] = flat[...].astype(jnp.bfloat16)


def join(messages, others, samples):
    groups, rows, _ = messages[0].shape
    groups -= 2
    width = rows // samples * HEAD_SIZE
    if groups % KEY_VALUE_HEADS == 0:
        shape = (groups // KEY_VALUE_HEADS * samples, KEY_VALUE_HEADS * width)
    else:
        shape = (groups, samples, width)
    count = len(messages)
    return pl.pallas_call(
        functools.partial(join_kernel, count, samples),
        out_shape=jax.ShapeDtypeStruct(shape, jnp.bfloat16),
        in_specs=[VMEM] * count + [ANY] * len(others),
        out_specs=VMEM,
        scratch_shapes=[
            pltpu.VMEM((count, KEY_VALUE_HEADS * rows, 8), jnp.float32),
            pltpu.VMEM(shape, jnp.float32),
        ],
        compiler_params=limit(8),
        cost_estimate=cost(4 * count * messages[0].size, 2 * count * messages[0].size),
        name="join",
    )(*messages, *others)


def fetch_kernel(weight_ref, *refs):
    out_ref, sem = refs[-2:]
    copies = []
    step = weight_ref.shape[0] // sem.shape[0]
    for n in range(sem.shape[0]):
        part = pl.ds(n * step, step)
        copies.append(pltpu.make_async_copy(weight_ref.at[part], out_ref.at[part], sem.at[n]))
        copies[-1].start()
    for copy in copies:
        copy.wait()


def fetch(weight, others):
    return pl.pallas_call(
        fetch_kernel,
        out_shape=jax.ShapeDtypeStruct(weight.shape, weight.dtype),
        in_specs=[HBM] + [ANY] * len(others),
        out_specs=VMEM,
        scratch_shapes=[pltpu.SemaphoreType.DMA((8,))],
        compiler_params=limit(36),
        cost_estimate=cost(0, 4 * weight.size),
        name="fetch",
    )(in_hbm(weight), *others)


def project_kernel(count, tile, *refs):
    part_refs, weight_ref, out_ref = refs[:count], refs[count], refs[count + 1]
    tp_index = lax.axis_index("tp")
    prompts, samples, width = out_ref.shape
    share = prompts // count
    left = jnp.concatenate([ref[...].astype(jnp.float32) for ref in part_refs], axis=0).astype(jnp.bfloat16)
    for first in range(0, width, tile):
        result = jnp.dot(left, weight_ref[:, first : first + tile], preferred_element_type=jnp.float32)
        for offset in range(count):
            for n in range(share):
                row = (offset * share + n) * samples
                block = result[row : row + samples].astype(out_ref.dtype)
                out_ref[(tp_index ^ offset) * share + n, :, first : first + tile] = block


def project(parts, weight, samples):
    count = len(parts)
    depth, width = weight.shape
    total = count * parts[0].shape[0]
    return pl.pallas_call(
        functools.partial(project_kernel, count, min(256, width)),
        out_shape=jax.ShapeDtypeStruct((total // samples, samples, width), jnp.bfloat16),
        in_specs=[VMEM] * (count + 1),
        out_specs=VMEM,
        compiler_params=limit(24),
        cost_estimate=cost(2 * total * depth * width, 2 * depth * width),
        name="project",
    )(*parts, weight)


def body(prompt_key_values, queries, routing, lengths, out_weight):
    section_count = lax.axis_size("sec")
    tp_count = lax.axis_size("tp")
    slot_count, samples, query_width = queries.shape[1:]
    routing = routing.reshape(-1)

    far = [(offset, 0, CAP) for offset in range(2, section_count)]
    near = [(offset, 0, CAP) for offset in range(2)]
    parts = pack(routing, prompt_key_values, [queries], far, section_count)
    far_caches, query_parts = parts[: len(far)], parts[len(far) :]
    own_queries = [swap(part, "sec", offset) for offset, part in enumerate(query_parts)]
    arrived = [swap(part, "sec", piece[0]) for part, piece in zip(far_caches, far)]
    near_caches = pack(routing, prompt_key_values, [], near, section_count)

    messages = attend(routing, lengths, far_caches + near_caches, far + near, own_queries, tp_count)
    partials = [swap(part, "tp", offset) for offset, part in enumerate(messages)]
    held_weight = fetch(out_weight, messages[:1])
    share = join(partials, [held_weight], samples)
    shares = [swap(share, "tp", offset) for offset in range(tp_count)]
    if share.ndim == 3:
        attended = jnp.stack(shares)[jnp.arange(tp_count) ^ lax.axis_index("tp")]
        attended = attended.reshape(REQ_GRP, KEY_VALUE_HEADS, samples, -1).transpose(0, 2, 1, 3)
        attended = attended.reshape(REQ_GRP * samples, query_width)
        layer_out = jnp.dot(attended, out_weight, preferred_element_type=jnp.float32)
        layer_out = layer_out.astype(jnp.bfloat16).reshape(REQ_GRP, samples, -1)
    else:
        layer_out = project(shares, held_weight, samples)

    near_parts = [swap(part, "sec", piece[0]) for part, piece in zip(near_caches, near)]
    stages = [([part], [piece]) for part, piece in zip(arrived, far)]
    stages.insert(-1, (near_parts, near))
    given = [layer_out]
    for parts, pieces in stages:
        given = [layer_out, place(given, parts, pieces, slot_count)]
    return (layer_out, given[1])


def solution(mesh):
    placed = (
        P(("rep", "sec"), None, "tp", None),
        P(("rep", "sec"), None, None, None),
        P("rep", None),
        P("rep"),
        P(None, "tp"),
    )
    return jax.shard_map(
        body,
        mesh=mesh,
        in_specs=placed,
        out_specs=(P(("rep", "sec"), None, "tp"), P(("rep", "sec"), None, None, "tp", None)),
        check_vma=False,
    )
```

```python
import functools

import jax
import jax.numpy as jnp
from jax import lax
from jax.experimental import pallas as pl
from jax.experimental.pallas import tpu as pltpu
from jax.sharding import PartitionSpec as P

HEAD_SIZE = 128
KEY_VALUE_HEADS = 4
REQ_GRP = 8
CAP = 2
HIDDEN = -1e30

ANY = pl.BlockSpec(memory_space=pl.ANY)
HBM = pl.BlockSpec(memory_space=pltpu.HBM)
VMEM = pl.BlockSpec(memory_space=pltpu.VMEM)
SMEM = pl.BlockSpec(memory_space=pltpu.SMEM)


def limit(mebibytes):
    return pltpu.CompilerParams(vmem_limit_bytes=mebibytes << 20)


def cost(flops, bytes_accessed, transcendentals=0):
    return pl.CostEstimate(flops=flops, bytes_accessed=bytes_accessed, transcendentals=transcendentals)


def swap(value, axis, offset):
    if offset == 0:
        return value
    count = lax.axis_size(axis)
    return lax.ppermute(value, axis, [(i, i ^ offset) for i in range(count)])


def own_slots(routing_ref, section, used, source):
    for t in range(used.shape[0]):
        used[t] = 0
    for i in range(REQ_GRP):
        target = routing_ref[section * REQ_GRP + i]
        order = used[target]
        used[target] = order + 1
        source[target * CAP + order] = i


def pack_kernel(pieces, section_count, routing_ref, cache_ref, query_ref, *refs):
    cache_out, query_out, (source, used, sem, query_sem) = refs[: len(pieces)], refs[len(pieces) : -4], refs[-4:]
    section = lax.axis_index("sec")
    full = section_count * CAP == REQ_GRP
    query_copies = []
    for offset, out_ref in enumerate(query_out):
        part = query_ref.at[0, pl.ds((section ^ offset) * CAP, CAP)]
        query_copies.append(pltpu.make_async_copy(part, out_ref, query_sem.at[offset]))
        query_copies[-1].start()
    own_slots(routing_ref, section, used, source)

    def copy(n, spot, row):
        offset, order, place = spot
        return pltpu.make_async_copy(cache_ref.at[row], cache_out[n].at[place], sem.at[offset * CAP + order])

    spots = [
        (n, (offset, first + place, place))
        for n, (offset, first, count) in enumerate(pieces)
        for place in range(count)
    ]
    for n, spot in spots:
        offset, order, place = spot
        target = section ^ offset
        if full:
            copy(n, spot, source[target * CAP + order]).start()
        else:

            @pl.when(order < used[target])
            def _():
                copy(n, spot, source[target * CAP + order]).start()

            @pl.when(order >= used[target])
            def _():
                cache_out[n][place] = jnp.zeros_like(cache_out[n][place])

    for n, spot in spots:
        if full:
            copy(n, spot, 0).wait()
        else:

            @pl.when(spot[1] < used[section ^ spot[0]])
            def _():
                copy(n, spot, 0).wait()

    for query_copy in query_copies:
        query_copy.wait()


def in_hbm(value):
    return pltpu.with_memory_space_constraint(value, pltpu.HBM)


def pack(routing, cache, queries, pieces, section_count):
    slots = section_count * CAP
    shapes = [jax.ShapeDtypeStruct((count,) + cache.shape[1:], cache.dtype) for _, _, count in pieces]
    shapes += [jax.ShapeDtypeStruct((CAP,) + queries.shape[2:], queries.dtype)] * section_count
    moved = sum(shape.size for shape in shapes)
    return pl.pallas_call(
        functools.partial(pack_kernel, pieces, section_count),
        out_shape=shapes,
        in_specs=[SMEM, HBM, HBM],
        out_specs=[VMEM] * len(shapes),
        scratch_shapes=[
            pltpu.SMEM((slots,), jnp.int32),
            pltpu.SMEM((section_count,), jnp.int32),
            pltpu.SemaphoreType.DMA((slots,)),
            pltpu.SemaphoreType.DMA((section_count,)),
        ],
        compiler_params=limit(16),
        cost_estimate=cost(0, 4 * moved),
        name="pack",
    )(in_hbm(routing), in_hbm(cache), in_hbm(queries))


def place_kernel(pieces, *refs):
    count = len(pieces)
    part_refs, out_ref, sem = refs[-2 - count : -2], refs[-2], refs[-1]
    section = lax.axis_index("sec")
    copies = []
    for n, (offset, first, size) in enumerate(pieces):
        slots = out_ref.at[0, pl.ds((section ^ offset) * CAP + first, size)]
        copies.append(pltpu.make_async_copy(part_refs[n], slots, sem.at[n]))
        copies[-1].start()
    for copy in copies:
        copy.wait()


def place(given, parts, pieces, slot_count):
    part = parts[0]
    return pl.pallas_call(
        functools.partial(place_kernel, pieces),
        out_shape=jax.ShapeDtypeStruct((1, slot_count) + part.shape[1:], part.dtype),
        in_specs=[HBM] * len(given) + [VMEM] * len(parts),
        out_specs=HBM,
        scratch_shapes=[pltpu.SemaphoreType.DMA((len(parts),))],
        input_output_aliases={0: 0} if given else {},
        compiler_params=limit(8),
        cost_estimate=cost(0, 4 * sum(piece.size for piece in parts)),
        name="place",
    )(*[in_hbm(value) for value in given], *parts)


def attend_kernel(pieces, section_count, tp_count, routing_ref, lengths_ref, *refs):
    cache_refs, query_refs = refs[: len(pieces)], refs[len(pieces) : len(pieces) + section_count]
    message_refs = refs[-5 - tp_count : -5]
    source, used, messages, stats, stacked = refs[-5:]
    section = lax.axis_index("sec")
    tp_index = lax.axis_index("tp")
    local = cache_refs[0].shape[2]
    groups, rows, _ = messages.shape[1:]
    span = KEY_VALUE_HEADS * rows
    prompts = max(1, groups // KEY_VALUE_HEADS)
    full = section_count * CAP == REQ_GRP
    own_slots(routing_ref, section, used, source)
    position = lax.broadcasted_iota(jnp.int32, (local, span), 0) + tp_index * local
    owner = lax.broadcasted_iota(jnp.int32, (HEAD_SIZE, span), 1) // rows

    def prompt(cache_ref, place, offset, order):
        row = source[(section ^ offset) * CAP + order]
        visible = position < lengths_ref[section * REQ_GRP + row]
        values = query_refs[offset][order].astype(jnp.float32)
        samples = values.shape[0]
        slot = offset * CAP + order
        for head in range(span // samples):
            stacked[slot, head * samples : (head + 1) * samples] = values[:, head * HEAD_SIZE : (head + 1) * HEAD_SIZE]
        query = stacked[slot].T.astype(jnp.bfloat16)
        query = [jnp.where(owner == k, query, jnp.zeros_like(query)) for k in range(KEY_VALUE_HEADS)]
        score = jnp.dot(
            cache_ref[place, 0], jnp.concatenate(query, axis=0), preferred_element_type=jnp.float32
        ) * HEAD_SIZE ** (-0.5)
        score = jnp.where(visible, score, HIDDEN)
        peak = jnp.max(score, axis=0, keepdims=True)
        weight = jnp.where(visible, jnp.exp(score - peak), 0.0)
        total = jnp.sum(weight, axis=0, keepdims=True)
        some = total > 0.0
        safe = jnp.where(some, total, 1.0)
        stats[pl.ds(row, 1)] = jnp.where(some, peak + jnp.log(safe), HIDDEN)
        weight = (weight * (1.0 / safe)).T.astype(jnp.bfloat16)
        for k in range(KEY_VALUE_HEADS):
            mixed = jnp.dot(
                weight[k * rows : (k + 1) * rows],
                cache_ref[place, 1, :, k * HEAD_SIZE : (k + 1) * HEAD_SIZE],
                preferred_element_type=jnp.float32,
            )
            group = row * KEY_VALUE_HEADS + k
            messages[group // groups, group % groups] = mixed.astype(jnp.bfloat16)

    for cache_ref, (offset, first, size) in zip(cache_refs, pieces):
        for place in range(size):
            one = functools.partial(prompt, cache_ref, place, offset, first + place)
            if full:
                one()
            else:
                pl.when(first + place < used[section ^ offset])(one)

    level = stats[...]
    high = level.astype(jnp.bfloat16).astype(jnp.float32)
    rest = level - high
    middle = rest.astype(jnp.bfloat16).astype(jnp.float32)
    stats[...] = high
    stats_middle, stats_low = middle, rest - middle
    for offset in range(tp_count):
        device = tp_index ^ offset
        message_refs[offset][0:groups] = messages[device]
        message_refs[offset][groups] = jnp.zeros((rows, HEAD_SIZE), jnp.bfloat16)
    for part, values in enumerate((high, stats_middle, stats_low)):
        stats[...] = values
        for offset in range(tp_count):
            first = (tp_index ^ offset) * groups // KEY_VALUE_HEADS
            block = jnp.concatenate(
                [stats[pl.ds(first + n, 1)] for n in range(prompts)]
                + [jnp.zeros((16 - prompts, span), jnp.float32)],
                axis=0,
            )
            if part < 2:
                message_refs[offset][groups, part * 16 : part * 16 + 16] = block.astype(jnp.bfloat16)
            else:
                message_refs[offset][groups + 1] = jnp.concatenate([block, jnp.zeros_like(block)], axis=0).astype(
                    jnp.bfloat16
                )


def attend(routing, lengths, caches, pieces, queries, others, tp_count):
    section_count = len(queries)
    samples, width = queries[0].shape[1:]
    span = width // HEAD_SIZE * samples
    rows = span // KEY_VALUE_HEADS
    groups = REQ_GRP * KEY_VALUE_HEADS // tp_count
    multiplies = REQ_GRP * span * HEAD_SIZE * caches[0].shape[2]
    return pl.pallas_call(
        functools.partial(attend_kernel, pieces, section_count, tp_count),
        out_shape=[jax.ShapeDtypeStruct((groups + 2, rows, HEAD_SIZE), jnp.bfloat16)] * tp_count,
        in_specs=[SMEM, SMEM] + [VMEM] * (len(caches) + section_count) + [ANY] * len(others),
        out_specs=[VMEM] * tp_count,
        scratch_shapes=[
            pltpu.SMEM((section_count * CAP,), jnp.int32),
            pltpu.SMEM((section_count,), jnp.int32),
            pltpu.VMEM((tp_count, groups, rows, HEAD_SIZE), jnp.bfloat16),
            pltpu.VMEM((REQ_GRP, span), jnp.float32),
            pltpu.VMEM((section_count * CAP, span, HEAD_SIZE), jnp.float32),
        ],
        compiler_params=limit(12),
        cost_estimate=cost(2 * 10**10, 2 * sum(part.size for part in caches), multiplies // HEAD_SIZE),
        name="attend",
    )(routing, lengths, *caches, *queries, *others)


def join_kernel(count, samples, *refs):
    message_refs, (out_ref, scaling, flat) = refs[:count], refs[-3:]
    groups, rows, _ = message_refs[0].shape
    groups -= 2
    heads = rows // samples
    tp_index = lax.axis_index("tp")
    levels = []
    for ref in message_refs:
        upper = ref[groups].astype(jnp.float32)
        lower = ref[groups + 1].astype(jnp.float32)
        levels.append(upper[0:8] + upper[16:24] + lower[0:8])
    summit = functools.reduce(jnp.maximum, levels)
    scales = [jnp.exp(level - summit) for level in levels]
    total = functools.reduce(jnp.add, scales)
    for n, scale in enumerate(scales):
        scaling[n] = (scale / total).T
    for inner in range(groups):
        if groups % KEY_VALUE_HEADS:
            first = (tp_index * groups + inner) % KEY_VALUE_HEADS * rows
            part = pl.ds(pl.multiple_of(first, rows), rows)
        else:
            part = pl.ds(inner % KEY_VALUE_HEADS * rows, rows)
        prompt = inner // KEY_VALUE_HEADS
        terms = [
            ref[inner].astype(jnp.float32) * scaling[n, part, prompt : prompt + 1]
            for n, ref in enumerate(message_refs)
        ]
        joined = functools.reduce(jnp.add, terms)
        for head in range(heads):
            block = joined[head * samples : (head + 1) * samples]
            if len(flat.shape) == 2:
                row = prompt * samples
                column = (inner % KEY_VALUE_HEADS * heads + head) * HEAD_SIZE
                flat[row : row + samples, column : column + HEAD_SIZE] = block
            else:
                flat[inner, :, head * HEAD_SIZE : (head + 1) * HEAD_SIZE] = block
    out_ref[...] = flat[...].astype(jnp.bfloat16)


def join(messages, others, samples):
    groups, rows, _ = messages[0].shape
    groups -= 2
    width = rows // samples * HEAD_SIZE
    if groups % KEY_VALUE_HEADS == 0:
        shape = (groups // KEY_VALUE_HEADS * samples, KEY_VALUE_HEADS * width)
    else:
        shape = (groups, samples, width)
    count = len(messages)
    return pl.pallas_call(
        functools.partial(join_kernel, count, samples),
        out_shape=jax.ShapeDtypeStruct(shape, jnp.bfloat16),
        in_specs=[VMEM] * count + [ANY] * len(others),
        out_specs=VMEM,
        scratch_shapes=[
            pltpu.VMEM((count, KEY_VALUE_HEADS * rows, 8), jnp.float32),
            pltpu.VMEM(shape, jnp.float32),
        ],
        compiler_params=limit(8),
        cost_estimate=cost(4 * count * messages[0].size, 2 * count * messages[0].size),
        name="join",
    )(*messages, *others)


def fetch_kernel(weight_ref, *refs):
    out_ref, sem = refs[-2:]
    copies = []
    step = weight_ref.shape[0] // sem.shape[0]
    for n in range(sem.shape[0]):
        part = pl.ds(n * step, step)
        copies.append(pltpu.make_async_copy(weight_ref.at[part], out_ref.at[part], sem.at[n]))
        copies[-1].start()
    for copy in copies:
        copy.wait()


def fetch(weight, others):
    return pl.pallas_call(
        fetch_kernel,
        out_shape=jax.ShapeDtypeStruct(weight.shape, weight.dtype),
        in_specs=[HBM] + [ANY] * len(others),
        out_specs=VMEM,
        scratch_shapes=[pltpu.SemaphoreType.DMA((8,))],
        compiler_params=limit(36),
        cost_estimate=cost(0, 4 * weight.size),
        name="fetch",
    )(in_hbm(weight), *others)


def project_kernel(count, tile, *refs):
    part_refs, weight_ref, out_ref = refs[:count], refs[count], refs[count + 1]
    tp_index = lax.axis_index("tp")
    prompts, samples, width = out_ref.shape
    share = prompts // count
    left = jnp.concatenate([ref[...].astype(jnp.float32) for ref in part_refs], axis=0).astype(jnp.bfloat16)
    for first in range(0, width, tile):
        result = jnp.dot(left, weight_ref[:, first : first + tile], preferred_element_type=jnp.float32)
        for offset in range(count):
            for n in range(share):
                row = (offset * share + n) * samples
                block = result[row : row + samples].astype(out_ref.dtype)
                out_ref[(tp_index ^ offset) * share + n, :, first : first + tile] = block


def project(parts, weight, samples):
    count = len(parts)
    depth, width = weight.shape
    total = count * parts[0].shape[0]
    return pl.pallas_call(
        functools.partial(project_kernel, count, min(256, width)),
        out_shape=jax.ShapeDtypeStruct((total // samples, samples, width), jnp.bfloat16),
        in_specs=[VMEM] * (count + 1),
        out_specs=VMEM,
        compiler_params=limit(24),
        cost_estimate=cost(2 * total * depth * width, 2 * depth * width),
        name="project",
    )(*parts, weight)


def body(prompt_key_values, queries, routing, lengths, out_weight):
    section_count = lax.axis_size("sec")
    tp_count = lax.axis_size("tp")
    slot_count, samples, query_width = queries.shape[1:]
    routing = routing.reshape(-1)

    near = [(offset, 0, CAP) for offset in range(2)]
    far = [(offset, 0, CAP) for offset in range(2, section_count)]
    pieces = far + near
    parts = pack(routing, prompt_key_values, queries, pieces, section_count)
    caches, query_parts = parts[: len(pieces)], parts[len(pieces) :]
    own_queries = [swap(part, "sec", offset) for offset, part in enumerate(query_parts)]
    arrived = [swap(part, "sec", piece[0]) for part, piece in zip(caches, pieces)]
    far_parts, near_parts = arrived[: len(far)], arrived[len(far) :]

    messages = attend(routing, lengths, caches, pieces, own_queries, near_parts[1:], tp_count)
    partials = [swap(part, "tp", offset) for offset, part in enumerate(messages)]
    held_weight = fetch(out_weight, messages[:1])
    share = join(partials, [held_weight], samples)
    shares = [swap(share, "tp", offset) for offset in range(tp_count)]
    if share.ndim == 3:
        attended = jnp.stack(shares)[jnp.arange(tp_count) ^ lax.axis_index("tp")]
        attended = attended.reshape(REQ_GRP, KEY_VALUE_HEADS, samples, -1).transpose(0, 2, 1, 3)
        attended = attended.reshape(REQ_GRP * samples, query_width)
        layer_out = jnp.dot(attended, out_weight, preferred_element_type=jnp.float32)
        layer_out = layer_out.astype(jnp.bfloat16).reshape(REQ_GRP, samples, -1)
    else:
        layer_out = project(shares, held_weight, samples)

    whole = place([], near_parts, near, slot_count)
    for part, piece in zip(far_parts, far):
        whole = place([whole, layer_out], [part], [piece], slot_count)
    return (layer_out, whole)


def solution(mesh):
    placed = (
        P(("rep", "sec"), None, "tp", None),
        P(("rep", "sec"), None, None, None),
        P("rep", None),
        P("rep"),
        P(None, "tp"),
    )
    return jax.shard_map(
        body,
        mesh=mesh,
        in_specs=placed,
        out_specs=(P(("rep", "sec"), None, "tp"), P(("rep", "sec"), None, None, "tp", None)),
        check_vma=False,
    )
```

```python
import functools

import jax
import jax.numpy as jnp
from jax import lax
from jax.experimental import pallas as pl
from jax.experimental.pallas import tpu as pltpu
from jax.sharding import PartitionSpec as P

HEAD_SIZE = 128
KEY_VALUE_HEADS = 4
REQ_GRP = 8
CAP = 2
HIDDEN = -1e30

ANY = pl.BlockSpec(memory_space=pl.ANY)
HBM = pl.BlockSpec(memory_space=pltpu.HBM)
VMEM = pl.BlockSpec(memory_space=pltpu.VMEM)
SMEM = pl.BlockSpec(memory_space=pltpu.SMEM)


def limit(mebibytes):
    return pltpu.CompilerParams(vmem_limit_bytes=mebibytes << 20)


def cost(flops, bytes_accessed, transcendentals=0):
    return pl.CostEstimate(flops=flops, bytes_accessed=bytes_accessed, transcendentals=transcendentals)


def swap(value, axis, offset):
    if offset == 0:
        return value
    count = lax.axis_size(axis)
    return lax.ppermute(value, axis, [(i, i ^ offset) for i in range(count)])


def own_slots(routing_ref, section, used, source):
    for t in range(used.shape[0]):
        used[t] = 0
    for i in range(REQ_GRP):
        target = routing_ref[section * REQ_GRP + i]
        order = used[target]
        used[target] = order + 1
        source[target * CAP + order] = i


def pack_kernel(pieces, shown, section_count, routing_ref, cache_ref, *refs):
    refs, (source, used, sem, query_sem) = refs[:-4], refs[-4:]
    cache_out = refs[len(refs) - shown :][: len(pieces)]
    query_ref, query_out = refs[0], refs[len(refs) - shown + len(pieces) :]
    section = lax.axis_index("sec")
    full = section_count * CAP == REQ_GRP
    query_copies = []
    for offset, out_ref in enumerate(query_out):
        part = query_ref.at[0, pl.ds((section ^ offset) * CAP, CAP)]
        query_copies.append(pltpu.make_async_copy(part, out_ref, query_sem.at[offset]))
        query_copies[-1].start()
    own_slots(routing_ref, section, used, source)

    def copy(n, spot, row):
        offset, order, place = spot
        return pltpu.make_async_copy(cache_ref.at[row], cache_out[n].at[place], sem.at[offset * CAP + order])

    spots = [
        (n, (offset, first + place, place))
        for n, (offset, first, count) in enumerate(pieces)
        for place in range(count)
    ]
    for n, spot in spots:
        offset, order, place = spot
        target = section ^ offset
        if full:
            copy(n, spot, source[target * CAP + order]).start()
        else:

            @pl.when(order < used[target])
            def _():
                copy(n, spot, source[target * CAP + order]).start()

            @pl.when(order >= used[target])
            def _():
                cache_out[n][place] = jnp.zeros_like(cache_out[n][place])

    for n, spot in spots:
        if full:
            copy(n, spot, 0).wait()
        else:

            @pl.when(spot[1] < used[section ^ spot[0]])
            def _():
                copy(n, spot, 0).wait()

    for query_copy in query_copies:
        query_copy.wait()


def in_hbm(value):
    return pltpu.with_memory_space_constraint(value, pltpu.HBM)


def pack(routing, cache, queries, others, pieces, section_count):
    slots = section_count * CAP
    shapes = [jax.ShapeDtypeStruct((count,) + cache.shape[1:], cache.dtype) for _, _, count in pieces]
    for query in queries:
        shapes += [jax.ShapeDtypeStruct((CAP,) + query.shape[2:], query.dtype)] * section_count
    moved = sum(shape.size for shape in shapes)
    return pl.pallas_call(
        functools.partial(pack_kernel, pieces, len(shapes), section_count),
        out_shape=shapes,
        in_specs=[SMEM, HBM] + [HBM] * len(queries) + [ANY] * len(others),
        out_specs=[VMEM] * len(shapes),
        scratch_shapes=[
            pltpu.SMEM((slots,), jnp.int32),
            pltpu.SMEM((section_count,), jnp.int32),
            pltpu.SemaphoreType.DMA((slots,)),
            pltpu.SemaphoreType.DMA((section_count,)),
        ],
        compiler_params=limit(16),
        cost_estimate=cost(0, 4 * moved),
        name="pack",
    )(in_hbm(routing), in_hbm(cache), *[in_hbm(query) for query in queries], *others)


def place_kernel(pieces, *refs):
    count = len(pieces)
    part_refs, out_ref, sem = refs[-2 - count : -2], refs[-2], refs[-1]
    section = lax.axis_index("sec")
    copies = []
    for n, (offset, first, size) in enumerate(pieces):
        slots = out_ref.at[0, pl.ds((section ^ offset) * CAP + first, size)]
        copies.append(pltpu.make_async_copy(part_refs[n], slots, sem.at[n]))
        copies[-1].start()
    for copy in copies:
        copy.wait()


def place(given, parts, pieces, slot_count):
    part = parts[0]
    return pl.pallas_call(
        functools.partial(place_kernel, pieces),
        out_shape=jax.ShapeDtypeStruct((1, slot_count) + part.shape[1:], part.dtype),
        in_specs=[HBM] * len(given) + [VMEM] * len(parts),
        out_specs=HBM,
        scratch_shapes=[pltpu.SemaphoreType.DMA((len(parts),))],
        input_output_aliases={0: 0} if given else {},
        compiler_params=limit(8),
        cost_estimate=cost(0, 4 * sum(piece.size for piece in parts)),
        name="place",
    )(*[in_hbm(value) for value in given], *parts)


def attend_kernel(pieces, section_count, tp_count, routing_ref, lengths_ref, *refs):
    cache_refs, query_refs = refs[: len(pieces)], refs[len(pieces) : len(pieces) + section_count]
    message_refs = refs[-5 - tp_count : -5]
    source, used, messages, stats, stacked = refs[-5:]
    section = lax.axis_index("sec")
    tp_index = lax.axis_index("tp")
    local = cache_refs[0].shape[2]
    groups, rows, _ = messages.shape[1:]
    span = KEY_VALUE_HEADS * rows
    prompts = max(1, groups // KEY_VALUE_HEADS)
    full = section_count * CAP == REQ_GRP
    own_slots(routing_ref, section, used, source)
    position = lax.broadcasted_iota(jnp.int32, (local, span), 0) + tp_index * local
    owner = lax.broadcasted_iota(jnp.int32, (HEAD_SIZE, span), 1) // rows

    def prompt(cache_ref, place, offset, order):
        row = source[(section ^ offset) * CAP + order]
        visible = position < lengths_ref[section * REQ_GRP + row]
        values = query_refs[offset][order].astype(jnp.float32)
        samples = values.shape[0]
        slot = offset * CAP + order
        for head in range(span // samples):
            stacked[slot, head * samples : (head + 1) * samples] = values[:, head * HEAD_SIZE : (head + 1) * HEAD_SIZE]
        query = stacked[slot].T.astype(jnp.bfloat16)
        query = [jnp.where(owner == k, query, jnp.zeros_like(query)) for k in range(KEY_VALUE_HEADS)]
        score = jnp.dot(
            cache_ref[place, 0], jnp.concatenate(query, axis=0), preferred_element_type=jnp.float32
        ) * HEAD_SIZE ** (-0.5)
        score = jnp.where(visible, score, HIDDEN)
        peak = jnp.max(score, axis=0, keepdims=True)
        weight = jnp.where(visible, jnp.exp(score - peak), 0.0)
        total = jnp.sum(weight, axis=0, keepdims=True)
        some = total > 0.0
        safe = jnp.where(some, total, 1.0)
        stats[pl.ds(row, 1)] = jnp.where(some, peak + jnp.log(safe), HIDDEN)
        weight = (weight * (1.0 / safe)).T.astype(jnp.bfloat16)
        for k in range(KEY_VALUE_HEADS):
            mixed = jnp.dot(
                weight[k * rows : (k + 1) * rows],
                cache_ref[place, 1, :, k * HEAD_SIZE : (k + 1) * HEAD_SIZE],
                preferred_element_type=jnp.float32,
            )
            group = row * KEY_VALUE_HEADS + k
            messages[group // groups, group % groups] = mixed.astype(jnp.bfloat16)

    for cache_ref, (offset, first, size) in zip(cache_refs, pieces):
        for place in range(size):
            one = functools.partial(prompt, cache_ref, place, offset, first + place)
            if full:
                one()
            else:
                pl.when(first + place < used[section ^ offset])(one)

    level = stats[...]
    high = level.astype(jnp.bfloat16).astype(jnp.float32)
    rest = level - high
    middle = rest.astype(jnp.bfloat16).astype(jnp.float32)
    stats[...] = high
    stats_middle, stats_low = middle, rest - middle
    for offset in range(tp_count):
        device = tp_index ^ offset
        message_refs[offset][0:groups] = messages[device]
        message_refs[offset][groups] = jnp.zeros((rows, HEAD_SIZE), jnp.bfloat16)
    for part, values in enumerate((high, stats_middle, stats_low)):
        stats[...] = values
        for offset in range(tp_count):
            first = (tp_index ^ offset) * groups // KEY_VALUE_HEADS
            block = jnp.concatenate(
                [stats[pl.ds(first + n, 1)] for n in range(prompts)]
                + [jnp.zeros((16 - prompts, span), jnp.float32)],
                axis=0,
            )
            if part < 2:
                message_refs[offset][groups, part * 16 : part * 16 + 16] = block.astype(jnp.bfloat16)
            else:
                message_refs[offset][groups + 1] = jnp.concatenate([block, jnp.zeros_like(block)], axis=0).astype(
                    jnp.bfloat16
                )


def attend(routing, lengths, caches, pieces, queries, tp_count):
    section_count = len(queries)
    samples, width = queries[0].shape[1:]
    span = width // HEAD_SIZE * samples
    rows = span // KEY_VALUE_HEADS
    groups = REQ_GRP * KEY_VALUE_HEADS // tp_count
    multiplies = REQ_GRP * span * HEAD_SIZE * caches[0].shape[2]
    return pl.pallas_call(
        functools.partial(attend_kernel, pieces, section_count, tp_count),
        out_shape=[jax.ShapeDtypeStruct((groups + 2, rows, HEAD_SIZE), jnp.bfloat16)] * tp_count,
        in_specs=[SMEM, SMEM] + [VMEM] * (len(caches) + section_count),
        out_specs=[VMEM] * tp_count,
        scratch_shapes=[
            pltpu.SMEM((section_count * CAP,), jnp.int32),
            pltpu.SMEM((section_count,), jnp.int32),
            pltpu.VMEM((tp_count, groups, rows, HEAD_SIZE), jnp.bfloat16),
            pltpu.VMEM((REQ_GRP, span), jnp.float32),
            pltpu.VMEM((section_count * CAP, span, HEAD_SIZE), jnp.float32),
        ],
        compiler_params=limit(12),
        cost_estimate=cost(2 * 10**10, 2 * sum(part.size for part in caches), multiplies // HEAD_SIZE),
        name="attend",
    )(routing, lengths, *caches, *queries)


def join_kernel(count, samples, *refs):
    message_refs, (out_ref, scaling, flat) = refs[:count], refs[-3:]
    groups, rows, _ = message_refs[0].shape
    groups -= 2
    heads = rows // samples
    tp_index = lax.axis_index("tp")
    levels = []
    for ref in message_refs:
        upper = ref[groups].astype(jnp.float32)
        lower = ref[groups + 1].astype(jnp.float32)
        levels.append(upper[0:8] + upper[16:24] + lower[0:8])
    summit = functools.reduce(jnp.maximum, levels)
    scales = [jnp.exp(level - summit) for level in levels]
    total = functools.reduce(jnp.add, scales)
    for n, scale in enumerate(scales):
        scaling[n] = (scale / total).T
    for inner in range(groups):
        if groups % KEY_VALUE_HEADS:
            first = (tp_index * groups + inner) % KEY_VALUE_HEADS * rows
            part = pl.ds(pl.multiple_of(first, rows), rows)
        else:
            part = pl.ds(inner % KEY_VALUE_HEADS * rows, rows)
        prompt = inner // KEY_VALUE_HEADS
        terms = [
            ref[inner].astype(jnp.float32) * scaling[n, part, prompt : prompt + 1]
            for n, ref in enumerate(message_refs)
        ]
        joined = functools.reduce(jnp.add, terms)
        for head in range(heads):
            block = joined[head * samples : (head + 1) * samples]
            if len(flat.shape) == 2:
                row = prompt * samples
                column = (inner % KEY_VALUE_HEADS * heads + head) * HEAD_SIZE
                flat[row : row + samples, column : column + HEAD_SIZE] = block
            else:
                flat[inner, :, head * HEAD_SIZE : (head + 1) * HEAD_SIZE] = block
    out_ref[...] = flat[...].astype(jnp.bfloat16)


def join(messages, others, samples):
    groups, rows, _ = messages[0].shape
    groups -= 2
    width = rows // samples * HEAD_SIZE
    if groups % KEY_VALUE_HEADS == 0:
        shape = (groups // KEY_VALUE_HEADS * samples, KEY_VALUE_HEADS * width)
    else:
        shape = (groups, samples, width)
    count = len(messages)
    return pl.pallas_call(
        functools.partial(join_kernel, count, samples),
        out_shape=jax.ShapeDtypeStruct(shape, jnp.bfloat16),
        in_specs=[VMEM] * count + [ANY] * len(others),
        out_specs=VMEM,
        scratch_shapes=[
            pltpu.VMEM((count, KEY_VALUE_HEADS * rows, 8), jnp.float32),
            pltpu.VMEM(shape, jnp.float32),
        ],
        compiler_params=limit(8),
        cost_estimate=cost(4 * count * messages[0].size, 2 * count * messages[0].size),
        name="join",
    )(*messages, *others)


def fetch_kernel(weight_ref, *refs):
    out_ref, sem = refs[-2:]
    copies = []
    step = weight_ref.shape[0] // sem.shape[0]
    for n in range(sem.shape[0]):
        part = pl.ds(n * step, step)
        copies.append(pltpu.make_async_copy(weight_ref.at[part], out_ref.at[part], sem.at[n]))
        copies[-1].start()
    for copy in copies:
        copy.wait()


def fetch(weight, others):
    return pl.pallas_call(
        fetch_kernel,
        out_shape=jax.ShapeDtypeStruct(weight.shape, weight.dtype),
        in_specs=[HBM] + [ANY] * len(others),
        out_specs=VMEM,
        scratch_shapes=[pltpu.SemaphoreType.DMA((8,))],
        compiler_params=limit(36),
        cost_estimate=cost(0, 4 * weight.size),
        name="fetch",
    )(in_hbm(weight), *others)


def project_kernel(count, tile, *refs):
    part_refs, weight_ref, out_ref = refs[:count], refs[count], refs[count + 1]
    tp_index = lax.axis_index("tp")
    prompts, samples, width = out_ref.shape
    share = prompts // count
    left = jnp.concatenate([ref[...].astype(jnp.float32) for ref in part_refs], axis=0).astype(jnp.bfloat16)
    for first in range(0, width, tile):
        result = jnp.dot(left, weight_ref[:, first : first + tile], preferred_element_type=jnp.float32)
        for offset in range(count):
            for n in range(share):
                row = (offset * share + n) * samples
                block = result[row : row + samples].astype(out_ref.dtype)
                out_ref[(tp_index ^ offset) * share + n, :, first : first + tile] = block


def project(parts, weight, samples):
    count = len(parts)
    depth, width = weight.shape
    total = count * parts[0].shape[0]
    return pl.pallas_call(
        functools.partial(project_kernel, count, min(256, width)),
        out_shape=jax.ShapeDtypeStruct((total // samples, samples, width), jnp.bfloat16),
        in_specs=[VMEM] * (count + 1),
        out_specs=VMEM,
        compiler_params=limit(24),
        cost_estimate=cost(2 * total * depth * width, 2 * depth * width),
        name="project",
    )(*parts, weight)


def body(prompt_key_values, queries, routing, lengths, out_weight):
    section_count = lax.axis_size("sec")
    tp_count = lax.axis_size("tp")
    slot_count, samples, query_width = queries.shape[1:]
    routing = routing.reshape(-1)

    near = [(offset, 0, CAP) for offset in range(2)]
    far = [(offset, 0, CAP) for offset in range(2, section_count)]
    parts = pack(routing, prompt_key_values, [queries], [], far, section_count)
    far_caches, query_parts = parts[: len(far)], parts[len(far) :]
    own_queries = [swap(query_parts[offset], "sec", offset) for offset in reversed(range(section_count))][::-1]
    far_parts = [swap(part, "sec", piece[0]) for part, piece in zip(far_caches, far)]
    near_caches = pack(routing, prompt_key_values, [], own_queries[1:2], near, section_count)
    near_parts = [swap(part, "sec", piece[0]) for part, piece in zip(near_caches, near)]

    messages = attend(routing, lengths, [*far_caches, *near_caches], far + near, own_queries, tp_count)
    partials = [swap(part, "tp", offset) for offset, part in enumerate(messages)]
    held_weight = fetch(out_weight, [messages[0], *near_parts[1:]])
    share = join(partials, [held_weight], samples)
    shares = [swap(share, "tp", offset) for offset in range(tp_count)]
    if share.ndim == 3:
        attended = jnp.stack(shares)[jnp.arange(tp_count) ^ lax.axis_index("tp")]
        attended = attended.reshape(REQ_GRP, KEY_VALUE_HEADS, samples, -1).transpose(0, 2, 1, 3)
        attended = attended.reshape(REQ_GRP * samples, query_width)
        layer_out = jnp.dot(attended, out_weight, preferred_element_type=jnp.float32)
        layer_out = layer_out.astype(jnp.bfloat16).reshape(REQ_GRP, samples, -1)
    else:
        layer_out = project(shares, held_weight, samples)

    whole = place([], near_parts, near, slot_count)
    for part, piece in zip(far_parts, far):
        whole = place([whole, layer_out], [part], [piece], slot_count)
    return (layer_out, whole)


def solution(mesh):
    placed = (
        P(("rep", "sec"), None, "tp", None),
        P(("rep", "sec"), None, None, None),
        P("rep", None),
        P("rep"),
        P(None, "tp"),
    )
    return jax.shard_map(
        body,
        mesh=mesh,
        in_specs=placed,
        out_specs=(P(("rep", "sec"), None, "tp"), P(("rep", "sec"), None, None, "tp", None)),
        check_vma=False,
    )
```

```python
import functools

import jax
import jax.numpy as jnp
from jax import lax
from jax.experimental import pallas as pl
from jax.experimental.pallas import tpu as pltpu
from jax.sharding import PartitionSpec as P

HEAD_SIZE = 128
KEY_VALUE_HEADS = 4
REQ_GRP = 8
CAP = 2
HIDDEN = -1e30

ANY = pl.BlockSpec(memory_space=pl.ANY)
HBM = pl.BlockSpec(memory_space=pltpu.HBM)
VMEM = pl.BlockSpec(memory_space=pltpu.VMEM)
SMEM = pl.BlockSpec(memory_space=pltpu.SMEM)


def limit(mebibytes):
    return pltpu.CompilerParams(vmem_limit_bytes=mebibytes << 20)


def cost(flops, bytes_accessed, transcendentals=0):
    return pl.CostEstimate(flops=flops, bytes_accessed=bytes_accessed, transcendentals=transcendentals)


def swap(value, axis, offset):
    if offset == 0:
        return value
    count = lax.axis_size(axis)
    return lax.ppermute(value, axis, [(i, i ^ offset) for i in range(count)])


def spread(value, axis):
    values = [value]
    while len(values) < lax.axis_size(axis):
        values += [swap(one, axis, len(values)) for one in values]
    return values


def own_slots(routing_ref, section, used, source):
    for t in range(used.shape[0]):
        used[t] = 0
    for i in range(REQ_GRP):
        target = routing_ref[section * REQ_GRP + i]
        order = used[target]
        used[target] = order + 1
        source[target * CAP + order] = i


def pack_slots(pieces, section_count):
    return [
        (n, place, offset, first + place)
        for n, (offset, first, count) in enumerate(pieces)
        for place in range(count)
    ]


def start_packing(pieces, section_count, routing_ref, cache_ref, out_refs, source, used, sem):
    section = lax.axis_index("sec")
    full = section_count * CAP == REQ_GRP
    own_slots(routing_ref, section, used, source)
    spots = pack_slots(pieces, section_count)

    def copy(n, place, offset, order, row):
        return pltpu.make_async_copy(cache_ref.at[row], out_refs[n].at[place], sem.at[offset * CAP + order])

    for n, place, offset, order in spots:
        target = section ^ offset
        if full:
            copy(n, place, offset, order, source[target * CAP + order]).start()
        else:

            @pl.when(order < used[target])
            def _():
                copy(n, place, offset, order, source[target * CAP + order]).start()

            @pl.when(order >= used[target])
            def _():
                out_refs[n][place] = jnp.zeros_like(out_refs[n][place])

    def finish():
        for n, place, offset, order in spots:
            if full:
                copy(n, place, offset, order, 0).wait()
            else:

                @pl.when(order < used[section ^ offset])
                def _():
                    copy(n, place, offset, order, 0).wait()

    return finish


def first_pack_kernel(pieces, section_count, routing_ref, cache_ref, query_ref, *refs):
    cache_out, query_out = refs[: len(pieces)], refs[len(pieces) : -4]
    source, used, sem, query_sem = refs[-4:]
    section = lax.axis_index("sec")
    query_copies = []
    for offset, out_ref in enumerate(query_out):
        width = out_ref.shape[2]
        columns = pl.ds(pl.multiple_of(lax.axis_index("tp") * width, width) if offset > 1 else 0, width)
        part = query_ref.at[0, pl.ds((section ^ offset) * CAP, CAP), :, columns]
        query_copies.append(pltpu.make_async_copy(part, out_ref, query_sem.at[offset]))
        query_copies[-1].start()
    finish = start_packing(pieces, section_count, routing_ref, cache_ref, cache_out, source, used, sem)
    finish()
    for copy in query_copies:
        copy.wait()


def second_pack_kernel(pieces, section_count, routing_ref, cache_ref, *refs):
    source, used, sem = refs[-3:]
    cache_out, merged_ref, query_refs = refs[-4 - len(pieces) : -4], refs[-4], refs[: -4 - len(pieces)]
    finish = start_packing(pieces, section_count, routing_ref, cache_ref, cache_out, source, used, sem)
    for n, query_ref in enumerate(query_refs):
        merged_ref[n] = query_ref[...]
    finish()


def in_hbm(value):
    return pltpu.with_memory_space_constraint(value, pltpu.HBM)


def first_pack(routing, cache, queries, pieces, section_count, tp_count):
    samples, width = queries.shape[2:]
    widths = [width if offset < 2 else width // tp_count for offset in range(section_count)]
    shapes = [jax.ShapeDtypeStruct((count,) + cache.shape[1:], cache.dtype) for _, _, count in pieces]
    shapes += [jax.ShapeDtypeStruct((CAP, samples, one), queries.dtype) for one in widths]
    parts = pl.pallas_call(
        functools.partial(first_pack_kernel, pieces, section_count),
        out_shape=shapes,
        in_specs=[SMEM, HBM, HBM],
        out_specs=[VMEM] * len(shapes),
        scratch_shapes=[
            pltpu.SMEM((section_count * CAP,), jnp.int32),
            pltpu.SMEM((section_count,), jnp.int32),
            pltpu.SemaphoreType.DMA((section_count * CAP,)),
            pltpu.SemaphoreType.DMA((section_count,)),
        ],
        compiler_params=limit(16),
        cost_estimate=cost(0, 4 * sum(shape.size for shape in shapes)),
        name="first_pack",
    )(in_hbm(routing), in_hbm(cache), in_hbm(queries))
    return parts[: len(pieces)], parts[len(pieces) :]


def second_pack(routing, cache, queries, pieces, section_count):
    shapes = [jax.ShapeDtypeStruct((count,) + cache.shape[1:], cache.dtype) for _, _, count in pieces]
    merged = jax.ShapeDtypeStruct((len(queries),) + queries[0].shape, queries[0].dtype)
    *parts, merged = pl.pallas_call(
        functools.partial(second_pack_kernel, pieces, section_count),
        out_shape=shapes + [merged],
        in_specs=[SMEM, HBM] + [VMEM] * len(queries),
        out_specs=[VMEM] * (len(shapes) + 1),
        scratch_shapes=[
            pltpu.SMEM((section_count * CAP,), jnp.int32),
            pltpu.SMEM((section_count,), jnp.int32),
            pltpu.SemaphoreType.DMA((section_count * CAP,)),
        ],
        compiler_params=limit(16),
        cost_estimate=cost(0, 10**8),
        name="second_pack",
    )(in_hbm(routing), in_hbm(cache), *queries)
    return parts, merged


def place_kernel(pieces, *refs):
    count = len(pieces)
    part_refs, out_ref, sem = refs[-2 - count : -2], refs[-2], refs[-1]
    section = lax.axis_index("sec")
    copies = []
    for n, (offset, first, size) in enumerate(pieces):
        slots = out_ref.at[0, pl.ds((section ^ offset) * CAP + first, size)]
        copies.append(pltpu.make_async_copy(part_refs[n], slots, sem.at[n]))
        copies[-1].start()
    for copy in copies:
        copy.wait()


def place(given, parts, pieces, slot_count):
    part = parts[0]
    return pl.pallas_call(
        functools.partial(place_kernel, pieces),
        out_shape=jax.ShapeDtypeStruct((1, slot_count) + part.shape[1:], part.dtype),
        in_specs=[HBM] * len(given) + [VMEM] * len(parts),
        out_specs=HBM,
        scratch_shapes=[pltpu.SemaphoreType.DMA((len(parts),))],
        input_output_aliases={0: 0} if len(given) > 1 else {},
        compiler_params=limit(8),
        cost_estimate=cost(0, 4 * sum(piece.size for piece in parts)),
        name="place",
    )(*[in_hbm(value) for value in given], *parts)


def attend_kernel(pieces, section_count, tp_count, routing_ref, lengths_ref, *refs):
    cache_refs, refs = refs[: len(pieces)], refs[len(pieces) :]
    query_refs, far_refs = refs[:2], refs[2 : 2 + tp_count]
    message_refs = refs[2 + tp_count : 2 + 2 * tp_count]
    source, used, messages, stats, stacked, far_queries = refs[2 + 2 * tp_count :]
    section = lax.axis_index("sec")
    tp_index = lax.axis_index("tp")
    local = cache_refs[0].shape[2]
    groups, rows, _ = messages.shape[1:]
    span = KEY_VALUE_HEADS * rows
    prompts = max(1, groups // KEY_VALUE_HEADS)
    full = section_count * CAP == REQ_GRP
    own_slots(routing_ref, section, used, source)
    samples = query_refs[0].shape[1]
    for offset, far_ref in enumerate(far_refs):
        far_queries[tp_index ^ offset] = far_ref[...]
    position = lax.broadcasted_iota(jnp.int32, (local, span), 0) + tp_index * local
    owner = lax.broadcasted_iota(jnp.int32, (HEAD_SIZE, span), 1) // rows

    def prompt(cache_ref, place, offset, order):
        row = source[(section ^ offset) * CAP + order]
        visible = position < lengths_ref[section * REQ_GRP + row]
        slot = offset * CAP + order
        for head in range(span // samples):
            first, part = head * HEAD_SIZE, far_queries.shape[-1]
            if offset < 2:
                values = query_refs[offset][order, :, first : first + HEAD_SIZE]
            else:
                inner = first % part
                values = far_queries[first // part, offset - 2, order, :, inner : inner + HEAD_SIZE]
            stacked[slot, head * samples : (head + 1) * samples] = values.astype(jnp.float32)
        query = stacked[slot].T.astype(jnp.bfloat16)
        query = [jnp.where(owner == k, query, jnp.zeros_like(query)) for k in range(KEY_VALUE_HEADS)]
        score = jnp.dot(
            cache_ref[place, 0], jnp.concatenate(query, axis=0), preferred_element_type=jnp.float32
        ) * HEAD_SIZE ** (-0.5)
        score = jnp.where(visible, score, HIDDEN)
        peak = jnp.max(score, axis=0, keepdims=True)
        weight = jnp.where(visible, jnp.exp(score - peak), 0.0)
        total = jnp.sum(weight, axis=0, keepdims=True)
        some = total > 0.0
        safe = jnp.where(some, total, 1.0)
        stats[pl.ds(row, 1)] = jnp.where(some, peak + jnp.log(safe), HIDDEN)
        weight = (weight * (1.0 / safe)).T.astype(jnp.bfloat16)
        for k in range(KEY_VALUE_HEADS):
            mixed = jnp.dot(
                weight[k * rows : (k + 1) * rows],
                cache_ref[place, 1, :, k * HEAD_SIZE : (k + 1) * HEAD_SIZE],
                preferred_element_type=jnp.float32,
            )
            group = row * KEY_VALUE_HEADS + k
            messages[group // groups, group % groups] = mixed.astype(jnp.bfloat16)

    for cache_ref, (offset, first, size) in zip(cache_refs, pieces):
        for place in range(size):
            one = functools.partial(prompt, cache_ref, place, offset, first + place)
            if full:
                one()
            else:
                pl.when(first + place < used[section ^ offset])(one)

    level = stats[...]
    high = level.astype(jnp.bfloat16).astype(jnp.float32)
    rest = level - high
    middle = rest.astype(jnp.bfloat16).astype(jnp.float32)
    stats[...] = high
    stats_middle, stats_low = middle, rest - middle
    for offset in range(tp_count):
        device = tp_index ^ offset
        message_refs[offset][0:groups] = messages[device]
        message_refs[offset][groups] = jnp.zeros((rows, HEAD_SIZE), jnp.bfloat16)
    for part, values in enumerate((high, stats_middle, stats_low)):
        stats[...] = values
        for offset in range(tp_count):
            first = (tp_index ^ offset) * groups // KEY_VALUE_HEADS
            block = jnp.concatenate(
                [stats[pl.ds(first + n, 1)] for n in range(prompts)]
                + [jnp.zeros((16 - prompts, span), jnp.float32)],
                axis=0,
            )
            if part < 2:
                message_refs[offset][groups, part * 16 : part * 16 + 16] = block.astype(jnp.bfloat16)
            else:
                message_refs[offset][groups + 1] = jnp.concatenate([block, jnp.zeros_like(block)], axis=0).astype(
                    jnp.bfloat16
                )


def attend(routing, lengths, caches, pieces, queries, far_queries):
    section_count = len(far_queries[0]) + 2
    tp_count = len(far_queries)
    samples, width = queries[0].shape[1:]
    span = width // HEAD_SIZE * samples
    rows = span // KEY_VALUE_HEADS
    groups = REQ_GRP * KEY_VALUE_HEADS // tp_count
    multiplies = REQ_GRP * span * HEAD_SIZE * caches[0].shape[2]
    return pl.pallas_call(
        functools.partial(attend_kernel, pieces, section_count, tp_count),
        out_shape=[jax.ShapeDtypeStruct((groups + 2, rows, HEAD_SIZE), jnp.bfloat16)] * tp_count,
        in_specs=[SMEM, SMEM] + [VMEM] * (len(caches) + len(queries) + tp_count),
        out_specs=[VMEM] * tp_count,
        scratch_shapes=[
            pltpu.SMEM((section_count * CAP,), jnp.int32),
            pltpu.SMEM((section_count,), jnp.int32),
            pltpu.VMEM((tp_count, groups, rows, HEAD_SIZE), jnp.bfloat16),
            pltpu.VMEM((REQ_GRP, span), jnp.float32),
            pltpu.VMEM((section_count * CAP, span, HEAD_SIZE), jnp.float32),
            pltpu.VMEM((tp_count,) + far_queries[0].shape, far_queries[0].dtype),
        ],
        compiler_params=limit(12),
        cost_estimate=cost(4 * multiplies, 2 * sum(part.size for part in caches), multiplies // HEAD_SIZE),
        name="attend",
    )(routing, lengths, *caches, *queries, *far_queries)


def join_kernel(count, samples, *refs):
    message_refs, (out_ref, scaling, flat) = refs[:count], refs[-3:]
    groups, rows, _ = message_refs[0].shape
    groups -= 2
    heads = rows // samples
    tp_index = lax.axis_index("tp")
    levels = []
    for ref in message_refs:
        upper = ref[groups].astype(jnp.float32)
        lower = ref[groups + 1].astype(jnp.float32)
        levels.append(upper[0:8] + upper[16:24] + lower[0:8])
    summit = functools.reduce(jnp.maximum, levels)
    scales = [jnp.exp(level - summit) for level in levels]
    total = functools.reduce(jnp.add, scales)
    for n, scale in enumerate(scales):
        scaling[n] = (scale / total).T
    for inner in range(groups):
        if groups % KEY_VALUE_HEADS:
            first = (tp_index * groups + inner) % KEY_VALUE_HEADS * rows
            part = pl.ds(pl.multiple_of(first, rows), rows)
        else:
            part = pl.ds(inner % KEY_VALUE_HEADS * rows, rows)
        prompt = inner // KEY_VALUE_HEADS
        terms = [
            ref[inner].astype(jnp.float32) * scaling[n, part, prompt : prompt + 1]
            for n, ref in enumerate(message_refs)
        ]
        joined = functools.reduce(jnp.add, terms)
        for head in range(heads):
            block = joined[head * samples : (head + 1) * samples]
            if len(flat.shape) == 2:
                row = prompt * samples
                column = (inner % KEY_VALUE_HEADS * heads + head) * HEAD_SIZE
                flat[row : row + samples, column : column + HEAD_SIZE] = block
            else:
                flat[inner, :, head * HEAD_SIZE : (head + 1) * HEAD_SIZE] = block
    out_ref[...] = flat[...].astype(jnp.bfloat16)


def join(messages, others, samples):
    groups, rows, _ = messages[0].shape
    groups -= 2
    width = rows // samples * HEAD_SIZE
    if groups % KEY_VALUE_HEADS == 0:
        shape = (groups // KEY_VALUE_HEADS * samples, KEY_VALUE_HEADS * width)
    else:
        shape = (groups, samples, width)
    count = len(messages)
    return pl.pallas_call(
        functools.partial(join_kernel, count, samples),
        out_shape=jax.ShapeDtypeStruct(shape, jnp.bfloat16),
        in_specs=[VMEM] * count + [ANY] * len(others),
        out_specs=VMEM,
        scratch_shapes=[
            pltpu.VMEM((count, KEY_VALUE_HEADS * rows, 8), jnp.float32),
            pltpu.VMEM(shape, jnp.float32),
        ],
        compiler_params=limit(8),
        cost_estimate=cost(4 * count * messages[0].size, 2 * count * messages[0].size),
        name="join",
    )(*messages, *others)


def fetch_kernel(weight_ref, *refs):
    out_ref, sem = refs[-2:]
    copies = []
    step = weight_ref.shape[0] // sem.shape[0]
    for n in range(sem.shape[0]):
        part = pl.ds(n * step, step)
        copies.append(pltpu.make_async_copy(weight_ref.at[part], out_ref.at[part], sem.at[n]))
        copies[-1].start()
    for copy in copies:
        copy.wait()


def fetch(weight, others):
    return pl.pallas_call(
        fetch_kernel,
        out_shape=jax.ShapeDtypeStruct(weight.shape, weight.dtype),
        in_specs=[HBM] + [ANY] * len(others),
        out_specs=VMEM,
        scratch_shapes=[pltpu.SemaphoreType.DMA((8,))],
        compiler_params=limit(36),
        cost_estimate=cost(0, 4 * weight.size),
        name="fetch",
    )(in_hbm(weight), *others)


def project_kernel(count, tile, *refs):
    part_refs, weight_ref, out_ref = refs[:count], refs[count], refs[count + 1]
    tp_index = lax.axis_index("tp")
    prompts, samples, width = out_ref.shape
    share = prompts // count
    left = jnp.concatenate([ref[...].astype(jnp.float32) for ref in part_refs], axis=0).astype(jnp.bfloat16)
    for first in range(0, width, tile):
        result = jnp.dot(left, weight_ref[:, first : first + tile], preferred_element_type=jnp.float32)
        for offset in range(count):
            for n in range(share):
                row = (offset * share + n) * samples
                block = result[row : row + samples].astype(out_ref.dtype)
                out_ref[(tp_index ^ offset) * share + n, :, first : first + tile] = block


def project(parts, weight, samples):
    count = len(parts)
    depth, width = weight.shape
    total = count * parts[0].shape[0]
    return pl.pallas_call(
        functools.partial(project_kernel, count, min(256, width)),
        out_shape=jax.ShapeDtypeStruct((total // samples, samples, width), jnp.bfloat16),
        in_specs=[VMEM] * (count + 1),
        out_specs=VMEM,
        compiler_params=limit(24),
        cost_estimate=cost(2 * total * depth * width, 2 * depth * width),
        name="project",
    )(*parts, weight)


def body(prompt_key_values, queries, routing, lengths, out_weight):
    section_count = lax.axis_size("sec")
    tp_count = lax.axis_size("tp")
    slot_count, samples, query_width = queries.shape[1:]
    routing = routing.reshape(-1)

    near = [(offset, 0, CAP) for offset in range(2)]
    far = [(offset, 0, CAP) for offset in range(2, section_count)]
    early, late = far[:1], far[1:] + near
    early_caches, query_parts = first_pack(
        routing, prompt_key_values, queries, early, section_count, tp_count
    )
    query_parts = [swap(part, "sec", offset) for offset, part in enumerate(query_parts)]
    late_caches, merged = second_pack(routing, prompt_key_values, query_parts[2:], late, section_count)
    far_queries = spread(merged, "tp")
    caches, pieces = [*early_caches, *late_caches], early + late
    arrived = [swap(part, "sec", piece[0]) for part, piece in zip(caches, pieces)]
    far_parts, near_parts = arrived[: len(far)], arrived[len(far) :]

    messages = attend(routing, lengths, caches, pieces, query_parts[:2], far_queries)
    partials = [swap(part, "tp", offset) for offset, part in enumerate(messages)]
    held_weight = fetch(out_weight, messages[:1])
    share = join(partials, [held_weight], samples)
    shares = spread(share, "tp")
    if share.ndim == 3:
        attended = jnp.stack(shares)[jnp.arange(tp_count) ^ lax.axis_index("tp")]
        attended = attended.reshape(REQ_GRP, KEY_VALUE_HEADS, samples, -1).transpose(0, 2, 1, 3)
        attended = attended.reshape(REQ_GRP * samples, query_width)
        layer_out = jnp.dot(attended, out_weight, preferred_element_type=jnp.float32)
        layer_out = layer_out.astype(jnp.bfloat16).reshape(REQ_GRP, samples, -1)
    else:
        layer_out = project(shares, held_weight, samples)

    stages = [([part], [piece]) for part, piece in zip(far_parts, far)]
    stages.insert(-1, (near_parts, near))
    whole = []
    for parts, pieces in stages:
        whole = [place(whole + [layer_out], parts, pieces, slot_count)]
    return (layer_out, *whole)


def solution(mesh):
    placed = (
        P(("rep", "sec"), None, "tp", None),
        P(("rep", "sec"), None, None, None),
        P("rep", None),
        P("rep"),
        P(None, "tp"),
    )
    return jax.shard_map(
        body,
        mesh=mesh,
        in_specs=placed,
        out_specs=(P(("rep", "sec"), None, "tp"), P(("rep", "sec"), None, None, "tp", None)),
        check_vma=False,
    )
```

```python
import functools

import jax
import jax.numpy as jnp
from jax import lax
from jax.experimental import pallas as pl
from jax.experimental.pallas import tpu as pltpu
from jax.sharding import PartitionSpec as P

HEAD_SIZE = 128
KEY_VALUE_HEADS = 4
REQ_GRP = 8
CAP = 2
HIDDEN = -1e30

ANY = pl.BlockSpec(memory_space=pl.ANY)
HBM = pl.BlockSpec(memory_space=pltpu.HBM)
VMEM = pl.BlockSpec(memory_space=pltpu.VMEM)
SMEM = pl.BlockSpec(memory_space=pltpu.SMEM)


def limit(mebibytes):
    return pltpu.CompilerParams(vmem_limit_bytes=mebibytes << 20)


def cost(flops, bytes_accessed, transcendentals=0):
    return pl.CostEstimate(flops=flops, bytes_accessed=bytes_accessed, transcendentals=transcendentals)


def swap(value, axis, offset):
    if offset == 0:
        return value
    count = lax.axis_size(axis)
    return lax.ppermute(value, axis, [(i, i ^ offset) for i in range(count)])


def spread(value, axis):
    return [swap(value, axis, offset) for offset in range(lax.axis_size(axis))]


def own_slots(routing_ref, section, used, source):
    for t in range(used.shape[0]):
        used[t] = 0
    for i in range(REQ_GRP):
        target = routing_ref[section * REQ_GRP + i]
        order = used[target]
        used[target] = order + 1
        source[target * CAP + order] = i


def pack_slots(pieces, section_count):
    return [
        (n, place, offset, first + place)
        for n, (offset, first, count) in enumerate(pieces)
        for place in range(count)
    ]


def start_packing(pieces, section_count, routing_ref, cache_ref, out_refs, source, used, sem):
    section = lax.axis_index("sec")
    full = section_count * CAP == REQ_GRP
    own_slots(routing_ref, section, used, source)
    spots = pack_slots(pieces, section_count)

    def copy(n, place, offset, order, row):
        return pltpu.make_async_copy(cache_ref.at[row], out_refs[n].at[place], sem.at[offset * CAP + order])

    for n, place, offset, order in spots:
        target = section ^ offset
        if full:
            copy(n, place, offset, order, source[target * CAP + order]).start()
        else:

            @pl.when(order < used[target])
            def _():
                copy(n, place, offset, order, source[target * CAP + order]).start()

            @pl.when(order >= used[target])
            def _():
                out_refs[n][place] = jnp.zeros_like(out_refs[n][place])

    def finish():
        for n, place, offset, order in spots:
            if full:
                copy(n, place, offset, order, 0).wait()
            else:

                @pl.when(order < used[section ^ offset])
                def _():
                    copy(n, place, offset, order, 0).wait()

    return finish


def first_pack_kernel(pieces, section_count, routing_ref, cache_ref, query_ref, *refs):
    cache_out, query_out = refs[: len(pieces)], refs[len(pieces) : -4]
    source, used, sem, query_sem = refs[-4:]
    section = lax.axis_index("sec")
    query_copies = []
    for offset, out_ref in enumerate(query_out):
        width = out_ref.shape[2]
        columns = pl.ds(pl.multiple_of(lax.axis_index("tp") * width, width) if offset > 1 else 0, width)
        part = query_ref.at[0, pl.ds((section ^ offset) * CAP, CAP), :, columns]
        query_copies.append(pltpu.make_async_copy(part, out_ref, query_sem.at[offset]))
        query_copies[-1].start()
    finish = start_packing(pieces, section_count, routing_ref, cache_ref, cache_out, source, used, sem)
    finish()
    for copy in query_copies:
        copy.wait()


def second_pack_kernel(pieces, section_count, routing_ref, cache_ref, *refs):
    cache_out, (source, used, sem) = refs[-3 - len(pieces) : -3], refs[-3:]
    start_packing(pieces, section_count, routing_ref, cache_ref, cache_out, source, used, sem)()


def merge_kernel(count, *refs):
    for n in range(count):
        refs[-1][n] = refs[n][...]


def merge(parts, others):
    shape = (len(parts),) + parts[0].shape
    return pl.pallas_call(
        functools.partial(merge_kernel, len(parts)),
        out_shape=jax.ShapeDtypeStruct(shape, parts[0].dtype),
        in_specs=[VMEM] * len(parts) + [ANY] * len(others),
        out_specs=VMEM,
        compiler_params=limit(8),
        cost_estimate=cost(0, 8 * len(parts) * parts[0].size),
        name="merge",
    )(*parts, *others)


def in_hbm(value):
    return pltpu.with_memory_space_constraint(value, pltpu.HBM)


def first_pack(routing, cache, queries, pieces, section_count, tp_count):
    samples, width = queries.shape[2:]
    widths = [width if offset < 2 else width // tp_count for offset in range(section_count)]
    shapes = [jax.ShapeDtypeStruct((count,) + cache.shape[1:], cache.dtype) for _, _, count in pieces]
    shapes += [jax.ShapeDtypeStruct((CAP, samples, one), queries.dtype) for one in widths]
    parts = pl.pallas_call(
        functools.partial(first_pack_kernel, pieces, section_count),
        out_shape=shapes,
        in_specs=[SMEM, HBM, HBM],
        out_specs=[VMEM] * len(shapes),
        scratch_shapes=[
            pltpu.SMEM((section_count * CAP,), jnp.int32),
            pltpu.SMEM((section_count,), jnp.int32),
            pltpu.SemaphoreType.DMA((section_count * CAP,)),
            pltpu.SemaphoreType.DMA((section_count,)),
        ],
        compiler_params=limit(16),
        cost_estimate=cost(0, 4 * sum(shape.size for shape in shapes)),
        name="first_pack",
    )(in_hbm(routing), in_hbm(cache), in_hbm(queries))
    return parts[: len(pieces)], parts[len(pieces) :]


def second_pack(routing, cache, others, pieces, section_count):
    shapes = [jax.ShapeDtypeStruct((count,) + cache.shape[1:], cache.dtype) for _, _, count in pieces]
    return pl.pallas_call(
        functools.partial(second_pack_kernel, pieces, section_count),
        out_shape=shapes,
        in_specs=[SMEM, HBM] + [ANY] * len(others),
        out_specs=[VMEM] * len(shapes),
        scratch_shapes=[
            pltpu.SMEM((section_count * CAP,), jnp.int32),
            pltpu.SMEM((section_count,), jnp.int32),
            pltpu.SemaphoreType.DMA((section_count * CAP,)),
        ],
        compiler_params=limit(16),
        cost_estimate=cost(10**10, 4 * sum(shape.size for shape in shapes)),
        name="second_pack",
    )(in_hbm(routing), in_hbm(cache), *others)


def place_kernel(pieces, *refs):
    count = len(pieces)
    part_refs, out_ref, sem = refs[-2 - count : -2], refs[-2], refs[-1]
    section = lax.axis_index("sec")
    copies = []
    for n, (offset, first, size) in enumerate(pieces):
        slots = out_ref.at[0, pl.ds((section ^ offset) * CAP + first, size)]
        copies.append(pltpu.make_async_copy(part_refs[n], slots, sem.at[n]))
        copies[-1].start()
    for copy in copies:
        copy.wait()


def place(given, parts, pieces, slot_count):
    part = parts[0]
    return pl.pallas_call(
        functools.partial(place_kernel, pieces),
        out_shape=jax.ShapeDtypeStruct((1, slot_count) + part.shape[1:], part.dtype),
        in_specs=[HBM] * len(given) + [VMEM] * len(parts),
        out_specs=HBM,
        scratch_shapes=[pltpu.SemaphoreType.DMA((len(parts),))],
        input_output_aliases={0: 0} if given else {},
        compiler_params=limit(8),
        cost_estimate=cost(0, 4 * sum(piece.size for piece in parts)),
        name="place",
    )(*[in_hbm(value) for value in given], *parts)


def attend_kernel(pieces, section_count, tp_count, routing_ref, lengths_ref, *refs):
    cache_refs, refs = refs[: len(pieces)], refs[len(pieces) :]
    query_refs, far_refs = refs[:2], refs[2 : 2 + tp_count]
    message_refs = refs[2 + tp_count : 2 + 2 * tp_count]
    source, used, messages, stats, stacked, far_queries = refs[2 + 2 * tp_count :]
    section = lax.axis_index("sec")
    tp_index = lax.axis_index("tp")
    local = cache_refs[0].shape[2]
    groups, rows, _ = messages.shape[1:]
    span = KEY_VALUE_HEADS * rows
    prompts = max(1, groups // KEY_VALUE_HEADS)
    full = section_count * CAP == REQ_GRP
    own_slots(routing_ref, section, used, source)
    samples = query_refs[0].shape[1]
    for offset, far_ref in enumerate(far_refs):
        far_queries[tp_index ^ offset] = far_ref[...]
    position = lax.broadcasted_iota(jnp.int32, (local, span), 0) + tp_index * local
    owner = lax.broadcasted_iota(jnp.int32, (HEAD_SIZE, span), 1) // rows

    def prompt(cache_ref, place, offset, order):
        row = source[(section ^ offset) * CAP + order]
        visible = position < lengths_ref[section * REQ_GRP + row]
        slot = offset * CAP + order
        for head in range(span // samples):
            first, part = head * HEAD_SIZE, far_queries.shape[-1]
            if offset < 2:
                values = query_refs[offset][order, :, first : first + HEAD_SIZE]
            else:
                inner = first % part
                values = far_queries[first // part, offset - 2, order, :, inner : inner + HEAD_SIZE]
            stacked[slot, head * samples : (head + 1) * samples] = values.astype(jnp.float32)
        query = stacked[slot].T.astype(jnp.bfloat16)
        query = [jnp.where(owner == k, query, jnp.zeros_like(query)) for k in range(KEY_VALUE_HEADS)]
        score = jnp.dot(
            cache_ref[place, 0], jnp.concatenate(query, axis=0), preferred_element_type=jnp.float32
        ) * HEAD_SIZE ** (-0.5)
        score = jnp.where(visible, score, HIDDEN)
        peak = jnp.max(score, axis=0, keepdims=True)
        weight = jnp.where(visible, jnp.exp(score - peak), 0.0)
        total = jnp.sum(weight, axis=0, keepdims=True)
        some = total > 0.0
        safe = jnp.where(some, total, 1.0)
        stats[pl.ds(row, 1)] = jnp.where(some, peak + jnp.log(safe), HIDDEN)
        weight = (weight * (1.0 / safe)).T.astype(jnp.bfloat16)
        for k in range(KEY_VALUE_HEADS):
            mixed = jnp.dot(
                weight[k * rows : (k + 1) * rows],
                cache_ref[place, 1, :, k * HEAD_SIZE : (k + 1) * HEAD_SIZE],
                preferred_element_type=jnp.float32,
            )
            group = row * KEY_VALUE_HEADS + k
            messages[group // groups, group % groups] = mixed.astype(jnp.bfloat16)

    for cache_ref, (offset, first, size) in zip(cache_refs, pieces):
        for place in range(size):
            one = functools.partial(prompt, cache_ref, place, offset, first + place)
            if full:
                one()
            else:
                pl.when(first + place < used[section ^ offset])(one)

    level = stats[...]
    high = level.astype(jnp.bfloat16).astype(jnp.float32)
    rest = level - high
    middle = rest.astype(jnp.bfloat16).astype(jnp.float32)
    stats[...] = high
    stats_middle, stats_low = middle, rest - middle
    for offset in range(tp_count):
        device = tp_index ^ offset
        message_refs[offset][0:groups] = messages[device]
        message_refs[offset][groups] = jnp.zeros((rows, HEAD_SIZE), jnp.bfloat16)
    for part, values in enumerate((high, stats_middle, stats_low)):
        stats[...] = values
        for offset in range(tp_count):
            first = (tp_index ^ offset) * groups // KEY_VALUE_HEADS
            block = jnp.concatenate(
                [stats[pl.ds(first + n, 1)] for n in range(prompts)]
                + [jnp.zeros((16 - prompts, span), jnp.float32)],
                axis=0,
            )
            if part < 2:
                message_refs[offset][groups, part * 16 : part * 16 + 16] = block.astype(jnp.bfloat16)
            else:
                message_refs[offset][groups + 1] = jnp.concatenate([block, jnp.zeros_like(block)], axis=0).astype(
                    jnp.bfloat16
                )


def attend(routing, lengths, caches, pieces, queries, far_queries):
    section_count = len(far_queries[0]) + 2
    tp_count = len(far_queries)
    samples, width = queries[0].shape[1:]
    span = width // HEAD_SIZE * samples
    rows = span // KEY_VALUE_HEADS
    groups = REQ_GRP * KEY_VALUE_HEADS // tp_count
    multiplies = REQ_GRP * span * HEAD_SIZE * caches[0].shape[2]
    return pl.pallas_call(
        functools.partial(attend_kernel, pieces, section_count, tp_count),
        out_shape=[jax.ShapeDtypeStruct((groups + 2, rows, HEAD_SIZE), jnp.bfloat16)] * tp_count,
        in_specs=[SMEM, SMEM] + [VMEM] * (len(caches) + len(queries) + tp_count),
        out_specs=[VMEM] * tp_count,
        scratch_shapes=[
            pltpu.SMEM((section_count * CAP,), jnp.int32),
            pltpu.SMEM((section_count,), jnp.int32),
            pltpu.VMEM((tp_count, groups, rows, HEAD_SIZE), jnp.bfloat16),
            pltpu.VMEM((REQ_GRP, span), jnp.float32),
            pltpu.VMEM((section_count * CAP, span, HEAD_SIZE), jnp.float32),
            pltpu.VMEM((tp_count,) + far_queries[0].shape, far_queries[0].dtype),
        ],
        compiler_params=limit(12),
        cost_estimate=cost(2 * 10**10, 2 * sum(part.size for part in caches), multiplies // HEAD_SIZE),
        name="attend",
    )(routing, lengths, *caches, *queries, *far_queries)


def join_kernel(count, samples, *refs):
    message_refs, (out_ref, scaling, flat) = refs[:count], refs[-3:]
    groups, rows, _ = message_refs[0].shape
    groups -= 2
    heads = rows // samples
    tp_index = lax.axis_index("tp")
    levels = []
    for ref in message_refs:
        upper = ref[groups].astype(jnp.float32)
        lower = ref[groups + 1].astype(jnp.float32)
        levels.append(upper[0:8] + upper[16:24] + lower[0:8])
    summit = functools.reduce(jnp.maximum, levels)
    scales = [jnp.exp(level - summit) for level in levels]
    total = functools.reduce(jnp.add, scales)
    for n, scale in enumerate(scales):
        scaling[n] = (scale / total).T
    for inner in range(groups):
        if groups % KEY_VALUE_HEADS:
            first = (tp_index * groups + inner) % KEY_VALUE_HEADS * rows
            part = pl.ds(pl.multiple_of(first, rows), rows)
        else:
            part = pl.ds(inner % KEY_VALUE_HEADS * rows, rows)
        prompt = inner // KEY_VALUE_HEADS
        terms = [
            ref[inner].astype(jnp.float32) * scaling[n, part, prompt : prompt + 1]
            for n, ref in enumerate(message_refs)
        ]
        joined = functools.reduce(jnp.add, terms)
        for head in range(heads):
            block = joined[head * samples : (head + 1) * samples]
            if len(flat.shape) == 2:
                row = prompt * samples
                column = (inner % KEY_VALUE_HEADS * heads + head) * HEAD_SIZE
                flat[row : row + samples, column : column + HEAD_SIZE] = block
            else:
                flat[inner, :, head * HEAD_SIZE : (head + 1) * HEAD_SIZE] = block
    out_ref[...] = flat[...].astype(jnp.bfloat16)


def join(messages, others, samples):
    groups, rows, _ = messages[0].shape
    groups -= 2
    width = rows // samples * HEAD_SIZE
    if groups % KEY_VALUE_HEADS == 0:
        shape = (groups // KEY_VALUE_HEADS * samples, KEY_VALUE_HEADS * width)
    else:
        shape = (groups, samples, width)
    count = len(messages)
    return pl.pallas_call(
        functools.partial(join_kernel, count, samples),
        out_shape=jax.ShapeDtypeStruct(shape, jnp.bfloat16),
        in_specs=[VMEM] * count + [ANY] * len(others),
        out_specs=VMEM,
        scratch_shapes=[
            pltpu.VMEM((count, KEY_VALUE_HEADS * rows, 8), jnp.float32),
            pltpu.VMEM(shape, jnp.float32),
        ],
        compiler_params=limit(8),
        cost_estimate=cost(4 * count * messages[0].size, 2 * count * messages[0].size),
        name="join",
    )(*messages, *others)


def fetch_kernel(weight_ref, *refs):
    out_ref, sem = refs[-2:]
    copies = []
    step = weight_ref.shape[0] // sem.shape[0]
    for n in range(sem.shape[0]):
        part = pl.ds(n * step, step)
        copies.append(pltpu.make_async_copy(weight_ref.at[part], out_ref.at[part], sem.at[n]))
        copies[-1].start()
    for copy in copies:
        copy.wait()


def fetch(weight, others):
    return pl.pallas_call(
        fetch_kernel,
        out_shape=jax.ShapeDtypeStruct(weight.shape, weight.dtype),
        in_specs=[HBM] + [ANY] * len(others),
        out_specs=VMEM,
        scratch_shapes=[pltpu.SemaphoreType.DMA((8,))],
        compiler_params=limit(36),
        cost_estimate=cost(0, 4 * weight.size),
        name="fetch",
    )(in_hbm(weight), *others)


def project_kernel(count, tile, *refs):
    part_refs, weight_ref, out_ref = refs[:count], refs[count], refs[count + 1]
    tp_index = lax.axis_index("tp")
    prompts, samples, width = out_ref.shape
    share = prompts // count
    left = jnp.concatenate([ref[...].astype(jnp.float32) for ref in part_refs], axis=0).astype(jnp.bfloat16)
    for first in range(0, width, tile):
        result = jnp.dot(left, weight_ref[:, first : first + tile], preferred_element_type=jnp.float32)
        for offset in range(count):
            for n in range(share):
                row = (offset * share + n) * samples
                block = result[row : row + samples].astype(out_ref.dtype)
                out_ref[(tp_index ^ offset) * share + n, :, first : first + tile] = block


def project(parts, weight, samples):
    count = len(parts)
    depth, width = weight.shape
    total = count * parts[0].shape[0]
    return pl.pallas_call(
        functools.partial(project_kernel, count, min(256, width)),
        out_shape=jax.ShapeDtypeStruct((total // samples, samples, width), jnp.bfloat16),
        in_specs=[VMEM] * (count + 1),
        out_specs=VMEM,
        compiler_params=limit(24),
        cost_estimate=cost(2 * total * depth * width, 2 * depth * width),
        name="project",
    )(*parts, weight)


def body(prompt_key_values, queries, routing, lengths, out_weight):
    section_count = lax.axis_size("sec")
    tp_count = lax.axis_size("tp")
    slot_count, samples, query_width = queries.shape[1:]
    routing = routing.reshape(-1)

    near = [(offset, 0, CAP) for offset in range(2)]
    far = [(offset, 0, CAP) for offset in range(2, section_count)]
    far_caches, query_parts = first_pack(routing, prompt_key_values, queries, far, section_count, tp_count)
    query_parts = [swap(part, "sec", offset) for offset, part in enumerate(query_parts)]
    far_parts = [swap(part, "sec", piece[0]) for part, piece in zip(far_caches, far)]
    merged = merge(query_parts[2:], query_parts[1:2])
    far_queries = spread(merged, "tp")
    near_caches = second_pack(routing, prompt_key_values, [merged], near, section_count)
    near_parts = [swap(part, "sec", piece[0]) for part, piece in zip(near_caches, near)]
    caches, pieces = [*far_caches, *near_caches], far + near

    messages = attend(routing, lengths, caches, pieces, query_parts[:2], far_queries)
    partials = [swap(part, "tp", offset) for offset, part in enumerate(messages)]
    held_weight = fetch(out_weight, [messages[0], *near_parts[1:]])
    share = join(partials, [held_weight], samples)
    shares = spread(share, "tp")
    if share.ndim == 3:
        attended = jnp.stack(shares)[jnp.arange(tp_count) ^ lax.axis_index("tp")]
        attended = attended.reshape(REQ_GRP, KEY_VALUE_HEADS, samples, -1).transpose(0, 2, 1, 3)
        attended = attended.reshape(REQ_GRP * samples, query_width)
        layer_out = jnp.dot(attended, out_weight, preferred_element_type=jnp.float32)
        layer_out = layer_out.astype(jnp.bfloat16).reshape(REQ_GRP, samples, -1)
    else:
        layer_out = project(shares, held_weight, samples)

    whole = place([], near_parts, near, slot_count)
    for part, piece in zip(far_parts, far):
        whole = place([whole, layer_out], [part], [piece], slot_count)
    return (layer_out, whole)


def solution(mesh):
    placed = (
        P(("rep", "sec"), None, "tp", None),
        P(("rep", "sec"), None, None, None),
        P("rep", None),
        P("rep"),
        P(None, "tp"),
    )
    return jax.shard_map(
        body,
        mesh=mesh,
        in_specs=placed,
        out_specs=(P(("rep", "sec"), None, "tp"), P(("rep", "sec"), None, None, "tp", None)),
        check_vma=False,
    )
```

```python
import functools

import jax
import jax.numpy as jnp
from jax import lax
from jax.experimental import pallas as pl
from jax.experimental.pallas import tpu as pltpu
from jax.sharding import PartitionSpec as P

HEAD_SIZE = 128
KEY_VALUE_HEADS = 4
REQ_GRP = 8
CAP = 2
HIDDEN = -1e30

ANY = pl.BlockSpec(memory_space=pl.ANY)
HBM = pl.BlockSpec(memory_space=pltpu.HBM)
VMEM = pl.BlockSpec(memory_space=pltpu.VMEM)
SMEM = pl.BlockSpec(memory_space=pltpu.SMEM)


def limit(mebibytes):
    return pltpu.CompilerParams(vmem_limit_bytes=mebibytes << 20)


def cost(flops, bytes_accessed, transcendentals=0):
    return pl.CostEstimate(flops=flops, bytes_accessed=bytes_accessed, transcendentals=transcendentals)


def swap(value, axis, offset):
    if offset == 0:
        return value
    count = lax.axis_size(axis)
    return lax.ppermute(value, axis, [(i, i ^ offset) for i in range(count)])


def spread(value, axis):
    return [swap(value, axis, offset) for offset in range(lax.axis_size(axis))]


def own_slots(routing_ref, section, used, source):
    for t in range(used.shape[0]):
        used[t] = 0
    for i in range(REQ_GRP):
        target = routing_ref[section * REQ_GRP + i]
        order = used[target]
        used[target] = order + 1
        source[target * CAP + order] = i


def halves_of(pieces):
    return [
        (n, place, offset, first + place)
        for n, (offset, first, count) in enumerate(pieces)
        for place in range(count)
    ]


def start_packing(pieces, section_count, routing_ref, cache_ref, out_refs, source, used, sem):
    section = lax.axis_index("sec")
    full = section_count * CAP == REQ_GRP
    own_slots(routing_ref, section, used, source)
    halves = halves_of(pieces)

    def copy(n, place, offset, half, row):
        return pltpu.make_async_copy(
            cache_ref.at[row, half % 2], out_refs[n].at[place], sem.at[offset * 2 * CAP + half]
        )

    for n, place, offset, half in halves:
        target, order = section ^ offset, half // 2
        if full:
            copy(n, place, offset, half, source[target * CAP + order]).start()
        else:

            @pl.when(order < used[target])
            def _():
                copy(n, place, offset, half, source[target * CAP + order]).start()

            @pl.when(order >= used[target])
            def _():
                out_refs[n][place] = jnp.zeros_like(out_refs[n][place])

    def finish():
        for n, place, offset, half in halves:
            if full:
                copy(n, place, offset, half, 0).wait()
            else:

                @pl.when(half // 2 < used[section ^ offset])
                def _():
                    copy(n, place, offset, half, 0).wait()

    return finish


def first_pack_kernel(pieces, section_count, routing_ref, cache_ref, query_ref, *refs):
    refs, (source, used, sem, query_sem) = refs[:-4], refs[-4:]
    query_out, cache_out = refs[-section_count:], refs[-section_count - len(pieces) : -section_count]
    section = lax.axis_index("sec")
    query_copies = []
    for offset, out_ref in enumerate(query_out):
        width = out_ref.shape[2]
        columns = pl.ds(pl.multiple_of(lax.axis_index("tp") * width, width) if offset > 1 else 0, width)
        part = query_ref.at[0, pl.ds((section ^ offset) * CAP, CAP), :, columns]
        query_copies.append(pltpu.make_async_copy(part, out_ref, query_sem.at[offset]))
        query_copies[-1].start()
    finish = start_packing(pieces, section_count, routing_ref, cache_ref, cache_out, source, used, sem)
    finish()
    for copy in query_copies:
        copy.wait()


def pack_kernel(pieces, section_count, routing_ref, cache_ref, *refs):
    cache_out, (source, used, sem) = refs[-3 - len(pieces) : -3], refs[-3:]
    start_packing(pieces, section_count, routing_ref, cache_ref, cache_out, source, used, sem)()


def merge_kernel(count, *refs):
    for n in range(count):
        refs[-1][n] = refs[n][...]


def merge(parts, others):
    shape = (len(parts),) + parts[0].shape
    return pl.pallas_call(
        functools.partial(merge_kernel, len(parts)),
        out_shape=jax.ShapeDtypeStruct(shape, parts[0].dtype),
        in_specs=[VMEM] * len(parts) + [ANY] * len(others),
        out_specs=VMEM,
        compiler_params=limit(8),
        cost_estimate=cost(0, 8 * len(parts) * parts[0].size),
        name="merge",
    )(*parts, *others)


def in_hbm(value):
    return pltpu.with_memory_space_constraint(value, pltpu.HBM)


def first_pack(routing, cache, queries, others, pieces, section_count, tp_count):
    samples, width = queries.shape[2:]
    widths = [width if offset < 2 else width // tp_count for offset in range(section_count)]
    shapes = [jax.ShapeDtypeStruct((count,) + cache.shape[2:], cache.dtype) for _, _, count in pieces]
    shapes += [jax.ShapeDtypeStruct((CAP, samples, one), queries.dtype) for one in widths]
    parts = pl.pallas_call(
        functools.partial(first_pack_kernel, pieces, section_count),
        out_shape=shapes,
        in_specs=[SMEM, HBM, HBM] + [ANY] * len(others),
        out_specs=[VMEM] * len(shapes),
        scratch_shapes=[
            pltpu.SMEM((section_count * CAP,), jnp.int32),
            pltpu.SMEM((section_count,), jnp.int32),
            pltpu.SemaphoreType.DMA((section_count * CAP * 2,)),
            pltpu.SemaphoreType.DMA((section_count,)),
        ],
        compiler_params=limit(16),
        cost_estimate=cost(0, 4 * sum(shape.size for shape in shapes)),
        name="first_pack",
    )(in_hbm(routing), in_hbm(cache), in_hbm(queries), *others)
    return parts[: len(pieces)], parts[len(pieces) :]


def pack(routing, cache, others, pieces, section_count, flops=0):
    shapes = [jax.ShapeDtypeStruct((count,) + cache.shape[2:], cache.dtype) for _, _, count in pieces]
    return pl.pallas_call(
        functools.partial(pack_kernel, pieces, section_count),
        out_shape=shapes,
        in_specs=[SMEM, HBM] + [ANY] * len(others),
        out_specs=[VMEM] * len(shapes),
        scratch_shapes=[
            pltpu.SMEM((section_count * CAP,), jnp.int32),
            pltpu.SMEM((section_count,), jnp.int32),
            pltpu.SemaphoreType.DMA((section_count * CAP * 2,)),
        ],
        compiler_params=limit(16),
        cost_estimate=cost(flops, 4 * sum(shape.size for shape in shapes)),
        name="pack",
    )(in_hbm(routing), in_hbm(cache), *others)


def place_kernel(pieces, *refs):
    count = len(pieces)
    part_refs, out_ref, sem = refs[-2 - count : -2], refs[-2], refs[-1]
    section = lax.axis_index("sec")
    copies = []
    for n, (offset, first, size) in enumerate(pieces):
        halves = out_ref.at[0, pl.ds((section ^ offset) * 2 * CAP + first, size)]
        copies.append(pltpu.make_async_copy(part_refs[n], halves, sem.at[n]))
        copies[-1].start()
    for copy in copies:
        copy.wait()


def place(given, parts, pieces, slot_count):
    part = parts[0]
    return pl.pallas_call(
        functools.partial(place_kernel, pieces),
        out_shape=jax.ShapeDtypeStruct((1, 2 * slot_count) + part.shape[1:], part.dtype),
        in_specs=[HBM] * len(given) + [VMEM] * len(parts),
        out_specs=HBM,
        scratch_shapes=[pltpu.SemaphoreType.DMA((len(parts),))],
        input_output_aliases={0: 0} if given else {},
        compiler_params=limit(8),
        cost_estimate=cost(0, 4 * sum(piece.size for piece in parts)),
        name="place",
    )(*[in_hbm(value) for value in given], *parts)


def attend_kernel(pieces, section_count, tp_count, routing_ref, lengths_ref, *refs):
    cache_refs, refs = refs[: len(pieces)], refs[len(pieces) :]
    query_refs, far_refs = refs[:2], refs[2 : 2 + tp_count]
    message_refs = refs[2 + tp_count : 2 + 2 * tp_count]
    source, used, messages, stats, stacked, far_queries = refs[2 + 2 * tp_count :]
    section = lax.axis_index("sec")
    tp_index = lax.axis_index("tp")
    local = cache_refs[0].shape[1]
    groups, rows, _ = messages.shape[1:]
    span = KEY_VALUE_HEADS * rows
    prompts = max(1, groups // KEY_VALUE_HEADS)
    full = section_count * CAP == REQ_GRP
    own_slots(routing_ref, section, used, source)
    samples = query_refs[0].shape[1]
    for offset, far_ref in enumerate(far_refs):
        far_queries[tp_index ^ offset] = far_ref[...]
    position = lax.broadcasted_iota(jnp.int32, (local, span), 0) + tp_index * local
    owner = lax.broadcasted_iota(jnp.int32, (HEAD_SIZE, span), 1) // rows

    held = {(offset, half): cache_refs[n].at[place] for n, place, offset, half in halves_of(pieces)}

    def prompt(offset, order):
        keys_ref, values_ref = held[offset, 2 * order], held[offset, 2 * order + 1]
        row = source[(section ^ offset) * CAP + order]
        visible = position < lengths_ref[section * REQ_GRP + row]
        slot = offset * CAP + order
        for head in range(span // samples):
            first, part = head * HEAD_SIZE, far_queries.shape[-1]
            if offset < 2:
                values = query_refs[offset][order, :, first : first + HEAD_SIZE]
            else:
                inner = first % part
                values = far_queries[first // part, offset - 2, order, :, inner : inner + HEAD_SIZE]
            stacked[slot, head * samples : (head + 1) * samples] = values.astype(jnp.float32)
        query = stacked[slot].T.astype(jnp.bfloat16)
        query = [jnp.where(owner == k, query, jnp.zeros_like(query)) for k in range(KEY_VALUE_HEADS)]
        score = jnp.dot(
            keys_ref[...], jnp.concatenate(query, axis=0), preferred_element_type=jnp.float32
        ) * HEAD_SIZE ** (-0.5)
        score = jnp.where(visible, score, HIDDEN)
        peak = jnp.max(score, axis=0, keepdims=True)
        weight = jnp.where(visible, jnp.exp(score - peak), 0.0)
        total = jnp.sum(weight, axis=0, keepdims=True)
        some = total > 0.0
        safe = jnp.where(some, total, 1.0)
        stats[pl.ds(row, 1)] = jnp.where(some, peak + jnp.log(safe), HIDDEN)
        weight = (weight * (1.0 / safe)).T.astype(jnp.bfloat16)
        for k in range(KEY_VALUE_HEADS):
            mixed = jnp.dot(
                weight[k * rows : (k + 1) * rows],
                values_ref[:, k * HEAD_SIZE : (k + 1) * HEAD_SIZE],
                preferred_element_type=jnp.float32,
            )
            group = row * KEY_VALUE_HEADS + k
            messages[group // groups, group % groups] = mixed.astype(jnp.bfloat16)

    for offset, half in held:
        if half % 2 == 0:
            one = functools.partial(prompt, offset, half // 2)
            if full:
                one()
            else:
                pl.when(half // 2 < used[section ^ offset])(one)

    level = stats[...]
    high = level.astype(jnp.bfloat16).astype(jnp.float32)
    rest = level - high
    middle = rest.astype(jnp.bfloat16).astype(jnp.float32)
    stats[...] = high
    stats_middle, stats_low = middle, rest - middle
    for offset in range(tp_count):
        device = tp_index ^ offset
        message_refs[offset][0:groups] = messages[device]
        message_refs[offset][groups] = jnp.zeros((rows, HEAD_SIZE), jnp.bfloat16)
    for part, values in enumerate((high, stats_middle, stats_low)):
        stats[...] = values
        for offset in range(tp_count):
            first = (tp_index ^ offset) * groups // KEY_VALUE_HEADS
            block = jnp.concatenate(
                [stats[pl.ds(first + n, 1)] for n in range(prompts)]
                + [jnp.zeros((16 - prompts, span), jnp.float32)],
                axis=0,
            )
            if part < 2:
                message_refs[offset][groups, part * 16 : part * 16 + 16] = block.astype(jnp.bfloat16)
            else:
                message_refs[offset][groups + 1] = jnp.concatenate([block, jnp.zeros_like(block)], axis=0).astype(
                    jnp.bfloat16
                )


def attend(routing, lengths, caches, pieces, queries, far_queries):
    section_count = len(far_queries[0]) + 2
    tp_count = len(far_queries)
    samples, width = queries[0].shape[1:]
    span = width // HEAD_SIZE * samples
    rows = span // KEY_VALUE_HEADS
    groups = REQ_GRP * KEY_VALUE_HEADS // tp_count
    multiplies = REQ_GRP * span * HEAD_SIZE * caches[0].shape[1]
    return pl.pallas_call(
        functools.partial(attend_kernel, pieces, section_count, tp_count),
        out_shape=[jax.ShapeDtypeStruct((groups + 2, rows, HEAD_SIZE), jnp.bfloat16)] * tp_count,
        in_specs=[SMEM, SMEM] + [VMEM] * (len(caches) + len(queries) + tp_count),
        out_specs=[VMEM] * tp_count,
        scratch_shapes=[
            pltpu.SMEM((section_count * CAP,), jnp.int32),
            pltpu.SMEM((section_count,), jnp.int32),
            pltpu.VMEM((tp_count, groups, rows, HEAD_SIZE), jnp.bfloat16),
            pltpu.VMEM((REQ_GRP, span), jnp.float32),
            pltpu.VMEM((section_count * CAP, span, HEAD_SIZE), jnp.float32),
            pltpu.VMEM((tp_count,) + far_queries[0].shape, far_queries[0].dtype),
        ],
        compiler_params=limit(12),
        cost_estimate=cost(2 * 10**10, 2 * sum(part.size for part in caches), multiplies // HEAD_SIZE),
        name="attend",
    )(routing, lengths, *caches, *queries, *far_queries)


def join_kernel(count, samples, *refs):
    message_refs, (out_ref, scaling, flat) = refs[:count], refs[-3:]
    groups, rows, _ = message_refs[0].shape
    groups -= 2
    heads = rows // samples
    tp_index = lax.axis_index("tp")
    levels = []
    for ref in message_refs:
        upper = ref[groups].astype(jnp.float32)
        lower = ref[groups + 1].astype(jnp.float32)
        levels.append(upper[0:8] + upper[16:24] + lower[0:8])
    summit = functools.reduce(jnp.maximum, levels)
    scales = [jnp.exp(level - summit) for level in levels]
    total = functools.reduce(jnp.add, scales)
    for n, scale in enumerate(scales):
        scaling[n] = (scale / total).T
    for inner in range(groups):
        if groups % KEY_VALUE_HEADS:
            first = (tp_index * groups + inner) % KEY_VALUE_HEADS * rows
            part = pl.ds(pl.multiple_of(first, rows), rows)
        else:
            part = pl.ds(inner % KEY_VALUE_HEADS * rows, rows)
        prompt = inner // KEY_VALUE_HEADS
        terms = [
            ref[inner].astype(jnp.float32) * scaling[n, part, prompt : prompt + 1]
            for n, ref in enumerate(message_refs)
        ]
        joined = functools.reduce(jnp.add, terms)
        for head in range(heads):
            block = joined[head * samples : (head + 1) * samples]
            if len(flat.shape) == 2:
                row = prompt * samples
                column = (inner % KEY_VALUE_HEADS * heads + head) * HEAD_SIZE
                flat[row : row + samples, column : column + HEAD_SIZE] = block
            else:
                flat[inner, :, head * HEAD_SIZE : (head + 1) * HEAD_SIZE] = block
    out_ref[...] = flat[...].astype(jnp.bfloat16)


def join(messages, others, samples):
    groups, rows, _ = messages[0].shape
    groups -= 2
    width = rows // samples * HEAD_SIZE
    if groups % KEY_VALUE_HEADS == 0:
        shape = (groups // KEY_VALUE_HEADS * samples, KEY_VALUE_HEADS * width)
    else:
        shape = (groups, samples, width)
    count = len(messages)
    return pl.pallas_call(
        functools.partial(join_kernel, count, samples),
        out_shape=jax.ShapeDtypeStruct(shape, jnp.bfloat16),
        in_specs=[VMEM] * count + [ANY] * len(others),
        out_specs=VMEM,
        scratch_shapes=[
            pltpu.VMEM((count, KEY_VALUE_HEADS * rows, 8), jnp.float32),
            pltpu.VMEM(shape, jnp.float32),
        ],
        compiler_params=limit(8),
        cost_estimate=cost(4 * count * messages[0].size, 2 * count * messages[0].size),
        name="join",
    )(*messages, *others)


def fetch_kernel(weight_ref, *refs):
    out_ref, sem = refs[-2:]
    copies = []
    step = weight_ref.shape[0] // sem.shape[0]
    for n in range(sem.shape[0]):
        part = pl.ds(n * step, step)
        copies.append(pltpu.make_async_copy(weight_ref.at[part], out_ref.at[part], sem.at[n]))
        copies[-1].start()
    for copy in copies:
        copy.wait()


def fetch(weight, others):
    return pl.pallas_call(
        fetch_kernel,
        out_shape=jax.ShapeDtypeStruct(weight.shape, weight.dtype),
        in_specs=[HBM] + [ANY] * len(others),
        out_specs=VMEM,
        scratch_shapes=[pltpu.SemaphoreType.DMA((8,))],
        compiler_params=limit(36),
        cost_estimate=cost(0, 4 * weight.size),
        name="fetch",
    )(in_hbm(weight), *others)


def project_kernel(count, tile, *refs):
    part_refs, weight_ref, out_ref = refs[:count], refs[count], refs[count + 1]
    tp_index = lax.axis_index("tp")
    prompts, samples, width = out_ref.shape
    share = prompts // count
    left = jnp.concatenate([ref[...].astype(jnp.float32) for ref in part_refs], axis=0).astype(jnp.bfloat16)
    for first in range(0, width, tile):
        result = jnp.dot(left, weight_ref[:, first : first + tile], preferred_element_type=jnp.float32)
        for offset in range(count):
            for n in range(share):
                row = (offset * share + n) * samples
                block = result[row : row + samples].astype(out_ref.dtype)
                out_ref[(tp_index ^ offset) * share + n, :, first : first + tile] = block


def project(parts, weight, samples):
    count = len(parts)
    depth, width = weight.shape
    total = count * parts[0].shape[0]
    return pl.pallas_call(
        functools.partial(project_kernel, count, min(256, width)),
        out_shape=jax.ShapeDtypeStruct((total // samples, samples, width), jnp.bfloat16),
        in_specs=[VMEM] * (count + 1),
        out_specs=VMEM,
        compiler_params=limit(24),
        cost_estimate=cost(2 * total * depth * width, 2 * depth * width),
        name="project",
    )(*parts, weight)


def body(prompt_key_values, queries, routing, lengths, out_weight):
    section_count = lax.axis_size("sec")
    tp_count = lax.axis_size("tp")
    slot_count, samples, query_width = queries.shape[1:]
    routing = routing.reshape(-1)

    whole = 2 * CAP
    near = [(offset, 0, whole) for offset in range(2)]
    head, tail = [(2, 0, 1)], [(2, 1, whole - 1)]
    far = tail + [(offset, 0, whole) for offset in range(3, section_count)]

    def across(parts, pieces):
        return [swap(part, "sec", piece[0]) for part, piece in zip(parts, pieces)]

    head_caches = pack(routing, prompt_key_values, [], head, section_count)
    head_parts = across(head_caches, head)
    far_caches, query_parts = first_pack(
        routing, prompt_key_values, queries, head_caches, far, section_count, tp_count
    )
    query_parts = [swap(part, "sec", offset) for offset, part in enumerate(query_parts)]
    far_parts = across(far_caches, far)
    merged = merge(query_parts[2:], head_parts)
    far_queries = spread(merged, "tp")
    near_caches = pack(routing, prompt_key_values, [merged, query_parts[1]], near, section_count, 10**10)
    near_parts = across(near_caches, near)
    caches, pieces = [*head_caches, *far_caches, *near_caches], head + far + near

    messages = attend(routing, lengths, caches, pieces, query_parts[:2], far_queries)
    partials = [swap(part, "tp", offset) for offset, part in enumerate(messages)]
    held_weight = fetch(out_weight, [messages[0], *near_parts[1:]])
    share = join(partials, [held_weight], samples)
    shares = spread(share, "tp")
    if share.ndim == 3:
        attended = jnp.stack(shares)[jnp.arange(tp_count) ^ lax.axis_index("tp")]
        attended = attended.reshape(REQ_GRP, KEY_VALUE_HEADS, samples, -1).transpose(0, 2, 1, 3)
        attended = attended.reshape(REQ_GRP * samples, query_width)
        layer_out = jnp.dot(attended, out_weight, preferred_element_type=jnp.float32)
        layer_out = layer_out.astype(jnp.bfloat16).reshape(REQ_GRP, samples, -1)
    else:
        layer_out = project(shares, held_weight, samples)

    held_cache = place([], near_parts + head_parts, near + head, slot_count)
    for part, piece in zip(far_parts, far):
        held_cache = place([held_cache, layer_out], [part], [piece], slot_count)
    held_cache = held_cache.reshape((1, slot_count) + prompt_key_values.shape[1:])
    return (layer_out, held_cache)


def solution(mesh):
    placed = (
        P(("rep", "sec"), None, "tp", None),
        P(("rep", "sec"), None, None, None),
        P("rep", None),
        P("rep"),
        P(None, "tp"),
    )
    return jax.shard_map(
        body,
        mesh=mesh,
        in_specs=placed,
        out_specs=(P(("rep", "sec"), None, "tp"), P(("rep", "sec"), None, None, "tp", None)),
        check_vma=False,
    )
```

```python
import functools

import jax
import jax.numpy as jnp
from jax import lax
from jax.experimental import pallas as pl
from jax.experimental.pallas import tpu as pltpu
from jax.sharding import PartitionSpec as P

HEAD_SIZE = 128
KEY_VALUE_HEADS = 4
REQ_GRP = 8
CAP = 2
HIDDEN = -1e30
STAT_ROWS = 16

ANY = pl.BlockSpec(memory_space=pl.ANY)
HBM = pl.BlockSpec(memory_space=pltpu.HBM)
VMEM = pl.BlockSpec(memory_space=pltpu.VMEM)
SMEM = pl.BlockSpec(memory_space=pltpu.SMEM)


def limit(mebibytes):
    return pltpu.CompilerParams(vmem_limit_bytes=mebibytes << 20)


def cost(flops, bytes_accessed, transcendentals=0):
    return pl.CostEstimate(flops=flops, bytes_accessed=bytes_accessed, transcendentals=transcendentals)


def swap(value, axis, offset):
    if offset == 0:
        return value
    count = lax.axis_size(axis)
    return lax.ppermute(value, axis, [(i, i ^ offset) for i in range(count)])


def spread(value, axis):
    return [swap(value, axis, offset) for offset in range(lax.axis_size(axis))]


def own_targets(routing_ref, section):
    return [routing_ref[section * REQ_GRP + i] for i in range(REQ_GRP)]


def slot_row(targets, group, order):
    row, before = jnp.int32(0), jnp.int32(0)
    for i, target in enumerate(targets):
        here = target == group
        row = jnp.where(here & (before == order), i, row)
        before = before + here.astype(jnp.int32)
    return row, before > order


def halves_of(pieces):
    return [
        (n, place, offset, first + place)
        for n, (offset, first, count) in enumerate(pieces)
        for place in range(count)
    ]


def start_packing(pieces, section_count, routing_ref, cache_ref, out_refs, sem):
    section = lax.axis_index("sec")
    full = section_count * CAP == REQ_GRP
    targets = own_targets(routing_ref, section)
    halves = halves_of(pieces)
    slots = {(offset, half // 2) for _, _, offset, half in halves}
    rows = {slot: slot_row(targets, section ^ slot[0], slot[1]) for slot in sorted(slots)}

    def copy(n, place, offset, half):
        row, _ = rows[offset, half // 2]
        return pltpu.make_async_copy(
            cache_ref.at[row, half % 2], out_refs[n].at[place], sem.at[offset * 2 * CAP + half]
        )

    for n, place, offset, half in halves:
        if full:
            copy(n, place, offset, half).start()
        else:
            _, filled = rows[offset, half // 2]

            @pl.when(filled)
            def _():
                copy(n, place, offset, half).start()

            @pl.when(jnp.logical_not(filled))
            def _():
                out_refs[n][place] = jnp.zeros_like(out_refs[n][place])

    def finish():
        for n, place, offset, half in halves:
            if full:
                copy(n, place, offset, half).wait()
            else:
                pl.when(rows[offset, half // 2][1])(copy(n, place, offset, half).wait)

    return finish


def first_pack_kernel(pieces, section_count, routing_ref, cache_ref, query_ref, *refs):
    refs, (sem, query_sem) = refs[:-2], refs[-2:]
    query_out, cache_out = refs[-section_count:], refs[-section_count - len(pieces) : -section_count]
    section = lax.axis_index("sec")
    query_copies = []
    for offset, out_ref in enumerate(query_out):
        width = out_ref.shape[2]
        columns = pl.ds(pl.multiple_of(lax.axis_index("tp") * width, width) if offset > 1 else 0, width)
        part = query_ref.at[0, pl.ds((section ^ offset) * CAP, CAP), :, columns]
        query_copies.append(pltpu.make_async_copy(part, out_ref, query_sem.at[offset]))
        query_copies[-1].start()
    finish = start_packing(pieces, section_count, routing_ref, cache_ref, cache_out, sem)
    finish()
    for copy in query_copies:
        copy.wait()


def pack_kernel(pieces, section_count, routing_ref, cache_ref, *refs):
    cache_out, sem = refs[-1 - len(pieces) : -1], refs[-1]
    start_packing(pieces, section_count, routing_ref, cache_ref, cache_out, sem)()


def merge_kernel(count, *refs):
    for n in range(count):
        refs[-1][n] = refs[n][...]


def merge(parts, others):
    shape = (len(parts),) + parts[0].shape
    return pl.pallas_call(
        functools.partial(merge_kernel, len(parts)),
        out_shape=jax.ShapeDtypeStruct(shape, parts[0].dtype),
        in_specs=[VMEM] * len(parts) + [ANY] * len(others),
        out_specs=VMEM,
        compiler_params=limit(8),
        cost_estimate=cost(0, 8 * len(parts) * parts[0].size),
        name="merge",
    )(*parts, *others)


def in_hbm(value):
    return pltpu.with_memory_space_constraint(value, pltpu.HBM)


def first_pack(routing, cache, queries, others, pieces, section_count, tp_count):
    samples, width = queries.shape[2:]
    widths = [width if offset < 2 else width // tp_count for offset in range(section_count)]
    shapes = [jax.ShapeDtypeStruct((count,) + cache.shape[2:], cache.dtype) for _, _, count in pieces]
    shapes += [jax.ShapeDtypeStruct((CAP, samples, one), queries.dtype) for one in widths]
    parts = pl.pallas_call(
        functools.partial(first_pack_kernel, pieces, section_count),
        out_shape=shapes,
        in_specs=[SMEM, HBM, HBM] + [ANY] * len(others),
        out_specs=[VMEM] * len(shapes),
        scratch_shapes=[
            pltpu.SemaphoreType.DMA((section_count * CAP * 2,)),
            pltpu.SemaphoreType.DMA((section_count,)),
        ],
        compiler_params=limit(16),
        cost_estimate=cost(0, 4 * sum(shape.size for shape in shapes)),
        name="first_pack",
    )(in_hbm(routing), in_hbm(cache), in_hbm(queries), *others)
    return parts[: len(pieces)], parts[len(pieces) :]


def pack(routing, cache, others, pieces, section_count, flops=0):
    shapes = [jax.ShapeDtypeStruct((count,) + cache.shape[2:], cache.dtype) for _, _, count in pieces]
    return pl.pallas_call(
        functools.partial(pack_kernel, pieces, section_count),
        out_shape=shapes,
        in_specs=[SMEM, HBM] + [ANY] * len(others),
        out_specs=[VMEM] * len(shapes),
        scratch_shapes=[
            pltpu.SemaphoreType.DMA((section_count * CAP * 2,)),
        ],
        compiler_params=limit(16),
        cost_estimate=cost(flops, 4 * sum(shape.size for shape in shapes)),
        name="pack",
    )(in_hbm(routing), in_hbm(cache), *others)


def place_kernel(pieces, *refs):
    count = len(pieces)
    part_refs, out_ref, sem = refs[-2 - count : -2], refs[-2], refs[-1]
    section = lax.axis_index("sec")
    copies = []
    for n, (offset, first, size) in enumerate(pieces):
        for place in range(size):
            half = out_ref.at[0, (section ^ offset) * 2 * CAP + first + place]
            copies.append(pltpu.make_async_copy(part_refs[n].at[place], half, sem.at[len(copies)]))
            copies[-1].start()
    for copy in copies:
        copy.wait()


def place(given, parts, pieces, slot_count):
    part = parts[0]
    return pl.pallas_call(
        functools.partial(place_kernel, pieces),
        out_shape=jax.ShapeDtypeStruct((1, 2 * slot_count) + part.shape[1:], part.dtype),
        in_specs=[HBM] * len(given) + [VMEM] * len(parts),
        out_specs=HBM,
        scratch_shapes=[pltpu.SemaphoreType.DMA((sum(len(part) for part in parts),))],
        input_output_aliases={0: 0} if given else {},
        compiler_params=limit(8),
        cost_estimate=cost(0, 4 * sum(piece.size for piece in parts)),
        name="place",
    )(*[in_hbm(value) for value in given], *parts)


def attend_kernel(pieces, section_count, tp_count, routing_ref, lengths_ref, *refs):
    cache_refs, refs = refs[: len(pieces)], refs[len(pieces) :]
    query_refs, far_refs = refs[:2], refs[2 : 2 + tp_count]
    message_refs = refs[2 + tp_count : 2 + 2 * tp_count]
    messages, stats, stacked, far_queries = refs[2 + 2 * tp_count :]
    section = lax.axis_index("sec")
    tp_index = lax.axis_index("tp")
    local = cache_refs[0].shape[1]
    groups, rows, _ = messages.shape[1:]
    span = KEY_VALUE_HEADS * rows
    prompts = max(1, groups // KEY_VALUE_HEADS)
    full = section_count * CAP == REQ_GRP
    targets = own_targets(routing_ref, section)
    samples = query_refs[0].shape[1]
    for offset, far_ref in enumerate(far_refs):
        far_queries[tp_index ^ offset] = far_ref[...]
    position = lax.broadcasted_iota(jnp.int32, (local, span), 0) + tp_index * local
    owner = lax.broadcasted_iota(jnp.int32, (HEAD_SIZE, span), 1) // rows

    held = {(offset, half): cache_refs[n].at[place] for n, place, offset, half in halves_of(pieces)}

    def prompt(offset, order):
        keys_ref, values_ref = held[offset, 2 * order], held[offset, 2 * order + 1]
        row, _ = slot_row(targets, section ^ offset, order)
        visible = position < lengths_ref[section * REQ_GRP + row]
        slot = offset * CAP + order
        for head in range(span // samples):
            first, part = head * HEAD_SIZE, far_queries.shape[-1]
            if offset < 2:
                values = query_refs[offset][order, :, first : first + HEAD_SIZE]
            else:
                inner = first % part
                values = far_queries[first // part, offset - 2, order, :, inner : inner + HEAD_SIZE]
            stacked[slot, head * samples : (head + 1) * samples] = values.astype(jnp.float32)
        query = stacked[slot].T.astype(jnp.bfloat16)
        query = [jnp.where(owner == k, query, jnp.zeros_like(query)) for k in range(KEY_VALUE_HEADS)]
        score = jnp.dot(
            keys_ref[...], jnp.concatenate(query, axis=0), preferred_element_type=jnp.float32
        ) * HEAD_SIZE ** (-0.5)
        score = jnp.where(visible, score, HIDDEN)
        peak = jnp.max(score, axis=0, keepdims=True)
        weight = jnp.where(visible, jnp.exp(score - peak), 0.0)
        total = jnp.sum(weight, axis=0, keepdims=True)
        some = total > 0.0
        safe = jnp.where(some, total, 1.0)
        stats[0, pl.ds(row, 1)] = jnp.where(some, peak + jnp.log(safe), HIDDEN)
        weight = (weight * (1.0 / safe)).T.astype(jnp.bfloat16)
        for k in range(KEY_VALUE_HEADS):
            mixed = jnp.dot(
                weight[k * rows : (k + 1) * rows],
                values_ref[:, k * HEAD_SIZE : (k + 1) * HEAD_SIZE],
                preferred_element_type=jnp.float32,
            )
            group = row * KEY_VALUE_HEADS + k
            messages[group // groups, group % groups] = mixed.astype(jnp.bfloat16)

    for offset, half in held:
        if half % 2 == 0:
            one = functools.partial(prompt, offset, half // 2)
            if full:
                one()
            else:
                pl.when(slot_row(targets, section ^ offset, half // 2)[1])(one)

    level = stats[0]
    high = level.astype(jnp.bfloat16).astype(jnp.float32)
    rest = level - high
    middle = rest.astype(jnp.bfloat16).astype(jnp.float32)
    stats[0], stats[1], stats[2] = high, middle, rest - middle
    for offset, message_ref in enumerate(message_refs):
        device = tp_index ^ offset
        for inner in range(groups):
            message_ref[inner * rows : (inner + 1) * rows] = messages[device, inner]
        first = device * groups // KEY_VALUE_HEADS
        lines = [stats[part, pl.ds(first + n, 1)] for part in range(3) for n in range(prompts)]
        lines.append(jnp.zeros((STAT_ROWS - 3 * prompts, span), jnp.float32))
        message_ref[groups * rows :] = jnp.concatenate(lines, axis=0).astype(jnp.bfloat16)


def attend(routing, lengths, caches, pieces, queries, far_queries):
    section_count = len(far_queries[0]) + 2
    tp_count = len(far_queries)
    samples, width = queries[0].shape[1:]
    span = width // HEAD_SIZE * samples
    rows = span // KEY_VALUE_HEADS
    groups = REQ_GRP * KEY_VALUE_HEADS // tp_count
    multiplies = REQ_GRP * span * HEAD_SIZE * caches[0].shape[1]
    return pl.pallas_call(
        functools.partial(attend_kernel, pieces, section_count, tp_count),
        out_shape=[jax.ShapeDtypeStruct((groups * rows + STAT_ROWS, HEAD_SIZE), jnp.bfloat16)] * tp_count,
        in_specs=[SMEM, SMEM] + [VMEM] * (len(caches) + len(queries) + tp_count),
        out_specs=[VMEM] * tp_count,
        scratch_shapes=[
            pltpu.VMEM((tp_count, groups, rows, HEAD_SIZE), jnp.bfloat16),
            pltpu.VMEM((3, REQ_GRP, span), jnp.float32),
            pltpu.VMEM((section_count * CAP, span, HEAD_SIZE), jnp.float32),
            pltpu.VMEM((tp_count,) + far_queries[0].shape, far_queries[0].dtype),
        ],
        compiler_params=limit(12),
        cost_estimate=cost(2 * 10**10, 2 * sum(part.size for part in caches), multiplies // HEAD_SIZE),
        name="attend",
    )(routing, lengths, *caches, *queries, *far_queries)


def join_kernel(count, samples, rows, *refs):
    message_refs, (out_ref, scaling, flat) = refs[:count], refs[-3:]
    groups = (message_refs[0].shape[0] - STAT_ROWS) // rows
    prompts = max(1, groups // KEY_VALUE_HEADS)
    heads = rows // samples
    tp_index = lax.axis_index("tp")
    levels = []
    for ref in message_refs:
        lines = ref[groups * rows :].astype(jnp.float32)[0:8]
        levels.append(lines + pltpu.roll(lines, 8 - prompts, 0) + pltpu.roll(lines, 8 - 2 * prompts, 0))
    summit = functools.reduce(jnp.maximum, levels)
    scales = [jnp.exp(level - summit) for level in levels]
    total = functools.reduce(jnp.add, scales)
    for n, scale in enumerate(scales):
        scaling[n] = (scale / total).T
    for inner in range(groups):
        if groups % KEY_VALUE_HEADS:
            first = (tp_index * groups + inner) % KEY_VALUE_HEADS * rows
            part = pl.ds(pl.multiple_of(first, rows), rows)
        else:
            part = pl.ds(inner % KEY_VALUE_HEADS * rows, rows)
        prompt = inner // KEY_VALUE_HEADS
        terms = [
            ref[inner * rows : (inner + 1) * rows].astype(jnp.float32) * scaling[n, part, prompt : prompt + 1]
            for n, ref in enumerate(message_refs)
        ]
        joined = functools.reduce(jnp.add, terms)
        for head in range(heads):
            block = joined[head * samples : (head + 1) * samples]
            if len(flat.shape) == 2:
                row = prompt * samples
                column = (inner % KEY_VALUE_HEADS * heads + head) * HEAD_SIZE
                flat[row : row + samples, column : column + HEAD_SIZE] = block
            else:
                flat[inner, :, head * HEAD_SIZE : (head + 1) * HEAD_SIZE] = block
    out_ref[...] = flat[...].astype(jnp.bfloat16)


def join(messages, others, samples, heads):
    rows = heads * samples
    groups = (messages[0].shape[0] - STAT_ROWS) // rows
    width = rows // samples * HEAD_SIZE
    if groups % KEY_VALUE_HEADS == 0:
        shape = (groups // KEY_VALUE_HEADS * samples, KEY_VALUE_HEADS * width)
    else:
        shape = (groups, samples, width)
    count = len(messages)
    return pl.pallas_call(
        functools.partial(join_kernel, count, samples, rows),
        out_shape=jax.ShapeDtypeStruct(shape, jnp.bfloat16),
        in_specs=[VMEM] * count + [ANY] * len(others),
        out_specs=VMEM,
        scratch_shapes=[
            pltpu.VMEM((count, KEY_VALUE_HEADS * rows, 8), jnp.float32),
            pltpu.VMEM(shape, jnp.float32),
        ],
        compiler_params=limit(8),
        cost_estimate=cost(4 * count * messages[0].size, 2 * count * messages[0].size),
        name="join",
    )(*messages, *others)


def fetch_kernel(first, weight_ref, *refs):
    out_ref, sem = refs[-2:]
    copies = []
    step = out_ref.shape[0] // sem.shape[0]
    for n in range(sem.shape[0]):
        rows = weight_ref.at[pl.ds(first + n * step, step)]
        copies.append(pltpu.make_async_copy(rows, out_ref.at[pl.ds(n * step, step)], sem.at[n]))
        copies[-1].start()
    for copy in copies:
        copy.wait()


def fetch(weight, others, number, count):
    size = weight.shape[0] // count
    return pl.pallas_call(
        functools.partial(fetch_kernel, number * size),
        out_shape=jax.ShapeDtypeStruct((size,) + weight.shape[1:], weight.dtype),
        in_specs=[HBM] + [ANY] * len(others),
        out_specs=VMEM,
        scratch_shapes=[pltpu.SemaphoreType.DMA((8,))],
        compiler_params=limit(24),
        cost_estimate=cost(0, 4 * weight.size // count),
        name="fetch",
    )(in_hbm(weight), *others)


def project_kernel(count, tile, *refs):
    part_refs, weight_refs, out_ref = refs[:count], refs[count:-1], refs[-1]
    tp_index = lax.axis_index("tp")
    prompts, samples, width = out_ref.shape
    share = prompts // count
    left = jnp.concatenate([ref[...].astype(jnp.float32) for ref in part_refs], axis=0).astype(jnp.bfloat16)
    size = weight_refs[0].shape[0]
    for first in range(0, width, tile):
        result = functools.reduce(
            jnp.add,
            [
                jnp.dot(
                    left[:, n * size : (n + 1) * size],
                    ref[:, first : first + tile],
                    preferred_element_type=jnp.float32,
                )
                for n, ref in enumerate(weight_refs)
            ],
        )
        for offset in range(count):
            for n in range(share):
                row = (offset * share + n) * samples
                block = result[row : row + samples].astype(out_ref.dtype)
                out_ref[(tp_index ^ offset) * share + n, :, first : first + tile] = block


def project(parts, weights, samples):
    count = len(parts)
    depth, width = weights[0].shape
    depth *= len(weights)
    total = count * parts[0].shape[0]
    return pl.pallas_call(
        functools.partial(project_kernel, count, min(256, width)),
        out_shape=jax.ShapeDtypeStruct((total // samples, samples, width), jnp.bfloat16),
        in_specs=[VMEM] * (count + len(weights)),
        out_specs=VMEM,
        compiler_params=limit(24),
        cost_estimate=cost(2 * total * depth * width, 2 * depth * width),
        name="project",
    )(*parts, *weights)


def body(prompt_key_values, queries, routing, lengths, out_weight):
    section_count = lax.axis_size("sec")
    tp_count = lax.axis_size("tp")
    slot_count, samples, query_width = queries.shape[1:]
    routing = routing.reshape(-1)

    whole = 2 * CAP
    near = [(offset, 0, whole) for offset in range(2)]
    head, tail = [(2, 0, 1)], [(2, 1, whole - 1)]
    far = [(offset, 0, whole) for offset in range(3, section_count)] + tail

    def across(parts, pieces):
        return [swap(part, "sec", piece[0]) for part, piece in zip(parts, pieces)]

    head_caches = pack(routing, prompt_key_values, [], head, section_count)
    head_parts = across(head_caches, head)
    far_caches, query_parts = first_pack(
        routing, prompt_key_values, queries, head_caches, far, section_count, tp_count
    )
    query_parts = [swap(part, "sec", offset) for offset, part in enumerate(query_parts)]
    far_parts = across(far_caches, far)
    merged = merge(query_parts[2:], head_parts)
    far_queries = spread(merged, "tp")
    near_caches = pack(routing, prompt_key_values, [merged, query_parts[1]], near, section_count, 10**10)
    near_parts = across(near_caches, near)
    caches, pieces = [*head_caches, *far_caches, *near_caches], head + far + near

    messages = attend(routing, lengths, caches, pieces, query_parts[:2], far_queries)
    partials = [swap(part, "tp", offset) for offset, part in enumerate(messages)]
    held_weight = [fetch(out_weight, [messages[0], *near_parts[1:]], 0, 2)]
    share = join(partials, held_weight, samples, query_width // HEAD_SIZE // KEY_VALUE_HEADS)
    shares = spread(share, "tp")
    held_weight.append(fetch(out_weight, [share], 1, 2))
    if share.ndim == 3:
        attended = jnp.stack(shares)[jnp.arange(tp_count) ^ lax.axis_index("tp")]
        attended = attended.reshape(REQ_GRP, KEY_VALUE_HEADS, samples, -1).transpose(0, 2, 1, 3)
        attended = attended.reshape(REQ_GRP * samples, query_width)
        layer_out = jnp.dot(attended, out_weight, preferred_element_type=jnp.float32)
        layer_out = layer_out.astype(jnp.bfloat16).reshape(REQ_GRP, samples, -1)
    else:
        layer_out = project(shares, held_weight, samples)

    held_cache = place([], near_parts + head_parts, near + head, slot_count)
    for part, piece in zip(far_parts, far):
        held_cache = place([held_cache, layer_out], [part], [piece], slot_count)
    held_cache = held_cache.reshape((1, slot_count) + prompt_key_values.shape[1:])
    return (layer_out, held_cache)


def solution(mesh):
    placed = (
        P(("rep", "sec"), None, "tp", None),
        P(("rep", "sec"), None, None, None),
        P("rep", None),
        P("rep"),
        P(None, "tp"),
    )
    return jax.shard_map(
        body,
        mesh=mesh,
        in_specs=placed,
        out_specs=(P(("rep", "sec"), None, "tp"), P(("rep", "sec"), None, None, "tp", None)),
        check_vma=False,
    )
```

```python
import functools

import jax
import jax.numpy as jnp
from jax import lax
from jax.experimental import pallas as pl
from jax.experimental.pallas import tpu as pltpu
from jax.sharding import PartitionSpec as P

HEAD_SIZE = 128
KEY_VALUE_HEADS = 4
REQ_GRP = 8
CAP = 2
HIDDEN = -1e30
STAT_ROWS = 16

ANY = pl.BlockSpec(memory_space=pl.ANY)
HBM = pl.BlockSpec(memory_space=pltpu.HBM)
VMEM = pl.BlockSpec(memory_space=pltpu.VMEM)
SMEM = pl.BlockSpec(memory_space=pltpu.SMEM)


def limit(mebibytes):
    return pltpu.CompilerParams(vmem_limit_bytes=mebibytes << 20)


def cost(flops, bytes_accessed, transcendentals=0):
    return pl.CostEstimate(flops=flops, bytes_accessed=bytes_accessed, transcendentals=transcendentals)


def swap(value, axis, offset):
    if offset == 0:
        return value
    count = lax.axis_size(axis)
    return lax.ppermute(value, axis, [(i, i ^ offset) for i in range(count)])


def spread(value, axis):
    return [swap(value, axis, offset) for offset in range(lax.axis_size(axis))]


def own_targets(routing_ref, section):
    return [routing_ref[section * REQ_GRP + i] for i in range(REQ_GRP)]


def slot_row(targets, group, order):
    row, before = jnp.int32(0), jnp.int32(0)
    for i, target in enumerate(targets):
        here = target == group
        row = jnp.where(here & (before == order), i, row)
        before = before + here.astype(jnp.int32)
    return row, before > order


def halves_of(pieces):
    return [
        (n, place, offset, first + place)
        for n, (offset, first, count) in enumerate(pieces)
        for place in range(count)
    ]


def start_packing(pieces, section_count, routing_ref, cache_ref, out_refs, sem):
    section = lax.axis_index("sec")
    full = section_count * CAP == REQ_GRP
    targets = own_targets(routing_ref, section)
    halves = halves_of(pieces)
    slots = {(offset, half // 2) for _, _, offset, half in halves}
    rows = {slot: slot_row(targets, section ^ slot[0], slot[1]) for slot in sorted(slots)}

    def copy(n, place, offset, half):
        row, _ = rows[offset, half // 2]
        return pltpu.make_async_copy(
            cache_ref.at[row, half % 2], out_refs[n].at[place], sem.at[offset * 2 * CAP + half]
        )

    for n, place, offset, half in halves:
        if full:
            copy(n, place, offset, half).start()
        else:
            _, filled = rows[offset, half // 2]

            @pl.when(filled)
            def _():
                copy(n, place, offset, half).start()

            @pl.when(jnp.logical_not(filled))
            def _():
                out_refs[n][place] = jnp.zeros_like(out_refs[n][place])

    def finish():
        for n, place, offset, half in halves:
            if full:
                copy(n, place, offset, half).wait()
            else:
                pl.when(rows[offset, half // 2][1])(copy(n, place, offset, half).wait)

    return finish


def first_pack_kernel(pieces, section_count, routing_ref, cache_ref, query_ref, *refs):
    refs, (sem, query_sem) = refs[:-2], refs[-2:]
    query_out, cache_out = refs[-section_count:], refs[-section_count - len(pieces) : -section_count]
    section = lax.axis_index("sec")
    query_copies = []
    for offset, out_ref in enumerate(query_out):
        width = out_ref.shape[2]
        columns = pl.ds(pl.multiple_of(lax.axis_index("tp") * width, width) if offset > 1 else 0, width)
        part = query_ref.at[0, pl.ds((section ^ offset) * CAP, CAP), :, columns]
        query_copies.append(pltpu.make_async_copy(part, out_ref, query_sem.at[offset]))
        query_copies[-1].start()
    finish = start_packing(pieces, section_count, routing_ref, cache_ref, cache_out, sem)
    finish()
    for copy in query_copies:
        copy.wait()


def pack_kernel(pieces, section_count, routing_ref, cache_ref, *refs):
    cache_out, sem = refs[-1 - len(pieces) : -1], refs[-1]
    start_packing(pieces, section_count, routing_ref, cache_ref, cache_out, sem)()


def merge_kernel(count, *refs):
    for n in range(count):
        refs[-1][n] = refs[n][...]


def merge(parts, others):
    shape = (len(parts),) + parts[0].shape
    return pl.pallas_call(
        functools.partial(merge_kernel, len(parts)),
        out_shape=jax.ShapeDtypeStruct(shape, parts[0].dtype),
        in_specs=[VMEM] * len(parts) + [ANY] * len(others),
        out_specs=VMEM,
        compiler_params=limit(8),
        cost_estimate=cost(0, 8 * len(parts) * parts[0].size),
        name="merge",
    )(*parts, *others)


def in_hbm(value):
    return pltpu.with_memory_space_constraint(value, pltpu.HBM)


def first_pack(routing, cache, queries, others, pieces, section_count, tp_count):
    samples, width = queries.shape[2:]
    widths = [width if offset < 2 else width // tp_count for offset in range(section_count)]
    shapes = [jax.ShapeDtypeStruct((count,) + cache.shape[2:], cache.dtype) for _, _, count in pieces]
    shapes += [jax.ShapeDtypeStruct((CAP, samples, one), queries.dtype) for one in widths]
    parts = pl.pallas_call(
        functools.partial(first_pack_kernel, pieces, section_count),
        out_shape=shapes,
        in_specs=[SMEM, HBM, HBM] + [ANY] * len(others),
        out_specs=[VMEM] * len(shapes),
        scratch_shapes=[
            pltpu.SemaphoreType.DMA((section_count * CAP * 2,)),
            pltpu.SemaphoreType.DMA((section_count,)),
        ],
        compiler_params=limit(16),
        cost_estimate=cost(0, 4 * sum(shape.size for shape in shapes)),
        name="first_pack",
    )(in_hbm(routing), in_hbm(cache), in_hbm(queries), *others)
    return parts[: len(pieces)], parts[len(pieces) :]


def pack(routing, cache, others, pieces, section_count, flops=0):
    shapes = [jax.ShapeDtypeStruct((count,) + cache.shape[2:], cache.dtype) for _, _, count in pieces]
    return pl.pallas_call(
        functools.partial(pack_kernel, pieces, section_count),
        out_shape=shapes,
        in_specs=[SMEM, HBM] + [ANY] * len(others),
        out_specs=[VMEM] * len(shapes),
        scratch_shapes=[
            pltpu.SemaphoreType.DMA((section_count * CAP * 2,)),
        ],
        compiler_params=limit(16),
        cost_estimate=cost(flops, 4 * sum(shape.size for shape in shapes)),
        name="pack",
    )(in_hbm(routing), in_hbm(cache), *others)


def place_kernel(pieces, *refs):
    count = len(pieces)
    part_refs, out_ref, sem = refs[-2 - count : -2], refs[-2], refs[-1]
    section = lax.axis_index("sec")
    copies = []
    for n, (offset, first, size) in enumerate(pieces):
        for place in range(size):
            half = out_ref.at[0, (section ^ offset) * 2 * CAP + first + place]
            copies.append(pltpu.make_async_copy(part_refs[n].at[place], half, sem.at[len(copies)]))
            copies[-1].start()
    for copy in copies:
        copy.wait()


def place(given, parts, pieces, slot_count):
    part = parts[0]
    return pl.pallas_call(
        functools.partial(place_kernel, pieces),
        out_shape=jax.ShapeDtypeStruct((1, 2 * slot_count) + part.shape[1:], part.dtype),
        in_specs=[HBM] * len(given) + [VMEM] * len(parts),
        out_specs=HBM,
        scratch_shapes=[pltpu.SemaphoreType.DMA((sum(len(part) for part in parts),))],
        input_output_aliases={0: 0} if given else {},
        compiler_params=limit(8),
        cost_estimate=cost(0, 4 * sum(piece.size for piece in parts)),
        name="place",
    )(*[in_hbm(value) for value in given], *parts)


def attend_kernel(pieces, section_count, tp_count, routing_ref, lengths_ref, *refs):
    cache_refs, refs = refs[: len(pieces)], refs[len(pieces) :]
    query_refs, far_refs = refs[:2], refs[2 : 2 + tp_count]
    message_refs = refs[2 + tp_count : 2 + 2 * tp_count]
    messages, stats, stacked, far_queries = refs[2 + 2 * tp_count :]
    section = lax.axis_index("sec")
    tp_index = lax.axis_index("tp")
    local = cache_refs[0].shape[1]
    groups, rows, _ = messages.shape[1:]
    span = KEY_VALUE_HEADS * rows
    prompts = max(1, groups // KEY_VALUE_HEADS)
    full = section_count * CAP == REQ_GRP
    targets = own_targets(routing_ref, section)
    samples = query_refs[0].shape[1]
    for offset, far_ref in enumerate(far_refs):
        far_queries[tp_index ^ offset] = far_ref[...]
    position = lax.broadcasted_iota(jnp.int32, (local, span), 0) + tp_index * local
    owner = lax.broadcasted_iota(jnp.int32, (HEAD_SIZE, span), 1) // rows

    held = {(offset, half): cache_refs[n].at[place] for n, place, offset, half in halves_of(pieces)}

    def prompt(offset, order):
        keys_ref, values_ref = held[offset, 2 * order], held[offset, 2 * order + 1]
        row, _ = slot_row(targets, section ^ offset, order)
        visible = position < lengths_ref[section * REQ_GRP + row]
        slot = offset * CAP + order
        for head in range(span // samples):
            first, part = head * HEAD_SIZE, far_queries.shape[-1]
            if offset < 2:
                values = query_refs[offset][order, :, first : first + HEAD_SIZE]
            else:
                inner = first % part
                values = far_queries[first // part, offset - 2, order, :, inner : inner + HEAD_SIZE]
            stacked[slot, head * samples : (head + 1) * samples] = values.astype(jnp.float32)
        query = stacked[slot].T.astype(jnp.bfloat16)
        query = [jnp.where(owner == k, query, jnp.zeros_like(query)) for k in range(KEY_VALUE_HEADS)]
        score = jnp.dot(
            keys_ref[...], jnp.concatenate(query, axis=0), preferred_element_type=jnp.float32
        ) * HEAD_SIZE ** (-0.5)
        score = jnp.where(visible, score, HIDDEN)
        peak = jnp.max(score, axis=0, keepdims=True)
        weight = jnp.where(visible, jnp.exp(score - peak), 0.0)
        total = jnp.sum(weight, axis=0, keepdims=True)
        some = total > 0.0
        safe = jnp.where(some, total, 1.0)
        stats[0, pl.ds(row, 1)] = jnp.where(some, peak + jnp.log(safe), HIDDEN)
        weight = (weight * (1.0 / safe)).T.astype(jnp.bfloat16)
        for k in range(KEY_VALUE_HEADS):
            mixed = jnp.dot(
                weight[k * rows : (k + 1) * rows],
                values_ref[:, k * HEAD_SIZE : (k + 1) * HEAD_SIZE],
                preferred_element_type=jnp.float32,
            )
            group = row * KEY_VALUE_HEADS + k
            messages[group // groups, group % groups] = mixed.astype(jnp.bfloat16)

    for offset, half in held:
        if half % 2 == 0:
            one = functools.partial(prompt, offset, half // 2)
            if full:
                one()
            else:
                pl.when(slot_row(targets, section ^ offset, half // 2)[1])(one)

    level = stats[0]
    high = level.astype(jnp.bfloat16).astype(jnp.float32)
    rest = level - high
    middle = rest.astype(jnp.bfloat16).astype(jnp.float32)
    stats[0], stats[1], stats[2] = high, middle, rest - middle
    for offset, message_ref in enumerate(message_refs):
        device = tp_index ^ offset
        for inner in range(groups):
            message_ref[inner * rows : (inner + 1) * rows] = messages[device, inner]
        first = device * groups // KEY_VALUE_HEADS
        lines = [stats[part, pl.ds(first + n, 1)] for part in range(3) for n in range(prompts)]
        lines.append(jnp.zeros((STAT_ROWS - 3 * prompts, span), jnp.float32))
        message_ref[groups * rows :] = jnp.concatenate(lines, axis=0).astype(jnp.bfloat16)


def attend(routing, lengths, caches, pieces, queries, far_queries):
    section_count = len(far_queries[0]) + 2
    tp_count = len(far_queries)
    samples, width = queries[0].shape[1:]
    span = width // HEAD_SIZE * samples
    rows = span // KEY_VALUE_HEADS
    groups = REQ_GRP * KEY_VALUE_HEADS // tp_count
    multiplies = REQ_GRP * span * HEAD_SIZE * caches[0].shape[1]
    return pl.pallas_call(
        functools.partial(attend_kernel, pieces, section_count, tp_count),
        out_shape=[jax.ShapeDtypeStruct((groups * rows + STAT_ROWS, HEAD_SIZE), jnp.bfloat16)] * tp_count,
        in_specs=[SMEM, SMEM] + [VMEM] * (len(caches) + len(queries) + tp_count),
        out_specs=[VMEM] * tp_count,
        scratch_shapes=[
            pltpu.VMEM((tp_count, groups, rows, HEAD_SIZE), jnp.bfloat16),
            pltpu.VMEM((3, REQ_GRP, span), jnp.float32),
            pltpu.VMEM((section_count * CAP, span, HEAD_SIZE), jnp.float32),
            pltpu.VMEM((tp_count,) + far_queries[0].shape, far_queries[0].dtype),
        ],
        compiler_params=limit(12),
        cost_estimate=cost(2 * 10**10, 2 * sum(part.size for part in caches), multiplies // HEAD_SIZE),
        name="attend",
    )(routing, lengths, *caches, *queries, *far_queries)


def join_kernel(count, samples, rows, *refs):
    message_refs, (out_ref, scaling, flat) = refs[:count], refs[-3:]
    groups = (message_refs[0].shape[0] - STAT_ROWS) // rows
    prompts = max(1, groups // KEY_VALUE_HEADS)
    heads = rows // samples
    tp_index = lax.axis_index("tp")
    levels = []
    for ref in message_refs:
        lines = ref[groups * rows :].astype(jnp.float32)[0:8]
        levels.append(lines + pltpu.roll(lines, 8 - prompts, 0) + pltpu.roll(lines, 8 - 2 * prompts, 0))
    summit = functools.reduce(jnp.maximum, levels)
    scales = [jnp.exp(level - summit) for level in levels]
    total = functools.reduce(jnp.add, scales)
    for n, scale in enumerate(scales):
        scaling[n] = (scale / total).T
    for inner in range(groups):
        if groups % KEY_VALUE_HEADS:
            first = (tp_index * groups + inner) % KEY_VALUE_HEADS * rows
            part = pl.ds(pl.multiple_of(first, rows), rows)
        else:
            part = pl.ds(inner % KEY_VALUE_HEADS * rows, rows)
        prompt = inner // KEY_VALUE_HEADS
        terms = [
            ref[inner * rows : (inner + 1) * rows].astype(jnp.float32) * scaling[n, part, prompt : prompt + 1]
            for n, ref in enumerate(message_refs)
        ]
        joined = functools.reduce(jnp.add, terms)
        for head in range(heads):
            block = joined[head * samples : (head + 1) * samples]
            if len(flat.shape) == 2:
                row = prompt * samples
                column = (inner % KEY_VALUE_HEADS * heads + head) * HEAD_SIZE
                flat[row : row + samples, column : column + HEAD_SIZE] = block
            else:
                flat[inner, :, head * HEAD_SIZE : (head + 1) * HEAD_SIZE] = block
    out_ref[...] = flat[...].astype(jnp.bfloat16)


def join(messages, others, samples, heads):
    rows = heads * samples
    groups = (messages[0].shape[0] - STAT_ROWS) // rows
    width = rows // samples * HEAD_SIZE
    if groups % KEY_VALUE_HEADS == 0:
        shape = (groups // KEY_VALUE_HEADS * samples, KEY_VALUE_HEADS * width)
    else:
        shape = (groups, samples, width)
    count = len(messages)
    return pl.pallas_call(
        functools.partial(join_kernel, count, samples, rows),
        out_shape=jax.ShapeDtypeStruct(shape, jnp.bfloat16),
        in_specs=[VMEM] * count + [ANY] * len(others),
        out_specs=VMEM,
        scratch_shapes=[
            pltpu.VMEM((count, KEY_VALUE_HEADS * rows, 8), jnp.float32),
            pltpu.VMEM(shape, jnp.float32),
        ],
        compiler_params=limit(8),
        cost_estimate=cost(4 * count * messages[0].size, 2 * count * messages[0].size),
        name="join",
    )(*messages, *others)


def fetch_kernel(first, weight_ref, *refs):
    out_ref, sem = refs[-2:]
    copies = []
    step = out_ref.shape[0] // sem.shape[0]
    for n in range(sem.shape[0]):
        rows = weight_ref.at[pl.ds(first + n * step, step)]
        copies.append(pltpu.make_async_copy(rows, out_ref.at[pl.ds(n * step, step)], sem.at[n]))
        copies[-1].start()
    for copy in copies:
        copy.wait()


def fetch(weight, others, number, count):
    size = weight.shape[0] // count
    return pl.pallas_call(
        functools.partial(fetch_kernel, number * size),
        out_shape=jax.ShapeDtypeStruct((size,) + weight.shape[1:], weight.dtype),
        in_specs=[HBM] + [ANY] * len(others),
        out_specs=VMEM,
        scratch_shapes=[pltpu.SemaphoreType.DMA((8,))],
        compiler_params=limit(24),
        cost_estimate=cost(0, 4 * weight.size // count),
        name="fetch",
    )(in_hbm(weight), *others)


def project_kernel(count, tile, *refs):
    part_refs, weight_refs, out_ref = refs[:count], refs[count:-1], refs[-1]
    tp_index = lax.axis_index("tp")
    prompts, samples, width = out_ref.shape
    share = prompts // count
    left = jnp.concatenate([ref[...].astype(jnp.float32) for ref in part_refs], axis=0).astype(jnp.bfloat16)
    size = weight_refs[0].shape[0]
    for first in range(0, width, tile):
        result = functools.reduce(
            jnp.add,
            [
                jnp.dot(
                    left[:, n * size : (n + 1) * size],
                    ref[:, first : first + tile],
                    preferred_element_type=jnp.float32,
                )
                for n, ref in enumerate(weight_refs)
            ],
        )
        for offset in range(count):
            for n in range(share):
                row = (offset * share + n) * samples
                block = result[row : row + samples].astype(out_ref.dtype)
                out_ref[(tp_index ^ offset) * share + n, :, first : first + tile] = block


def project(parts, weights, samples):
    count = len(parts)
    depth, width = weights[0].shape
    depth *= len(weights)
    total = count * parts[0].shape[0]
    return pl.pallas_call(
        functools.partial(project_kernel, count, min(256, width)),
        out_shape=jax.ShapeDtypeStruct((total // samples, samples, width), jnp.bfloat16),
        in_specs=[VMEM] * (count + len(weights)),
        out_specs=VMEM,
        compiler_params=limit(24),
        cost_estimate=cost(2 * total * depth * width, 2 * depth * width),
        name="project",
    )(*parts, *weights)


def body(prompt_key_values, queries, routing, lengths, out_weight):
    section_count = lax.axis_size("sec")
    tp_count = lax.axis_size("tp")
    slot_count, samples, query_width = queries.shape[1:]
    routing = routing.reshape(-1)

    whole = 2 * CAP
    near = [(offset, 0, whole) for offset in range(2)]
    head, tail = [(2, 0, 1)], [(2, 1, whole - 1)]
    far = tail + [(offset, 0, whole) for offset in range(3, section_count)]

    def across(parts, pieces):
        return [swap(part, "sec", piece[0]) for part, piece in zip(parts, pieces)]

    head_caches = pack(routing, prompt_key_values, [], head, section_count)
    head_parts = across(head_caches, head)
    far_caches, query_parts = first_pack(
        routing, prompt_key_values, queries, head_caches, far, section_count, tp_count
    )
    query_parts = [swap(part, "sec", offset) for offset, part in enumerate(query_parts)]
    far_parts = across(far_caches, far)
    merged = merge(query_parts[2:], head_parts)
    far_queries = spread(merged, "tp")
    near_caches = pack(routing, prompt_key_values, [merged, query_parts[1]], near, section_count, 10**10)
    near_parts = across(near_caches, near)
    caches, pieces = [*head_caches, *far_caches, *near_caches], head + far + near

    messages = attend(routing, lengths, caches, pieces, query_parts[:2], far_queries)
    partials = [swap(part, "tp", offset) for offset, part in enumerate(messages)]
    held_weight = [fetch(out_weight, [messages[0], *near_parts[1:]], 0, 2)]
    share = join(partials, held_weight, samples, query_width // HEAD_SIZE // KEY_VALUE_HEADS)
    shares = spread(share, "tp")
    held_weight.append(fetch(out_weight, [share], 1, 2))
    if share.ndim == 3:
        attended = jnp.stack(shares)[jnp.arange(tp_count) ^ lax.axis_index("tp")]
        attended = attended.reshape(REQ_GRP, KEY_VALUE_HEADS, samples, -1).transpose(0, 2, 1, 3)
        attended = attended.reshape(REQ_GRP * samples, query_width)
        layer_out = jnp.dot(attended, out_weight, preferred_element_type=jnp.float32)
        layer_out = layer_out.astype(jnp.bfloat16).reshape(REQ_GRP, samples, -1)
    else:
        layer_out = project(shares, held_weight, samples)

    held_cache = place([], near_parts + head_parts, near + head, slot_count)
    for part, piece in zip(far_parts, far):
        held_cache = place([held_cache, layer_out], [part], [piece], slot_count)
    held_cache = held_cache.reshape((1, slot_count) + prompt_key_values.shape[1:])
    return (layer_out, held_cache)


def solution(mesh):
    placed = (
        P(("rep", "sec"), None, "tp", None),
        P(("rep", "sec"), None, None, None),
        P("rep", None),
        P("rep"),
        P(None, "tp"),
    )
    return jax.shard_map(
        body,
        mesh=mesh,
        in_specs=placed,
        out_specs=(P(("rep", "sec"), None, "tp"), P(("rep", "sec"), None, None, "tp", None)),
        check_vma=False,
    )
```

```python
import functools

import jax
import jax.numpy as jnp
from jax import lax
from jax.experimental import pallas as pl
from jax.experimental.pallas import tpu as pltpu
from jax.sharding import PartitionSpec as P

HEAD_SIZE = 128
KEY_VALUE_HEADS = 4
REQ_GRP = 8
CAP = 2
HIDDEN = -1e30
STAT_ROWS = 16

ANY = pl.BlockSpec(memory_space=pl.ANY)
HBM = pl.BlockSpec(memory_space=pltpu.HBM)
VMEM = pl.BlockSpec(memory_space=pltpu.VMEM)
SMEM = pl.BlockSpec(memory_space=pltpu.SMEM)


def limit(mebibytes):
    return pltpu.CompilerParams(vmem_limit_bytes=mebibytes << 20)


def cost(flops, bytes_accessed, transcendentals=0):
    return pl.CostEstimate(flops=flops, bytes_accessed=bytes_accessed, transcendentals=transcendentals)


def swap(value, axis, offset):
    if offset == 0:
        return value
    count = lax.axis_size(axis)
    return lax.ppermute(value, axis, [(i, i ^ offset) for i in range(count)])


def spread(value, axis):
    return [swap(value, axis, offset) for offset in range(lax.axis_size(axis))]


def own_targets(routing_ref, section):
    return [routing_ref[section * REQ_GRP + i] for i in range(REQ_GRP)]


def slot_row(targets, group, order):
    row, before = jnp.int32(0), jnp.int32(0)
    for i, target in enumerate(targets):
        here = target == group
        row = jnp.where(here & (before == order), i, row)
        before = before + here.astype(jnp.int32)
    return row, before > order


def halves_of(pieces):
    return [
        (n, place, offset, first + place)
        for n, (offset, first, count) in enumerate(pieces)
        for place in range(count)
    ]


def start_packing(pieces, section_count, routing_ref, cache_ref, out_refs, sem):
    section = lax.axis_index("sec")
    full = section_count * CAP == REQ_GRP
    targets = own_targets(routing_ref, section)
    halves = halves_of(pieces)
    slots = {(offset, half // 2) for _, _, offset, half in halves}
    rows = {slot: slot_row(targets, section ^ slot[0], slot[1]) for slot in sorted(slots)}

    def copy(n, place, offset, half):
        row, _ = rows[offset, half // 2]
        return pltpu.make_async_copy(
            cache_ref.at[row, half % 2], out_refs[n].at[place], sem.at[offset * 2 * CAP + half]
        )

    for n, place, offset, half in halves:
        if full:
            copy(n, place, offset, half).start()
        else:
            _, filled = rows[offset, half // 2]

            @pl.when(filled)
            def _():
                copy(n, place, offset, half).start()

            @pl.when(jnp.logical_not(filled))
            def _():
                out_refs[n][place] = jnp.zeros_like(out_refs[n][place])

    def finish():
        for n, place, offset, half in halves:
            if full:
                copy(n, place, offset, half).wait()
            else:
                pl.when(rows[offset, half // 2][1])(copy(n, place, offset, half).wait)

    return finish


def head_kernel(piece, full, routing_ref, cache_ref, out_ref, routed, held, routing_sem, sem):
    offset, half, _ = piece
    section = lax.axis_index("sec")
    copies = [pltpu.make_async_copy(routing_ref, routed, routing_sem)]
    for i in range(REQ_GRP):
        copies.append(pltpu.make_async_copy(cache_ref.at[i, half % 2], held.at[i], sem.at[i]))
    for copy in copies:
        copy.start()
    copies[0].wait()
    row, filled = slot_row(own_targets(routed, section), section ^ offset, half // 2)
    for copy in copies[1:]:
        copy.wait()
    chosen = held[row]
    out_ref[0] = chosen if full else jnp.where(filled, chosen, jnp.zeros_like(chosen))


def pack_head(routing, cache, piece, section_count):
    shape = cache.shape[2:]
    return pl.pallas_call(
        functools.partial(head_kernel, piece, section_count * CAP == REQ_GRP),
        out_shape=jax.ShapeDtypeStruct((1,) + shape, cache.dtype),
        in_specs=[HBM, HBM],
        out_specs=VMEM,
        scratch_shapes=[
            pltpu.SMEM(routing.shape, jnp.int32),
            pltpu.VMEM((REQ_GRP,) + shape, cache.dtype),
            pltpu.SemaphoreType.DMA,
            pltpu.SemaphoreType.DMA((REQ_GRP,)),
        ],
        compiler_params=limit(16),
        cost_estimate=cost(0, cache.size),
        name="pack_head",
    )(in_hbm(routing), in_hbm(cache))


def first_pack_kernel(pieces, section_count, routing_ref, cache_ref, query_ref, *refs):
    refs, (sem, query_sem) = refs[:-2], refs[-2:]
    query_out, cache_out = refs[-section_count:], refs[-section_count - len(pieces) : -section_count]
    section = lax.axis_index("sec")
    query_copies = []
    for offset, out_ref in enumerate(query_out):
        width = out_ref.shape[2]
        columns = pl.ds(pl.multiple_of(lax.axis_index("tp") * width, width) if offset > 1 else 0, width)
        part = query_ref.at[0, pl.ds((section ^ offset) * CAP, CAP), :, columns]
        query_copies.append(pltpu.make_async_copy(part, out_ref, query_sem.at[offset]))
        query_copies[-1].start()
    finish = start_packing(pieces, section_count, routing_ref, cache_ref, cache_out, sem)
    finish()
    for copy in query_copies:
        copy.wait()


def pack_kernel(pieces, section_count, routing_ref, cache_ref, *refs):
    cache_out, sem = refs[-1 - len(pieces) : -1], refs[-1]
    start_packing(pieces, section_count, routing_ref, cache_ref, cache_out, sem)()


def merge_kernel(count, *refs):
    for n in range(count):
        refs[-1][n] = refs[n][...]


def merge(parts, others):
    shape = (len(parts),) + parts[0].shape
    return pl.pallas_call(
        functools.partial(merge_kernel, len(parts)),
        out_shape=jax.ShapeDtypeStruct(shape, parts[0].dtype),
        in_specs=[VMEM] * len(parts) + [ANY] * len(others),
        out_specs=VMEM,
        compiler_params=limit(8),
        cost_estimate=cost(0, 8 * len(parts) * parts[0].size),
        name="merge",
    )(*parts, *others)


def in_hbm(value):
    return pltpu.with_memory_space_constraint(value, pltpu.HBM)


def first_pack(routing, cache, queries, others, pieces, section_count, tp_count):
    samples, width = queries.shape[2:]
    widths = [width if offset < 2 else width // tp_count for offset in range(section_count)]
    shapes = [jax.ShapeDtypeStruct((count,) + cache.shape[2:], cache.dtype) for _, _, count in pieces]
    shapes += [jax.ShapeDtypeStruct((CAP, samples, one), queries.dtype) for one in widths]
    parts = pl.pallas_call(
        functools.partial(first_pack_kernel, pieces, section_count),
        out_shape=shapes,
        in_specs=[SMEM, HBM, HBM] + [ANY] * len(others),
        out_specs=[VMEM] * len(shapes),
        scratch_shapes=[
            pltpu.SemaphoreType.DMA((section_count * CAP * 2,)),
            pltpu.SemaphoreType.DMA((section_count,)),
        ],
        compiler_params=limit(16),
        cost_estimate=cost(0, 4 * sum(shape.size for shape in shapes)),
        name="first_pack",
    )(in_hbm(routing), in_hbm(cache), in_hbm(queries), *others)
    return parts[: len(pieces)], parts[len(pieces) :]


def pack(routing, cache, others, pieces, section_count, flops=0):
    shapes = [jax.ShapeDtypeStruct((count,) + cache.shape[2:], cache.dtype) for _, _, count in pieces]
    return pl.pallas_call(
        functools.partial(pack_kernel, pieces, section_count),
        out_shape=shapes,
        in_specs=[SMEM, HBM] + [ANY] * len(others),
        out_specs=[VMEM] * len(shapes),
        scratch_shapes=[
            pltpu.SemaphoreType.DMA((section_count * CAP * 2,)),
        ],
        compiler_params=limit(16),
        cost_estimate=cost(flops, 4 * sum(shape.size for shape in shapes)),
        name="pack",
    )(in_hbm(routing), in_hbm(cache), *others)


def place_kernel(pieces, *refs):
    count = len(pieces)
    part_refs, out_ref, sem = refs[-2 - count : -2], refs[-2], refs[-1]
    section = lax.axis_index("sec")
    copies = []
    for n, (offset, first, size) in enumerate(pieces):
        for place in range(size):
            half = out_ref.at[0, (section ^ offset) * 2 * CAP + first + place]
            copies.append(pltpu.make_async_copy(part_refs[n].at[place], half, sem.at[len(copies)]))
            copies[-1].start()
    for copy in copies:
        copy.wait()


def place(given, parts, pieces, slot_count):
    part = parts[0]
    return pl.pallas_call(
        functools.partial(place_kernel, pieces),
        out_shape=jax.ShapeDtypeStruct((1, 2 * slot_count) + part.shape[1:], part.dtype),
        in_specs=[HBM] * len(given) + [VMEM] * len(parts),
        out_specs=HBM,
        scratch_shapes=[pltpu.SemaphoreType.DMA((sum(len(part) for part in parts),))],
        input_output_aliases={0: 0} if given else {},
        compiler_params=limit(8),
        cost_estimate=cost(0, 4 * sum(piece.size for piece in parts)),
        name="place",
    )(*[in_hbm(value) for value in given], *parts)


def attend_kernel(pieces, section_count, tp_count, routing_ref, lengths_ref, *refs):
    cache_refs, refs = refs[: len(pieces)], refs[len(pieces) :]
    query_refs, far_refs = refs[:2], refs[2 : 2 + tp_count]
    message_refs = refs[2 + tp_count : 2 + 2 * tp_count]
    messages, stats, stacked, far_queries = refs[2 + 2 * tp_count :]
    section = lax.axis_index("sec")
    tp_index = lax.axis_index("tp")
    local = cache_refs[0].shape[1]
    groups, rows, _ = messages.shape[1:]
    span = KEY_VALUE_HEADS * rows
    prompts = max(1, groups // KEY_VALUE_HEADS)
    full = section_count * CAP == REQ_GRP
    targets = own_targets(routing_ref, section)
    samples = query_refs[0].shape[1]
    for offset, far_ref in enumerate(far_refs):
        far_queries[tp_index ^ offset] = far_ref[...]
    position = lax.broadcasted_iota(jnp.int32, (local, span), 0) + tp_index * local
    owner = lax.broadcasted_iota(jnp.int32, (HEAD_SIZE, span), 1) // rows

    held = {(offset, half): cache_refs[n].at[place] for n, place, offset, half in halves_of(pieces)}

    def prompt(offset, order):
        keys_ref, values_ref = held[offset, 2 * order], held[offset, 2 * order + 1]
        row, _ = slot_row(targets, section ^ offset, order)
        visible = position < lengths_ref[section * REQ_GRP + row]
        slot = offset * CAP + order
        for head in range(span // samples):
            first, part = head * HEAD_SIZE, far_queries.shape[-1]
            if offset < 2:
                values = query_refs[offset][order, :, first : first + HEAD_SIZE]
            else:
                inner = first % part
                values = far_queries[first // part, offset - 2, order, :, inner : inner + HEAD_SIZE]
            stacked[slot, head * samples : (head + 1) * samples] = values.astype(jnp.float32)
        query = stacked[slot].T.astype(jnp.bfloat16)
        query = [jnp.where(owner == k, query, jnp.zeros_like(query)) for k in range(KEY_VALUE_HEADS)]
        score = jnp.dot(
            keys_ref[...], jnp.concatenate(query, axis=0), preferred_element_type=jnp.float32
        ) * HEAD_SIZE ** (-0.5)
        score = jnp.where(visible, score, HIDDEN)
        peak = jnp.max(score, axis=0, keepdims=True)
        weight = jnp.where(visible, jnp.exp(score - peak), 0.0)
        total = jnp.sum(weight, axis=0, keepdims=True)
        some = total > 0.0
        safe = jnp.where(some, total, 1.0)
        stats[0, pl.ds(row, 1)] = jnp.where(some, peak + jnp.log(safe), HIDDEN)
        weight = (weight * (1.0 / safe)).T.astype(jnp.bfloat16)
        for k in range(KEY_VALUE_HEADS):
            mixed = jnp.dot(
                weight[k * rows : (k + 1) * rows],
                values_ref[:, k * HEAD_SIZE : (k + 1) * HEAD_SIZE],
                preferred_element_type=jnp.float32,
            )
            group = row * KEY_VALUE_HEADS + k
            messages[group // groups, group % groups] = mixed.astype(jnp.bfloat16)

    for offset, half in held:
        if half % 2 == 0:
            one = functools.partial(prompt, offset, half // 2)
            if full:
                one()
            else:
                pl.when(slot_row(targets, section ^ offset, half // 2)[1])(one)

    level = stats[0]
    high = level.astype(jnp.bfloat16).astype(jnp.float32)
    rest = level - high
    middle = rest.astype(jnp.bfloat16).astype(jnp.float32)
    stats[0], stats[1], stats[2] = high, middle, rest - middle
    for offset, message_ref in enumerate(message_refs):
        device = tp_index ^ offset
        for inner in range(groups):
            message_ref[inner * rows : (inner + 1) * rows] = messages[device, inner]
        first = device * groups // KEY_VALUE_HEADS
        lines = [stats[part, pl.ds(first + n, 1)] for part in range(3) for n in range(prompts)]
        lines.append(jnp.zeros((STAT_ROWS - 3 * prompts, span), jnp.float32))
        message_ref[groups * rows :] = jnp.concatenate(lines, axis=0).astype(jnp.bfloat16)


def attend(routing, lengths, caches, pieces, queries, far_queries):
    section_count = len(far_queries[0]) + 2
    tp_count = len(far_queries)
    samples, width = queries[0].shape[1:]
    span = width // HEAD_SIZE * samples
    rows = span // KEY_VALUE_HEADS
    groups = REQ_GRP * KEY_VALUE_HEADS // tp_count
    multiplies = REQ_GRP * span * HEAD_SIZE * caches[0].shape[1]
    return pl.pallas_call(
        functools.partial(attend_kernel, pieces, section_count, tp_count),
        out_shape=[jax.ShapeDtypeStruct((groups * rows + STAT_ROWS, HEAD_SIZE), jnp.bfloat16)] * tp_count,
        in_specs=[SMEM, SMEM] + [VMEM] * (len(caches) + len(queries) + tp_count),
        out_specs=[VMEM] * tp_count,
        scratch_shapes=[
            pltpu.VMEM((tp_count, groups, rows, HEAD_SIZE), jnp.bfloat16),
            pltpu.VMEM((3, REQ_GRP, span), jnp.float32),
            pltpu.VMEM((section_count * CAP, span, HEAD_SIZE), jnp.float32),
            pltpu.VMEM((tp_count,) + far_queries[0].shape, far_queries[0].dtype),
        ],
        compiler_params=limit(12),
        cost_estimate=cost(2 * 10**10, 2 * sum(part.size for part in caches), multiplies // HEAD_SIZE),
        name="attend",
    )(routing, lengths, *caches, *queries, *far_queries)


def join_kernel(count, samples, rows, *refs):
    message_refs, (out_ref, scaling, flat) = refs[:count], refs[-3:]
    groups = (message_refs[0].shape[0] - STAT_ROWS) // rows
    prompts = max(1, groups // KEY_VALUE_HEADS)
    heads = rows // samples
    tp_index = lax.axis_index("tp")
    levels = []
    for ref in message_refs:
        lines = ref[groups * rows :].astype(jnp.float32)[0:8]
        levels.append(lines + pltpu.roll(lines, 8 - prompts, 0) + pltpu.roll(lines, 8 - 2 * prompts, 0))
    summit = functools.reduce(jnp.maximum, levels)
    scales = [jnp.exp(level - summit) for level in levels]
    total = functools.reduce(jnp.add, scales)
    for n, scale in enumerate(scales):
        scaling[n] = (scale / total).T
    for inner in range(groups):
        if groups % KEY_VALUE_HEADS:
            first = (tp_index * groups + inner) % KEY_VALUE_HEADS * rows
            part = pl.ds(pl.multiple_of(first, rows), rows)
        else:
            part = pl.ds(inner % KEY_VALUE_HEADS * rows, rows)
        prompt = inner // KEY_VALUE_HEADS
        terms = [
            ref[inner * rows : (inner + 1) * rows].astype(jnp.float32) * scaling[n, part, prompt : prompt + 1]
            for n, ref in enumerate(message_refs)
        ]
        joined = functools.reduce(jnp.add, terms)
        for head in range(heads):
            block = joined[head * samples : (head + 1) * samples]
            if len(flat.shape) == 2:
                row = prompt * samples
                column = (inner % KEY_VALUE_HEADS * heads + head) * HEAD_SIZE
                flat[row : row + samples, column : column + HEAD_SIZE] = block
            else:
                flat[inner, :, head * HEAD_SIZE : (head + 1) * HEAD_SIZE] = block
    out_ref[...] = flat[...].astype(jnp.bfloat16)


def join(messages, others, samples, heads):
    rows = heads * samples
    groups = (messages[0].shape[0] - STAT_ROWS) // rows
    width = rows // samples * HEAD_SIZE
    if groups % KEY_VALUE_HEADS == 0:
        shape = (groups // KEY_VALUE_HEADS * samples, KEY_VALUE_HEADS * width)
    else:
        shape = (groups, samples, width)
    count = len(messages)
    return pl.pallas_call(
        functools.partial(join_kernel, count, samples, rows),
        out_shape=jax.ShapeDtypeStruct(shape, jnp.bfloat16),
        in_specs=[VMEM] * count + [ANY] * len(others),
        out_specs=VMEM,
        scratch_shapes=[
            pltpu.VMEM((count, KEY_VALUE_HEADS * rows, 8), jnp.float32),
            pltpu.VMEM(shape, jnp.float32),
        ],
        compiler_params=limit(8),
        cost_estimate=cost(4 * count * messages[0].size, 2 * count * messages[0].size),
        name="join",
    )(*messages, *others)


def fetch_kernel(first, weight_ref, *refs):
    out_ref, sem = refs[-2:]
    copies = []
    step = out_ref.shape[0] // sem.shape[0]
    for n in range(sem.shape[0]):
        rows = weight_ref.at[pl.ds(first + n * step, step)]
        copies.append(pltpu.make_async_copy(rows, out_ref.at[pl.ds(n * step, step)], sem.at[n]))
        copies[-1].start()
    for copy in copies:
        copy.wait()


def fetch(weight, others, number, count):
    size = weight.shape[0] // count
    return pl.pallas_call(
        functools.partial(fetch_kernel, number * size),
        out_shape=jax.ShapeDtypeStruct((size,) + weight.shape[1:], weight.dtype),
        in_specs=[HBM] + [ANY] * len(others),
        out_specs=VMEM,
        scratch_shapes=[pltpu.SemaphoreType.DMA((8,))],
        compiler_params=limit(24),
        cost_estimate=cost(0, 4 * weight.size // count),
        name="fetch",
    )(in_hbm(weight), *others)


def project_kernel(count, tile, *refs):
    part_refs, weight_refs, out_ref = refs[:count], refs[count:-1], refs[-1]
    tp_index = lax.axis_index("tp")
    prompts, samples, width = out_ref.shape
    share = prompts // count
    left = jnp.concatenate([ref[...].astype(jnp.float32) for ref in part_refs], axis=0).astype(jnp.bfloat16)
    size = weight_refs[0].shape[0]
    for first in range(0, width, tile):
        result = functools.reduce(
            jnp.add,
            [
                jnp.dot(
                    left[:, n * size : (n + 1) * size],
                    ref[:, first : first + tile],
                    preferred_element_type=jnp.float32,
                )
                for n, ref in enumerate(weight_refs)
            ],
        )
        for offset in range(count):
            for n in range(share):
                row = (offset * share + n) * samples
                block = result[row : row + samples].astype(out_ref.dtype)
                out_ref[(tp_index ^ offset) * share + n, :, first : first + tile] = block


def project(parts, weights, samples):
    count = len(parts)
    depth, width = weights[0].shape
    depth *= len(weights)
    total = count * parts[0].shape[0]
    return pl.pallas_call(
        functools.partial(project_kernel, count, min(256, width)),
        out_shape=jax.ShapeDtypeStruct((total // samples, samples, width), jnp.bfloat16),
        in_specs=[VMEM] * (count + len(weights)),
        out_specs=VMEM,
        compiler_params=limit(24),
        cost_estimate=cost(2 * total * depth * width, 2 * depth * width),
        name="project",
    )(*parts, *weights)


def body(prompt_key_values, queries, routing, lengths, out_weight):
    section_count = lax.axis_size("sec")
    tp_count = lax.axis_size("tp")
    slot_count, samples, query_width = queries.shape[1:]
    routing = routing.reshape(-1)

    whole = 2 * CAP
    near = [(offset, 0, whole) for offset in range(2)]
    head, tail = [(2, 0, 1)], [(2, 1, whole - 1)]
    far = tail + [(offset, 0, whole) for offset in range(3, section_count)]

    def across(parts, pieces):
        return [swap(part, "sec", piece[0]) for part, piece in zip(parts, pieces)]

    head_caches = [pack_head(routing, prompt_key_values, head[0], section_count)]
    head_parts = across(head_caches, head)
    far_caches, query_parts = first_pack(
        routing, prompt_key_values, queries, head_caches, far, section_count, tp_count
    )
    query_parts = [swap(part, "sec", offset) for offset, part in enumerate(query_parts)]
    far_parts = across(far_caches, far)
    merged = merge(query_parts[2:], head_parts)
    far_queries = spread(merged, "tp")
    near_caches = pack(routing, prompt_key_values, [merged, query_parts[1]], near, section_count, 10**10)
    near_parts = across(near_caches, near)
    caches, pieces = [*head_caches, *far_caches, *near_caches], head + far + near

    messages = attend(routing, lengths, caches, pieces, query_parts[:2], far_queries)
    partials = [swap(part, "tp", offset) for offset, part in enumerate(messages)]
    held_weight = [fetch(out_weight, [messages[0], *near_parts[1:]], 0, 2)]
    share = join(partials, held_weight, samples, query_width // HEAD_SIZE // KEY_VALUE_HEADS)
    shares = spread(share, "tp")
    held_weight.append(fetch(out_weight, [share], 1, 2))
    if share.ndim == 3:
        attended = jnp.stack(shares)[jnp.arange(tp_count) ^ lax.axis_index("tp")]
        attended = attended.reshape(REQ_GRP, KEY_VALUE_HEADS, samples, -1).transpose(0, 2, 1, 3)
        attended = attended.reshape(REQ_GRP * samples, query_width)
        layer_out = jnp.dot(attended, out_weight, preferred_element_type=jnp.float32)
        layer_out = layer_out.astype(jnp.bfloat16).reshape(REQ_GRP, samples, -1)
    else:
        layer_out = project(shares, held_weight, samples)

    held_cache = place([], near_parts + head_parts, near + head, slot_count)
    for part, piece in zip(far_parts, far):
        held_cache = place([held_cache, layer_out], [part], [piece], slot_count)
    held_cache = held_cache.reshape((1, slot_count) + prompt_key_values.shape[1:])
    return (layer_out, held_cache)


def solution(mesh):
    placed = (
        P(("rep", "sec"), None, "tp", None),
        P(("rep", "sec"), None, None, None),
        P("rep", None),
        P("rep"),
        P(None, "tp"),
    )
    return jax.shard_map(
        body,
        mesh=mesh,
        in_specs=placed,
        out_specs=(P(("rep", "sec"), None, "tp"), P(("rep", "sec"), None, None, "tp", None)),
        check_vma=False,
    )
```

```python
import functools

import jax
import jax.numpy as jnp
from jax import lax
from jax.experimental import pallas as pl
from jax.experimental.pallas import tpu as pltpu
from jax.sharding import PartitionSpec as P

HEAD_SIZE = 128
KEY_VALUE_HEADS = 4
REQ_GRP = 8
CAP = 2
HIDDEN = -1e30
STAT_ROWS = 16

ANY = pl.BlockSpec(memory_space=pl.ANY)
HBM = pl.BlockSpec(memory_space=pltpu.HBM)
VMEM = pl.BlockSpec(memory_space=pltpu.VMEM)
SMEM = pl.BlockSpec(memory_space=pltpu.SMEM)


def limit(mebibytes):
    return pltpu.CompilerParams(vmem_limit_bytes=mebibytes << 20)


def cost(flops, bytes_accessed, transcendentals=0):
    return pl.CostEstimate(flops=flops, bytes_accessed=bytes_accessed, transcendentals=transcendentals)


def swap(value, axis, offset):
    if offset == 0:
        return value
    count = lax.axis_size(axis)
    return lax.ppermute(value, axis, [(i, i ^ offset) for i in range(count)])


def spread(value, axis):
    return [swap(value, axis, offset) for offset in range(lax.axis_size(axis))]


def own_targets(routing_ref, section):
    return [routing_ref[section * REQ_GRP + i] for i in range(REQ_GRP)]


def slot_row(targets, group, order):
    row, before = jnp.int32(0), jnp.int32(0)
    for i, target in enumerate(targets):
        here = target == group
        row = jnp.where(here & (before == order), i, row)
        before = before + here.astype(jnp.int32)
    return row, before > order


def halves_of(pieces):
    return [
        (n, place, offset, first + place)
        for n, (offset, first, count) in enumerate(pieces)
        for place in range(count)
    ]


def start_packing(pieces, section_count, routing_ref, cache_ref, out_refs, sem):
    section = lax.axis_index("sec")
    full = section_count * CAP == REQ_GRP
    targets = own_targets(routing_ref, section)
    halves = halves_of(pieces)
    slots = {(offset, half // 2) for _, _, offset, half in halves}
    rows = {slot: slot_row(targets, section ^ slot[0], slot[1]) for slot in sorted(slots)}

    def copy(n, place, offset, half):
        row, _ = rows[offset, half // 2]
        return pltpu.make_async_copy(
            cache_ref.at[row, half % 2], out_refs[n].at[place], sem.at[offset * 2 * CAP + half]
        )

    for n, place, offset, half in halves:
        if full:
            copy(n, place, offset, half).start()
        else:
            _, filled = rows[offset, half // 2]

            @pl.when(filled)
            def _():
                copy(n, place, offset, half).start()

            @pl.when(jnp.logical_not(filled))
            def _():
                out_refs[n][place] = jnp.zeros_like(out_refs[n][place])

    def finish():
        for n, place, offset, half in halves:
            if full:
                copy(n, place, offset, half).wait()
            else:
                pl.when(rows[offset, half // 2][1])(copy(n, place, offset, half).wait)

    return finish


def head_kernel(piece, full, routing_ref, cache_ref, out_ref, routed, held, routing_sem, sem):
    offset, half, _ = piece
    section = lax.axis_index("sec")
    copies = [pltpu.make_async_copy(routing_ref, routed, routing_sem)]
    for i in range(REQ_GRP):
        copies.append(pltpu.make_async_copy(cache_ref.at[i, half % 2], held.at[i], sem.at[i]))
    for copy in copies:
        copy.start()
    copies[0].wait()
    row, filled = slot_row(own_targets(routed, section), section ^ offset, half // 2)
    for copy in copies[1:]:
        copy.wait()
    chosen = held[row]
    out_ref[0] = chosen if full else jnp.where(filled, chosen, jnp.zeros_like(chosen))


def pack_head(routing, cache, piece, section_count):
    shape = cache.shape[2:]
    return pl.pallas_call(
        functools.partial(head_kernel, piece, section_count * CAP == REQ_GRP),
        out_shape=jax.ShapeDtypeStruct((1,) + shape, cache.dtype),
        in_specs=[HBM, HBM],
        out_specs=VMEM,
        scratch_shapes=[
            pltpu.SMEM(routing.shape, jnp.int32),
            pltpu.VMEM((REQ_GRP,) + shape, cache.dtype),
            pltpu.SemaphoreType.DMA,
            pltpu.SemaphoreType.DMA((REQ_GRP,)),
        ],
        compiler_params=limit(16),
        cost_estimate=cost(0, cache.size),
        name="pack_head",
    )(in_hbm(routing), in_hbm(cache))


def first_pack_kernel(pieces, section_count, routing_ref, cache_ref, query_ref, *refs):
    refs, (sem, query_sem) = refs[:-2], refs[-2:]
    query_out, cache_out = refs[-section_count:], refs[-section_count - len(pieces) : -section_count]
    section = lax.axis_index("sec")
    query_copies = []
    for offset, out_ref in enumerate(query_out):
        width = out_ref.shape[2]
        columns = pl.ds(pl.multiple_of(lax.axis_index("tp") * width, width) if offset > 1 else 0, width)
        part = query_ref.at[0, pl.ds((section ^ offset) * CAP, CAP), :, columns]
        query_copies.append(pltpu.make_async_copy(part, out_ref, query_sem.at[offset]))
        query_copies[-1].start()
    finish = start_packing(pieces, section_count, routing_ref, cache_ref, cache_out, sem)
    finish()
    for copy in query_copies:
        copy.wait()


def pack_kernel(pieces, section_count, routing_ref, cache_ref, *refs):
    cache_out, sem = refs[-1 - len(pieces) : -1], refs[-1]
    start_packing(pieces, section_count, routing_ref, cache_ref, cache_out, sem)()


def merge_kernel(count, *refs):
    for n in range(count):
        refs[-1][n] = refs[n][...]


def merge(parts, others):
    shape = (len(parts),) + parts[0].shape
    return pl.pallas_call(
        functools.partial(merge_kernel, len(parts)),
        out_shape=jax.ShapeDtypeStruct(shape, parts[0].dtype),
        in_specs=[VMEM] * len(parts) + [ANY] * len(others),
        out_specs=VMEM,
        compiler_params=limit(8),
        cost_estimate=cost(0, 8 * len(parts) * parts[0].size),
        name="merge",
    )(*parts, *others)


def in_hbm(value):
    return pltpu.with_memory_space_constraint(value, pltpu.HBM)


def first_pack(routing, cache, queries, others, pieces, section_count, tp_count):
    samples, width = queries.shape[2:]
    widths = [width if offset < 2 else width // tp_count for offset in range(section_count)]
    shapes = [jax.ShapeDtypeStruct((count,) + cache.shape[2:], cache.dtype) for _, _, count in pieces]
    shapes += [jax.ShapeDtypeStruct((CAP, samples, one), queries.dtype) for one in widths]
    parts = pl.pallas_call(
        functools.partial(first_pack_kernel, pieces, section_count),
        out_shape=shapes,
        in_specs=[SMEM, HBM, HBM] + [ANY] * len(others),
        out_specs=[VMEM] * len(shapes),
        scratch_shapes=[
            pltpu.SemaphoreType.DMA((section_count * CAP * 2,)),
            pltpu.SemaphoreType.DMA((section_count,)),
        ],
        compiler_params=limit(16),
        cost_estimate=cost(0, 4 * sum(shape.size for shape in shapes)),
        name="first_pack",
    )(in_hbm(routing), in_hbm(cache), in_hbm(queries), *others)
    return parts[: len(pieces)], parts[len(pieces) :]


def pack(routing, cache, others, pieces, section_count, flops=0):
    shapes = [jax.ShapeDtypeStruct((count,) + cache.shape[2:], cache.dtype) for _, _, count in pieces]
    return pl.pallas_call(
        functools.partial(pack_kernel, pieces, section_count),
        out_shape=shapes,
        in_specs=[SMEM, HBM] + [ANY] * len(others),
        out_specs=[VMEM] * len(shapes),
        scratch_shapes=[
            pltpu.SemaphoreType.DMA((section_count * CAP * 2,)),
        ],
        compiler_params=limit(16),
        cost_estimate=cost(flops, 4 * sum(shape.size for shape in shapes)),
        name="pack",
    )(in_hbm(routing), in_hbm(cache), *others)


def place_kernel(pieces, *refs):
    count = len(pieces)
    part_refs, out_ref, sem = refs[-2 - count : -2], refs[-2], refs[-1]
    section = lax.axis_index("sec")
    copies = []
    for n, (offset, first, size) in enumerate(pieces):
        for place in range(size):
            half = out_ref.at[0, (section ^ offset) * 2 * CAP + first + place]
            copies.append(pltpu.make_async_copy(part_refs[n].at[place], half, sem.at[len(copies)]))
            copies[-1].start()
    for copy in copies:
        copy.wait()


def place(given, parts, pieces, slot_count):
    part = parts[0]
    return pl.pallas_call(
        functools.partial(place_kernel, pieces),
        out_shape=jax.ShapeDtypeStruct((1, 2 * slot_count) + part.shape[1:], part.dtype),
        in_specs=[HBM] * len(given) + [VMEM] * len(parts),
        out_specs=HBM,
        scratch_shapes=[pltpu.SemaphoreType.DMA((sum(len(part) for part in parts),))],
        input_output_aliases={0: 0} if given else {},
        compiler_params=limit(8),
        cost_estimate=cost(0, 4 * sum(piece.size for piece in parts)),
        name="place",
    )(*[in_hbm(value) for value in given], *parts)


def attend_kernel(pieces, section_count, tp_count, routing_ref, lengths_ref, *refs):
    cache_refs, refs = refs[: len(pieces)], refs[len(pieces) :]
    query_refs, far_refs = refs[:2], refs[2 : 2 + tp_count]
    message_refs = refs[2 + tp_count : 2 + 2 * tp_count]
    messages, stats, stacked, far_queries = refs[2 + 2 * tp_count :]
    section = lax.axis_index("sec")
    tp_index = lax.axis_index("tp")
    local = cache_refs[0].shape[1]
    groups, rows, _ = messages.shape[1:]
    span = KEY_VALUE_HEADS * rows
    prompts = max(1, groups // KEY_VALUE_HEADS)
    full = section_count * CAP == REQ_GRP
    targets = own_targets(routing_ref, section)
    samples = query_refs[0].shape[1]
    for offset, far_ref in enumerate(far_refs):
        far_queries[tp_index ^ offset] = far_ref[...]
    position = lax.broadcasted_iota(jnp.int32, (local, span), 0) + tp_index * local
    owner = lax.broadcasted_iota(jnp.int32, (HEAD_SIZE, span), 1) // rows

    held = {(offset, half): cache_refs[n].at[place] for n, place, offset, half in halves_of(pieces)}

    def prompt(offset, order):
        keys_ref, values_ref = held[offset, 2 * order], held[offset, 2 * order + 1]
        row, _ = slot_row(targets, section ^ offset, order)
        visible = position < lengths_ref[section * REQ_GRP + row]
        slot = offset * CAP + order
        for head in range(span // samples):
            first, part = head * HEAD_SIZE, far_queries.shape[-1]
            if offset < 2:
                values = query_refs[offset][order, :, first : first + HEAD_SIZE]
            else:
                inner = first % part
                values = far_queries[first // part, offset - 2, order, :, inner : inner + HEAD_SIZE]
            stacked[slot, head * samples : (head + 1) * samples] = values.astype(jnp.float32)
        query = stacked[slot].T.astype(jnp.bfloat16)
        query = [jnp.where(owner == k, query, jnp.zeros_like(query)) for k in range(KEY_VALUE_HEADS)]
        score = jnp.dot(
            keys_ref[...], jnp.concatenate(query, axis=0), preferred_element_type=jnp.float32
        ) * HEAD_SIZE ** (-0.5)
        score = jnp.where(visible, score, HIDDEN)
        peak = jnp.max(score, axis=0, keepdims=True)
        weight = jnp.where(visible, jnp.exp(score - peak), 0.0)
        total = jnp.sum(weight, axis=0, keepdims=True)
        some = total > 0.0
        safe = jnp.where(some, total, 1.0)
        stats[0, pl.ds(row, 1)] = jnp.where(some, peak + jnp.log(safe), HIDDEN)
        weight = (weight * (1.0 / safe)).T.astype(jnp.bfloat16)
        for k in range(KEY_VALUE_HEADS):
            mixed = jnp.dot(
                weight[k * rows : (k + 1) * rows],
                values_ref[:, k * HEAD_SIZE : (k + 1) * HEAD_SIZE],
                preferred_element_type=jnp.float32,
            )
            group = row * KEY_VALUE_HEADS + k
            messages[group // groups, group % groups] = mixed.astype(jnp.bfloat16)

    for offset, half in held:
        if half % 2 == 0:
            one = functools.partial(prompt, offset, half // 2)
            if full:
                one()
            else:
                pl.when(slot_row(targets, section ^ offset, half // 2)[1])(one)

    level = stats[0]
    high = level.astype(jnp.bfloat16).astype(jnp.float32)
    rest = level - high
    middle = rest.astype(jnp.bfloat16).astype(jnp.float32)
    stats[0], stats[1], stats[2] = high, middle, rest - middle
    for offset, message_ref in enumerate(message_refs):
        device = tp_index ^ offset
        for inner in range(groups):
            message_ref[inner * rows : (inner + 1) * rows] = messages[device, inner]
        first = device * groups // KEY_VALUE_HEADS
        lines = [stats[part, pl.ds(first + n, 1)] for part in range(3) for n in range(prompts)]
        lines.append(jnp.zeros((STAT_ROWS - 3 * prompts, span), jnp.float32))
        message_ref[groups * rows :] = jnp.concatenate(lines, axis=0).astype(jnp.bfloat16)


def attend(routing, lengths, caches, pieces, queries, far_queries):
    section_count = len(far_queries[0]) + 2
    tp_count = len(far_queries)
    samples, width = queries[0].shape[1:]
    span = width // HEAD_SIZE * samples
    rows = span // KEY_VALUE_HEADS
    groups = REQ_GRP * KEY_VALUE_HEADS // tp_count
    multiplies = REQ_GRP * span * HEAD_SIZE * caches[0].shape[1]
    return pl.pallas_call(
        functools.partial(attend_kernel, pieces, section_count, tp_count),
        out_shape=[jax.ShapeDtypeStruct((groups * rows + STAT_ROWS, HEAD_SIZE), jnp.bfloat16)] * tp_count,
        in_specs=[SMEM, SMEM] + [VMEM] * (len(caches) + len(queries) + tp_count),
        out_specs=[VMEM] * tp_count,
        scratch_shapes=[
            pltpu.VMEM((tp_count, groups, rows, HEAD_SIZE), jnp.bfloat16),
            pltpu.VMEM((3, REQ_GRP, span), jnp.float32),
            pltpu.VMEM((section_count * CAP, span, HEAD_SIZE), jnp.float32),
            pltpu.VMEM((tp_count,) + far_queries[0].shape, far_queries[0].dtype),
        ],
        compiler_params=limit(12),
        cost_estimate=cost(2 * 10**10, 2 * sum(part.size for part in caches), multiplies // HEAD_SIZE),
        name="attend",
    )(routing, lengths, *caches, *queries, *far_queries)


def join_kernel(count, samples, rows, *refs):
    message_refs, (out_ref, scaling, flat) = refs[:count], refs[-3:]
    groups = (message_refs[0].shape[0] - STAT_ROWS) // rows
    prompts = max(1, groups // KEY_VALUE_HEADS)
    heads = rows // samples
    tp_index = lax.axis_index("tp")
    levels = []
    for ref in message_refs:
        lines = ref[groups * rows :].astype(jnp.float32)[0:8]
        levels.append(lines + pltpu.roll(lines, 8 - prompts, 0) + pltpu.roll(lines, 8 - 2 * prompts, 0))
    summit = functools.reduce(jnp.maximum, levels)
    scales = [jnp.exp(level - summit) for level in levels]
    total = functools.reduce(jnp.add, scales)
    for n, scale in enumerate(scales):
        scaling[n] = (scale / total).T
    for inner in range(groups):
        if groups % KEY_VALUE_HEADS:
            first = (tp_index * groups + inner) % KEY_VALUE_HEADS * rows
            part = pl.ds(pl.multiple_of(first, rows), rows)
        else:
            part = pl.ds(inner % KEY_VALUE_HEADS * rows, rows)
        prompt = inner // KEY_VALUE_HEADS
        terms = [
            ref[inner * rows : (inner + 1) * rows].astype(jnp.float32) * scaling[n, part, prompt : prompt + 1]
            for n, ref in enumerate(message_refs)
        ]
        joined = functools.reduce(jnp.add, terms)
        for head in range(heads):
            block = joined[head * samples : (head + 1) * samples]
            if len(flat.shape) == 2:
                row = prompt * samples
                column = (inner % KEY_VALUE_HEADS * heads + head) * HEAD_SIZE
                flat[row : row + samples, column : column + HEAD_SIZE] = block
            else:
                flat[inner, :, head * HEAD_SIZE : (head + 1) * HEAD_SIZE] = block
    out_ref[...] = flat[...].astype(jnp.bfloat16)


def join(messages, others, samples, heads):
    rows = heads * samples
    groups = (messages[0].shape[0] - STAT_ROWS) // rows
    width = rows // samples * HEAD_SIZE
    if groups % KEY_VALUE_HEADS == 0:
        shape = (groups // KEY_VALUE_HEADS * samples, KEY_VALUE_HEADS * width)
    else:
        shape = (groups, samples, width)
    count = len(messages)
    return pl.pallas_call(
        functools.partial(join_kernel, count, samples, rows),
        out_shape=jax.ShapeDtypeStruct(shape, jnp.bfloat16),
        in_specs=[VMEM] * count + [ANY] * len(others),
        out_specs=VMEM,
        scratch_shapes=[
            pltpu.VMEM((count, KEY_VALUE_HEADS * rows, 8), jnp.float32),
            pltpu.VMEM(shape, jnp.float32),
        ],
        compiler_params=limit(8),
        cost_estimate=cost(4 * count * messages[0].size, 2 * count * messages[0].size),
        name="join",
    )(*messages, *others)


def fetch_kernel(first, weight_ref, *refs):
    out_ref, sem = refs[-2:]
    copies = []
    step = out_ref.shape[0] // sem.shape[0]
    for n in range(sem.shape[0]):
        rows = weight_ref.at[pl.ds(first + n * step, step)]
        copies.append(pltpu.make_async_copy(rows, out_ref.at[pl.ds(n * step, step)], sem.at[n]))
        copies[-1].start()
    for copy in copies:
        copy.wait()


def fetch(weight, others, number, count):
    size = weight.shape[0] // count
    return pl.pallas_call(
        functools.partial(fetch_kernel, number * size),
        out_shape=jax.ShapeDtypeStruct((size,) + weight.shape[1:], weight.dtype),
        in_specs=[HBM] + [ANY] * len(others),
        out_specs=VMEM,
        scratch_shapes=[pltpu.SemaphoreType.DMA((8,))],
        compiler_params=limit(24),
        cost_estimate=cost(0, 4 * weight.size // count),
        name="fetch",
    )(in_hbm(weight), *others)


def project_kernel(count, tile, *refs):
    part_refs, weight_refs, out_ref = refs[:count], refs[count:-1], refs[-1]
    tp_index = lax.axis_index("tp")
    prompts, samples, width = out_ref.shape
    share = prompts // count
    left = jnp.concatenate([ref[...].astype(jnp.float32) for ref in part_refs], axis=0).astype(jnp.bfloat16)
    size = weight_refs[0].shape[0]
    for first in range(0, width, tile):
        result = functools.reduce(
            jnp.add,
            [
                jnp.dot(
                    left[:, n * size : (n + 1) * size],
                    ref[:, first : first + tile],
                    preferred_element_type=jnp.float32,
                )
                for n, ref in enumerate(weight_refs)
            ],
        )
        for offset in range(count):
            for n in range(share):
                row = (offset * share + n) * samples
                block = result[row : row + samples].astype(out_ref.dtype)
                out_ref[(tp_index ^ offset) * share + n, :, first : first + tile] = block


def project(parts, weights, samples):
    count = len(parts)
    depth, width = weights[0].shape
    depth *= len(weights)
    total = count * parts[0].shape[0]
    return pl.pallas_call(
        functools.partial(project_kernel, count, min(256, width)),
        out_shape=jax.ShapeDtypeStruct((total // samples, samples, width), jnp.bfloat16),
        in_specs=[VMEM] * (count + len(weights)),
        out_specs=VMEM,
        compiler_params=limit(24),
        cost_estimate=cost(2 * total * depth * width, 2 * depth * width),
        name="project",
    )(*parts, *weights)


def body(prompt_key_values, queries, routing, lengths, out_weight):
    section_count = lax.axis_size("sec")
    tp_count = lax.axis_size("tp")
    slot_count, samples, query_width = queries.shape[1:]
    routing = routing.reshape(-1)

    whole = 2 * CAP
    near = [(offset, 0, whole) for offset in range(2)]
    head, tail = [(2, 0, 1)], [(2, 1, whole - 1)]
    far = tail + [(offset, 0, whole) for offset in range(3, section_count)]

    def across(parts, pieces):
        return [swap(part, "sec", piece[0]) for part, piece in zip(parts, pieces)]

    head_caches = [pack_head(routing, prompt_key_values, head[0], section_count)]
    head_parts = across(head_caches, head)
    far_caches, query_parts = first_pack(
        routing, prompt_key_values, queries, head_caches, far, section_count, tp_count
    )
    query_parts = [swap(part, "sec", offset) for offset, part in enumerate(query_parts)]
    far_parts = across(far_caches, far)
    merged = merge(query_parts[2:], head_parts)
    far_queries = spread(merged, "tp")
    near_caches = pack(routing, prompt_key_values, [merged, query_parts[1]], near, section_count, 10**10)
    near_parts = across(near_caches, near)
    caches, pieces = [*head_caches, *far_caches, *near_caches], head + far + near

    messages = attend(routing, lengths, caches, pieces, query_parts[:2], far_queries)
    partials = [swap(part, "tp", offset) for offset, part in enumerate(messages)]
    held_weight = [fetch(out_weight, [messages[0], *near_parts[1:]], 0, 2)]
    share = join(partials, held_weight, samples, query_width // HEAD_SIZE // KEY_VALUE_HEADS)
    shares = spread(share, "tp")
    held_weight.append(fetch(out_weight, [share], 1, 2))
    if share.ndim == 3:
        attended = jnp.stack(shares)[jnp.arange(tp_count) ^ lax.axis_index("tp")]
        attended = attended.reshape(REQ_GRP, KEY_VALUE_HEADS, samples, -1).transpose(0, 2, 1, 3)
        attended = attended.reshape(REQ_GRP * samples, query_width)
        layer_out = jnp.dot(attended, out_weight, preferred_element_type=jnp.float32)
        layer_out = layer_out.astype(jnp.bfloat16).reshape(REQ_GRP, samples, -1)
    else:
        layer_out = project(shares, held_weight, samples)

    held_cache = place([], near_parts + head_parts, near + head, slot_count)
    for part, piece in zip(far_parts[:-1], far[:-1]):
        held_cache = place([held_cache, layer_out], [part], [piece], slot_count)
    first = (lax.axis_index("sec") ^ far[-1][0]) * whole + far[-1][1]
    held_cache = lax.dynamic_update_slice(held_cache, far_parts[-1][None], (0, first, 0, 0))
    held_cache = held_cache.reshape((1, slot_count) + prompt_key_values.shape[1:])
    return (layer_out, held_cache)


def solution(mesh):
    placed = (
        P(("rep", "sec"), None, "tp", None),
        P(("rep", "sec"), None, None, None),
        P("rep", None),
        P("rep"),
        P(None, "tp"),
    )
    return jax.shard_map(
        body,
        mesh=mesh,
        in_specs=placed,
        out_specs=(P(("rep", "sec"), None, "tp"), P(("rep", "sec"), None, None, "tp", None)),
        check_vma=False,
    )
```

```python
import functools

import jax
import jax.numpy as jnp
from jax import lax
from jax.experimental import pallas as pl
from jax.experimental.pallas import tpu as pltpu
from jax.sharding import PartitionSpec as P

HEAD_SIZE = 128
KEY_VALUE_HEADS = 4
REQ_GRP = 8
CAP = 2
HIDDEN = -1e30
STAT_ROWS = 16

ANY = pl.BlockSpec(memory_space=pl.ANY)
HBM = pl.BlockSpec(memory_space=pltpu.HBM)
VMEM = pl.BlockSpec(memory_space=pltpu.VMEM)
SMEM = pl.BlockSpec(memory_space=pltpu.SMEM)


def limit(mebibytes):
    return pltpu.CompilerParams(vmem_limit_bytes=mebibytes << 20)


def cost(flops, bytes_accessed, transcendentals=0):
    return pl.CostEstimate(flops=flops, bytes_accessed=bytes_accessed, transcendentals=transcendentals)


def swap(value, axis, offset):
    if offset == 0:
        return value
    count = lax.axis_size(axis)
    return lax.ppermute(value, axis, [(i, i ^ offset) for i in range(count)])


def spread(value, axis):
    return [swap(value, axis, offset) for offset in range(lax.axis_size(axis))]


def own_targets(routing_ref, section):
    return [routing_ref[section * REQ_GRP + i] for i in range(REQ_GRP)]


def slot_row(targets, group, order):
    row, before = jnp.int32(0), jnp.int32(0)
    for i, target in enumerate(targets):
        here = target == group
        row = jnp.where(here & (before == order), i, row)
        before = before + here.astype(jnp.int32)
    return row, before > order


def halves_of(pieces):
    return [
        (n, place, offset, first + place)
        for n, (offset, first, count) in enumerate(pieces)
        for place in range(count)
    ]


def start_packing(pieces, section_count, routing_ref, cache_ref, out_refs, sem):
    section = lax.axis_index("sec")
    full = section_count * CAP == REQ_GRP
    targets = own_targets(routing_ref, section)
    halves = halves_of(pieces)
    slots = {(offset, half // 2) for _, _, offset, half in halves}
    rows = {slot: slot_row(targets, section ^ slot[0], slot[1]) for slot in sorted(slots)}

    def copy(n, place, offset, half):
        row, _ = rows[offset, half // 2]
        return pltpu.make_async_copy(
            cache_ref.at[row, half % 2], out_refs[n].at[place], sem.at[offset * 2 * CAP + half]
        )

    for n, place, offset, half in halves:
        if full:
            copy(n, place, offset, half).start()
        else:
            _, filled = rows[offset, half // 2]

            @pl.when(filled)
            def _():
                copy(n, place, offset, half).start()

            @pl.when(jnp.logical_not(filled))
            def _():
                out_refs[n][place] = jnp.zeros_like(out_refs[n][place])

    def finish():
        for n, place, offset, half in halves:
            if full:
                copy(n, place, offset, half).wait()
            else:
                pl.when(rows[offset, half // 2][1])(copy(n, place, offset, half).wait)

    return finish


def start_queries(query_ref, out_refs, offsets, sem):
    section = lax.axis_index("sec")
    copies = []
    for n, (offset, out_ref) in enumerate(zip(offsets, out_refs)):
        width = out_ref.shape[2]
        columns = pl.ds(pl.multiple_of(lax.axis_index("tp") * width, width) if offset > 1 else 0, width)
        part = query_ref.at[0, pl.ds((section ^ offset) * CAP, CAP), :, columns]
        copies.append(pltpu.make_async_copy(part, out_ref, sem.at[n]))
        copies[-1].start()
    return copies


def query_shapes(queries, offsets, tp_count):
    samples, width = queries.shape[2:]
    widths = [width if offset < 2 else width // tp_count for offset in offsets]
    return [jax.ShapeDtypeStruct((CAP, samples, one), queries.dtype) for one in widths]


def head_kernel(piece, offsets, full, routing_ref, cache_ref, query_ref, *refs):
    out_ref, query_out, (routed, held, routing_sem, sem, query_sem) = refs[0], refs[1:-5], refs[-5:]
    offset, half, _ = piece
    section = lax.axis_index("sec")
    copies = [pltpu.make_async_copy(routing_ref, routed, routing_sem)]
    for i in range(REQ_GRP):
        copies.append(pltpu.make_async_copy(cache_ref.at[i, half % 2], held.at[i], sem.at[i]))
    for copy in copies:
        copy.start()
    query_copies = start_queries(query_ref, query_out, offsets, query_sem)
    copies[0].wait()
    row, filled = slot_row(own_targets(routed, section), section ^ offset, half // 2)
    for copy in copies[1:] + query_copies:
        copy.wait()
    chosen = held[row]
    out_ref[0] = chosen if full else jnp.where(filled, chosen, jnp.zeros_like(chosen))


def pack_head(routing, cache, queries, piece, section_count, tp_count):
    shape = cache.shape[2:]
    offsets = range(2, section_count)
    shapes = [jax.ShapeDtypeStruct((1,) + shape, cache.dtype)] + query_shapes(queries, offsets, tp_count)
    head, *parts = pl.pallas_call(
        functools.partial(head_kernel, piece, offsets, section_count * CAP == REQ_GRP),
        out_shape=shapes,
        in_specs=[HBM, HBM, HBM],
        out_specs=[VMEM] * len(shapes),
        scratch_shapes=[
            pltpu.SMEM(routing.shape, jnp.int32),
            pltpu.VMEM((REQ_GRP,) + shape, cache.dtype),
            pltpu.SemaphoreType.DMA,
            pltpu.SemaphoreType.DMA((REQ_GRP,)),
            pltpu.SemaphoreType.DMA((section_count,)),
        ],
        compiler_params=limit(16),
        cost_estimate=cost(0, cache.size),
        name="pack_head",
    )(in_hbm(routing), in_hbm(cache), in_hbm(queries))
    return [head], parts


def first_pack_kernel(pieces, section_count, routing_ref, cache_ref, query_ref, *refs):
    refs, (sem, query_sem) = refs[:-2], refs[-2:]
    query_out, cache_out = refs[-2:], refs[-2 - len(pieces) : -2]
    query_copies = start_queries(query_ref, query_out, range(2), query_sem)
    start_packing(pieces, section_count, routing_ref, cache_ref, cache_out, sem)()
    for copy in query_copies:
        copy.wait()


def pack_kernel(pieces, section_count, routing_ref, cache_ref, *refs):
    cache_out, sem = refs[-1 - len(pieces) : -1], refs[-1]
    start_packing(pieces, section_count, routing_ref, cache_ref, cache_out, sem)()


def merge_kernel(count, *refs):
    for n in range(count):
        refs[-1][n] = refs[n][...]


def merge(parts, others):
    shape = (len(parts),) + parts[0].shape
    return pl.pallas_call(
        functools.partial(merge_kernel, len(parts)),
        out_shape=jax.ShapeDtypeStruct(shape, parts[0].dtype),
        in_specs=[VMEM] * len(parts) + [ANY] * len(others),
        out_specs=VMEM,
        compiler_params=limit(8),
        cost_estimate=cost(3 * 10**9, 8 * len(parts) * parts[0].size),
        name="merge",
    )(*parts, *others)


def in_hbm(value):
    return pltpu.with_memory_space_constraint(value, pltpu.HBM)


def first_pack(routing, cache, queries, others, pieces, section_count):
    shapes = [jax.ShapeDtypeStruct((count,) + cache.shape[2:], cache.dtype) for _, _, count in pieces]
    shapes += query_shapes(queries, range(2), 1)
    parts = pl.pallas_call(
        functools.partial(first_pack_kernel, pieces, section_count),
        out_shape=shapes,
        in_specs=[SMEM, HBM, HBM] + [ANY] * len(others),
        out_specs=[VMEM] * len(shapes),
        scratch_shapes=[
            pltpu.SemaphoreType.DMA((section_count * CAP * 2,)),
            pltpu.SemaphoreType.DMA((2,)),
        ],
        compiler_params=limit(16),
        cost_estimate=cost(0, 4 * sum(shape.size for shape in shapes)),
        name="first_pack",
    )(routing, in_hbm(cache), in_hbm(queries), *others)
    return parts[: len(pieces)], parts[len(pieces) :]


def pack(routing, cache, others, pieces, section_count, flops=0):
    shapes = [jax.ShapeDtypeStruct((count,) + cache.shape[2:], cache.dtype) for _, _, count in pieces]
    return pl.pallas_call(
        functools.partial(pack_kernel, pieces, section_count),
        out_shape=shapes,
        in_specs=[SMEM, HBM] + [ANY] * len(others),
        out_specs=[VMEM] * len(shapes),
        scratch_shapes=[
            pltpu.SemaphoreType.DMA((section_count * CAP * 2,)),
        ],
        compiler_params=limit(16),
        cost_estimate=cost(flops, 4 * sum(shape.size for shape in shapes)),
        name="pack",
    )(routing, in_hbm(cache), *others)


def place_kernel(pieces, *refs):
    count = len(pieces)
    part_refs, out_ref, sem = refs[-2 - count : -2], refs[-2], refs[-1]
    section = lax.axis_index("sec")
    copies = []
    for n, (offset, first, size) in enumerate(pieces):
        for place in range(size):
            half = out_ref.at[0, (section ^ offset) * 2 * CAP + first + place]
            copies.append(pltpu.make_async_copy(part_refs[n].at[place], half, sem.at[len(copies)]))
            copies[-1].start()
    for copy in copies:
        copy.wait()


def place(given, parts, pieces, slot_count):
    part = parts[0]
    return pl.pallas_call(
        functools.partial(place_kernel, pieces),
        out_shape=jax.ShapeDtypeStruct((1, 2 * slot_count) + part.shape[1:], part.dtype),
        in_specs=[HBM] * len(given) + [VMEM] * len(parts),
        out_specs=HBM,
        scratch_shapes=[pltpu.SemaphoreType.DMA((sum(len(part) for part in parts),))],
        input_output_aliases={0: 0} if given else {},
        compiler_params=limit(8),
        cost_estimate=cost(0, 4 * sum(piece.size for piece in parts)),
        name="place",
    )(*[in_hbm(value) for value in given], *parts)


def attend_kernel(pieces, section_count, tp_count, routing_ref, lengths_ref, *refs):
    cache_refs, refs = refs[: len(pieces)], refs[len(pieces) :]
    query_refs, far_refs = refs[:2], refs[2 : 2 + tp_count]
    message_refs = refs[2 + tp_count : 2 + 2 * tp_count]
    messages, stats, stacked, far_queries = refs[2 + 2 * tp_count :]
    section = lax.axis_index("sec")
    tp_index = lax.axis_index("tp")
    local = cache_refs[0].shape[1]
    groups, rows, _ = messages.shape[1:]
    span = KEY_VALUE_HEADS * rows
    prompts = max(1, groups // KEY_VALUE_HEADS)
    full = section_count * CAP == REQ_GRP
    targets = own_targets(routing_ref, section)
    samples = query_refs[0].shape[1]
    for offset, far_ref in enumerate(far_refs):
        far_queries[tp_index ^ offset] = far_ref[...]
    position = lax.broadcasted_iota(jnp.int32, (local, span), 0) + tp_index * local
    owner = lax.broadcasted_iota(jnp.int32, (HEAD_SIZE, span), 1) // rows

    held = {(offset, half): cache_refs[n].at[place] for n, place, offset, half in halves_of(pieces)}

    def prompt(offset, order):
        keys_ref, values_ref = held[offset, 2 * order], held[offset, 2 * order + 1]
        row, _ = slot_row(targets, section ^ offset, order)
        visible = position < lengths_ref[section * REQ_GRP + row]
        slot = offset * CAP + order
        for head in range(span // samples):
            first, part = head * HEAD_SIZE, far_queries.shape[-1]
            if offset < 2:
                values = query_refs[offset][order, :, first : first + HEAD_SIZE]
            else:
                inner = first % part
                values = far_queries[first // part, offset - 2, order, :, inner : inner + HEAD_SIZE]
            stacked[slot, head * samples : (head + 1) * samples] = values.astype(jnp.float32)
        query = stacked[slot].T.astype(jnp.bfloat16)
        query = [jnp.where(owner == k, query, jnp.zeros_like(query)) for k in range(KEY_VALUE_HEADS)]
        score = jnp.dot(
            keys_ref[...], jnp.concatenate(query, axis=0), preferred_element_type=jnp.float32
        ) * HEAD_SIZE ** (-0.5)
        score = jnp.where(visible, score, HIDDEN)
        peak = jnp.max(score, axis=0, keepdims=True)
        weight = jnp.where(visible, jnp.exp(score - peak), 0.0)
        total = jnp.sum(weight, axis=0, keepdims=True)
        some = total > 0.0
        safe = jnp.where(some, total, 1.0)
        stats[0, pl.ds(row, 1)] = jnp.where(some, peak + jnp.log(safe), HIDDEN)
        weight = (weight * (1.0 / safe)).T.astype(jnp.bfloat16)
        for k in range(KEY_VALUE_HEADS):
            mixed = jnp.dot(
                weight[k * rows : (k + 1) * rows],
                values_ref[:, k * HEAD_SIZE : (k + 1) * HEAD_SIZE],
                preferred_element_type=jnp.float32,
            )
            group = row * KEY_VALUE_HEADS + k
            messages[group // groups, group % groups] = mixed.astype(jnp.bfloat16)

    for offset, half in held:
        if half % 2 == 0:
            one = functools.partial(prompt, offset, half // 2)
            if full:
                one()
            else:
                pl.when(slot_row(targets, section ^ offset, half // 2)[1])(one)

    level = stats[0]
    high = level.astype(jnp.bfloat16).astype(jnp.float32)
    rest = level - high
    middle = rest.astype(jnp.bfloat16).astype(jnp.float32)
    stats[0], stats[1], stats[2] = high, middle, rest - middle
    for offset, message_ref in enumerate(message_refs):
        device = tp_index ^ offset
        for inner in range(groups):
            message_ref[inner * rows : (inner + 1) * rows] = messages[device, inner]
        first = device * groups // KEY_VALUE_HEADS
        lines = [stats[part, pl.ds(first + n, 1)] for part in range(3) for n in range(prompts)]
        lines.append(jnp.zeros((STAT_ROWS - 3 * prompts, span), jnp.float32))
        message_ref[groups * rows :] = jnp.concatenate(lines, axis=0).astype(jnp.bfloat16)


def attend(routing, lengths, caches, pieces, queries, far_queries):
    section_count = len(far_queries[0]) + 2
    tp_count = len(far_queries)
    samples, width = queries[0].shape[1:]
    span = width // HEAD_SIZE * samples
    rows = span // KEY_VALUE_HEADS
    groups = REQ_GRP * KEY_VALUE_HEADS // tp_count
    multiplies = REQ_GRP * span * HEAD_SIZE * caches[0].shape[1]
    return pl.pallas_call(
        functools.partial(attend_kernel, pieces, section_count, tp_count),
        out_shape=[jax.ShapeDtypeStruct((groups * rows + STAT_ROWS, HEAD_SIZE), jnp.bfloat16)] * tp_count,
        in_specs=[SMEM, SMEM] + [VMEM] * (len(caches) + len(queries) + tp_count),
        out_specs=[VMEM] * tp_count,
        scratch_shapes=[
            pltpu.VMEM((tp_count, groups, rows, HEAD_SIZE), jnp.bfloat16),
            pltpu.VMEM((3, REQ_GRP, span), jnp.float32),
            pltpu.VMEM((section_count * CAP, span, HEAD_SIZE), jnp.float32),
            pltpu.VMEM((tp_count,) + far_queries[0].shape, far_queries[0].dtype),
        ],
        compiler_params=limit(12),
        cost_estimate=cost(2 * 10**10, 2 * sum(part.size for part in caches), multiplies // HEAD_SIZE),
        name="attend",
    )(routing, lengths, *caches, *queries, *far_queries)


def join_kernel(count, samples, rows, *refs):
    message_refs, (out_ref, scaling, flat) = refs[:count], refs[-3:]
    groups = (message_refs[0].shape[0] - STAT_ROWS) // rows
    prompts = max(1, groups // KEY_VALUE_HEADS)
    heads = rows // samples
    tp_index = lax.axis_index("tp")
    levels = []
    for ref in message_refs:
        lines = ref[groups * rows :].astype(jnp.float32)[0:8]
        levels.append(lines + pltpu.roll(lines, 8 - prompts, 0) + pltpu.roll(lines, 8 - 2 * prompts, 0))
    summit = functools.reduce(jnp.maximum, levels)
    scales = [jnp.exp(level - summit) for level in levels]
    total = functools.reduce(jnp.add, scales)
    for n, scale in enumerate(scales):
        scaling[n] = (scale / total).T
    for inner in range(groups):
        if groups % KEY_VALUE_HEADS:
            first = (tp_index * groups + inner) % KEY_VALUE_HEADS * rows
            part = pl.ds(pl.multiple_of(first, rows), rows)
        else:
            part = pl.ds(inner % KEY_VALUE_HEADS * rows, rows)
        prompt = inner // KEY_VALUE_HEADS
        terms = [
            ref[inner * rows : (inner + 1) * rows].astype(jnp.float32) * scaling[n, part, prompt : prompt + 1]
            for n, ref in enumerate(message_refs)
        ]
        joined = functools.reduce(jnp.add, terms)
        for head in range(heads):
            block = joined[head * samples : (head + 1) * samples]
            if len(flat.shape) == 2:
                row = prompt * samples
                column = (inner % KEY_VALUE_HEADS * heads + head) * HEAD_SIZE
                flat[row : row + samples, column : column + HEAD_SIZE] = block
            else:
                flat[inner, :, head * HEAD_SIZE : (head + 1) * HEAD_SIZE] = block
    out_ref[...] = flat[...].astype(jnp.bfloat16)


def join(messages, others, samples, heads):
    rows = heads * samples
    groups = (messages[0].shape[0] - STAT_ROWS) // rows
    width = rows // samples * HEAD_SIZE
    if groups % KEY_VALUE_HEADS == 0:
        shape = (groups // KEY_VALUE_HEADS * samples, KEY_VALUE_HEADS * width)
    else:
        shape = (groups, samples, width)
    count = len(messages)
    return pl.pallas_call(
        functools.partial(join_kernel, count, samples, rows),
        out_shape=jax.ShapeDtypeStruct(shape, jnp.bfloat16),
        in_specs=[VMEM] * count + [ANY] * len(others),
        out_specs=VMEM,
        scratch_shapes=[
            pltpu.VMEM((count, KEY_VALUE_HEADS * rows, 8), jnp.float32),
            pltpu.VMEM(shape, jnp.float32),
        ],
        compiler_params=limit(8),
        cost_estimate=cost(4 * count * messages[0].size, 2 * count * messages[0].size),
        name="join",
    )(*messages, *others)


def fetch_kernel(first, weight_ref, *refs):
    out_ref, sem = refs[-2:]
    copies = []
    step = out_ref.shape[0] // sem.shape[0]
    for n in range(sem.shape[0]):
        rows = weight_ref.at[pl.ds(first + n * step, step)]
        copies.append(pltpu.make_async_copy(rows, out_ref.at[pl.ds(n * step, step)], sem.at[n]))
        copies[-1].start()
    for copy in copies:
        copy.wait()


def fetch(weight, others, number, count):
    size = weight.shape[0] // count
    return pl.pallas_call(
        functools.partial(fetch_kernel, number * size),
        out_shape=jax.ShapeDtypeStruct((size,) + weight.shape[1:], weight.dtype),
        in_specs=[HBM] + [ANY] * len(others),
        out_specs=VMEM,
        scratch_shapes=[pltpu.SemaphoreType.DMA((8,))],
        compiler_params=limit(24),
        cost_estimate=cost(0, 4 * weight.size // count),
        name="fetch",
    )(in_hbm(weight), *others)


def project_kernel(count, tile, *refs):
    part_refs, weight_refs, out_ref = refs[:count], refs[count:-1], refs[-1]
    tp_index = lax.axis_index("tp")
    prompts, samples, width = out_ref.shape
    share = prompts // count
    left = jnp.concatenate([ref[...].astype(jnp.float32) for ref in part_refs], axis=0).astype(jnp.bfloat16)
    size = weight_refs[0].shape[0]
    for first in range(0, width, tile):
        result = functools.reduce(
            jnp.add,
            [
                jnp.dot(
                    left[:, n * size : (n + 1) * size],
                    ref[:, first : first + tile],
                    preferred_element_type=jnp.float32,
                )
                for n, ref in enumerate(weight_refs)
            ],
        )
        for offset in range(count):
            for n in range(share):
                row = (offset * share + n) * samples
                block = result[row : row + samples].astype(out_ref.dtype)
                out_ref[(tp_index ^ offset) * share + n, :, first : first + tile] = block


def project(parts, weights, samples):
    count = len(parts)
    depth, width = weights[0].shape
    depth *= len(weights)
    total = count * parts[0].shape[0]
    return pl.pallas_call(
        functools.partial(project_kernel, count, min(256, width)),
        out_shape=jax.ShapeDtypeStruct((total // samples, samples, width), jnp.bfloat16),
        in_specs=[VMEM] * (count + len(weights)),
        out_specs=VMEM,
        compiler_params=limit(24),
        cost_estimate=cost(2 * total * depth * width, 2 * depth * width),
        name="project",
    )(*parts, *weights)


def body(prompt_key_values, queries, routing, lengths, out_weight):
    section_count = lax.axis_size("sec")
    tp_count = lax.axis_size("tp")
    slot_count, samples, query_width = queries.shape[1:]
    routing = routing.reshape(-1)

    whole = 2 * CAP
    near = [(offset, 0, whole) for offset in range(2)]
    head, tail = [(2, 0, 1)], [(2, 1, whole - 1)]
    far = tail + [(offset, 0, whole) for offset in range(3, section_count)]

    def across(parts, pieces):
        return [swap(part, "sec", piece[0]) for part, piece in zip(parts, pieces)]

    head_caches, far_queries = pack_head(
        routing, prompt_key_values, queries, head[0], section_count, tp_count
    )
    head_parts = across(head_caches, head)
    far_queries = [swap(part, "sec", n + 2) for n, part in enumerate(far_queries)]
    far_caches, query_parts = first_pack(
        routing, prompt_key_values, queries, head_caches, far, section_count
    )
    far_parts = across(far_caches, far)
    query_parts = [swap(part, "sec", offset) for offset, part in enumerate(query_parts)]
    merged = merge(far_queries, head_parts)
    far_queries = spread(merged, "tp")
    near_caches = pack(routing, prompt_key_values, [merged, query_parts[1]], near, section_count, 10**10)
    near_parts = across(near_caches, near)
    caches, pieces = [*head_caches, *far_caches, *near_caches], head + far + near

    messages = attend(routing, lengths, caches, pieces, query_parts, far_queries)
    partials = [swap(part, "tp", offset) for offset, part in enumerate(messages)]
    held_weight = [fetch(out_weight, [messages[0], *near_parts[1:]], 0, 2)]
    share = join(partials, held_weight, samples, query_width // HEAD_SIZE // KEY_VALUE_HEADS)
    shares = spread(share, "tp")
    held_weight.append(fetch(out_weight, [share], 1, 2))
    if share.ndim == 3:
        attended = jnp.stack(shares)[jnp.arange(tp_count) ^ lax.axis_index("tp")]
        attended = attended.reshape(REQ_GRP, KEY_VALUE_HEADS, samples, -1).transpose(0, 2, 1, 3)
        attended = attended.reshape(REQ_GRP * samples, query_width)
        layer_out = jnp.dot(attended, out_weight, preferred_element_type=jnp.float32)
        layer_out = layer_out.astype(jnp.bfloat16).reshape(REQ_GRP, samples, -1)
    else:
        layer_out = project(shares, held_weight, samples)

    held_cache = place([], near_parts + head_parts, near + head, slot_count)
    for part, piece in zip(far_parts, far):
        held_cache = place([held_cache, layer_out], [part], [piece], slot_count)
    held_cache = held_cache.reshape((1, slot_count) + prompt_key_values.shape[1:])
    return (layer_out, held_cache)


def solution(mesh):
    placed = (
        P(("rep", "sec"), None, "tp", None),
        P(("rep", "sec"), None, None, None),
        P("rep", None),
        P("rep"),
        P(None, "tp"),
    )
    return jax.shard_map(
        body,
        mesh=mesh,
        in_specs=placed,
        out_specs=(P(("rep", "sec"), None, "tp"), P(("rep", "sec"), None, None, "tp", None)),
        check_vma=False,
    )
```

```python
import functools

import jax
import jax.numpy as jnp
from jax import lax
from jax.experimental import pallas as pl
from jax.experimental.pallas import tpu as pltpu
from jax.sharding import PartitionSpec as P

HEAD_SIZE = 128
KEY_VALUE_HEADS = 4
REQ_GRP = 8
CAP = 2
HIDDEN = -1e30
STAT_ROWS = 16

ANY = pl.BlockSpec(memory_space=pl.ANY)
HBM = pl.BlockSpec(memory_space=pltpu.HBM)
VMEM = pl.BlockSpec(memory_space=pltpu.VMEM)
SMEM = pl.BlockSpec(memory_space=pltpu.SMEM)


def limit(mebibytes):
    return pltpu.CompilerParams(vmem_limit_bytes=mebibytes << 20)


def cost(flops, bytes_accessed, transcendentals=0):
    return pl.CostEstimate(flops=flops, bytes_accessed=bytes_accessed, transcendentals=transcendentals)


def swap(value, axis, offset):
    if offset == 0:
        return value
    count = lax.axis_size(axis)
    return lax.ppermute(value, axis, [(i, i ^ offset) for i in range(count)])


def spread(value, axis):
    return [swap(value, axis, offset) for offset in range(lax.axis_size(axis))]


def own_targets(routing_ref, section):
    return [routing_ref[section * REQ_GRP + i] for i in range(REQ_GRP)]


def slot_row(targets, group, order):
    row, before = jnp.int32(0), jnp.int32(0)
    for i, target in enumerate(targets):
        here = target == group
        row = jnp.where(here & (before == order), i, row)
        before = before + here.astype(jnp.int32)
    return row, before > order


def halves_of(pieces):
    return [
        (n, place, offset, first + place)
        for n, (offset, first, count) in enumerate(pieces)
        for place in range(count)
    ]


def start_packing(pieces, section_count, routing_ref, cache_ref, out_refs, sem):
    section = lax.axis_index("sec")
    full = section_count * CAP == REQ_GRP
    targets = own_targets(routing_ref, section)
    halves = halves_of(pieces)
    slots = {(offset, half // 2) for _, _, offset, half in halves}
    rows = {slot: slot_row(targets, section ^ slot[0], slot[1]) for slot in sorted(slots)}

    def copy(n, place, offset, half):
        row, _ = rows[offset, half // 2]
        return pltpu.make_async_copy(
            cache_ref.at[row, half % 2], out_refs[n].at[place], sem.at[offset * 2 * CAP + half]
        )

    for n, place, offset, half in halves:
        if full:
            copy(n, place, offset, half).start()
        else:
            _, filled = rows[offset, half // 2]

            @pl.when(filled)
            def _():
                copy(n, place, offset, half).start()

            @pl.when(jnp.logical_not(filled))
            def _():
                out_refs[n][place] = jnp.zeros_like(out_refs[n][place])

    def finish():
        for n, place, offset, half in halves:
            if full:
                copy(n, place, offset, half).wait()
            else:
                pl.when(rows[offset, half // 2][1])(copy(n, place, offset, half).wait)

    return finish


def start_queries(query_ref, out_refs, offsets, sem):
    section = lax.axis_index("sec")
    copies = []
    for n, (offset, out_ref) in enumerate(zip(offsets, out_refs)):
        width = out_ref.shape[2]
        columns = pl.ds(pl.multiple_of(lax.axis_index("tp") * width, width) if offset > 1 else 0, width)
        part = query_ref.at[0, pl.ds((section ^ offset) * CAP, CAP), :, columns]
        copies.append(pltpu.make_async_copy(part, out_ref, sem.at[n]))
        copies[-1].start()
    return copies


def query_shapes(queries, offsets, tp_count):
    samples, width = queries.shape[2:]
    widths = [width if offset < 2 else width // tp_count for offset in offsets]
    return [jax.ShapeDtypeStruct((CAP, samples, one), queries.dtype) for one in widths]


def head_kernel(piece, offsets, full, routing_ref, cache_ref, query_ref, *refs):
    out_ref, query_out, (routed, held, routing_sem, sem, query_sem) = refs[0], refs[1:-5], refs[-5:]
    offset, half, _ = piece
    section = lax.axis_index("sec")
    copies = [pltpu.make_async_copy(routing_ref, routed, routing_sem)]
    for i in range(REQ_GRP):
        copies.append(pltpu.make_async_copy(cache_ref.at[i, half % 2], held.at[i], sem.at[i]))
    for copy in copies:
        copy.start()
    query_copies = start_queries(query_ref, query_out, offsets, query_sem)
    copies[0].wait()
    row, filled = slot_row(own_targets(routed, section), section ^ offset, half // 2)
    for copy in copies[1:] + query_copies:
        copy.wait()
    chosen = held[row]
    out_ref[0] = chosen if full else jnp.where(filled, chosen, jnp.zeros_like(chosen))


def pack_head(routing, cache, queries, piece, section_count, tp_count):
    shape = cache.shape[2:]
    offsets = range(2, section_count)
    shapes = [jax.ShapeDtypeStruct((1,) + shape, cache.dtype)] + query_shapes(queries, offsets, tp_count)
    head, *parts = pl.pallas_call(
        functools.partial(head_kernel, piece, offsets, section_count * CAP == REQ_GRP),
        out_shape=shapes,
        in_specs=[HBM, HBM, HBM],
        out_specs=[VMEM] * len(shapes),
        scratch_shapes=[
            pltpu.SMEM(routing.shape, jnp.int32),
            pltpu.VMEM((REQ_GRP,) + shape, cache.dtype),
            pltpu.SemaphoreType.DMA,
            pltpu.SemaphoreType.DMA((REQ_GRP,)),
            pltpu.SemaphoreType.DMA((section_count,)),
        ],
        compiler_params=limit(16),
        cost_estimate=cost(0, cache.size),
        name="pack_head",
    )(in_hbm(routing), in_hbm(cache), in_hbm(queries))
    return [head], parts


def first_pack_kernel(pieces, section_count, routing_ref, cache_ref, query_ref, *refs):
    refs, (sem, query_sem) = refs[:-2], refs[-2:]
    query_out, cache_out = refs[-2:], refs[-2 - len(pieces) : -2]
    query_copies = start_queries(query_ref, query_out, range(2), query_sem)
    start_packing(pieces, section_count, routing_ref, cache_ref, cache_out, sem)()
    for copy in query_copies:
        copy.wait()


def pack_kernel(pieces, section_count, routing_ref, cache_ref, *refs):
    cache_out, sem = refs[-1 - len(pieces) : -1], refs[-1]
    start_packing(pieces, section_count, routing_ref, cache_ref, cache_out, sem)()


def merge_kernel(count, *refs):
    for n in range(count):
        refs[-1][n] = refs[n][...]


def merge(parts, others):
    shape = (len(parts),) + parts[0].shape
    return pl.pallas_call(
        functools.partial(merge_kernel, len(parts)),
        out_shape=jax.ShapeDtypeStruct(shape, parts[0].dtype),
        in_specs=[VMEM] * len(parts) + [ANY] * len(others),
        out_specs=VMEM,
        compiler_params=limit(8),
        cost_estimate=cost(3 * 10**9, 8 * len(parts) * parts[0].size),
        name="merge",
    )(*parts, *others)


def in_hbm(value):
    return pltpu.with_memory_space_constraint(value, pltpu.HBM)


def first_pack(routing, cache, queries, others, pieces, section_count):
    shapes = [jax.ShapeDtypeStruct((count,) + cache.shape[2:], cache.dtype) for _, _, count in pieces]
    shapes += query_shapes(queries, range(2), 1)
    parts = pl.pallas_call(
        functools.partial(first_pack_kernel, pieces, section_count),
        out_shape=shapes,
        in_specs=[SMEM, HBM, HBM] + [ANY] * len(others),
        out_specs=[VMEM] * len(shapes),
        scratch_shapes=[
            pltpu.SemaphoreType.DMA((section_count * CAP * 2,)),
            pltpu.SemaphoreType.DMA((2,)),
        ],
        compiler_params=limit(16),
        cost_estimate=cost(0, 4 * sum(shape.size for shape in shapes)),
        name="first_pack",
    )(routing, in_hbm(cache), in_hbm(queries), *others)
    return parts[: len(pieces)], parts[len(pieces) :]


def pack(routing, cache, others, pieces, section_count, flops=0):
    shapes = [jax.ShapeDtypeStruct((count,) + cache.shape[2:], cache.dtype) for _, _, count in pieces]
    return pl.pallas_call(
        functools.partial(pack_kernel, pieces, section_count),
        out_shape=shapes,
        in_specs=[SMEM, HBM] + [ANY] * len(others),
        out_specs=[VMEM] * len(shapes),
        scratch_shapes=[
            pltpu.SemaphoreType.DMA((section_count * CAP * 2,)),
        ],
        compiler_params=limit(16),
        cost_estimate=cost(flops, 4 * sum(shape.size for shape in shapes)),
        name="pack",
    )(routing, in_hbm(cache), *others)


def place_kernel(pieces, *refs):
    count = len(pieces)
    part_refs, out_ref, sem = refs[-2 - count : -2], refs[-2], refs[-1]
    section = lax.axis_index("sec")
    copies = []
    for n, (offset, first, size) in enumerate(pieces):
        for place in range(size):
            half = out_ref.at[0, (section ^ offset) * 2 * CAP + first + place]
            copies.append(pltpu.make_async_copy(part_refs[n].at[place], half, sem.at[len(copies)]))
            copies[-1].start()
    for copy in copies:
        copy.wait()


def place(given, parts, pieces, slot_count):
    part = parts[0]
    return pl.pallas_call(
        functools.partial(place_kernel, pieces),
        out_shape=jax.ShapeDtypeStruct((1, 2 * slot_count) + part.shape[1:], part.dtype),
        in_specs=[HBM] * len(given) + [VMEM] * len(parts),
        out_specs=HBM,
        scratch_shapes=[pltpu.SemaphoreType.DMA((sum(len(part) for part in parts),))],
        input_output_aliases={0: 0} if given else {},
        compiler_params=limit(8),
        cost_estimate=cost(0, 4 * sum(piece.size for piece in parts)),
        name="place",
    )(*[in_hbm(value) for value in given], *parts)


def attend_kernel(pieces, section_count, tp_count, routing_ref, lengths_ref, *refs):
    cache_refs, refs = refs[: len(pieces)], refs[len(pieces) :]
    query_refs, far_refs = refs[:2], refs[2 : 2 + tp_count]
    message_refs = refs[2 + tp_count : 2 + 2 * tp_count]
    messages, stats, stacked, far_queries = refs[2 + 2 * tp_count :]
    section = lax.axis_index("sec")
    tp_index = lax.axis_index("tp")
    local = cache_refs[0].shape[1]
    groups, rows, _ = messages.shape[1:]
    span = KEY_VALUE_HEADS * rows
    prompts = max(1, groups // KEY_VALUE_HEADS)
    full = section_count * CAP == REQ_GRP
    targets = own_targets(routing_ref, section)
    samples = query_refs[0].shape[1]
    for offset, far_ref in enumerate(far_refs):
        far_queries[tp_index ^ offset] = far_ref[...]
    position = lax.broadcasted_iota(jnp.int32, (local, span), 0) + tp_index * local
    owner = lax.broadcasted_iota(jnp.int32, (HEAD_SIZE, span), 1) // rows

    held = {(offset, half): cache_refs[n].at[place] for n, place, offset, half in halves_of(pieces)}

    def prompt(offset, order):
        keys_ref, values_ref = held[offset, 2 * order], held[offset, 2 * order + 1]
        row, _ = slot_row(targets, section ^ offset, order)
        visible = position < lengths_ref[section * REQ_GRP + row]
        slot = offset * CAP + order
        for head in range(span // samples):
            first, part = head * HEAD_SIZE, far_queries.shape[-1]
            if offset < 2:
                values = query_refs[offset][order, :, first : first + HEAD_SIZE]
            else:
                inner = first % part
                values = far_queries[first // part, offset - 2, order, :, inner : inner + HEAD_SIZE]
            stacked[slot, head * samples : (head + 1) * samples] = values.astype(jnp.float32)
        query = stacked[slot].T.astype(jnp.bfloat16)
        query = [jnp.where(owner == k, query, jnp.zeros_like(query)) for k in range(KEY_VALUE_HEADS)]
        score = jnp.dot(
            keys_ref[...], jnp.concatenate(query, axis=0), preferred_element_type=jnp.float32
        ) * HEAD_SIZE ** (-0.5)
        score = jnp.where(visible, score, HIDDEN)
        peak = jnp.max(score, axis=0, keepdims=True)
        weight = jnp.where(visible, jnp.exp(score - peak), 0.0)
        total = jnp.sum(weight, axis=0, keepdims=True)
        some = total > 0.0
        safe = jnp.where(some, total, 1.0)
        stats[0, pl.ds(row, 1)] = jnp.where(some, peak + jnp.log(safe), HIDDEN)
        weight = (weight * (1.0 / safe)).T.astype(jnp.bfloat16)
        for k in range(KEY_VALUE_HEADS):
            mixed = jnp.dot(
                weight[k * rows : (k + 1) * rows],
                values_ref[:, k * HEAD_SIZE : (k + 1) * HEAD_SIZE],
                preferred_element_type=jnp.float32,
            )
            group = row * KEY_VALUE_HEADS + k
            messages[group // groups, group % groups] = mixed.astype(jnp.bfloat16)

    for offset, half in held:
        if half % 2 == 0:
            one = functools.partial(prompt, offset, half // 2)
            if full:
                one()
            else:
                pl.when(slot_row(targets, section ^ offset, half // 2)[1])(one)

    level = stats[0]
    high = level.astype(jnp.bfloat16).astype(jnp.float32)
    rest = level - high
    middle = rest.astype(jnp.bfloat16).astype(jnp.float32)
    stats[0], stats[1], stats[2] = high, middle, rest - middle
    for offset, message_ref in enumerate(message_refs):
        device = tp_index ^ offset
        for inner in range(groups):
            message_ref[inner * rows : (inner + 1) * rows] = messages[device, inner]
        first = device * groups // KEY_VALUE_HEADS
        lines = [stats[part, pl.ds(first + n, 1)] for part in range(3) for n in range(prompts)]
        lines.append(jnp.zeros((STAT_ROWS - 3 * prompts, span), jnp.float32))
        message_ref[groups * rows :] = jnp.concatenate(lines, axis=0).astype(jnp.bfloat16)


def attend(routing, lengths, caches, pieces, queries, far_queries):
    section_count = len(far_queries[0]) + 2
    tp_count = len(far_queries)
    samples, width = queries[0].shape[1:]
    span = width // HEAD_SIZE * samples
    rows = span // KEY_VALUE_HEADS
    groups = REQ_GRP * KEY_VALUE_HEADS // tp_count
    multiplies = REQ_GRP * span * HEAD_SIZE * caches[0].shape[1]
    return pl.pallas_call(
        functools.partial(attend_kernel, pieces, section_count, tp_count),
        out_shape=[jax.ShapeDtypeStruct((groups * rows + STAT_ROWS, HEAD_SIZE), jnp.bfloat16)] * tp_count,
        in_specs=[SMEM, SMEM] + [VMEM] * (len(caches) + len(queries) + tp_count),
        out_specs=[VMEM] * tp_count,
        scratch_shapes=[
            pltpu.VMEM((tp_count, groups, rows, HEAD_SIZE), jnp.bfloat16),
            pltpu.VMEM((3, REQ_GRP, span), jnp.float32),
            pltpu.VMEM((section_count * CAP, span, HEAD_SIZE), jnp.float32),
            pltpu.VMEM((tp_count,) + far_queries[0].shape, far_queries[0].dtype),
        ],
        compiler_params=limit(12),
        cost_estimate=cost(2 * 10**10, 2 * sum(part.size for part in caches), multiplies // HEAD_SIZE),
        name="attend",
    )(routing, lengths, *caches, *queries, *far_queries)


def join_kernel(count, samples, rows, *refs):
    message_refs, (out_ref, scaling, flat) = refs[:count], refs[-3:]
    groups = (message_refs[0].shape[0] - STAT_ROWS) // rows
    prompts = max(1, groups // KEY_VALUE_HEADS)
    heads = rows // samples
    tp_index = lax.axis_index("tp")
    levels = []
    for ref in message_refs:
        lines = ref[groups * rows :].astype(jnp.float32)[0:8]
        levels.append(lines + pltpu.roll(lines, 8 - prompts, 0) + pltpu.roll(lines, 8 - 2 * prompts, 0))
    summit = functools.reduce(jnp.maximum, levels)
    scales = [jnp.exp(level - summit) for level in levels]
    total = functools.reduce(jnp.add, scales)
    for n, scale in enumerate(scales):
        scaling[n] = (scale / total).T
    for inner in range(groups):
        if groups % KEY_VALUE_HEADS:
            first = (tp_index * groups + inner) % KEY_VALUE_HEADS * rows
            part = pl.ds(pl.multiple_of(first, rows), rows)
        else:
            part = pl.ds(inner % KEY_VALUE_HEADS * rows, rows)
        prompt = inner // KEY_VALUE_HEADS
        terms = [
            ref[inner * rows : (inner + 1) * rows].astype(jnp.float32) * scaling[n, part, prompt : prompt + 1]
            for n, ref in enumerate(message_refs)
        ]
        joined = functools.reduce(jnp.add, terms)
        for head in range(heads):
            block = joined[head * samples : (head + 1) * samples]
            if len(flat.shape) == 2:
                row = prompt * samples
                column = (inner % KEY_VALUE_HEADS * heads + head) * HEAD_SIZE
                flat[row : row + samples, column : column + HEAD_SIZE] = block
            else:
                flat[inner, :, head * HEAD_SIZE : (head + 1) * HEAD_SIZE] = block
    out_ref[...] = flat[...].astype(jnp.bfloat16)


def join(messages, others, samples, heads):
    rows = heads * samples
    groups = (messages[0].shape[0] - STAT_ROWS) // rows
    width = rows // samples * HEAD_SIZE
    if groups % KEY_VALUE_HEADS == 0:
        shape = (groups // KEY_VALUE_HEADS * samples, KEY_VALUE_HEADS * width)
    else:
        shape = (groups, samples, width)
    count = len(messages)
    return pl.pallas_call(
        functools.partial(join_kernel, count, samples, rows),
        out_shape=jax.ShapeDtypeStruct(shape, jnp.bfloat16),
        in_specs=[VMEM] * count + [ANY] * len(others),
        out_specs=VMEM,
        scratch_shapes=[
            pltpu.VMEM((count, KEY_VALUE_HEADS * rows, 8), jnp.float32),
            pltpu.VMEM(shape, jnp.float32),
        ],
        compiler_params=limit(8),
        cost_estimate=cost(4 * count * messages[0].size, 2 * count * messages[0].size),
        name="join",
    )(*messages, *others)


def fetch_kernel(first, weight_ref, *refs):
    out_ref, sem = refs[-2:]
    copies = []
    step = out_ref.shape[0] // sem.shape[0]
    for n in range(sem.shape[0]):
        rows = weight_ref.at[pl.ds(first + n * step, step)]
        copies.append(pltpu.make_async_copy(rows, out_ref.at[pl.ds(n * step, step)], sem.at[n]))
        copies[-1].start()
    for copy in copies:
        copy.wait()


def fetch(weight, others, number, count):
    size = weight.shape[0] // count
    return pl.pallas_call(
        functools.partial(fetch_kernel, number * size),
        out_shape=jax.ShapeDtypeStruct((size,) + weight.shape[1:], weight.dtype),
        in_specs=[HBM] + [ANY] * len(others),
        out_specs=VMEM,
        scratch_shapes=[pltpu.SemaphoreType.DMA((8,))],
        compiler_params=limit(24),
        cost_estimate=cost(0, 4 * weight.size // count),
        name="fetch",
    )(in_hbm(weight), *others)


def project_kernel(count, tile, skipped, *refs):
    refs = refs[skipped:]
    part_refs, weight_refs, out_ref = refs[:count], refs[count:-1], refs[-1]
    tp_index = lax.axis_index("tp")
    prompts, samples, width = out_ref.shape
    share = prompts // count
    left = jnp.concatenate([ref[...].astype(jnp.float32) for ref in part_refs], axis=0).astype(jnp.bfloat16)
    size = weight_refs[0].shape[0]
    for first in range(0, width, tile):
        result = functools.reduce(
            jnp.add,
            [
                jnp.dot(
                    left[:, n * size : (n + 1) * size],
                    ref[:, first : first + tile],
                    preferred_element_type=jnp.float32,
                )
                for n, ref in enumerate(weight_refs)
            ],
        )
        for offset in range(count):
            for n in range(share):
                row = (offset * share + n) * samples
                block = result[row : row + samples].astype(out_ref.dtype)
                out_ref[(tp_index ^ offset) * share + n, :, first : first + tile] = block


def project(parts, weights, others, samples):
    count = len(parts)
    depth, width = weights[0].shape
    depth *= len(weights)
    total = count * parts[0].shape[0]
    return pl.pallas_call(
        functools.partial(project_kernel, count, min(256, width), len(others)),
        out_shape=jax.ShapeDtypeStruct((total // samples, samples, width), jnp.bfloat16),
        in_specs=[ANY] * len(others) + [VMEM] * (count + len(weights)),
        out_specs=VMEM,
        compiler_params=limit(24),
        cost_estimate=cost(2 * total * depth * width, 2 * depth * width),
        name="project",
    )(*others, *parts, *weights)


def body(prompt_key_values, queries, routing, lengths, out_weight):
    section_count = lax.axis_size("sec")
    tp_count = lax.axis_size("tp")
    slot_count, samples, query_width = queries.shape[1:]
    routing = routing.reshape(-1)

    whole = 2 * CAP
    near = [(offset, 0, whole) for offset in range(2)]
    head, tail = [(2, 0, 1)], [(2, 1, whole - 1)]
    far = tail + [(offset, 0, whole) for offset in range(3, section_count)]

    def across(parts, pieces):
        return [swap(part, "sec", piece[0]) for part, piece in zip(parts, pieces)]

    head_caches, far_queries = pack_head(
        routing, prompt_key_values, queries, head[0], section_count, tp_count
    )
    head_parts = across(head_caches, head)
    far_queries = [swap(part, "sec", n + 2) for n, part in enumerate(far_queries)]
    far_caches, query_parts = first_pack(
        routing, prompt_key_values, queries, head_caches, far, section_count
    )
    far_parts = across(far_caches, far)
    query_parts = [swap(part, "sec", offset) for offset, part in enumerate(query_parts)]
    merged = merge(far_queries, head_parts)
    far_queries = spread(merged, "tp")
    near_caches = pack(routing, prompt_key_values, [merged, query_parts[1]], near, section_count, 10**10)
    near_parts = across(near_caches, near)
    caches, pieces = [*head_caches, *far_caches, *near_caches], head + far + near

    messages = attend(routing, lengths, caches, pieces, query_parts, far_queries)
    partials = [swap(part, "tp", offset) for offset, part in enumerate(messages)]
    held_weight = [fetch(out_weight, [messages[0], *near_parts[1:]], 0, 2)]
    share = join(partials, held_weight, samples, query_width // HEAD_SIZE // KEY_VALUE_HEADS)
    shares = spread(share, "tp")
    held_weight.append(fetch(out_weight, [share], 1, 2))
    if share.ndim == 3:
        attended = jnp.stack(shares)[jnp.arange(tp_count) ^ lax.axis_index("tp")]
        attended = attended.reshape(REQ_GRP, KEY_VALUE_HEADS, samples, -1).transpose(0, 2, 1, 3)
        attended = attended.reshape(REQ_GRP * samples, query_width)
        layer_out = jnp.dot(attended, out_weight, preferred_element_type=jnp.float32)
        layer_out = layer_out.astype(jnp.bfloat16).reshape(REQ_GRP, samples, -1)
    else:
        layer_out = project(shares, held_weight, far_parts[:-1], samples)

    held_cache = place([], near_parts + head_parts, near + head, slot_count)
    held_cache = place([held_cache, share], far_parts[:-1], far[:-1], slot_count)
    held_cache = place([held_cache, layer_out], far_parts[-1:], far[-1:], slot_count)
    held_cache = held_cache.reshape((1, slot_count) + prompt_key_values.shape[1:])
    return (layer_out, held_cache)


def solution(mesh):
    placed = (
        P(("rep", "sec"), None, "tp", None),
        P(("rep", "sec"), None, None, None),
        P("rep", None),
        P("rep"),
        P(None, "tp"),
    )
    return jax.shard_map(
        body,
        mesh=mesh,
        in_specs=placed,
        out_specs=(P(("rep", "sec"), None, "tp"), P(("rep", "sec"), None, None, "tp", None)),
        check_vma=False,
    )
```

```python
import functools

import jax
import jax.numpy as jnp
from jax import lax
from jax.experimental import pallas as pl
from jax.experimental.pallas import tpu as pltpu
from jax.sharding import PartitionSpec as P

HEAD_SIZE = 128
KEY_VALUE_HEADS = 4
REQ_GRP = 8
CAP = 2
HIDDEN = -1e30
STAT_ROWS = 16

ANY = pl.BlockSpec(memory_space=pl.ANY)
HBM = pl.BlockSpec(memory_space=pltpu.HBM)
VMEM = pl.BlockSpec(memory_space=pltpu.VMEM)
SMEM = pl.BlockSpec(memory_space=pltpu.SMEM)


def limit(mebibytes):
    return pltpu.CompilerParams(vmem_limit_bytes=mebibytes << 20)


def cost(flops, bytes_accessed, transcendentals=0):
    return pl.CostEstimate(flops=flops, bytes_accessed=bytes_accessed, transcendentals=transcendentals)


def swap(value, axis, offset):
    if offset == 0:
        return value
    count = lax.axis_size(axis)
    return lax.ppermute(value, axis, [(i, i ^ offset) for i in range(count)])


def spread(value, axis):
    return [swap(value, axis, offset) for offset in range(lax.axis_size(axis))]


def own_targets(routing_ref, section):
    return [routing_ref[section * REQ_GRP + i] for i in range(REQ_GRP)]


def slot_row(targets, group, order):
    row, before = jnp.int32(0), jnp.int32(0)
    for i, target in enumerate(targets):
        here = target == group
        row = jnp.where(here & (before == order), i, row)
        before = before + here.astype(jnp.int32)
    return row, before > order


def halves_of(pieces):
    return [
        (n, place, offset, first + place)
        for n, (offset, first, count) in enumerate(pieces)
        for place in range(count)
    ]


def start_packing(pieces, section_count, routing_ref, cache_ref, out_refs, sem):
    section = lax.axis_index("sec")
    full = section_count * CAP == REQ_GRP
    targets = own_targets(routing_ref, section)
    halves = halves_of(pieces)
    slots = {(offset, half // 2) for _, _, offset, half in halves}
    rows = {slot: slot_row(targets, section ^ slot[0], slot[1]) for slot in sorted(slots)}

    def copy(n, place, offset, half):
        row, _ = rows[offset, half // 2]
        return pltpu.make_async_copy(
            cache_ref.at[row, half % 2], out_refs[n].at[place], sem.at[offset * 2 * CAP + half]
        )

    for n, place, offset, half in halves:
        if full:
            copy(n, place, offset, half).start()
        else:
            _, filled = rows[offset, half // 2]

            @pl.when(filled)
            def _():
                copy(n, place, offset, half).start()

            @pl.when(jnp.logical_not(filled))
            def _():
                out_refs[n][place] = jnp.zeros_like(out_refs[n][place])

    def finish():
        for n, place, offset, half in halves:
            if full:
                copy(n, place, offset, half).wait()
            else:
                pl.when(rows[offset, half // 2][1])(copy(n, place, offset, half).wait)

    return finish


def start_queries(query_ref, out_refs, offsets, sem):
    section = lax.axis_index("sec")
    copies = []
    for n, (offset, out_ref) in enumerate(zip(offsets, out_refs)):
        width = out_ref.shape[2]
        columns = pl.ds(pl.multiple_of(lax.axis_index("tp") * width, width) if offset > 1 else 0, width)
        part = query_ref.at[0, pl.ds((section ^ offset) * CAP, CAP), :, columns]
        copies.append(pltpu.make_async_copy(part, out_ref, sem.at[n]))
        copies[-1].start()
    return copies


def query_shapes(queries, offsets, tp_count):
    samples, width = queries.shape[2:]
    widths = [width if offset < 2 else width // tp_count for offset in offsets]
    return [jax.ShapeDtypeStruct((CAP, samples, one), queries.dtype) for one in widths]


def head_kernel(piece, offsets, full, routing_ref, cache_ref, query_ref, *refs):
    out_ref, query_out, (routed, held, routing_sem, sem, query_sem) = refs[0], refs[1:-5], refs[-5:]
    offset, half, _ = piece
    section = lax.axis_index("sec")
    copies = [pltpu.make_async_copy(routing_ref, routed, routing_sem)]
    for i in range(REQ_GRP):
        copies.append(pltpu.make_async_copy(cache_ref.at[i, half % 2], held.at[i], sem.at[i]))
    for copy in copies:
        copy.start()
    query_copies = start_queries(query_ref, query_out, offsets, query_sem)
    copies[0].wait()
    row, filled = slot_row(own_targets(routed, section), section ^ offset, half // 2)
    for copy in copies[1:] + query_copies:
        copy.wait()
    chosen = held[row]
    out_ref[0] = chosen if full else jnp.where(filled, chosen, jnp.zeros_like(chosen))


def pack_head(routing, cache, queries, piece, section_count, tp_count):
    shape = cache.shape[2:]
    offsets = range(2, section_count)
    shapes = [jax.ShapeDtypeStruct((1,) + shape, cache.dtype)] + query_shapes(queries, offsets, tp_count)
    head, *parts = pl.pallas_call(
        functools.partial(head_kernel, piece, offsets, section_count * CAP == REQ_GRP),
        out_shape=shapes,
        in_specs=[HBM, HBM, HBM],
        out_specs=[VMEM] * len(shapes),
        scratch_shapes=[
            pltpu.SMEM(routing.shape, jnp.int32),
            pltpu.VMEM((REQ_GRP,) + shape, cache.dtype),
            pltpu.SemaphoreType.DMA,
            pltpu.SemaphoreType.DMA((REQ_GRP,)),
            pltpu.SemaphoreType.DMA((section_count,)),
        ],
        compiler_params=limit(16),
        cost_estimate=cost(0, cache.size),
        name="pack_head",
    )(in_hbm(routing), in_hbm(cache), in_hbm(queries))
    return [head], parts


def first_pack_kernel(pieces, section_count, routing_ref, cache_ref, query_ref, *refs):
    refs, (sem, query_sem) = refs[:-2], refs[-2:]
    query_out, cache_out = refs[-2:], refs[-2 - len(pieces) : -2]
    query_copies = start_queries(query_ref, query_out, range(2), query_sem)
    start_packing(pieces, section_count, routing_ref, cache_ref, cache_out, sem)()
    for copy in query_copies:
        copy.wait()


def pack_kernel(pieces, section_count, routing_ref, cache_ref, *refs):
    cache_out, sem = refs[-1 - len(pieces) : -1], refs[-1]
    start_packing(pieces, section_count, routing_ref, cache_ref, cache_out, sem)()


def merge_kernel(count, *refs):
    for n in range(count):
        refs[-1][n] = refs[n][...]


def merge(parts, others):
    shape = (len(parts),) + parts[0].shape
    return pl.pallas_call(
        functools.partial(merge_kernel, len(parts)),
        out_shape=jax.ShapeDtypeStruct(shape, parts[0].dtype),
        in_specs=[VMEM] * len(parts) + [ANY] * len(others),
        out_specs=VMEM,
        compiler_params=limit(8),
        cost_estimate=cost(3 * 10**9, 8 * len(parts) * parts[0].size),
        name="merge",
    )(*parts, *others)


def in_hbm(value):
    return pltpu.with_memory_space_constraint(value, pltpu.HBM)


def first_pack(routing, cache, queries, others, pieces, section_count):
    shapes = [jax.ShapeDtypeStruct((count,) + cache.shape[2:], cache.dtype) for _, _, count in pieces]
    shapes += query_shapes(queries, range(2), 1)
    parts = pl.pallas_call(
        functools.partial(first_pack_kernel, pieces, section_count),
        out_shape=shapes,
        in_specs=[SMEM, HBM, HBM] + [ANY] * len(others),
        out_specs=[VMEM] * len(shapes),
        scratch_shapes=[
            pltpu.SemaphoreType.DMA((section_count * CAP * 2,)),
            pltpu.SemaphoreType.DMA((2,)),
        ],
        compiler_params=limit(16),
        cost_estimate=cost(0, 4 * sum(shape.size for shape in shapes)),
        name="first_pack",
    )(routing, in_hbm(cache), in_hbm(queries), *others)
    return parts[: len(pieces)], parts[len(pieces) :]


def pack(routing, cache, others, pieces, section_count, flops=0):
    shapes = [jax.ShapeDtypeStruct((count,) + cache.shape[2:], cache.dtype) for _, _, count in pieces]
    return pl.pallas_call(
        functools.partial(pack_kernel, pieces, section_count),
        out_shape=shapes,
        in_specs=[SMEM, HBM] + [ANY] * len(others),
        out_specs=[VMEM] * len(shapes),
        scratch_shapes=[
            pltpu.SemaphoreType.DMA((section_count * CAP * 2,)),
        ],
        compiler_params=limit(16),
        cost_estimate=cost(flops, 4 * sum(shape.size for shape in shapes)),
        name="pack",
    )(routing, in_hbm(cache), *others)


def place_kernel(pieces, *refs):
    count = len(pieces)
    part_refs, out_ref, sem = refs[-2 - count : -2], refs[-2], refs[-1]
    section = lax.axis_index("sec")
    copies = []
    for n, (offset, first, size) in enumerate(pieces):
        for place in range(size):
            half = out_ref.at[0, (section ^ offset) * 2 * CAP + first + place]
            copies.append(pltpu.make_async_copy(part_refs[n].at[place], half, sem.at[len(copies)]))
            copies[-1].start()
    for copy in copies:
        copy.wait()


def place(given, parts, pieces, slot_count):
    part = parts[0]
    return pl.pallas_call(
        functools.partial(place_kernel, pieces),
        out_shape=jax.ShapeDtypeStruct((1, 2 * slot_count) + part.shape[1:], part.dtype),
        in_specs=[HBM] * len(given) + [VMEM] * len(parts),
        out_specs=HBM,
        scratch_shapes=[pltpu.SemaphoreType.DMA((sum(len(part) for part in parts),))],
        input_output_aliases={0: 0} if given else {},
        compiler_params=limit(8),
        cost_estimate=cost(0, 4 * sum(piece.size for piece in parts)),
        name="place",
    )(*[in_hbm(value) for value in given], *parts)


def attend_kernel(pieces, section_count, tp_count, routing_ref, lengths_ref, *refs):
    cache_refs, refs = refs[: len(pieces)], refs[len(pieces) :]
    query_refs, far_refs = refs[:2], refs[2 : 2 + tp_count]
    message_refs = refs[2 + tp_count : 2 + 2 * tp_count]
    messages, stats, stacked, far_queries = refs[2 + 2 * tp_count :]
    section = lax.axis_index("sec")
    tp_index = lax.axis_index("tp")
    local = cache_refs[0].shape[1]
    groups, rows, _ = messages.shape[1:]
    span = KEY_VALUE_HEADS * rows
    prompts = max(1, groups // KEY_VALUE_HEADS)
    full = section_count * CAP == REQ_GRP
    targets = own_targets(routing_ref, section)
    samples = query_refs[0].shape[1]
    for offset, far_ref in enumerate(far_refs):
        far_queries[tp_index ^ offset] = far_ref[...]
    position = lax.broadcasted_iota(jnp.int32, (local, span), 0) + tp_index * local
    owner = lax.broadcasted_iota(jnp.int32, (HEAD_SIZE, span), 1) // rows

    held = {(offset, half): cache_refs[n].at[place] for n, place, offset, half in halves_of(pieces)}

    def prompt(offset, order):
        keys_ref, values_ref = held[offset, 2 * order], held[offset, 2 * order + 1]
        row, _ = slot_row(targets, section ^ offset, order)
        visible = position < lengths_ref[section * REQ_GRP + row]
        slot = offset * CAP + order
        for head in range(span // samples):
            first, part = head * HEAD_SIZE, far_queries.shape[-1]
            if offset < 2:
                values = query_refs[offset][order, :, first : first + HEAD_SIZE]
            else:
                inner = first % part
                values = far_queries[first // part, offset - 2, order, :, inner : inner + HEAD_SIZE]
            stacked[slot, head * samples : (head + 1) * samples] = values.astype(jnp.float32)
        query = stacked[slot].T.astype(jnp.bfloat16)
        query = [jnp.where(owner == k, query, jnp.zeros_like(query)) for k in range(KEY_VALUE_HEADS)]
        score = jnp.dot(
            keys_ref[...], jnp.concatenate(query, axis=0), preferred_element_type=jnp.float32
        ) * HEAD_SIZE ** (-0.5)
        score = jnp.where(visible, score, HIDDEN)
        peak = jnp.max(score, axis=0, keepdims=True)
        weight = jnp.where(visible, jnp.exp(score - peak), 0.0)
        total = jnp.sum(weight, axis=0, keepdims=True)
        some = total > 0.0
        safe = jnp.where(some, total, 1.0)
        stats[0, pl.ds(row, 1)] = jnp.where(some, peak + jnp.log(safe), HIDDEN)
        weight = (weight * (1.0 / safe)).T.astype(jnp.bfloat16)
        for k in range(KEY_VALUE_HEADS):
            mixed = jnp.dot(
                weight[k * rows : (k + 1) * rows],
                values_ref[:, k * HEAD_SIZE : (k + 1) * HEAD_SIZE],
                preferred_element_type=jnp.float32,
            )
            group = row * KEY_VALUE_HEADS + k
            messages[group // groups, group % groups] = mixed.astype(jnp.bfloat16)

    for offset, half in held:
        if half % 2 == 0:
            one = functools.partial(prompt, offset, half // 2)
            if full:
                one()
            else:
                pl.when(slot_row(targets, section ^ offset, half // 2)[1])(one)

    level = stats[0]
    high = level.astype(jnp.bfloat16).astype(jnp.float32)
    rest = level - high
    middle = rest.astype(jnp.bfloat16).astype(jnp.float32)
    stats[0], stats[1], stats[2] = high, middle, rest - middle
    for offset, message_ref in enumerate(message_refs):
        device = tp_index ^ offset
        for inner in range(groups):
            message_ref[inner * rows : (inner + 1) * rows] = messages[device, inner]
        first = device * groups // KEY_VALUE_HEADS
        lines = [stats[part, pl.ds(first + n, 1)] for part in range(3) for n in range(prompts)]
        lines.append(jnp.zeros((STAT_ROWS - 3 * prompts, span), jnp.float32))
        message_ref[groups * rows :] = jnp.concatenate(lines, axis=0).astype(jnp.bfloat16)


def attend(routing, lengths, caches, pieces, queries, far_queries):
    section_count = len(far_queries[0]) + 2
    tp_count = len(far_queries)
    samples, width = queries[0].shape[1:]
    span = width // HEAD_SIZE * samples
    rows = span // KEY_VALUE_HEADS
    groups = REQ_GRP * KEY_VALUE_HEADS // tp_count
    multiplies = REQ_GRP * span * HEAD_SIZE * caches[0].shape[1]
    return pl.pallas_call(
        functools.partial(attend_kernel, pieces, section_count, tp_count),
        out_shape=[jax.ShapeDtypeStruct((groups * rows + STAT_ROWS, HEAD_SIZE), jnp.bfloat16)] * tp_count,
        in_specs=[SMEM, SMEM] + [VMEM] * (len(caches) + len(queries) + tp_count),
        out_specs=[VMEM] * tp_count,
        scratch_shapes=[
            pltpu.VMEM((tp_count, groups, rows, HEAD_SIZE), jnp.bfloat16),
            pltpu.VMEM((3, REQ_GRP, span), jnp.float32),
            pltpu.VMEM((section_count * CAP, span, HEAD_SIZE), jnp.float32),
            pltpu.VMEM((tp_count,) + far_queries[0].shape, far_queries[0].dtype),
        ],
        compiler_params=limit(12),
        cost_estimate=cost(2 * 10**10, 2 * sum(part.size for part in caches), multiplies // HEAD_SIZE),
        name="attend",
    )(routing, lengths, *caches, *queries, *far_queries)


def join_kernel(count, samples, rows, *refs):
    message_refs, (out_ref, scaling, flat) = refs[:count], refs[-3:]
    groups = (message_refs[0].shape[0] - STAT_ROWS) // rows
    prompts = max(1, groups // KEY_VALUE_HEADS)
    heads = rows // samples
    tp_index = lax.axis_index("tp")
    levels = []
    for ref in message_refs:
        lines = ref[groups * rows :].astype(jnp.float32)[0:8]
        levels.append(lines + pltpu.roll(lines, 8 - prompts, 0) + pltpu.roll(lines, 8 - 2 * prompts, 0))
    summit = functools.reduce(jnp.maximum, levels)
    scales = [jnp.exp(level - summit) for level in levels]
    total = functools.reduce(jnp.add, scales)
    for n, scale in enumerate(scales):
        scaling[n] = (scale / total).T
    for inner in range(groups):
        if groups % KEY_VALUE_HEADS:
            first = (tp_index * groups + inner) % KEY_VALUE_HEADS * rows
            part = pl.ds(pl.multiple_of(first, rows), rows)
        else:
            part = pl.ds(inner % KEY_VALUE_HEADS * rows, rows)
        prompt = inner // KEY_VALUE_HEADS
        terms = [
            ref[inner * rows : (inner + 1) * rows].astype(jnp.float32) * scaling[n, part, prompt : prompt + 1]
            for n, ref in enumerate(message_refs)
        ]
        joined = functools.reduce(jnp.add, terms)
        for head in range(heads):
            block = joined[head * samples : (head + 1) * samples]
            if len(flat.shape) == 2:
                row = prompt * samples
                column = (inner % KEY_VALUE_HEADS * heads + head) * HEAD_SIZE
                flat[row : row + samples, column : column + HEAD_SIZE] = block
            else:
                flat[inner, :, head * HEAD_SIZE : (head + 1) * HEAD_SIZE] = block
    out_ref[...] = flat[...].astype(jnp.bfloat16)


def join(messages, others, samples, heads):
    rows = heads * samples
    groups = (messages[0].shape[0] - STAT_ROWS) // rows
    width = rows // samples * HEAD_SIZE
    if groups % KEY_VALUE_HEADS == 0:
        shape = (groups // KEY_VALUE_HEADS * samples, KEY_VALUE_HEADS * width)
    else:
        shape = (groups, samples, width)
    count = len(messages)
    return pl.pallas_call(
        functools.partial(join_kernel, count, samples, rows),
        out_shape=jax.ShapeDtypeStruct(shape, jnp.bfloat16),
        in_specs=[VMEM] * count + [ANY] * len(others),
        out_specs=VMEM,
        scratch_shapes=[
            pltpu.VMEM((count, KEY_VALUE_HEADS * rows, 8), jnp.float32),
            pltpu.VMEM(shape, jnp.float32),
        ],
        compiler_params=limit(8),
        cost_estimate=cost(4 * count * messages[0].size, 2 * count * messages[0].size),
        name="join",
    )(*messages, *others)


def fetch_kernel(first, weight_ref, *refs):
    out_ref, sem = refs[-2:]
    copies = []
    step = out_ref.shape[0] // sem.shape[0]
    for n in range(sem.shape[0]):
        rows = weight_ref.at[pl.ds(first + n * step, step)]
        copies.append(pltpu.make_async_copy(rows, out_ref.at[pl.ds(n * step, step)], sem.at[n]))
        copies[-1].start()
    for copy in copies:
        copy.wait()


def fetch(weight, others, number, count):
    size = weight.shape[0] // count
    return pl.pallas_call(
        functools.partial(fetch_kernel, number * size),
        out_shape=jax.ShapeDtypeStruct((size,) + weight.shape[1:], weight.dtype),
        in_specs=[HBM] + [ANY] * len(others),
        out_specs=VMEM,
        scratch_shapes=[pltpu.SemaphoreType.DMA((8,))],
        compiler_params=limit(24),
        cost_estimate=cost(0, 4 * weight.size // count),
        name="fetch",
    )(in_hbm(weight), *others)


def project_kernel(count, tile, skipped, *refs):
    refs = refs[skipped:]
    part_refs, weight_refs, out_ref = refs[:count], refs[count:-1], refs[-1]
    tp_index = lax.axis_index("tp")
    prompts, samples, width = out_ref.shape
    share = prompts // count
    left = jnp.concatenate([ref[...].astype(jnp.float32) for ref in part_refs], axis=0).astype(jnp.bfloat16)
    size = weight_refs[0].shape[0]
    for first in range(0, width, tile):
        result = functools.reduce(
            jnp.add,
            [
                jnp.dot(
                    left[:, n * size : (n + 1) * size],
                    ref[:, first : first + tile],
                    preferred_element_type=jnp.float32,
                )
                for n, ref in enumerate(weight_refs)
            ],
        )
        for offset in range(count):
            for n in range(share):
                row = (offset * share + n) * samples
                block = result[row : row + samples].astype(out_ref.dtype)
                out_ref[(tp_index ^ offset) * share + n, :, first : first + tile] = block


def project(parts, weights, others, samples):
    count = len(parts)
    depth, width = weights[0].shape
    depth *= len(weights)
    total = count * parts[0].shape[0]
    return pl.pallas_call(
        functools.partial(project_kernel, count, min(256, width), len(others)),
        out_shape=jax.ShapeDtypeStruct((total // samples, samples, width), jnp.bfloat16),
        in_specs=[ANY] * len(others) + [VMEM] * (count + len(weights)),
        out_specs=VMEM,
        compiler_params=limit(24),
        cost_estimate=cost(2 * total * depth * width, 2 * depth * width),
        name="project",
    )(*others, *parts, *weights)


def body(prompt_key_values, queries, routing, lengths, out_weight):
    section_count = lax.axis_size("sec")
    tp_count = lax.axis_size("tp")
    slot_count, samples, query_width = queries.shape[1:]
    routing = routing.reshape(-1)

    whole = 2 * CAP
    near = [(offset, 0, whole) for offset in range(2)]
    head, tail = [(2, 0, 1)], [(2, 1, whole - 1)]
    far = tail + [(offset, 0, whole) for offset in range(3, section_count)]

    def across(parts, pieces):
        return [swap(part, "sec", piece[0]) for part, piece in zip(parts, pieces)]

    head_caches, far_queries = pack_head(
        routing, prompt_key_values, queries, head[0], section_count, tp_count
    )
    head_parts = across(head_caches, head)
    far_queries = [swap(part, "sec", n + 2) for n, part in enumerate(far_queries)]
    far_caches, query_parts = first_pack(
        routing, prompt_key_values, queries, head_caches, far, section_count
    )
    far_parts = across(far_caches, far)
    query_parts = [swap(part, "sec", offset) for offset, part in enumerate(query_parts)]
    merged = merge(far_queries, head_parts)
    far_queries = spread(merged, "tp")
    near_caches = pack(routing, prompt_key_values, [merged, query_parts[1]], near, section_count, 10**10)
    near_parts = across(near_caches, near)
    caches, pieces = [*head_caches, *far_caches, *near_caches], head + far + near

    messages = attend(routing, lengths, caches, pieces, query_parts, far_queries)
    partials = [swap(part, "tp", offset) for offset, part in enumerate(messages)]
    held_weight = [fetch(out_weight, [messages[0], *near_parts[1:]], 0, 2)]
    held_cache = place([], near_parts + head_parts, near + head, slot_count)
    share = join(partials, [*held_weight, held_cache], samples, query_width // HEAD_SIZE // KEY_VALUE_HEADS)
    shares = spread(share, "tp")
    held_weight.append(fetch(out_weight, [share], 1, 2))
    if share.ndim == 3:
        attended = jnp.stack(shares)[jnp.arange(tp_count) ^ lax.axis_index("tp")]
        attended = attended.reshape(REQ_GRP, KEY_VALUE_HEADS, samples, -1).transpose(0, 2, 1, 3)
        attended = attended.reshape(REQ_GRP * samples, query_width)
        layer_out = jnp.dot(attended, out_weight, preferred_element_type=jnp.float32)
        layer_out = layer_out.astype(jnp.bfloat16).reshape(REQ_GRP, samples, -1)
    else:
        layer_out = project(shares, held_weight, far_parts[:-1], samples)

    held_cache = place([held_cache, share], far_parts[:-1], far[:-1], slot_count)
    held_cache = place([held_cache, layer_out], far_parts[-1:], far[-1:], slot_count)
    held_cache = held_cache.reshape((1, slot_count) + prompt_key_values.shape[1:])
    return (layer_out, held_cache)


def solution(mesh):
    placed = (
        P(("rep", "sec"), None, "tp", None),
        P(("rep", "sec"), None, None, None),
        P("rep", None),
        P("rep"),
        P(None, "tp"),
    )
    return jax.shard_map(
        body,
        mesh=mesh,
        in_specs=placed,
        out_specs=(P(("rep", "sec"), None, "tp"), P(("rep", "sec"), None, None, "tp", None)),
        check_vma=False,
    )
```

```python
import functools

import jax
import jax.numpy as jnp
from jax import lax
from jax.experimental import pallas as pl
from jax.experimental.pallas import tpu as pltpu
from jax.sharding import PartitionSpec as P

HEAD_SIZE = 128
KEY_VALUE_HEADS = 4
REQ_GRP = 8
CAP = 2
HIDDEN = -1e30
STAT_ROWS = 16

ANY = pl.BlockSpec(memory_space=pl.ANY)
HBM = pl.BlockSpec(memory_space=pltpu.HBM)
VMEM = pl.BlockSpec(memory_space=pltpu.VMEM)
SMEM = pl.BlockSpec(memory_space=pltpu.SMEM)


def limit(mebibytes):
    return pltpu.CompilerParams(vmem_limit_bytes=mebibytes << 20)


def cost(flops, bytes_accessed, transcendentals=0):
    return pl.CostEstimate(flops=flops, bytes_accessed=bytes_accessed, transcendentals=transcendentals)


def swap(value, axis, offset):
    if offset == 0:
        return value
    count = lax.axis_size(axis)
    return lax.ppermute(value, axis, [(i, i ^ offset) for i in range(count)])


def spread(value, axis):
    return [swap(value, axis, offset) for offset in range(lax.axis_size(axis))]


def own_targets(routing_ref, section):
    return [routing_ref[section * REQ_GRP + i] for i in range(REQ_GRP)]


def slot_row(targets, group, order):
    row, before = jnp.int32(0), jnp.int32(0)
    for i, target in enumerate(targets):
        here = target == group
        row = jnp.where(here & (before == order), i, row)
        before = before + here.astype(jnp.int32)
    return row, before > order


def halves_of(pieces):
    return [
        (n, place, offset, first + place)
        for n, (offset, first, count) in enumerate(pieces)
        for place in range(count)
    ]


def start_packing(pieces, section_count, routing_ref, cache_ref, out_refs, sem):
    section = lax.axis_index("sec")
    full = section_count * CAP == REQ_GRP
    targets = own_targets(routing_ref, section)
    halves = halves_of(pieces)
    slots = {(offset, half // 2) for _, _, offset, half in halves}
    rows = {slot: slot_row(targets, section ^ slot[0], slot[1]) for slot in sorted(slots)}

    def copy(n, place, offset, half):
        row, _ = rows[offset, half // 2]
        return pltpu.make_async_copy(
            cache_ref.at[row, half % 2], out_refs[n].at[place], sem.at[offset * 2 * CAP + half]
        )

    for n, place, offset, half in halves:
        if full:
            copy(n, place, offset, half).start()
        else:
            _, filled = rows[offset, half // 2]

            @pl.when(filled)
            def _():
                copy(n, place, offset, half).start()

            @pl.when(jnp.logical_not(filled))
            def _():
                out_refs[n][place] = jnp.zeros_like(out_refs[n][place])

    def finish():
        for n, place, offset, half in halves:
            if full:
                copy(n, place, offset, half).wait()
            else:
                pl.when(rows[offset, half // 2][1])(copy(n, place, offset, half).wait)

    return finish


def start_queries(query_ref, out_refs, offsets, sem):
    section = lax.axis_index("sec")
    copies = []
    for n, (offset, out_ref) in enumerate(zip(offsets, out_refs)):
        width = out_ref.shape[2]
        columns = pl.ds(pl.multiple_of(lax.axis_index("tp") * width, width) if offset > 1 else 0, width)
        part = query_ref.at[0, pl.ds((section ^ offset) * CAP, CAP), :, columns]
        copies.append(pltpu.make_async_copy(part, out_ref, sem.at[n]))
        copies[-1].start()
    return copies


def query_shapes(queries, offsets, tp_count):
    samples, width = queries.shape[2:]
    widths = [width if offset < 2 else width // tp_count for offset in offsets]
    return [jax.ShapeDtypeStruct((CAP, samples, one), queries.dtype) for one in widths]


def head_kernel(piece, offsets, full, routing_ref, cache_ref, query_ref, *refs):
    out_ref, query_out, (routed, held, routing_sem, sem, query_sem) = refs[0], refs[1:-5], refs[-5:]
    offset, half, _ = piece
    section = lax.axis_index("sec")
    copies = [pltpu.make_async_copy(routing_ref, routed, routing_sem)]
    for i in range(REQ_GRP):
        copies.append(pltpu.make_async_copy(cache_ref.at[i, half % 2], held.at[i], sem.at[i]))
    for copy in copies:
        copy.start()
    query_copies = start_queries(query_ref, query_out, offsets, query_sem)
    copies[0].wait()
    row, filled = slot_row(own_targets(routed, section), section ^ offset, half // 2)
    for copy in copies[1:] + query_copies:
        copy.wait()
    chosen = held[row]
    out_ref[0] = chosen if full else jnp.where(filled, chosen, jnp.zeros_like(chosen))


def pack_head(routing, cache, queries, piece, section_count, tp_count):
    shape = cache.shape[2:]
    offsets = range(2, section_count)
    shapes = [jax.ShapeDtypeStruct((1,) + shape, cache.dtype)] + query_shapes(queries, offsets, tp_count)
    head, *parts = pl.pallas_call(
        functools.partial(head_kernel, piece, offsets, section_count * CAP == REQ_GRP),
        out_shape=shapes,
        in_specs=[HBM, HBM, HBM],
        out_specs=[VMEM] * len(shapes),
        scratch_shapes=[
            pltpu.SMEM(routing.shape, jnp.int32),
            pltpu.VMEM((REQ_GRP,) + shape, cache.dtype),
            pltpu.SemaphoreType.DMA,
            pltpu.SemaphoreType.DMA((REQ_GRP,)),
            pltpu.SemaphoreType.DMA((section_count,)),
        ],
        compiler_params=limit(16),
        cost_estimate=cost(0, cache.size),
        name="pack_head",
    )(in_hbm(routing), in_hbm(cache), in_hbm(queries))
    return [head], parts


def first_pack_kernel(pieces, section_count, routing_ref, cache_ref, query_ref, *refs):
    refs, (sem, query_sem) = refs[:-2], refs[-2:]
    query_out, cache_out = refs[-2:], refs[-2 - len(pieces) : -2]
    query_copies = start_queries(query_ref, query_out, range(2), query_sem)
    start_packing(pieces, section_count, routing_ref, cache_ref, cache_out, sem)()
    for copy in query_copies:
        copy.wait()


def pack_kernel(pieces, section_count, routing_ref, cache_ref, *refs):
    cache_out, sem = refs[-1 - len(pieces) : -1], refs[-1]
    start_packing(pieces, section_count, routing_ref, cache_ref, cache_out, sem)()


def merge_kernel(count, *refs):
    for n in range(count):
        refs[-1][n] = refs[n][...]


def merge(parts, others):
    shape = (len(parts),) + parts[0].shape
    return pl.pallas_call(
        functools.partial(merge_kernel, len(parts)),
        out_shape=jax.ShapeDtypeStruct(shape, parts[0].dtype),
        in_specs=[VMEM] * len(parts) + [ANY] * len(others),
        out_specs=VMEM,
        compiler_params=limit(8),
        cost_estimate=cost(3 * 10**9, 8 * len(parts) * parts[0].size),
        name="merge",
    )(*parts, *others)


def in_hbm(value):
    return pltpu.with_memory_space_constraint(value, pltpu.HBM)


def first_pack(routing, cache, queries, others, pieces, section_count):
    shapes = [jax.ShapeDtypeStruct((count,) + cache.shape[2:], cache.dtype) for _, _, count in pieces]
    shapes += query_shapes(queries, range(2), 1)
    parts = pl.pallas_call(
        functools.partial(first_pack_kernel, pieces, section_count),
        out_shape=shapes,
        in_specs=[SMEM, HBM, HBM] + [ANY] * len(others),
        out_specs=[VMEM] * len(shapes),
        scratch_shapes=[
            pltpu.SemaphoreType.DMA((section_count * CAP * 2,)),
            pltpu.SemaphoreType.DMA((2,)),
        ],
        compiler_params=limit(16),
        cost_estimate=cost(0, 4 * sum(shape.size for shape in shapes)),
        name="first_pack",
    )(routing, in_hbm(cache), in_hbm(queries), *others)
    return parts[: len(pieces)], parts[len(pieces) :]


def pack(routing, cache, others, pieces, section_count, flops=0):
    shapes = [jax.ShapeDtypeStruct((count,) + cache.shape[2:], cache.dtype) for _, _, count in pieces]
    return pl.pallas_call(
        functools.partial(pack_kernel, pieces, section_count),
        out_shape=shapes,
        in_specs=[SMEM, HBM] + [ANY] * len(others),
        out_specs=[VMEM] * len(shapes),
        scratch_shapes=[
            pltpu.SemaphoreType.DMA((section_count * CAP * 2,)),
        ],
        compiler_params=limit(16),
        cost_estimate=cost(flops, 4 * sum(shape.size for shape in shapes)),
        name="pack",
    )(routing, in_hbm(cache), *others)


def gate_kernel(*refs):
    pass


def gate(values, others):
    count = len(values)
    return pl.pallas_call(
        gate_kernel,
        out_shape=[jax.ShapeDtypeStruct(value.shape, value.dtype) for value in values],
        in_specs=[ANY] * (count + len(others)),
        out_specs=[ANY] * count,
        input_output_aliases={n: n for n in range(count)},
        compiler_params=limit(1),
        cost_estimate=cost(0, 0),
        name="gate",
    )(*values, *others)


def place_kernel(pieces, *refs):
    count = len(pieces)
    part_refs, out_ref, sem = refs[-2 - count : -2], refs[-2], refs[-1]
    section = lax.axis_index("sec")
    copies = []
    for n, (offset, first, size) in enumerate(pieces):
        for place in range(size):
            half = out_ref.at[0, (section ^ offset) * 2 * CAP + first + place]
            copies.append(pltpu.make_async_copy(part_refs[n].at[place], half, sem.at[len(copies)]))
            copies[-1].start()
    for copy in copies:
        copy.wait()


def place(given, parts, pieces, slot_count):
    part = parts[0]
    return pl.pallas_call(
        functools.partial(place_kernel, pieces),
        out_shape=jax.ShapeDtypeStruct((1, 2 * slot_count) + part.shape[1:], part.dtype),
        in_specs=[HBM] * len(given) + [VMEM] * len(parts),
        out_specs=HBM,
        scratch_shapes=[pltpu.SemaphoreType.DMA((sum(len(part) for part in parts),))],
        input_output_aliases={0: 0} if given else {},
        compiler_params=limit(8),
        cost_estimate=cost(0, 4 * sum(piece.size for piece in parts)),
        name="place",
    )(*[in_hbm(value) for value in given], *parts)


def attend_kernel(pieces, section_count, tp_count, routing_ref, lengths_ref, *refs):
    cache_refs, refs = refs[: len(pieces)], refs[len(pieces) :]
    query_refs, far_refs = refs[:2], refs[2 : 2 + tp_count]
    message_refs = refs[2 + tp_count : 2 + 2 * tp_count]
    messages, stats, stacked, far_queries = refs[2 + 2 * tp_count :]
    section = lax.axis_index("sec")
    tp_index = lax.axis_index("tp")
    local = cache_refs[0].shape[1]
    groups, rows, _ = messages.shape[1:]
    span = KEY_VALUE_HEADS * rows
    prompts = max(1, groups // KEY_VALUE_HEADS)
    full = section_count * CAP == REQ_GRP
    targets = own_targets(routing_ref, section)
    samples = query_refs[0].shape[1]
    for offset, far_ref in enumerate(far_refs):
        far_queries[tp_index ^ offset] = far_ref[...]
    position = lax.broadcasted_iota(jnp.int32, (local, span), 0) + tp_index * local
    owner = lax.broadcasted_iota(jnp.int32, (HEAD_SIZE, span), 1) // rows

    held = {(offset, half): cache_refs[n].at[place] for n, place, offset, half in halves_of(pieces)}

    def prompt(offset, order):
        keys_ref, values_ref = held[offset, 2 * order], held[offset, 2 * order + 1]
        row, _ = slot_row(targets, section ^ offset, order)
        visible = position < lengths_ref[section * REQ_GRP + row]
        slot = offset * CAP + order
        for head in range(span // samples):
            first, part = head * HEAD_SIZE, far_queries.shape[-1]
            if offset < 2:
                values = query_refs[offset][order, :, first : first + HEAD_SIZE]
            else:
                inner = first % part
                values = far_queries[first // part, offset - 2, order, :, inner : inner + HEAD_SIZE]
            stacked[slot, head * samples : (head + 1) * samples] = values.astype(jnp.float32)
        query = stacked[slot].T.astype(jnp.bfloat16)
        query = [jnp.where(owner == k, query, jnp.zeros_like(query)) for k in range(KEY_VALUE_HEADS)]
        score = jnp.dot(
            keys_ref[...], jnp.concatenate(query, axis=0), preferred_element_type=jnp.float32
        ) * HEAD_SIZE ** (-0.5)
        score = jnp.where(visible, score, HIDDEN)
        peak = jnp.max(score, axis=0, keepdims=True)
        weight = jnp.where(visible, jnp.exp(score - peak), 0.0)
        total = jnp.sum(weight, axis=0, keepdims=True)
        some = total > 0.0
        safe = jnp.where(some, total, 1.0)
        stats[0, pl.ds(row, 1)] = jnp.where(some, peak + jnp.log(safe), HIDDEN)
        weight = (weight * (1.0 / safe)).T.astype(jnp.bfloat16)
        for k in range(KEY_VALUE_HEADS):
            mixed = jnp.dot(
                weight[k * rows : (k + 1) * rows],
                values_ref[:, k * HEAD_SIZE : (k + 1) * HEAD_SIZE],
                preferred_element_type=jnp.float32,
            )
            group = row * KEY_VALUE_HEADS + k
            messages[group // groups, group % groups] = mixed.astype(jnp.bfloat16)

    for offset, half in held:
        if half % 2 == 0:
            one = functools.partial(prompt, offset, half // 2)
            if full:
                one()
            else:
                pl.when(slot_row(targets, section ^ offset, half // 2)[1])(one)

    level = stats[0]
    high = level.astype(jnp.bfloat16).astype(jnp.float32)
    rest = level - high
    middle = rest.astype(jnp.bfloat16).astype(jnp.float32)
    stats[0], stats[1], stats[2] = high, middle, rest - middle
    for offset, message_ref in enumerate(message_refs):
        device = tp_index ^ offset
        for inner in range(groups):
            message_ref[inner * rows : (inner + 1) * rows] = messages[device, inner]
        first = device * groups // KEY_VALUE_HEADS
        lines = [stats[part, pl.ds(first + n, 1)] for part in range(3) for n in range(prompts)]
        lines.append(jnp.zeros((STAT_ROWS - 3 * prompts, span), jnp.float32))
        message_ref[groups * rows :] = jnp.concatenate(lines, axis=0).astype(jnp.bfloat16)


def attend(routing, lengths, caches, pieces, queries, far_queries):
    section_count = len(far_queries[0]) + 2
    tp_count = len(far_queries)
    samples, width = queries[0].shape[1:]
    span = width // HEAD_SIZE * samples
    rows = span // KEY_VALUE_HEADS
    groups = REQ_GRP * KEY_VALUE_HEADS // tp_count
    multiplies = REQ_GRP * span * HEAD_SIZE * caches[0].shape[1]
    return pl.pallas_call(
        functools.partial(attend_kernel, pieces, section_count, tp_count),
        out_shape=[jax.ShapeDtypeStruct((groups * rows + STAT_ROWS, HEAD_SIZE), jnp.bfloat16)] * tp_count,
        in_specs=[SMEM, SMEM] + [VMEM] * (len(caches) + len(queries) + tp_count),
        out_specs=[VMEM] * tp_count,
        scratch_shapes=[
            pltpu.VMEM((tp_count, groups, rows, HEAD_SIZE), jnp.bfloat16),
            pltpu.VMEM((3, REQ_GRP, span), jnp.float32),
            pltpu.VMEM((section_count * CAP, span, HEAD_SIZE), jnp.float32),
            pltpu.VMEM((tp_count,) + far_queries[0].shape, far_queries[0].dtype),
        ],
        compiler_params=limit(12),
        cost_estimate=cost(2 * 10**10, 2 * sum(part.size for part in caches), multiplies // HEAD_SIZE),
        name="attend",
    )(routing, lengths, *caches, *queries, *far_queries)


def join_kernel(count, samples, rows, *refs):
    message_refs, (out_ref, scaling, flat) = refs[:count], refs[-3:]
    groups = (message_refs[0].shape[0] - STAT_ROWS) // rows
    prompts = max(1, groups // KEY_VALUE_HEADS)
    heads = rows // samples
    tp_index = lax.axis_index("tp")
    levels = []
    for ref in message_refs:
        lines = ref[groups * rows :].astype(jnp.float32)[0:8]
        levels.append(lines + pltpu.roll(lines, 8 - prompts, 0) + pltpu.roll(lines, 8 - 2 * prompts, 0))
    summit = functools.reduce(jnp.maximum, levels)
    scales = [jnp.exp(level - summit) for level in levels]
    total = functools.reduce(jnp.add, scales)
    for n, scale in enumerate(scales):
        scaling[n] = (scale / total).T
    for inner in range(groups):
        if groups % KEY_VALUE_HEADS:
            first = (tp_index * groups + inner) % KEY_VALUE_HEADS * rows
            part = pl.ds(pl.multiple_of(first, rows), rows)
        else:
            part = pl.ds(inner % KEY_VALUE_HEADS * rows, rows)
        prompt = inner // KEY_VALUE_HEADS
        terms = [
            ref[inner * rows : (inner + 1) * rows].astype(jnp.float32) * scaling[n, part, prompt : prompt + 1]
            for n, ref in enumerate(message_refs)
        ]
        joined = functools.reduce(jnp.add, terms)
        for head in range(heads):
            block = joined[head * samples : (head + 1) * samples]
            if len(flat.shape) == 2:
                row = prompt * samples
                column = (inner % KEY_VALUE_HEADS * heads + head) * HEAD_SIZE
                flat[row : row + samples, column : column + HEAD_SIZE] = block
            else:
                flat[inner, :, head * HEAD_SIZE : (head + 1) * HEAD_SIZE] = block
    out_ref[...] = flat[...].astype(jnp.bfloat16)


def join(messages, others, samples, heads):
    rows = heads * samples
    groups = (messages[0].shape[0] - STAT_ROWS) // rows
    width = rows // samples * HEAD_SIZE
    if groups % KEY_VALUE_HEADS == 0:
        shape = (groups // KEY_VALUE_HEADS * samples, KEY_VALUE_HEADS * width)
    else:
        shape = (groups, samples, width)
    count = len(messages)
    return pl.pallas_call(
        functools.partial(join_kernel, count, samples, rows),
        out_shape=jax.ShapeDtypeStruct(shape, jnp.bfloat16),
        in_specs=[VMEM] * count + [ANY] * len(others),
        out_specs=VMEM,
        scratch_shapes=[
            pltpu.VMEM((count, KEY_VALUE_HEADS * rows, 8), jnp.float32),
            pltpu.VMEM(shape, jnp.float32),
        ],
        compiler_params=limit(8),
        cost_estimate=cost(4 * count * messages[0].size, 2 * count * messages[0].size),
        name="join",
    )(*messages, *others)


def fetch_kernel(first, weight_ref, *refs):
    out_ref, sem = refs[-2:]
    copies = []
    step = out_ref.shape[0] // sem.shape[0]
    for n in range(sem.shape[0]):
        rows = weight_ref.at[pl.ds(first + n * step, step)]
        copies.append(pltpu.make_async_copy(rows, out_ref.at[pl.ds(n * step, step)], sem.at[n]))
        copies[-1].start()
    for copy in copies:
        copy.wait()


def fetch(weight, others, number, count):
    size = weight.shape[0] // count
    return pl.pallas_call(
        functools.partial(fetch_kernel, number * size),
        out_shape=jax.ShapeDtypeStruct((size,) + weight.shape[1:], weight.dtype),
        in_specs=[HBM] + [ANY] * len(others),
        out_specs=VMEM,
        scratch_shapes=[pltpu.SemaphoreType.DMA((8,))],
        compiler_params=limit(24),
        cost_estimate=cost(0, 4 * weight.size // count),
        name="fetch",
    )(in_hbm(weight), *others)


def project_kernel(count, tile, skipped, *refs):
    refs = refs[skipped:]
    part_refs, weight_refs, out_ref = refs[:count], refs[count:-1], refs[-1]
    tp_index = lax.axis_index("tp")
    prompts, samples, width = out_ref.shape
    share = prompts // count
    left = jnp.concatenate([ref[...].astype(jnp.float32) for ref in part_refs], axis=0).astype(jnp.bfloat16)
    size = weight_refs[0].shape[0]
    for first in range(0, width, tile):
        result = functools.reduce(
            jnp.add,
            [
                jnp.dot(
                    left[:, n * size : (n + 1) * size],
                    ref[:, first : first + tile],
                    preferred_element_type=jnp.float32,
                )
                for n, ref in enumerate(weight_refs)
            ],
        )
        for offset in range(count):
            for n in range(share):
                row = (offset * share + n) * samples
                block = result[row : row + samples].astype(out_ref.dtype)
                out_ref[(tp_index ^ offset) * share + n, :, first : first + tile] = block


def project(parts, weights, others, samples):
    count = len(parts)
    depth, width = weights[0].shape
    depth *= len(weights)
    total = count * parts[0].shape[0]
    return pl.pallas_call(
        functools.partial(project_kernel, count, min(256, width), len(others)),
        out_shape=jax.ShapeDtypeStruct((total // samples, samples, width), jnp.bfloat16),
        in_specs=[ANY] * len(others) + [VMEM] * (count + len(weights)),
        out_specs=VMEM,
        compiler_params=limit(24),
        cost_estimate=cost(2 * total * depth * width, 2 * depth * width),
        name="project",
    )(*others, *parts, *weights)


def body(prompt_key_values, queries, routing, lengths, out_weight):
    section_count = lax.axis_size("sec")
    tp_count = lax.axis_size("tp")
    slot_count, samples, query_width = queries.shape[1:]
    routing = routing.reshape(-1)

    whole = 2 * CAP
    near = [(offset, 0, whole) for offset in range(2)]
    head, tail = [(2, 0, 1)], [(2, 1, whole - 1)]
    far = tail + [(offset, 0, whole) for offset in range(3, section_count - 1)]
    far += [(section_count - 1, 0, whole - 1), (section_count - 1, whole - 1, 1)]

    def across(parts, pieces):
        return [swap(part, "sec", piece[0]) for part, piece in zip(parts, pieces)]

    head_caches, far_queries = pack_head(
        routing, prompt_key_values, queries, head[0], section_count, tp_count
    )
    head_parts = across(head_caches, head)
    far_queries = [swap(part, "sec", n + 2) for n, part in enumerate(far_queries)]
    far_caches, query_parts = first_pack(
        routing, prompt_key_values, queries, head_caches, far, section_count
    )
    far_parts = across(far_caches[:-1], far[:-1])
    query_parts = [swap(part, "sec", offset) for offset, part in enumerate(query_parts)]
    merged = merge(far_queries, head_parts)
    far_queries = spread(merged, "tp")
    near_caches = pack(routing, prompt_key_values, [merged, query_parts[1]], near, section_count, 10**10)
    near_parts = across(near_caches, near)
    caches, pieces = [*head_caches, *far_caches, *near_caches], head + far + near

    messages = attend(routing, lengths, caches, pieces, query_parts, far_queries)
    partials = [swap(part, "tp", offset) for offset, part in enumerate(messages)]
    held_weight = [fetch(out_weight, [messages[0], *near_parts[1:]], 0, 2)]
    held_cache = place([], near_parts + head_parts, near + head, slot_count)
    share = join(partials, [*held_weight, held_cache, *far_parts[:-1]], samples, query_width // HEAD_SIZE // KEY_VALUE_HEADS)
    far_parts += across(gate(far_caches[-1:], [share]), far[-1:])
    shares = spread(share, "tp")
    held_weight.append(fetch(out_weight, [share], 1, 2))
    if share.ndim == 3:
        attended = jnp.stack(shares)[jnp.arange(tp_count) ^ lax.axis_index("tp")]
        attended = attended.reshape(REQ_GRP, KEY_VALUE_HEADS, samples, -1).transpose(0, 2, 1, 3)
        attended = attended.reshape(REQ_GRP * samples, query_width)
        layer_out = jnp.dot(attended, out_weight, preferred_element_type=jnp.float32)
        layer_out = layer_out.astype(jnp.bfloat16).reshape(REQ_GRP, samples, -1)
    else:
        layer_out = project(shares, held_weight, far_parts[:-2], samples)

    held_cache = place([held_cache, share], far_parts[:-2], far[:-2], slot_count)
    for part, piece in zip(far_parts[-2:], far[-2:]):
        held_cache = place([held_cache, layer_out], [part], [piece], slot_count)
    held_cache = held_cache.reshape((1, slot_count) + prompt_key_values.shape[1:])
    return (layer_out, held_cache)


def solution(mesh):
    placed = (
        P(("rep", "sec"), None, "tp", None),
        P(("rep", "sec"), None, None, None),
        P("rep", None),
        P("rep"),
        P(None, "tp"),
    )
    return jax.shard_map(
        body,
        mesh=mesh,
        in_specs=placed,
        out_specs=(P(("rep", "sec"), None, "tp"), P(("rep", "sec"), None, None, "tp", None)),
        check_vma=False,
    )
```

```python
import functools

import jax
import jax.numpy as jnp
from jax import lax
from jax.experimental import pallas as pl
from jax.experimental.pallas import tpu as pltpu
from jax.sharding import PartitionSpec as P

HEAD_SIZE = 128
KEY_VALUE_HEADS = 4
REQ_GRP = 8
CAP = 2
HIDDEN = -1e30
STAT_ROWS = 16

ANY = pl.BlockSpec(memory_space=pl.ANY)
HBM = pl.BlockSpec(memory_space=pltpu.HBM)
VMEM = pl.BlockSpec(memory_space=pltpu.VMEM)
SMEM = pl.BlockSpec(memory_space=pltpu.SMEM)


def limit(mebibytes):
    return pltpu.CompilerParams(vmem_limit_bytes=mebibytes << 20)


def cost(flops, bytes_accessed, transcendentals=0):
    return pl.CostEstimate(flops=flops, bytes_accessed=bytes_accessed, transcendentals=transcendentals)


def swap(value, axis, offset):
    if offset == 0:
        return value
    count = lax.axis_size(axis)
    return lax.ppermute(value, axis, [(i, i ^ offset) for i in range(count)])


def spread(value, axis):
    return [swap(value, axis, offset) for offset in range(lax.axis_size(axis))]


def own_targets(routing_ref, section):
    return [routing_ref[section * REQ_GRP + i] for i in range(REQ_GRP)]


def slot_row(targets, group, order):
    row, before = jnp.int32(0), jnp.int32(0)
    for i, target in enumerate(targets):
        here = target == group
        row = jnp.where(here & (before == order), i, row)
        before = before + here.astype(jnp.int32)
    return row, before > order


def halves_of(pieces):
    return [
        (n, place, offset, first + place)
        for n, (offset, first, count) in enumerate(pieces)
        for place in range(count)
    ]


def start_packing(pieces, section_count, routing_ref, cache_ref, out_refs, sem):
    section = lax.axis_index("sec")
    full = section_count * CAP == REQ_GRP
    targets = own_targets(routing_ref, section)
    halves = halves_of(pieces)
    slots = {(offset, half // 2) for _, _, offset, half in halves}
    rows = {slot: slot_row(targets, section ^ slot[0], slot[1]) for slot in sorted(slots)}

    def copy(n, place, offset, half):
        row, _ = rows[offset, half // 2]
        return pltpu.make_async_copy(
            cache_ref.at[row, half % 2], out_refs[n].at[place], sem.at[offset * 2 * CAP + half]
        )

    for n, place, offset, half in halves:
        if full:
            copy(n, place, offset, half).start()
        else:
            _, filled = rows[offset, half // 2]

            @pl.when(filled)
            def _():
                copy(n, place, offset, half).start()

            @pl.when(jnp.logical_not(filled))
            def _():
                out_refs[n][place] = jnp.zeros_like(out_refs[n][place])

    def finish():
        for n, place, offset, half in halves:
            if full:
                copy(n, place, offset, half).wait()
            else:
                pl.when(rows[offset, half // 2][1])(copy(n, place, offset, half).wait)

    return finish


def start_queries(query_ref, out_refs, offsets, sem):
    section = lax.axis_index("sec")
    copies = []
    for n, (offset, out_ref) in enumerate(zip(offsets, out_refs)):
        width = out_ref.shape[2]
        columns = pl.ds(pl.multiple_of(lax.axis_index("tp") * width, width) if offset > 1 else 0, width)
        part = query_ref.at[0, pl.ds((section ^ offset) * CAP, CAP), :, columns]
        copies.append(pltpu.make_async_copy(part, out_ref, sem.at[n]))
        copies[-1].start()
    return copies


def query_shapes(queries, offsets, tp_count):
    samples, width = queries.shape[2:]
    widths = [width if offset < 2 else width // tp_count for offset in offsets]
    return [jax.ShapeDtypeStruct((CAP, samples, one), queries.dtype) for one in widths]


def head_kernel(piece, offsets, full, routing_ref, cache_ref, query_ref, *refs):
    out_ref, query_out, (routed, held, routing_sem, sem, query_sem) = refs[0], refs[1:-5], refs[-5:]
    offset, half, _ = piece
    section = lax.axis_index("sec")
    copies = [pltpu.make_async_copy(routing_ref, routed, routing_sem)]
    for i in range(REQ_GRP):
        copies.append(pltpu.make_async_copy(cache_ref.at[i, half % 2], held.at[i], sem.at[i]))
    for copy in copies:
        copy.start()
    query_copies = start_queries(query_ref, query_out, offsets, query_sem)
    copies[0].wait()
    row, filled = slot_row(own_targets(routed, section), section ^ offset, half // 2)
    for copy in copies[1:] + query_copies:
        copy.wait()
    chosen = held[row]
    out_ref[0] = chosen if full else jnp.where(filled, chosen, jnp.zeros_like(chosen))


def pack_head(routing, cache, queries, piece, section_count, tp_count):
    shape = cache.shape[2:]
    offsets = range(2, section_count)
    shapes = [jax.ShapeDtypeStruct((1,) + shape, cache.dtype)] + query_shapes(queries, offsets, tp_count)
    head, *parts = pl.pallas_call(
        functools.partial(head_kernel, piece, offsets, section_count * CAP == REQ_GRP),
        out_shape=shapes,
        in_specs=[HBM, HBM, HBM],
        out_specs=[VMEM] * len(shapes),
        scratch_shapes=[
            pltpu.SMEM(routing.shape, jnp.int32),
            pltpu.VMEM((REQ_GRP,) + shape, cache.dtype),
            pltpu.SemaphoreType.DMA,
            pltpu.SemaphoreType.DMA((REQ_GRP,)),
            pltpu.SemaphoreType.DMA((section_count,)),
        ],
        compiler_params=limit(16),
        cost_estimate=cost(0, cache.size),
        name="pack_head",
    )(in_hbm(routing), in_hbm(cache), in_hbm(queries))
    return [head], parts


def first_pack_kernel(pieces, section_count, routing_ref, cache_ref, query_ref, *refs):
    refs, (sem, query_sem) = refs[:-2], refs[-2:]
    query_out, cache_out = refs[-2:], refs[-2 - len(pieces) : -2]
    query_copies = start_queries(query_ref, query_out, range(2), query_sem)
    start_packing(pieces, section_count, routing_ref, cache_ref, cache_out, sem)()
    for copy in query_copies:
        copy.wait()


def pack_kernel(pieces, section_count, routing_ref, cache_ref, *refs):
    cache_out, sem = refs[-1 - len(pieces) : -1], refs[-1]
    start_packing(pieces, section_count, routing_ref, cache_ref, cache_out, sem)()


def merge_kernel(count, *refs):
    for n in range(count):
        refs[-1][n] = refs[n][...]


def merge(parts, others):
    shape = (len(parts),) + parts[0].shape
    return pl.pallas_call(
        functools.partial(merge_kernel, len(parts)),
        out_shape=jax.ShapeDtypeStruct(shape, parts[0].dtype),
        in_specs=[VMEM] * len(parts) + [ANY] * len(others),
        out_specs=VMEM,
        compiler_params=limit(8),
        cost_estimate=cost(3 * 10**9, 8 * len(parts) * parts[0].size),
        name="merge",
    )(*parts, *others)


def in_hbm(value):
    return pltpu.with_memory_space_constraint(value, pltpu.HBM)


def first_pack(routing, cache, queries, others, pieces, section_count):
    shapes = [jax.ShapeDtypeStruct((count,) + cache.shape[2:], cache.dtype) for _, _, count in pieces]
    shapes += query_shapes(queries, range(2), 1)
    parts = pl.pallas_call(
        functools.partial(first_pack_kernel, pieces, section_count),
        out_shape=shapes,
        in_specs=[SMEM, HBM, HBM] + [ANY] * len(others),
        out_specs=[VMEM] * len(shapes),
        scratch_shapes=[
            pltpu.SemaphoreType.DMA((section_count * CAP * 2,)),
            pltpu.SemaphoreType.DMA((2,)),
        ],
        compiler_params=limit(16),
        cost_estimate=cost(0, 4 * sum(shape.size for shape in shapes)),
        name="first_pack",
    )(routing, in_hbm(cache), in_hbm(queries), *others)
    return parts[: len(pieces)], parts[len(pieces) :]


def pack(routing, cache, others, pieces, section_count, flops=0):
    shapes = [jax.ShapeDtypeStruct((count,) + cache.shape[2:], cache.dtype) for _, _, count in pieces]
    return pl.pallas_call(
        functools.partial(pack_kernel, pieces, section_count),
        out_shape=shapes,
        in_specs=[SMEM, HBM] + [ANY] * len(others),
        out_specs=[VMEM] * len(shapes),
        scratch_shapes=[
            pltpu.SemaphoreType.DMA((section_count * CAP * 2,)),
        ],
        compiler_params=limit(16),
        cost_estimate=cost(flops, 4 * sum(shape.size for shape in shapes)),
        name="pack",
    )(routing, in_hbm(cache), *others)


def gate_kernel(*refs):
    pass


def gate(values, others):
    count = len(values)
    return pl.pallas_call(
        gate_kernel,
        out_shape=[jax.ShapeDtypeStruct(value.shape, value.dtype) for value in values],
        in_specs=[ANY] * (count + len(others)),
        out_specs=[ANY] * count,
        input_output_aliases={n: n for n in range(count)},
        compiler_params=limit(1),
        cost_estimate=cost(0, 0),
        name="gate",
    )(*values, *others)


def place_kernel(pieces, *refs):
    count = len(pieces)
    part_refs, out_ref, sem = refs[-2 - count : -2], refs[-2], refs[-1]
    section = lax.axis_index("sec")
    copies = []
    for n, (offset, first, size) in enumerate(pieces):
        for place in range(size):
            half = out_ref.at[0, (section ^ offset) * 2 * CAP + first + place]
            copies.append(pltpu.make_async_copy(part_refs[n].at[place], half, sem.at[len(copies)]))
            copies[-1].start()
    for copy in copies:
        copy.wait()


def place(given, others, parts, pieces, slot_count):
    part = parts[0]
    return pl.pallas_call(
        functools.partial(place_kernel, pieces),
        out_shape=jax.ShapeDtypeStruct((1, 2 * slot_count) + part.shape[1:], part.dtype),
        in_specs=[HBM] * len(given) + [ANY] * len(others) + [VMEM] * len(parts),
        out_specs=HBM,
        scratch_shapes=[pltpu.SemaphoreType.DMA((sum(len(part) for part in parts),))],
        input_output_aliases={0: 0} if given else {},
        compiler_params=limit(8),
        cost_estimate=cost(0, 4 * sum(piece.size for piece in parts)),
        name="place",
    )(*[in_hbm(value) for value in given], *others, *parts)


def attend_kernel(pieces, section_count, tp_count, routing_ref, lengths_ref, *refs):
    cache_refs, refs = refs[: len(pieces)], refs[len(pieces) :]
    query_refs, far_refs = refs[:2], refs[2 : 2 + tp_count]
    message_refs = refs[2 + tp_count : 2 + 2 * tp_count]
    messages, stats, stacked, far_queries = refs[2 + 2 * tp_count :]
    section = lax.axis_index("sec")
    tp_index = lax.axis_index("tp")
    local = cache_refs[0].shape[1]
    groups, rows, _ = messages.shape[1:]
    span = KEY_VALUE_HEADS * rows
    prompts = max(1, groups // KEY_VALUE_HEADS)
    full = section_count * CAP == REQ_GRP
    targets = own_targets(routing_ref, section)
    samples = query_refs[0].shape[1]
    for offset, far_ref in enumerate(far_refs):
        far_queries[tp_index ^ offset] = far_ref[...]
    position = lax.broadcasted_iota(jnp.int32, (local, span), 0) + tp_index * local
    owner = lax.broadcasted_iota(jnp.int32, (HEAD_SIZE, span), 1) // rows

    held = {(offset, half): cache_refs[n].at[place] for n, place, offset, half in halves_of(pieces)}

    def prompt(offset, order):
        keys_ref, values_ref = held[offset, 2 * order], held[offset, 2 * order + 1]
        row, _ = slot_row(targets, section ^ offset, order)
        visible = position < lengths_ref[section * REQ_GRP + row]
        slot = offset * CAP + order
        for head in range(span // samples):
            first, part = head * HEAD_SIZE, far_queries.shape[-1]
            if offset < 2:
                values = query_refs[offset][order, :, first : first + HEAD_SIZE]
            else:
                inner = first % part
                values = far_queries[first // part, offset - 2, order, :, inner : inner + HEAD_SIZE]
            stacked[slot, head * samples : (head + 1) * samples] = values.astype(jnp.float32)
        query = stacked[slot].T.astype(jnp.bfloat16)
        query = [jnp.where(owner == k, query, jnp.zeros_like(query)) for k in range(KEY_VALUE_HEADS)]
        score = jnp.dot(
            keys_ref[...], jnp.concatenate(query, axis=0), preferred_element_type=jnp.float32
        ) * HEAD_SIZE ** (-0.5)
        score = jnp.where(visible, score, HIDDEN)
        peak = jnp.max(score, axis=0, keepdims=True)
        weight = jnp.where(visible, jnp.exp(score - peak), 0.0)
        total = jnp.sum(weight, axis=0, keepdims=True)
        some = total > 0.0
        safe = jnp.where(some, total, 1.0)
        stats[0, pl.ds(row, 1)] = jnp.where(some, peak + jnp.log(safe), HIDDEN)
        weight = (weight * (1.0 / safe)).T.astype(jnp.bfloat16)
        for k in range(KEY_VALUE_HEADS):
            mixed = jnp.dot(
                weight[k * rows : (k + 1) * rows],
                values_ref[:, k * HEAD_SIZE : (k + 1) * HEAD_SIZE],
                preferred_element_type=jnp.float32,
            )
            group = row * KEY_VALUE_HEADS + k
            messages[group // groups, group % groups] = mixed.astype(jnp.bfloat16)

    for offset, half in held:
        if half % 2 == 0:
            one = functools.partial(prompt, offset, half // 2)
            if full:
                one()
            else:
                pl.when(slot_row(targets, section ^ offset, half // 2)[1])(one)

    level = stats[0]
    high = level.astype(jnp.bfloat16).astype(jnp.float32)
    rest = level - high
    middle = rest.astype(jnp.bfloat16).astype(jnp.float32)
    stats[0], stats[1], stats[2] = high, middle, rest - middle
    for offset, message_ref in enumerate(message_refs):
        device = tp_index ^ offset
        for inner in range(groups):
            message_ref[inner * rows : (inner + 1) * rows] = messages[device, inner]
        first = device * groups // KEY_VALUE_HEADS
        lines = [stats[part, pl.ds(first + n, 1)] for part in range(3) for n in range(prompts)]
        lines.append(jnp.zeros((STAT_ROWS - 3 * prompts, span), jnp.float32))
        message_ref[groups * rows :] = jnp.concatenate(lines, axis=0).astype(jnp.bfloat16)


def attend(routing, lengths, caches, pieces, queries, far_queries):
    section_count = len(far_queries[0]) + 2
    tp_count = len(far_queries)
    samples, width = queries[0].shape[1:]
    span = width // HEAD_SIZE * samples
    rows = span // KEY_VALUE_HEADS
    groups = REQ_GRP * KEY_VALUE_HEADS // tp_count
    multiplies = REQ_GRP * span * HEAD_SIZE * caches[0].shape[1]
    return pl.pallas_call(
        functools.partial(attend_kernel, pieces, section_count, tp_count),
        out_shape=[jax.ShapeDtypeStruct((groups * rows + STAT_ROWS, HEAD_SIZE), jnp.bfloat16)] * tp_count,
        in_specs=[SMEM, SMEM] + [VMEM] * (len(caches) + len(queries) + tp_count),
        out_specs=[VMEM] * tp_count,
        scratch_shapes=[
            pltpu.VMEM((tp_count, groups, rows, HEAD_SIZE), jnp.bfloat16),
            pltpu.VMEM((3, REQ_GRP, span), jnp.float32),
            pltpu.VMEM((section_count * CAP, span, HEAD_SIZE), jnp.float32),
            pltpu.VMEM((tp_count,) + far_queries[0].shape, far_queries[0].dtype),
        ],
        compiler_params=limit(12),
        cost_estimate=cost(2 * 10**10, 2 * sum(part.size for part in caches), multiplies // HEAD_SIZE),
        name="attend",
    )(routing, lengths, *caches, *queries, *far_queries)


def join_kernel(count, samples, rows, *refs):
    message_refs, (out_ref, scaling, flat) = refs[:count], refs[-3:]
    groups = (message_refs[0].shape[0] - STAT_ROWS) // rows
    prompts = max(1, groups // KEY_VALUE_HEADS)
    heads = rows // samples
    tp_index = lax.axis_index("tp")
    levels = []
    for ref in message_refs:
        lines = ref[groups * rows :].astype(jnp.float32)[0:8]
        levels.append(lines + pltpu.roll(lines, 8 - prompts, 0) + pltpu.roll(lines, 8 - 2 * prompts, 0))
    summit = functools.reduce(jnp.maximum, levels)
    scales = [jnp.exp(level - summit) for level in levels]
    total = functools.reduce(jnp.add, scales)
    for n, scale in enumerate(scales):
        scaling[n] = (scale / total).T
    for inner in range(groups):
        if groups % KEY_VALUE_HEADS:
            first = (tp_index * groups + inner) % KEY_VALUE_HEADS * rows
            part = pl.ds(pl.multiple_of(first, rows), rows)
        else:
            part = pl.ds(inner % KEY_VALUE_HEADS * rows, rows)
        prompt = inner // KEY_VALUE_HEADS
        terms = [
            ref[inner * rows : (inner + 1) * rows].astype(jnp.float32) * scaling[n, part, prompt : prompt + 1]
            for n, ref in enumerate(message_refs)
        ]
        joined = functools.reduce(jnp.add, terms)
        for head in range(heads):
            block = joined[head * samples : (head + 1) * samples]
            if len(flat.shape) == 2:
                row = prompt * samples
                column = (inner % KEY_VALUE_HEADS * heads + head) * HEAD_SIZE
                flat[row : row + samples, column : column + HEAD_SIZE] = block
            else:
                flat[inner, :, head * HEAD_SIZE : (head + 1) * HEAD_SIZE] = block
    out_ref[...] = flat[...].astype(jnp.bfloat16)


def join(messages, others, samples, heads):
    rows = heads * samples
    groups = (messages[0].shape[0] - STAT_ROWS) // rows
    width = rows // samples * HEAD_SIZE
    if groups % KEY_VALUE_HEADS == 0:
        shape = (groups // KEY_VALUE_HEADS * samples, KEY_VALUE_HEADS * width)
    else:
        shape = (groups, samples, width)
    count = len(messages)
    return pl.pallas_call(
        functools.partial(join_kernel, count, samples, rows),
        out_shape=jax.ShapeDtypeStruct(shape, jnp.bfloat16),
        in_specs=[VMEM] * count + [ANY] * len(others),
        out_specs=VMEM,
        scratch_shapes=[
            pltpu.VMEM((count, KEY_VALUE_HEADS * rows, 8), jnp.float32),
            pltpu.VMEM(shape, jnp.float32),
        ],
        compiler_params=limit(8),
        cost_estimate=cost(4 * count * messages[0].size, 2 * count * messages[0].size),
        name="join",
    )(*messages, *others)


def fetch_kernel(first, weight_ref, *refs):
    out_ref, sem = refs[-2:]
    copies = []
    step = out_ref.shape[0] // sem.shape[0]
    for n in range(sem.shape[0]):
        rows = weight_ref.at[pl.ds(first + n * step, step)]
        copies.append(pltpu.make_async_copy(rows, out_ref.at[pl.ds(n * step, step)], sem.at[n]))
        copies[-1].start()
    for copy in copies:
        copy.wait()


def fetch(weight, others, number, count):
    size = weight.shape[0] // count
    return pl.pallas_call(
        functools.partial(fetch_kernel, number * size),
        out_shape=jax.ShapeDtypeStruct((size,) + weight.shape[1:], weight.dtype),
        in_specs=[HBM] + [ANY] * len(others),
        out_specs=VMEM,
        scratch_shapes=[pltpu.SemaphoreType.DMA((8,))],
        compiler_params=limit(24),
        cost_estimate=cost(0, 4 * weight.size // count),
        name="fetch",
    )(in_hbm(weight), *others)


def project_kernel(count, tile, skipped, *refs):
    refs = refs[skipped:]
    part_refs, weight_refs, out_ref = refs[:count], refs[count:-1], refs[-1]
    tp_index = lax.axis_index("tp")
    prompts, samples, width = out_ref.shape
    share = prompts // count
    left = jnp.concatenate([ref[...].astype(jnp.float32) for ref in part_refs], axis=0).astype(jnp.bfloat16)
    size = weight_refs[0].shape[0]
    for first in range(0, width, tile):
        result = functools.reduce(
            jnp.add,
            [
                jnp.dot(
                    left[:, n * size : (n + 1) * size],
                    ref[:, first : first + tile],
                    preferred_element_type=jnp.float32,
                )
                for n, ref in enumerate(weight_refs)
            ],
        )
        for offset in range(count):
            for n in range(share):
                row = (offset * share + n) * samples
                block = result[row : row + samples].astype(out_ref.dtype)
                out_ref[(tp_index ^ offset) * share + n, :, first : first + tile] = block


def project(parts, weights, others, samples):
    count = len(parts)
    depth, width = weights[0].shape
    depth *= len(weights)
    total = count * parts[0].shape[0]
    return pl.pallas_call(
        functools.partial(project_kernel, count, min(256, width), len(others)),
        out_shape=jax.ShapeDtypeStruct((total // samples, samples, width), jnp.bfloat16),
        in_specs=[ANY] * len(others) + [VMEM] * (count + len(weights)),
        out_specs=VMEM,
        compiler_params=limit(24),
        cost_estimate=cost(2 * total * depth * width, 2 * depth * width),
        name="project",
    )(*others, *parts, *weights)


def body(prompt_key_values, queries, routing, lengths, out_weight):
    section_count = lax.axis_size("sec")
    tp_count = lax.axis_size("tp")
    slot_count, samples, query_width = queries.shape[1:]
    routing = routing.reshape(-1)

    whole = 2 * CAP
    near = [(offset, 0, whole) for offset in range(2)]
    head, tail = [(2, 0, 1)], [(2, 1, whole - 1)]
    far = tail + [(offset, 0, whole) for offset in range(3, section_count - 1)]
    far += [(section_count - 1, 0, whole - 1), (section_count - 1, whole - 1, 1)]

    def across(parts, pieces):
        return [swap(part, "sec", piece[0]) for part, piece in zip(parts, pieces)]

    head_caches, far_queries = pack_head(
        routing, prompt_key_values, queries, head[0], section_count, tp_count
    )
    head_parts = across(head_caches, head)
    far_queries = [swap(part, "sec", n + 2) for n, part in enumerate(far_queries)]
    far_caches, query_parts = first_pack(
        routing, prompt_key_values, queries, head_caches, far, section_count
    )
    far_parts = across(far_caches[:-1], far[:-1])
    query_parts = [swap(part, "sec", offset) for offset, part in enumerate(query_parts)]
    merged = merge(far_queries, head_parts)
    far_queries = spread(merged, "tp")
    near_caches = pack(routing, prompt_key_values, [merged, query_parts[1]], near, section_count, 10**10)
    near_parts = across(near_caches, near)
    caches, pieces = [*head_caches, *far_caches, *near_caches], head + far + near

    messages = attend(routing, lengths, caches, pieces, query_parts, far_queries)
    partials = [swap(part, "tp", offset) for offset, part in enumerate(messages)]
    held_weight = [fetch(out_weight, [messages[0], *near_parts[1:]], 0, 2)]
    held_cache = place([], [], near_parts + head_parts, near + head, slot_count)
    share = join(partials, [in_hbm(held_cache), *held_weight, *far_parts[:-1]], samples, query_width // HEAD_SIZE // KEY_VALUE_HEADS)
    far_parts += across(gate(far_caches[-1:], [share]), far[-1:])
    shares = spread(share, "tp")
    held_weight.append(fetch(out_weight, [share], 1, 2))
    if share.ndim == 3:
        attended = jnp.stack(shares)[jnp.arange(tp_count) ^ lax.axis_index("tp")]
        attended = attended.reshape(REQ_GRP, KEY_VALUE_HEADS, samples, -1).transpose(0, 2, 1, 3)
        attended = attended.reshape(REQ_GRP * samples, query_width)
        layer_out = jnp.dot(attended, out_weight, preferred_element_type=jnp.float32)
        layer_out = layer_out.astype(jnp.bfloat16).reshape(REQ_GRP, samples, -1)
    else:
        layer_out = project(shares, held_weight, far_parts[:-2], samples)

    held_cache = place([held_cache], [share], far_parts[:-2], far[:-2], slot_count)
    for part, piece in zip(far_parts[-2:], far[-2:]):
        held_cache = place([held_cache, layer_out], [], [part], [piece], slot_count)
    held_cache = held_cache.reshape((1, slot_count) + prompt_key_values.shape[1:])
    return (layer_out, held_cache)


def solution(mesh):
    placed = (
        P(("rep", "sec"), None, "tp", None),
        P(("rep", "sec"), None, None, None),
        P("rep", None),
        P("rep"),
        P(None, "tp"),
    )
    return jax.shard_map(
        body,
        mesh=mesh,
        in_specs=placed,
        out_specs=(P(("rep", "sec"), None, "tp"), P(("rep", "sec"), None, None, "tp", None)),
        check_vma=False,
    )
```

```python
import functools

import jax
import jax.numpy as jnp
from jax import lax
from jax.experimental import pallas as pl
from jax.experimental.pallas import tpu as pltpu
from jax.sharding import PartitionSpec as P

HEAD_SIZE = 128
KEY_VALUE_HEADS = 4
REQ_GRP = 8
CAP = 2
HIDDEN = -1e30
STAT_ROWS = 16

ANY = pl.BlockSpec(memory_space=pl.ANY)
HBM = pl.BlockSpec(memory_space=pltpu.HBM)
VMEM = pl.BlockSpec(memory_space=pltpu.VMEM)
SMEM = pl.BlockSpec(memory_space=pltpu.SMEM)


def limit(mebibytes):
    return pltpu.CompilerParams(vmem_limit_bytes=mebibytes << 20)


def cost(flops, bytes_accessed, transcendentals=0):
    return pl.CostEstimate(flops=flops, bytes_accessed=bytes_accessed, transcendentals=transcendentals)


def swap(value, axis, offset):
    if offset == 0:
        return value
    count = lax.axis_size(axis)
    return lax.ppermute(value, axis, [(i, i ^ offset) for i in range(count)])


def spread(value, axis):
    return [swap(value, axis, offset) for offset in range(lax.axis_size(axis))]


def own_targets(routing_ref, section):
    return [routing_ref[section * REQ_GRP + i] for i in range(REQ_GRP)]


def slot_row(targets, group, order):
    row, before = jnp.int32(0), jnp.int32(0)
    for i, target in enumerate(targets):
        here = target == group
        row = jnp.where(here & (before == order), i, row)
        before = before + here.astype(jnp.int32)
    return row, before > order


def halves_of(pieces):
    return [
        (n, place, offset, first + place)
        for n, (offset, first, count) in enumerate(pieces)
        for place in range(count)
    ]


def start_packing(pieces, section_count, routing_ref, cache_ref, out_refs, sem):
    section = lax.axis_index("sec")
    full = section_count * CAP == REQ_GRP
    targets = own_targets(routing_ref, section)
    halves = halves_of(pieces)
    slots = {(offset, half // 2) for _, _, offset, half in halves}
    rows = {slot: slot_row(targets, section ^ slot[0], slot[1]) for slot in sorted(slots)}

    def copy(n, place, offset, half):
        row, _ = rows[offset, half // 2]
        return pltpu.make_async_copy(
            cache_ref.at[row, half % 2], out_refs[n].at[place], sem.at[offset * 2 * CAP + half]
        )

    for n, place, offset, half in halves:
        if full:
            copy(n, place, offset, half).start()
        else:
            _, filled = rows[offset, half // 2]

            @pl.when(filled)
            def _():
                copy(n, place, offset, half).start()

            @pl.when(jnp.logical_not(filled))
            def _():
                out_refs[n][place] = jnp.zeros_like(out_refs[n][place])

    def finish():
        for n, place, offset, half in halves:
            if full:
                copy(n, place, offset, half).wait()
            else:
                pl.when(rows[offset, half // 2][1])(copy(n, place, offset, half).wait)

    return finish


def start_queries(query_ref, out_refs, offsets, sem):
    section = lax.axis_index("sec")
    copies = []
    for n, (offset, out_ref) in enumerate(zip(offsets, out_refs)):
        width = out_ref.shape[2]
        columns = pl.ds(pl.multiple_of(lax.axis_index("tp") * width, width) if offset > 1 else 0, width)
        part = query_ref.at[0, pl.ds((section ^ offset) * CAP, CAP), :, columns]
        copies.append(pltpu.make_async_copy(part, out_ref, sem.at[n]))
        copies[-1].start()
    return copies


def query_shapes(queries, offsets, tp_count):
    samples, width = queries.shape[2:]
    widths = [width if offset < 2 else width // tp_count for offset in offsets]
    return [jax.ShapeDtypeStruct((CAP, samples, one), queries.dtype) for one in widths]


def head_kernel(piece, offsets, full, routing_ref, cache_ref, query_ref, *refs):
    out_ref, query_out, (routed, held, routing_sem, sem, query_sem) = refs[0], refs[1:-5], refs[-5:]
    offset, half, _ = piece
    section = lax.axis_index("sec")
    copies = [pltpu.make_async_copy(routing_ref, routed, routing_sem)]
    for i in range(REQ_GRP - CAP + 1 if full and half < 2 else REQ_GRP):
        copies.append(pltpu.make_async_copy(cache_ref.at[i, half % 2], held.at[i], sem.at[i]))
    for copy in copies:
        copy.start()
    query_copies = start_queries(query_ref, query_out, offsets, query_sem)
    copies[0].wait()
    row, filled = slot_row(own_targets(routed, section), section ^ offset, half // 2)
    for copy in copies[1:] + query_copies:
        copy.wait()
    block = min(32, held.shape[1])
    for first in range(0, held.shape[1], block):
        chosen = held[row, first : first + block]
        out_ref[0, first : first + block] = chosen if full else jnp.where(filled, chosen, jnp.zeros_like(chosen))


def pack_head(routing, cache, queries, piece, section_count, tp_count):
    shape = cache.shape[2:]
    offsets = range(2, section_count)
    shapes = [jax.ShapeDtypeStruct((1,) + shape, cache.dtype)] + query_shapes(queries, offsets, tp_count)
    head, *parts = pl.pallas_call(
        functools.partial(head_kernel, piece, offsets, section_count * CAP == REQ_GRP),
        out_shape=shapes,
        in_specs=[HBM, HBM, HBM],
        out_specs=[VMEM] * len(shapes),
        scratch_shapes=[
            pltpu.SMEM(routing.shape, jnp.int32),
            pltpu.VMEM((REQ_GRP,) + shape, cache.dtype),
            pltpu.SemaphoreType.DMA,
            pltpu.SemaphoreType.DMA((REQ_GRP,)),
            pltpu.SemaphoreType.DMA((section_count,)),
        ],
        compiler_params=limit(16),
        cost_estimate=cost(0, cache.size),
        name="pack_head",
    )(in_hbm(routing), in_hbm(cache), in_hbm(queries))
    return [head], parts


def first_pack_kernel(pieces, section_count, routing_ref, cache_ref, query_ref, *refs):
    refs, (sem, query_sem) = refs[:-2], refs[-2:]
    query_out, cache_out = refs[-2:], refs[-2 - len(pieces) : -2]
    query_copies = start_queries(query_ref, query_out, range(2), query_sem)
    start_packing(pieces, section_count, routing_ref, cache_ref, cache_out, sem)()
    for copy in query_copies:
        copy.wait()


def pack_kernel(pieces, section_count, routing_ref, cache_ref, *refs):
    cache_out, sem = refs[-1 - len(pieces) : -1], refs[-1]
    start_packing(pieces, section_count, routing_ref, cache_ref, cache_out, sem)()


def merge_kernel(count, *refs):
    for n in range(count):
        refs[-1][n] = refs[n][...]


def merge(parts, others):
    shape = (len(parts),) + parts[0].shape
    return pl.pallas_call(
        functools.partial(merge_kernel, len(parts)),
        out_shape=jax.ShapeDtypeStruct(shape, parts[0].dtype),
        in_specs=[VMEM] * len(parts) + [ANY] * len(others),
        out_specs=VMEM,
        compiler_params=limit(8),
        cost_estimate=cost(3 * 10**9, 8 * len(parts) * parts[0].size),
        name="merge",
    )(*parts, *others)


def in_hbm(value):
    return pltpu.with_memory_space_constraint(value, pltpu.HBM)


def first_pack(routing, cache, queries, others, pieces, section_count):
    shapes = [jax.ShapeDtypeStruct((count,) + cache.shape[2:], cache.dtype) for _, _, count in pieces]
    shapes += query_shapes(queries, range(2), 1)
    parts = pl.pallas_call(
        functools.partial(first_pack_kernel, pieces, section_count),
        out_shape=shapes,
        in_specs=[SMEM, HBM, HBM] + [ANY] * len(others),
        out_specs=[VMEM] * len(shapes),
        scratch_shapes=[
            pltpu.SemaphoreType.DMA((section_count * CAP * 2,)),
            pltpu.SemaphoreType.DMA((2,)),
        ],
        compiler_params=limit(16),
        cost_estimate=cost(0, 4 * sum(shape.size for shape in shapes)),
        name="first_pack",
    )(routing, in_hbm(cache), in_hbm(queries), *others)
    return parts[: len(pieces)], parts[len(pieces) :]


def pack(routing, cache, others, pieces, section_count, flops=0):
    shapes = [jax.ShapeDtypeStruct((count,) + cache.shape[2:], cache.dtype) for _, _, count in pieces]
    return pl.pallas_call(
        functools.partial(pack_kernel, pieces, section_count),
        out_shape=shapes,
        in_specs=[SMEM, HBM] + [ANY] * len(others),
        out_specs=[VMEM] * len(shapes),
        scratch_shapes=[
            pltpu.SemaphoreType.DMA((section_count * CAP * 2,)),
        ],
        compiler_params=limit(16),
        cost_estimate=cost(flops, 4 * sum(shape.size for shape in shapes)),
        name="pack",
    )(routing, in_hbm(cache), *others)


def gate_kernel(*refs):
    pass


def gate(values, others):
    count = len(values)
    return pl.pallas_call(
        gate_kernel,
        out_shape=[jax.ShapeDtypeStruct(value.shape, value.dtype) for value in values],
        in_specs=[ANY] * (count + len(others)),
        out_specs=[ANY] * count,
        input_output_aliases={n: n for n in range(count)},
        compiler_params=limit(1),
        cost_estimate=cost(0, 0),
        name="gate",
    )(*values, *others)


def place_kernel(pieces, *refs):
    count = len(pieces)
    part_refs, out_ref, sem = refs[-2 - count : -2], refs[-2], refs[-1]
    section = lax.axis_index("sec")
    copies = []
    for n, (offset, first, size) in enumerate(pieces):
        for place in range(size):
            half = out_ref.at[0, (section ^ offset) * 2 * CAP + first + place]
            copies.append(pltpu.make_async_copy(part_refs[n].at[place], half, sem.at[len(copies)]))
            copies[-1].start()
    for copy in copies:
        copy.wait()


def place(given, others, parts, pieces, slot_count):
    part = parts[0]
    return pl.pallas_call(
        functools.partial(place_kernel, pieces),
        out_shape=jax.ShapeDtypeStruct((1, 2 * slot_count) + part.shape[1:], part.dtype),
        in_specs=[HBM] * len(given) + [ANY] * len(others) + [VMEM] * len(parts),
        out_specs=HBM,
        scratch_shapes=[pltpu.SemaphoreType.DMA((sum(len(part) for part in parts),))],
        input_output_aliases={0: 0} if given else {},
        compiler_params=limit(8),
        cost_estimate=cost(0, 4 * sum(piece.size for piece in parts)),
        name="place",
    )(*[in_hbm(value) for value in given], *others, *parts)


def attend_kernel(pieces, section_count, tp_count, routing_ref, lengths_ref, *refs):
    cache_refs, refs = refs[: len(pieces)], refs[len(pieces) :]
    query_refs, far_refs = refs[:2], refs[2 : 2 + tp_count]
    message_refs = refs[2 + tp_count : 2 + 2 * tp_count]
    messages, stats, stacked, far_queries = refs[2 + 2 * tp_count :]
    section = lax.axis_index("sec")
    tp_index = lax.axis_index("tp")
    local = cache_refs[0].shape[1]
    groups, rows, _ = messages.shape[1:]
    span = KEY_VALUE_HEADS * rows
    prompts = max(1, groups // KEY_VALUE_HEADS)
    full = section_count * CAP == REQ_GRP
    targets = own_targets(routing_ref, section)
    samples = query_refs[0].shape[1]
    for offset, far_ref in enumerate(far_refs):
        far_queries[tp_index ^ offset] = far_ref[...]
    position = lax.broadcasted_iota(jnp.int32, (local, span), 0) + tp_index * local
    owner = lax.broadcasted_iota(jnp.int32, (HEAD_SIZE, span), 1) // rows

    held = {(offset, half): cache_refs[n].at[place] for n, place, offset, half in halves_of(pieces)}

    def prompt(offset, order):
        keys_ref, values_ref = held[offset, 2 * order], held[offset, 2 * order + 1]
        row, _ = slot_row(targets, section ^ offset, order)
        visible = position < lengths_ref[section * REQ_GRP + row]
        slot = offset * CAP + order
        for head in range(span // samples):
            first, part = head * HEAD_SIZE, far_queries.shape[-1]
            if offset < 2:
                values = query_refs[offset][order, :, first : first + HEAD_SIZE]
            else:
                inner = first % part
                values = far_queries[first // part, offset - 2, order, :, inner : inner + HEAD_SIZE]
            stacked[slot, head * samples : (head + 1) * samples] = values.astype(jnp.float32)
        query = stacked[slot].T.astype(jnp.bfloat16)
        query = [jnp.where(owner == k, query, jnp.zeros_like(query)) for k in range(KEY_VALUE_HEADS)]
        score = jnp.dot(
            keys_ref[...], jnp.concatenate(query, axis=0), preferred_element_type=jnp.float32
        ) * HEAD_SIZE ** (-0.5)
        score = jnp.where(visible, score, HIDDEN)
        peak = jnp.max(score, axis=0, keepdims=True)
        weight = jnp.where(visible, jnp.exp(score - peak), 0.0)
        total = jnp.sum(weight, axis=0, keepdims=True)
        some = total > 0.0
        safe = jnp.where(some, total, 1.0)
        stats[0, pl.ds(row, 1)] = jnp.where(some, peak + jnp.log(safe), HIDDEN)
        weight = (weight * (1.0 / safe)).T.astype(jnp.bfloat16)
        for k in range(KEY_VALUE_HEADS):
            mixed = jnp.dot(
                weight[k * rows : (k + 1) * rows],
                values_ref[:, k * HEAD_SIZE : (k + 1) * HEAD_SIZE],
                preferred_element_type=jnp.float32,
            )
            group = row * KEY_VALUE_HEADS + k
            messages[group // groups, group % groups] = mixed.astype(jnp.bfloat16)

    for offset, half in held:
        if half % 2 == 0:
            one = functools.partial(prompt, offset, half // 2)
            if full:
                one()
            else:
                pl.when(slot_row(targets, section ^ offset, half // 2)[1])(one)

    level = stats[0]
    high = level.astype(jnp.bfloat16).astype(jnp.float32)
    rest = level - high
    middle = rest.astype(jnp.bfloat16).astype(jnp.float32)
    stats[0], stats[1], stats[2] = high, middle, rest - middle
    for offset, message_ref in enumerate(message_refs):
        device = tp_index ^ offset
        for inner in range(groups):
            message_ref[inner * rows : (inner + 1) * rows] = messages[device, inner]
        first = device * groups // KEY_VALUE_HEADS
        lines = [stats[part, pl.ds(first + n, 1)] for part in range(3) for n in range(prompts)]
        lines.append(jnp.zeros((STAT_ROWS - 3 * prompts, span), jnp.float32))
        message_ref[groups * rows :] = jnp.concatenate(lines, axis=0).astype(jnp.bfloat16)


def attend(routing, lengths, caches, pieces, queries, far_queries):
    section_count = len(far_queries[0]) + 2
    tp_count = len(far_queries)
    samples, width = queries[0].shape[1:]
    span = width // HEAD_SIZE * samples
    rows = span // KEY_VALUE_HEADS
    groups = REQ_GRP * KEY_VALUE_HEADS // tp_count
    multiplies = REQ_GRP * span * HEAD_SIZE * caches[0].shape[1]
    return pl.pallas_call(
        functools.partial(attend_kernel, pieces, section_count, tp_count),
        out_shape=[jax.ShapeDtypeStruct((groups * rows + STAT_ROWS, HEAD_SIZE), jnp.bfloat16)] * tp_count,
        in_specs=[SMEM, SMEM] + [VMEM] * (len(caches) + len(queries) + tp_count),
        out_specs=[VMEM] * tp_count,
        scratch_shapes=[
            pltpu.VMEM((tp_count, groups, rows, HEAD_SIZE), jnp.bfloat16),
            pltpu.VMEM((3, REQ_GRP, span), jnp.float32),
            pltpu.VMEM((section_count * CAP, span, HEAD_SIZE), jnp.float32),
            pltpu.VMEM((tp_count,) + far_queries[0].shape, far_queries[0].dtype),
        ],
        compiler_params=limit(12),
        cost_estimate=cost(2 * 10**10, 2 * sum(part.size for part in caches), multiplies // HEAD_SIZE),
        name="attend",
    )(routing, lengths, *caches, *queries, *far_queries)


def join_kernel(count, samples, rows, *refs):
    message_refs, (out_ref, scaling, flat) = refs[:count], refs[-3:]
    groups = (message_refs[0].shape[0] - STAT_ROWS) // rows
    prompts = max(1, groups // KEY_VALUE_HEADS)
    heads = rows // samples
    tp_index = lax.axis_index("tp")
    levels = []
    for ref in message_refs:
        lines = ref[groups * rows :].astype(jnp.float32)[0:8]
        levels.append(lines + pltpu.roll(lines, 8 - prompts, 0) + pltpu.roll(lines, 8 - 2 * prompts, 0))
    summit = functools.reduce(jnp.maximum, levels)
    scales = [jnp.exp(level - summit) for level in levels]
    total = functools.reduce(jnp.add, scales)
    for n, scale in enumerate(scales):
        scaling[n] = (scale / total).T
    for inner in range(groups):
        if groups % KEY_VALUE_HEADS:
            first = (tp_index * groups + inner) % KEY_VALUE_HEADS * rows
            part = pl.ds(pl.multiple_of(first, rows), rows)
        else:
            part = pl.ds(inner % KEY_VALUE_HEADS * rows, rows)
        prompt = inner // KEY_VALUE_HEADS
        terms = [
            ref[inner * rows : (inner + 1) * rows].astype(jnp.float32) * scaling[n, part, prompt : prompt + 1]
            for n, ref in enumerate(message_refs)
        ]
        joined = functools.reduce(jnp.add, terms)
        for head in range(heads):
            block = joined[head * samples : (head + 1) * samples]
            if len(flat.shape) == 2:
                row = prompt * samples
                column = (inner % KEY_VALUE_HEADS * heads + head) * HEAD_SIZE
                flat[row : row + samples, column : column + HEAD_SIZE] = block
            else:
                flat[inner, :, head * HEAD_SIZE : (head + 1) * HEAD_SIZE] = block
    out_ref[...] = flat[...].astype(jnp.bfloat16)


def join(messages, others, samples, heads):
    rows = heads * samples
    groups = (messages[0].shape[0] - STAT_ROWS) // rows
    width = rows // samples * HEAD_SIZE
    if groups % KEY_VALUE_HEADS == 0:
        shape = (groups // KEY_VALUE_HEADS * samples, KEY_VALUE_HEADS * width)
    else:
        shape = (groups, samples, width)
    count = len(messages)
    return pl.pallas_call(
        functools.partial(join_kernel, count, samples, rows),
        out_shape=jax.ShapeDtypeStruct(shape, jnp.bfloat16),
        in_specs=[VMEM] * count + [ANY] * len(others),
        out_specs=VMEM,
        scratch_shapes=[
            pltpu.VMEM((count, KEY_VALUE_HEADS * rows, 8), jnp.float32),
            pltpu.VMEM(shape, jnp.float32),
        ],
        compiler_params=limit(8),
        cost_estimate=cost(4 * count * messages[0].size, 2 * count * messages[0].size),
        name="join",
    )(*messages, *others)


def fetch_kernel(first, weight_ref, *refs):
    out_ref, sem = refs[-2:]
    copies = []
    step = out_ref.shape[0] // sem.shape[0]
    for n in range(sem.shape[0]):
        rows = weight_ref.at[pl.ds(first + n * step, step)]
        copies.append(pltpu.make_async_copy(rows, out_ref.at[pl.ds(n * step, step)], sem.at[n]))
        copies[-1].start()
    for copy in copies:
        copy.wait()


def fetch(weight, others, number, count):
    size = weight.shape[0] // count
    return pl.pallas_call(
        functools.partial(fetch_kernel, number * size),
        out_shape=jax.ShapeDtypeStruct((size,) + weight.shape[1:], weight.dtype),
        in_specs=[HBM] + [ANY] * len(others),
        out_specs=VMEM,
        scratch_shapes=[pltpu.SemaphoreType.DMA((8,))],
        compiler_params=limit(24),
        cost_estimate=cost(0, 4 * weight.size // count),
        name="fetch",
    )(in_hbm(weight), *others)


def project_kernel(count, tile, skipped, *refs):
    refs = refs[skipped:]
    part_refs, weight_refs, out_ref = refs[:count], refs[count:-1], refs[-1]
    tp_index = lax.axis_index("tp")
    prompts, samples, width = out_ref.shape
    share = prompts // count
    left = jnp.concatenate([ref[...].astype(jnp.float32) for ref in part_refs], axis=0).astype(jnp.bfloat16)
    size = weight_refs[0].shape[0]
    for first in range(0, width, tile):
        result = functools.reduce(
            jnp.add,
            [
                jnp.dot(
                    left[:, n * size : (n + 1) * size],
                    ref[:, first : first + tile],
                    preferred_element_type=jnp.float32,
                )
                for n, ref in enumerate(weight_refs)
            ],
        )
        for offset in range(count):
            for n in range(share):
                row = (offset * share + n) * samples
                block = result[row : row + samples].astype(out_ref.dtype)
                out_ref[(tp_index ^ offset) * share + n, :, first : first + tile] = block


def project(parts, weights, others, samples):
    count = len(parts)
    depth, width = weights[0].shape
    depth *= len(weights)
    total = count * parts[0].shape[0]
    return pl.pallas_call(
        functools.partial(project_kernel, count, min(256, width), len(others)),
        out_shape=jax.ShapeDtypeStruct((total // samples, samples, width), jnp.bfloat16),
        in_specs=[ANY] * len(others) + [VMEM] * (count + len(weights)),
        out_specs=VMEM,
        compiler_params=limit(24),
        cost_estimate=cost(2 * total * depth * width, 2 * depth * width),
        name="project",
    )(*others, *parts, *weights)


def body(prompt_key_values, queries, routing, lengths, out_weight):
    section_count = lax.axis_size("sec")
    tp_count = lax.axis_size("tp")
    slot_count, samples, query_width = queries.shape[1:]
    routing = routing.reshape(-1)

    whole = 2 * CAP
    near = [(offset, 0, whole) for offset in range(2)]
    head, tail = [(2, 0, 1)], [(2, 1, whole - 1)]
    far = tail + [(offset, 0, whole) for offset in range(3, section_count - 1)]
    far += [(section_count - 1, 0, whole - 1), (section_count - 1, whole - 1, 1)]

    def across(parts, pieces):
        return [swap(part, "sec", piece[0]) for part, piece in zip(parts, pieces)]

    head_caches, far_queries = pack_head(
        routing, prompt_key_values, queries, head[0], section_count, tp_count
    )
    head_parts = across(head_caches, head)
    far_queries = [swap(part, "sec", n + 2) for n, part in enumerate(far_queries)]
    far_caches, query_parts = first_pack(
        routing, prompt_key_values, queries, head_caches, far, section_count
    )
    far_parts = across(far_caches[:-1], far[:-1])
    query_parts = [swap(part, "sec", offset) for offset, part in enumerate(query_parts)]
    merged = merge(far_queries, head_parts)
    far_queries = spread(merged, "tp")
    near_caches = pack(routing, prompt_key_values, [merged, query_parts[1]], near, section_count, 10**10)
    near_parts = across(near_caches, near)
    caches, pieces = [*head_caches, *far_caches, *near_caches], head + far + near

    messages = attend(routing, lengths, caches, pieces, query_parts, far_queries)
    partials = [swap(part, "tp", offset) for offset, part in enumerate(messages)]
    held_weight = [fetch(out_weight, [messages[0], *near_parts[1:]], 0, 2)]
    held_cache = place([], [], near_parts + head_parts, near + head, slot_count)
    share = join(partials, [in_hbm(held_cache), *held_weight, *far_parts[:-1]], samples, query_width // HEAD_SIZE // KEY_VALUE_HEADS)
    far_parts += across(gate(far_caches[-1:], [share]), far[-1:])
    shares = spread(share, "tp")
    held_weight.append(fetch(out_weight, [share], 1, 2))
    if share.ndim == 3:
        attended = jnp.stack(shares)[jnp.arange(tp_count) ^ lax.axis_index("tp")]
        attended = attended.reshape(REQ_GRP, KEY_VALUE_HEADS, samples, -1).transpose(0, 2, 1, 3)
        attended = attended.reshape(REQ_GRP * samples, query_width)
        layer_out = jnp.dot(attended, out_weight, preferred_element_type=jnp.float32)
        layer_out = layer_out.astype(jnp.bfloat16).reshape(REQ_GRP, samples, -1)
    else:
        layer_out = project(shares, held_weight, far_parts[:-2], samples)

    held_cache = place([held_cache], [share], far_parts[:-2], far[:-2], slot_count)
    for part, piece in zip(far_parts[-2:], far[-2:]):
        held_cache = place([held_cache, layer_out], [], [part], [piece], slot_count)
    held_cache = held_cache.reshape((1, slot_count) + prompt_key_values.shape[1:])
    return (layer_out, held_cache)


def solution(mesh):
    placed = (
        P(("rep", "sec"), None, "tp", None),
        P(("rep", "sec"), None, None, None),
        P("rep", None),
        P("rep"),
        P(None, "tp"),
    )
    return jax.shard_map(
        body,
        mesh=mesh,
        in_specs=placed,
        out_specs=(P(("rep", "sec"), None, "tp"), P(("rep", "sec"), None, None, "tp", None)),
        check_vma=False,
    )
```

```python
import functools

import jax
import jax.numpy as jnp
from jax import lax
from jax.experimental import pallas as pl
from jax.experimental.pallas import tpu as pltpu
from jax.sharding import PartitionSpec as P

HEAD_SIZE = 128
KEY_VALUE_HEADS = 4
REQ_GRP = 8
CAP = 2
HIDDEN = -1e30
STAT_ROWS = 16

ANY = pl.BlockSpec(memory_space=pl.ANY)
HBM = pl.BlockSpec(memory_space=pltpu.HBM)
VMEM = pl.BlockSpec(memory_space=pltpu.VMEM)
SMEM = pl.BlockSpec(memory_space=pltpu.SMEM)


def limit(mebibytes):
    return pltpu.CompilerParams(vmem_limit_bytes=mebibytes << 20)


def cost(flops, bytes_accessed, transcendentals=0):
    return pl.CostEstimate(flops=flops, bytes_accessed=bytes_accessed, transcendentals=transcendentals)


def swap(value, axis, offset):
    if offset == 0:
        return value
    count = lax.axis_size(axis)
    return lax.ppermute(value, axis, [(i, i ^ offset) for i in range(count)])


def spread(value, axis):
    return [swap(value, axis, offset) for offset in range(lax.axis_size(axis))]


def own_targets(routing_ref, section):
    return [routing_ref[section * REQ_GRP + i] for i in range(REQ_GRP)]


def slot_row(targets, group, order):
    row, before = jnp.int32(0), jnp.int32(0)
    for i, target in enumerate(targets):
        here = target == group
        row = jnp.where(here & (before == order), i, row)
        before = before + here.astype(jnp.int32)
    return row, before > order


def halves_of(pieces):
    return [
        (n, place, offset, first + place)
        for n, (offset, first, count) in enumerate(pieces)
        for place in range(count)
    ]


def start_packing(pieces, section_count, routing_ref, cache_ref, out_refs, sem):
    section = lax.axis_index("sec")
    full = section_count * CAP == REQ_GRP
    targets = own_targets(routing_ref, section)
    halves = halves_of(pieces)
    slots = {(offset, half // 2) for _, _, offset, half in halves}
    rows = {slot: slot_row(targets, section ^ slot[0], slot[1]) for slot in sorted(slots)}

    def copy(n, place, offset, half):
        row, _ = rows[offset, half // 2]
        return pltpu.make_async_copy(
            cache_ref.at[row, half % 2], out_refs[n].at[place], sem.at[offset * 2 * CAP + half]
        )

    for n, place, offset, half in halves:
        if full:
            copy(n, place, offset, half).start(priority=half % 2)
        else:
            _, filled = rows[offset, half // 2]

            @pl.when(filled)
            def _():
                copy(n, place, offset, half).start()

            @pl.when(jnp.logical_not(filled))
            def _():
                out_refs[n][place] = jnp.zeros_like(out_refs[n][place])

    def finish():
        for n, place, offset, half in halves:
            if full:
                copy(n, place, offset, half).wait()
            else:
                pl.when(rows[offset, half // 2][1])(copy(n, place, offset, half).wait)

    return finish


def start_queries(query_ref, out_refs, offsets, sem):
    section = lax.axis_index("sec")
    copies = []
    for n, (offset, out_ref) in enumerate(zip(offsets, out_refs)):
        width = out_ref.shape[2]
        columns = pl.ds(pl.multiple_of(lax.axis_index("tp") * width, width) if offset > 1 else 0, width)
        part = query_ref.at[0, pl.ds((section ^ offset) * CAP, CAP), :, columns]
        copies.append(pltpu.make_async_copy(part, out_ref, sem.at[n]))
        copies[-1].start()
    return copies


def query_shapes(queries, offsets, tp_count):
    samples, width = queries.shape[2:]
    widths = [width if offset < 2 else width // tp_count for offset in offsets]
    return [jax.ShapeDtypeStruct((CAP, samples, one), queries.dtype) for one in widths]


def head_kernel(piece, offsets, full, routing_ref, cache_ref, query_ref, *refs):
    out_ref, query_out, (routed, held, routing_sem, sem, query_sem) = refs[0], refs[1:-5], refs[-5:]
    offset, half, _ = piece
    section = lax.axis_index("sec")
    copies = [pltpu.make_async_copy(routing_ref, routed, routing_sem)]
    for i in range(REQ_GRP - CAP + 1 if full and half < 2 else REQ_GRP):
        copies.append(pltpu.make_async_copy(cache_ref.at[i, half % 2], held.at[i], sem.at[i]))
    for n, copy in enumerate(copies):
        copy.start(priority=n % 2)
    query_copies = start_queries(query_ref, query_out, offsets, query_sem)
    copies[0].wait()
    row, filled = slot_row(own_targets(routed, section), section ^ offset, half // 2)
    pltpu.make_async_copy(cache_ref.at[row, half % 2], held.at[row], sem.at[row]).wait()
    block = min(32, held.shape[1])
    for first in range(0, held.shape[1], block):
        chosen = held[row, first : first + block]
        out_ref[0, first : first + block] = chosen if full else jnp.where(filled, chosen, jnp.zeros_like(chosen))
    for i, copy in enumerate(copies[1:]):
        pl.when(i != row)(copy.wait)
    for copy in query_copies:
        copy.wait()


def pack_head(routing, cache, queries, piece, section_count, tp_count):
    shape = cache.shape[2:]
    offsets = range(2, section_count)
    shapes = [jax.ShapeDtypeStruct((1,) + shape, cache.dtype)] + query_shapes(queries, offsets, tp_count)
    head, *parts = pl.pallas_call(
        functools.partial(head_kernel, piece, offsets, section_count * CAP == REQ_GRP),
        out_shape=shapes,
        in_specs=[HBM, HBM, HBM],
        out_specs=[VMEM] * len(shapes),
        scratch_shapes=[
            pltpu.SMEM(routing.shape, jnp.int32),
            pltpu.VMEM((REQ_GRP,) + shape, cache.dtype),
            pltpu.SemaphoreType.DMA,
            pltpu.SemaphoreType.DMA((REQ_GRP,)),
            pltpu.SemaphoreType.DMA((section_count,)),
        ],
        compiler_params=limit(16),
        cost_estimate=cost(0, cache.size),
        name="pack_head",
    )(in_hbm(routing), in_hbm(cache), in_hbm(queries))
    return [head], parts


def first_pack_kernel(pieces, section_count, routing_ref, cache_ref, query_ref, *refs):
    refs, (sem, query_sem) = refs[:-2], refs[-2:]
    query_out, cache_out = refs[-2:], refs[-2 - len(pieces) : -2]
    query_copies = start_queries(query_ref, query_out, range(2), query_sem)
    start_packing(pieces, section_count, routing_ref, cache_ref, cache_out, sem)()
    for copy in query_copies:
        copy.wait()


def pack_kernel(pieces, section_count, routing_ref, cache_ref, *refs):
    cache_out, sem = refs[-1 - len(pieces) : -1], refs[-1]
    start_packing(pieces, section_count, routing_ref, cache_ref, cache_out, sem)()


def merge_kernel(count, *refs):
    for n in range(count):
        refs[-1][n] = refs[n][...]


def merge(parts, others):
    shape = (len(parts),) + parts[0].shape
    return pl.pallas_call(
        functools.partial(merge_kernel, len(parts)),
        out_shape=jax.ShapeDtypeStruct(shape, parts[0].dtype),
        in_specs=[VMEM] * len(parts) + [ANY] * len(others),
        out_specs=VMEM,
        compiler_params=limit(8),
        cost_estimate=cost(3 * 10**9, 8 * len(parts) * parts[0].size),
        name="merge",
    )(*parts, *others)


def in_hbm(value):
    return pltpu.with_memory_space_constraint(value, pltpu.HBM)


def first_pack(routing, cache, queries, others, pieces, section_count):
    shapes = [jax.ShapeDtypeStruct((count,) + cache.shape[2:], cache.dtype) for _, _, count in pieces]
    shapes += query_shapes(queries, range(2), 1)
    parts = pl.pallas_call(
        functools.partial(first_pack_kernel, pieces, section_count),
        out_shape=shapes,
        in_specs=[SMEM, HBM, HBM] + [ANY] * len(others),
        out_specs=[VMEM] * len(shapes),
        scratch_shapes=[
            pltpu.SemaphoreType.DMA((section_count * CAP * 2,)),
            pltpu.SemaphoreType.DMA((2,)),
        ],
        compiler_params=limit(16),
        cost_estimate=cost(0, 4 * sum(shape.size for shape in shapes)),
        name="first_pack",
    )(routing, in_hbm(cache), in_hbm(queries), *others)
    return parts[: len(pieces)], parts[len(pieces) :]


def pack(routing, cache, others, pieces, section_count, flops=0):
    shapes = [jax.ShapeDtypeStruct((count,) + cache.shape[2:], cache.dtype) for _, _, count in pieces]
    return pl.pallas_call(
        functools.partial(pack_kernel, pieces, section_count),
        out_shape=shapes,
        in_specs=[SMEM, HBM] + [ANY] * len(others),
        out_specs=[VMEM] * len(shapes),
        scratch_shapes=[
            pltpu.SemaphoreType.DMA((section_count * CAP * 2,)),
        ],
        compiler_params=limit(16),
        cost_estimate=cost(flops, 4 * sum(shape.size for shape in shapes)),
        name="pack",
    )(routing, in_hbm(cache), *others)


def gate_kernel(*refs):
    pass


def gate(values, others):
    count = len(values)
    return pl.pallas_call(
        gate_kernel,
        out_shape=[jax.ShapeDtypeStruct(value.shape, value.dtype) for value in values],
        in_specs=[ANY] * (count + len(others)),
        out_specs=[ANY] * count,
        input_output_aliases={n: n for n in range(count)},
        compiler_params=limit(1),
        cost_estimate=cost(0, 0),
        name="gate",
    )(*values, *others)


def place_kernel(pieces, *refs):
    count = len(pieces)
    part_refs, out_ref, sem = refs[-2 - count : -2], refs[-2], refs[-1]
    section = lax.axis_index("sec")
    copies = []
    for n, (offset, first, size) in enumerate(pieces):
        for place in range(size):
            half = out_ref.at[0, (section ^ offset) * 2 * CAP + first + place]
            copies.append(pltpu.make_async_copy(part_refs[n].at[place], half, sem.at[len(copies)]))
            copies[-1].start(priority=len(copies) % 2)
    for copy in copies:
        copy.wait()


def place(given, others, parts, pieces, slot_count):
    part = parts[0]
    return pl.pallas_call(
        functools.partial(place_kernel, pieces),
        out_shape=jax.ShapeDtypeStruct((1, 2 * slot_count) + part.shape[1:], part.dtype),
        in_specs=[HBM] * len(given) + [ANY] * len(others) + [VMEM] * len(parts),
        out_specs=HBM,
        scratch_shapes=[pltpu.SemaphoreType.DMA((sum(len(part) for part in parts),))],
        input_output_aliases={0: 0} if given else {},
        compiler_params=limit(8),
        cost_estimate=cost(0, 4 * sum(piece.size for piece in parts)),
        name="place",
    )(*[in_hbm(value) for value in given], *others, *parts)


def attend_kernel(pieces, section_count, tp_count, routing_ref, lengths_ref, *refs):
    cache_refs, refs = refs[: len(pieces)], refs[len(pieces) :]
    query_refs, far_refs = refs[:2], refs[2 : 2 + tp_count]
    message_refs = refs[2 + tp_count : 2 + 2 * tp_count]
    messages, stats, stacked, far_queries = refs[2 + 2 * tp_count :]
    section = lax.axis_index("sec")
    tp_index = lax.axis_index("tp")
    local = cache_refs[0].shape[1]
    groups, rows, _ = messages.shape[1:]
    span = KEY_VALUE_HEADS * rows
    prompts = max(1, groups // KEY_VALUE_HEADS)
    full = section_count * CAP == REQ_GRP
    targets = own_targets(routing_ref, section)
    samples = query_refs[0].shape[1]
    for offset, far_ref in enumerate(far_refs):
        far_queries[tp_index ^ offset] = far_ref[...]
    position = lax.broadcasted_iota(jnp.int32, (local, span), 0) + tp_index * local
    owner = lax.broadcasted_iota(jnp.int32, (HEAD_SIZE, span), 1) // rows

    held = {(offset, half): cache_refs[n].at[place] for n, place, offset, half in halves_of(pieces)}

    def prompt(offset, order):
        keys_ref, values_ref = held[offset, 2 * order], held[offset, 2 * order + 1]
        row, _ = slot_row(targets, section ^ offset, order)
        visible = position < lengths_ref[section * REQ_GRP + row]
        slot = offset * CAP + order
        for head in range(span // samples):
            first, part = head * HEAD_SIZE, far_queries.shape[-1]
            if offset < 2:
                values = query_refs[offset][order, :, first : first + HEAD_SIZE]
            else:
                inner = first % part
                values = far_queries[first // part, offset - 2, order, :, inner : inner + HEAD_SIZE]
            stacked[slot, head * samples : (head + 1) * samples] = values.astype(jnp.float32)
        query = stacked[slot].T.astype(jnp.bfloat16)
        query = [jnp.where(owner == k, query, jnp.zeros_like(query)) for k in range(KEY_VALUE_HEADS)]
        score = jnp.dot(
            keys_ref[...], jnp.concatenate(query, axis=0), preferred_element_type=jnp.float32
        ) * HEAD_SIZE ** (-0.5)
        score = jnp.where(visible, score, HIDDEN)
        peak = jnp.max(score, axis=0, keepdims=True)
        weight = jnp.where(visible, jnp.exp(score - peak), 0.0)
        total = jnp.sum(weight, axis=0, keepdims=True)
        some = total > 0.0
        safe = jnp.where(some, total, 1.0)
        stats[0, pl.ds(row, 1)] = jnp.where(some, peak + jnp.log(safe), HIDDEN)
        weight = (weight * (1.0 / safe)).T.astype(jnp.bfloat16)
        for k in range(KEY_VALUE_HEADS):
            mixed = jnp.dot(
                weight[k * rows : (k + 1) * rows],
                values_ref[:, k * HEAD_SIZE : (k + 1) * HEAD_SIZE],
                preferred_element_type=jnp.float32,
            )
            group = row * KEY_VALUE_HEADS + k
            messages[group // groups, group % groups] = mixed.astype(jnp.bfloat16)

    for offset, half in held:
        if half % 2 == 0:
            one = functools.partial(prompt, offset, half // 2)
            if full:
                one()
            else:
                pl.when(slot_row(targets, section ^ offset, half // 2)[1])(one)

    level = stats[0]
    high = level.astype(jnp.bfloat16).astype(jnp.float32)
    rest = level - high
    middle = rest.astype(jnp.bfloat16).astype(jnp.float32)
    stats[0], stats[1], stats[2] = high, middle, rest - middle
    for offset, message_ref in enumerate(message_refs):
        device = tp_index ^ offset
        for inner in range(groups):
            message_ref[inner * rows : (inner + 1) * rows] = messages[device, inner]
        first = device * groups // KEY_VALUE_HEADS
        lines = [stats[part, pl.ds(first + n, 1)] for part in range(3) for n in range(prompts)]
        lines.append(jnp.zeros((STAT_ROWS - 3 * prompts, span), jnp.float32))
        message_ref[groups * rows :] = jnp.concatenate(lines, axis=0).astype(jnp.bfloat16)


def attend(routing, lengths, caches, pieces, queries, far_queries):
    section_count = len(far_queries[0]) + 2
    tp_count = len(far_queries)
    samples, width = queries[0].shape[1:]
    span = width // HEAD_SIZE * samples
    rows = span // KEY_VALUE_HEADS
    groups = REQ_GRP * KEY_VALUE_HEADS // tp_count
    multiplies = REQ_GRP * span * HEAD_SIZE * caches[0].shape[1]
    return pl.pallas_call(
        functools.partial(attend_kernel, pieces, section_count, tp_count),
        out_shape=[jax.ShapeDtypeStruct((groups * rows + STAT_ROWS, HEAD_SIZE), jnp.bfloat16)] * tp_count,
        in_specs=[SMEM, SMEM] + [VMEM] * (len(caches) + len(queries) + tp_count),
        out_specs=[VMEM] * tp_count,
        scratch_shapes=[
            pltpu.VMEM((tp_count, groups, rows, HEAD_SIZE), jnp.bfloat16),
            pltpu.VMEM((3, REQ_GRP, span), jnp.float32),
            pltpu.VMEM((section_count * CAP, span, HEAD_SIZE), jnp.float32),
            pltpu.VMEM((tp_count,) + far_queries[0].shape, far_queries[0].dtype),
        ],
        compiler_params=limit(12),
        cost_estimate=cost(2 * 10**10, 2 * sum(part.size for part in caches), multiplies // HEAD_SIZE),
        name="attend",
    )(routing, lengths, *caches, *queries, *far_queries)


def join_kernel(count, samples, rows, *refs):
    message_refs, (out_ref, scaling, flat) = refs[:count], refs[-3:]
    groups = (message_refs[0].shape[0] - STAT_ROWS) // rows
    prompts = max(1, groups // KEY_VALUE_HEADS)
    heads = rows // samples
    tp_index = lax.axis_index("tp")
    levels = []
    for ref in message_refs:
        lines = ref[groups * rows :].astype(jnp.float32)[0:8]
        levels.append(lines + pltpu.roll(lines, 8 - prompts, 0) + pltpu.roll(lines, 8 - 2 * prompts, 0))
    summit = functools.reduce(jnp.maximum, levels)
    scales = [jnp.exp(level - summit) for level in levels]
    total = functools.reduce(jnp.add, scales)
    for n, scale in enumerate(scales):
        scaling[n] = (scale / total).T
    for inner in range(groups):
        if groups % KEY_VALUE_HEADS:
            first = (tp_index * groups + inner) % KEY_VALUE_HEADS * rows
            part = pl.ds(pl.multiple_of(first, rows), rows)
        else:
            part = pl.ds(inner % KEY_VALUE_HEADS * rows, rows)
        prompt = inner // KEY_VALUE_HEADS
        terms = [
            ref[inner * rows : (inner + 1) * rows].astype(jnp.float32) * scaling[n, part, prompt : prompt + 1]
            for n, ref in enumerate(message_refs)
        ]
        joined = functools.reduce(jnp.add, terms)
        for head in range(heads):
            block = joined[head * samples : (head + 1) * samples]
            if len(flat.shape) == 2:
                row = prompt * samples
                column = (inner % KEY_VALUE_HEADS * heads + head) * HEAD_SIZE
                flat[row : row + samples, column : column + HEAD_SIZE] = block
            else:
                flat[inner, :, head * HEAD_SIZE : (head + 1) * HEAD_SIZE] = block
    out_ref[...] = flat[...].astype(jnp.bfloat16)


def join(messages, others, samples, heads):
    rows = heads * samples
    groups = (messages[0].shape[0] - STAT_ROWS) // rows
    width = rows // samples * HEAD_SIZE
    if groups % KEY_VALUE_HEADS == 0:
        shape = (groups // KEY_VALUE_HEADS * samples, KEY_VALUE_HEADS * width)
    else:
        shape = (groups, samples, width)
    count = len(messages)
    return pl.pallas_call(
        functools.partial(join_kernel, count, samples, rows),
        out_shape=jax.ShapeDtypeStruct(shape, jnp.bfloat16),
        in_specs=[VMEM] * count + [ANY] * len(others),
        out_specs=VMEM,
        scratch_shapes=[
            pltpu.VMEM((count, KEY_VALUE_HEADS * rows, 8), jnp.float32),
            pltpu.VMEM(shape, jnp.float32),
        ],
        compiler_params=limit(8),
        cost_estimate=cost(4 * count * messages[0].size, 2 * count * messages[0].size),
        name="join",
    )(*messages, *others)


def fetch_kernel(first, weight_ref, *refs):
    out_ref, sem = refs[-2:]
    copies = []
    step = out_ref.shape[0] // sem.shape[0]
    for n in range(sem.shape[0]):
        rows = weight_ref.at[pl.ds(first + n * step, step)]
        copies.append(pltpu.make_async_copy(rows, out_ref.at[pl.ds(n * step, step)], sem.at[n]))
        copies[-1].start(priority=n % 2)
    for copy in copies:
        copy.wait()


def fetch(weight, others, number, count):
    size = weight.shape[0] // count
    return pl.pallas_call(
        functools.partial(fetch_kernel, number * size),
        out_shape=jax.ShapeDtypeStruct((size,) + weight.shape[1:], weight.dtype),
        in_specs=[HBM] + [ANY] * len(others),
        out_specs=VMEM,
        scratch_shapes=[pltpu.SemaphoreType.DMA((8,))],
        compiler_params=limit(24),
        cost_estimate=cost(0, 4 * weight.size // count),
        name="fetch",
    )(in_hbm(weight), *others)


def project_kernel(count, tile, skipped, *refs):
    refs = refs[skipped:]
    part_refs, weight_refs, out_ref = refs[:count], refs[count:-1], refs[-1]
    tp_index = lax.axis_index("tp")
    prompts, samples, width = out_ref.shape
    share = prompts // count
    left = jnp.concatenate([ref[...].astype(jnp.float32) for ref in part_refs], axis=0).astype(jnp.bfloat16)
    size = weight_refs[0].shape[0]
    for first in range(0, width, tile):
        result = functools.reduce(
            jnp.add,
            [
                jnp.dot(
                    left[:, n * size : (n + 1) * size],
                    ref[:, first : first + tile],
                    preferred_element_type=jnp.float32,
                )
                for n, ref in enumerate(weight_refs)
            ],
        )
        for offset in range(count):
            for n in range(share):
                row = (offset * share + n) * samples
                block = result[row : row + samples].astype(out_ref.dtype)
                out_ref[(tp_index ^ offset) * share + n, :, first : first + tile] = block


def project(parts, weights, others, samples):
    count = len(parts)
    depth, width = weights[0].shape
    depth *= len(weights)
    total = count * parts[0].shape[0]
    return pl.pallas_call(
        functools.partial(project_kernel, count, min(256, width), len(others)),
        out_shape=jax.ShapeDtypeStruct((total // samples, samples, width), jnp.bfloat16),
        in_specs=[ANY] * len(others) + [VMEM] * (count + len(weights)),
        out_specs=VMEM,
        compiler_params=limit(24),
        cost_estimate=cost(2 * total * depth * width, 2 * depth * width),
        name="project",
    )(*others, *parts, *weights)


def body(prompt_key_values, queries, routing, lengths, out_weight):
    section_count = lax.axis_size("sec")
    tp_count = lax.axis_size("tp")
    slot_count, samples, query_width = queries.shape[1:]
    routing = routing.reshape(-1)

    whole = 2 * CAP
    near = [(offset, 0, whole) for offset in range(2)]
    head, tail = [(2, 0, 1)], [(2, 1, whole - 1)]
    far = tail + [(offset, 0, whole) for offset in range(3, section_count - 1)]
    far += [(section_count - 1, 0, whole - 1), (section_count - 1, whole - 1, 1)]

    def across(parts, pieces):
        return [swap(part, "sec", piece[0]) for part, piece in zip(parts, pieces)]

    head_caches, far_queries = pack_head(
        routing, prompt_key_values, queries, head[0], section_count, tp_count
    )
    head_parts = across(head_caches, head)
    far_queries = [swap(part, "sec", n + 2) for n, part in enumerate(far_queries)]
    far_caches, query_parts = first_pack(
        routing, prompt_key_values, queries, head_caches, far, section_count
    )
    far_parts = across(far_caches[:-1], far[:-1])
    query_parts = [swap(part, "sec", offset) for offset, part in enumerate(query_parts)]
    merged = merge(far_queries, head_parts)
    far_queries = spread(merged, "tp")
    near_caches = pack(routing, prompt_key_values, [merged, query_parts[1]], near, section_count, 10**10)
    near_parts = across(near_caches, near)
    caches, pieces = [*head_caches, *far_caches, *near_caches], head + far + near

    messages = attend(routing, lengths, caches, pieces, query_parts, far_queries)
    partials = [swap(part, "tp", offset) for offset, part in enumerate(messages)]
    held_weight = [fetch(out_weight, [messages[0], *near_parts[1:]], 0, 2)]
    held_cache = place([], [], near_parts + head_parts, near + head, slot_count)
    share = join(partials, [in_hbm(held_cache), *held_weight, *far_parts[:-1]], samples, query_width // HEAD_SIZE // KEY_VALUE_HEADS)
    far_parts += across(gate(far_caches[-1:], [share]), far[-1:])
    shares = spread(share, "tp")
    held_weight.append(fetch(out_weight, [share], 1, 2))
    if share.ndim == 3:
        attended = jnp.stack(shares)[jnp.arange(tp_count) ^ lax.axis_index("tp")]
        attended = attended.reshape(REQ_GRP, KEY_VALUE_HEADS, samples, -1).transpose(0, 2, 1, 3)
        attended = attended.reshape(REQ_GRP * samples, query_width)
        layer_out = jnp.dot(attended, out_weight, preferred_element_type=jnp.float32)
        layer_out = layer_out.astype(jnp.bfloat16).reshape(REQ_GRP, samples, -1)
    else:
        layer_out = project(shares, held_weight, far_parts[:-2], samples)

    held_cache = place([held_cache], [share], far_parts[:-2], far[:-2], slot_count)
    for part, piece in zip(far_parts[-2:], far[-2:]):
        held_cache = place([held_cache, layer_out], [], [part], [piece], slot_count)
    held_cache = held_cache.reshape((1, slot_count) + prompt_key_values.shape[1:])
    return (layer_out, held_cache)


def solution(mesh):
    placed = (
        P(("rep", "sec"), None, "tp", None),
        P(("rep", "sec"), None, None, None),
        P("rep", None),
        P("rep"),
        P(None, "tp"),
    )
    return jax.shard_map(
        body,
        mesh=mesh,
        in_specs=placed,
        out_specs=(P(("rep", "sec"), None, "tp"), P(("rep", "sec"), None, None, "tp", None)),
        check_vma=False,
    )
```

```python
import functools

import jax
import jax.numpy as jnp
from jax import lax
from jax.experimental import pallas as pl
from jax.experimental.pallas import tpu as pltpu
from jax.sharding import PartitionSpec as P

HEAD_SIZE = 128
KEY_VALUE_HEADS = 4
REQ_GRP = 8
CAP = 2
HIDDEN = -1e30
STAT_ROWS = 16
EARLY_ROWS = 4

ANY = pl.BlockSpec(memory_space=pl.ANY)
HBM = pl.BlockSpec(memory_space=pltpu.HBM)
VMEM = pl.BlockSpec(memory_space=pltpu.VMEM)
SMEM = pl.BlockSpec(memory_space=pltpu.SMEM)


def limit(mebibytes):
    return pltpu.CompilerParams(vmem_limit_bytes=mebibytes << 20)


def cost(flops, bytes_accessed, transcendentals=0):
    return pl.CostEstimate(flops=flops, bytes_accessed=bytes_accessed, transcendentals=transcendentals)


def swap(value, axis, offset):
    if offset == 0:
        return value
    count = lax.axis_size(axis)
    return lax.ppermute(value, axis, [(i, i ^ offset) for i in range(count)])


def spread(value, axis):
    return [swap(value, axis, offset) for offset in range(lax.axis_size(axis))]


def own_targets(routing_ref, section):
    return [routing_ref[section * REQ_GRP + i] for i in range(REQ_GRP)]


def slot_row(targets, group, order):
    row, before = jnp.int32(0), jnp.int32(0)
    for i, target in enumerate(targets):
        here = target == group
        row = jnp.where(here & (before == order), i, row)
        before = before + here.astype(jnp.int32)
    return row, before > order


def halves_of(pieces):
    return [
        (n, place, offset, first + place)
        for n, (offset, first, count) in enumerate(pieces)
        for place in range(count)
    ]


def start_packing(pieces, section_count, routing_ref, cache_ref, out_refs, sem):
    section = lax.axis_index("sec")
    full = section_count * CAP == REQ_GRP
    targets = own_targets(routing_ref, section)
    halves = halves_of(pieces)
    slots = {(offset, half // 2) for _, _, offset, half in halves}
    rows = {slot: slot_row(targets, section ^ slot[0], slot[1]) for slot in sorted(slots)}

    def copy(n, place, offset, half):
        row, _ = rows[offset, half // 2]
        return pltpu.make_async_copy(
            cache_ref.at[row, half % 2], out_refs[n].at[place], sem.at[offset * 2 * CAP + half]
        )

    for n, place, offset, half in halves:
        if full:
            copy(n, place, offset, half).start()
        else:
            _, filled = rows[offset, half // 2]

            @pl.when(filled)
            def _():
                copy(n, place, offset, half).start()

            @pl.when(jnp.logical_not(filled))
            def _():
                out_refs[n][place] = jnp.zeros_like(out_refs[n][place])

    def finish():
        for n, place, offset, half in halves:
            if full:
                copy(n, place, offset, half).wait()
            else:
                pl.when(rows[offset, half // 2][1])(copy(n, place, offset, half).wait)

    return finish


def start_queries(query_ref, out_refs, offsets, sem):
    section = lax.axis_index("sec")
    copies = []
    for n, (offset, out_ref) in enumerate(zip(offsets, out_refs)):
        width = out_ref.shape[2]
        columns = pl.ds(pl.multiple_of(lax.axis_index("tp") * width, width) if offset > 1 else 0, width)
        part = query_ref.at[0, pl.ds((section ^ offset) * CAP, CAP), :, columns]
        copies.append(pltpu.make_async_copy(part, out_ref, sem.at[n]))
        copies[-1].start()
    return copies


def query_shapes(queries, offsets, tp_count):
    samples, width = queries.shape[2:]
    widths = [width if offset < 2 else width // tp_count for offset in offsets]
    return [jax.ShapeDtypeStruct((CAP, samples, one), queries.dtype) for one in widths]


def head_kernel(piece, offsets, full, routing_ref, cache_ref, query_ref, *refs):
    out_ref, query_out, (routed, held, routing_sem, sem, query_sem) = refs[0], refs[1:-5], refs[-5:]
    offset, half, _ = piece
    section = lax.axis_index("sec")
    copies = [pltpu.make_async_copy(routing_ref, routed, routing_sem)]
    for i in range(EARLY_ROWS):
        copies.append(pltpu.make_async_copy(cache_ref.at[i, half % 2], held.at[i], sem.at[i]))
    for copy in copies:
        copy.start()
    query_copies = start_queries(query_ref, query_out, offsets, query_sem)
    copies[0].wait()
    row, filled = slot_row(own_targets(routed, section), section ^ offset, half // 2)
    wanted = pltpu.make_async_copy(cache_ref.at[row, half % 2], held.at[row], sem.at[row])
    pl.when(row >= EARLY_ROWS)(wanted.start)
    wanted.wait()
    block = min(32, held.shape[1])
    for first in range(0, held.shape[1], block):
        chosen = held[row, first : first + block]
        out_ref[0, first : first + block] = chosen if full else jnp.where(filled, chosen, jnp.zeros_like(chosen))
    for i, copy in enumerate(copies[1:]):
        pl.when(i != row)(copy.wait)
    for copy in query_copies:
        copy.wait()


def pack_head(routing, cache, queries, piece, section_count, tp_count):
    shape = cache.shape[2:]
    offsets = range(2, section_count)
    shapes = [jax.ShapeDtypeStruct((1,) + shape, cache.dtype)] + query_shapes(queries, offsets, tp_count)
    head, *parts = pl.pallas_call(
        functools.partial(head_kernel, piece, offsets, section_count * CAP == REQ_GRP),
        out_shape=shapes,
        in_specs=[HBM, HBM, HBM],
        out_specs=[VMEM] * len(shapes),
        scratch_shapes=[
            pltpu.SMEM(routing.shape, jnp.int32),
            pltpu.VMEM((REQ_GRP,) + shape, cache.dtype),
            pltpu.SemaphoreType.DMA,
            pltpu.SemaphoreType.DMA((REQ_GRP,)),
            pltpu.SemaphoreType.DMA((section_count,)),
        ],
        compiler_params=limit(16),
        cost_estimate=cost(0, cache.size),
        name="pack_head",
    )(in_hbm(routing), in_hbm(cache), in_hbm(queries))
    return [head], parts


def first_pack_kernel(pieces, section_count, routing_ref, cache_ref, query_ref, *refs):
    refs, (sem, query_sem) = refs[:-2], refs[-2:]
    query_out, cache_out = refs[-2:], refs[-2 - len(pieces) : -2]
    query_copies = start_queries(query_ref, query_out, range(2), query_sem)
    start_packing(pieces, section_count, routing_ref, cache_ref, cache_out, sem)()
    for copy in query_copies:
        copy.wait()


def pack_kernel(pieces, section_count, routing_ref, cache_ref, *refs):
    cache_out, sem = refs[-1 - len(pieces) : -1], refs[-1]
    start_packing(pieces, section_count, routing_ref, cache_ref, cache_out, sem)()


def merge_kernel(count, *refs):
    for n in range(count):
        refs[-1][n] = refs[n][...]


def merge(parts, others):
    shape = (len(parts),) + parts[0].shape
    return pl.pallas_call(
        functools.partial(merge_kernel, len(parts)),
        out_shape=jax.ShapeDtypeStruct(shape, parts[0].dtype),
        in_specs=[VMEM] * len(parts) + [ANY] * len(others),
        out_specs=VMEM,
        compiler_params=limit(8),
        cost_estimate=cost(3 * 10**9, 8 * len(parts) * parts[0].size),
        name="merge",
    )(*parts, *others)


def in_hbm(value):
    return pltpu.with_memory_space_constraint(value, pltpu.HBM)


def first_pack(routing, cache, queries, others, pieces, section_count):
    shapes = [jax.ShapeDtypeStruct((count,) + cache.shape[2:], cache.dtype) for _, _, count in pieces]
    shapes += query_shapes(queries, range(2), 1)
    parts = pl.pallas_call(
        functools.partial(first_pack_kernel, pieces, section_count),
        out_shape=shapes,
        in_specs=[SMEM, HBM, HBM] + [ANY] * len(others),
        out_specs=[VMEM] * len(shapes),
        scratch_shapes=[
            pltpu.SemaphoreType.DMA((section_count * CAP * 2,)),
            pltpu.SemaphoreType.DMA((2,)),
        ],
        compiler_params=limit(16),
        cost_estimate=cost(0, 4 * sum(shape.size for shape in shapes)),
        name="first_pack",
    )(routing, in_hbm(cache), in_hbm(queries), *others)
    return parts[: len(pieces)], parts[len(pieces) :]


def pack(routing, cache, others, pieces, section_count, flops=0):
    shapes = [jax.ShapeDtypeStruct((count,) + cache.shape[2:], cache.dtype) for _, _, count in pieces]
    return pl.pallas_call(
        functools.partial(pack_kernel, pieces, section_count),
        out_shape=shapes,
        in_specs=[SMEM, HBM] + [ANY] * len(others),
        out_specs=[VMEM] * len(shapes),
        scratch_shapes=[
            pltpu.SemaphoreType.DMA((section_count * CAP * 2,)),
        ],
        compiler_params=limit(16),
        cost_estimate=cost(flops, 4 * sum(shape.size for shape in shapes)),
        name="pack",
    )(routing, in_hbm(cache), *others)


def gate_kernel(*refs):
    pass


def gate(values, others):
    count = len(values)
    return pl.pallas_call(
        gate_kernel,
        out_shape=[jax.ShapeDtypeStruct(value.shape, value.dtype) for value in values],
        in_specs=[ANY] * (count + len(others)),
        out_specs=[ANY] * count,
        input_output_aliases={n: n for n in range(count)},
        compiler_params=limit(1),
        cost_estimate=cost(0, 0),
        name="gate",
    )(*values, *others)


def place_kernel(pieces, *refs):
    count = len(pieces)
    part_refs, out_ref, sem = refs[-2 - count : -2], refs[-2], refs[-1]
    section = lax.axis_index("sec")
    copies = []
    for n, (offset, first, size) in enumerate(pieces):
        for place in range(size):
            half = out_ref.at[0, (section ^ offset) * 2 * CAP + first + place]
            copies.append(pltpu.make_async_copy(part_refs[n].at[place], half, sem.at[len(copies)]))
            copies[-1].start()
    for copy in copies:
        copy.wait()


def place(given, others, parts, pieces, slot_count):
    part = parts[0]
    return pl.pallas_call(
        functools.partial(place_kernel, pieces),
        out_shape=jax.ShapeDtypeStruct((1, 2 * slot_count) + part.shape[1:], part.dtype),
        in_specs=[HBM] * len(given) + [ANY] * len(others) + [VMEM] * len(parts),
        out_specs=HBM,
        scratch_shapes=[pltpu.SemaphoreType.DMA((sum(len(part) for part in parts),))],
        input_output_aliases={0: 0} if given else {},
        compiler_params=limit(8),
        cost_estimate=cost(0, 4 * sum(piece.size for piece in parts)),
        name="place",
    )(*[in_hbm(value) for value in given], *others, *parts)


def attend_kernel(pieces, section_count, tp_count, routing_ref, lengths_ref, *refs):
    cache_refs, refs = refs[: len(pieces)], refs[len(pieces) :]
    query_refs, far_refs = refs[:2], refs[2 : 2 + tp_count]
    message_refs = refs[2 + tp_count : 2 + 2 * tp_count]
    messages, stats, stacked, far_queries = refs[2 + 2 * tp_count :]
    section = lax.axis_index("sec")
    tp_index = lax.axis_index("tp")
    local = cache_refs[0].shape[1]
    groups, rows, _ = messages.shape[1:]
    span = KEY_VALUE_HEADS * rows
    prompts = max(1, groups // KEY_VALUE_HEADS)
    full = section_count * CAP == REQ_GRP
    targets = own_targets(routing_ref, section)
    samples = query_refs[0].shape[1]
    for offset, far_ref in enumerate(far_refs):
        far_queries[tp_index ^ offset] = far_ref[...]
    position = lax.broadcasted_iota(jnp.int32, (local, span), 0) + tp_index * local
    owner = lax.broadcasted_iota(jnp.int32, (HEAD_SIZE, span), 1) // rows

    held = {(offset, half): cache_refs[n].at[place] for n, place, offset, half in halves_of(pieces)}

    def prompt(offset, order):
        keys_ref, values_ref = held[offset, 2 * order], held[offset, 2 * order + 1]
        row, _ = slot_row(targets, section ^ offset, order)
        visible = position < lengths_ref[section * REQ_GRP + row]
        slot = offset * CAP + order
        for head in range(span // samples):
            first, part = head * HEAD_SIZE, far_queries.shape[-1]
            if offset < 2:
                values = query_refs[offset][order, :, first : first + HEAD_SIZE]
            else:
                inner = first % part
                values = far_queries[first // part, offset - 2, order, :, inner : inner + HEAD_SIZE]
            stacked[slot, head * samples : (head + 1) * samples] = values.astype(jnp.float32)
        query = stacked[slot].T.astype(jnp.bfloat16)
        query = [jnp.where(owner == k, query, jnp.zeros_like(query)) for k in range(KEY_VALUE_HEADS)]
        score = jnp.dot(
            keys_ref[...], jnp.concatenate(query, axis=0), preferred_element_type=jnp.float32
        ) * HEAD_SIZE ** (-0.5)
        score = jnp.where(visible, score, HIDDEN)
        peak = jnp.max(score, axis=0, keepdims=True)
        weight = jnp.where(visible, jnp.exp(score - peak), 0.0)
        total = jnp.sum(weight, axis=0, keepdims=True)
        some = total > 0.0
        safe = jnp.where(some, total, 1.0)
        stats[0, pl.ds(row, 1)] = jnp.where(some, peak + jnp.log(safe), HIDDEN)
        weight = (weight * (1.0 / safe)).T.astype(jnp.bfloat16)
        for k in range(KEY_VALUE_HEADS):
            mixed = jnp.dot(
                weight[k * rows : (k + 1) * rows],
                values_ref[:, k * HEAD_SIZE : (k + 1) * HEAD_SIZE],
                preferred_element_type=jnp.float32,
            )
            group = row * KEY_VALUE_HEADS + k
            messages[group // groups, group % groups] = mixed.astype(jnp.bfloat16)

    for offset, half in held:
        if half % 2 == 0:
            one = functools.partial(prompt, offset, half // 2)
            if full:
                one()
            else:
                pl.when(slot_row(targets, section ^ offset, half // 2)[1])(one)

    level = stats[0]
    high = level.astype(jnp.bfloat16).astype(jnp.float32)
    rest = level - high
    middle = rest.astype(jnp.bfloat16).astype(jnp.float32)
    stats[0], stats[1], stats[2] = high, middle, rest - middle
    for offset, message_ref in enumerate(message_refs):
        device = tp_index ^ offset
        for inner in range(groups):
            message_ref[inner * rows : (inner + 1) * rows] = messages[device, inner]
        first = device * groups // KEY_VALUE_HEADS
        lines = [stats[part, pl.ds(first + n, 1)] for part in range(3) for n in range(prompts)]
        lines.append(jnp.zeros((STAT_ROWS - 3 * prompts, span), jnp.float32))
        message_ref[groups * rows :] = jnp.concatenate(lines, axis=0).astype(jnp.bfloat16)


def attend(routing, lengths, caches, pieces, queries, far_queries):
    section_count = len(far_queries[0]) + 2
    tp_count = len(far_queries)
    samples, width = queries[0].shape[1:]
    span = width // HEAD_SIZE * samples
    rows = span // KEY_VALUE_HEADS
    groups = REQ_GRP * KEY_VALUE_HEADS // tp_count
    multiplies = REQ_GRP * span * HEAD_SIZE * caches[0].shape[1]
    return pl.pallas_call(
        functools.partial(attend_kernel, pieces, section_count, tp_count),
        out_shape=[jax.ShapeDtypeStruct((groups * rows + STAT_ROWS, HEAD_SIZE), jnp.bfloat16)] * tp_count,
        in_specs=[SMEM, SMEM] + [VMEM] * (len(caches) + len(queries) + tp_count),
        out_specs=[VMEM] * tp_count,
        scratch_shapes=[
            pltpu.VMEM((tp_count, groups, rows, HEAD_SIZE), jnp.bfloat16),
            pltpu.VMEM((3, REQ_GRP, span), jnp.float32),
            pltpu.VMEM((section_count * CAP, span, HEAD_SIZE), jnp.float32),
            pltpu.VMEM((tp_count,) + far_queries[0].shape, far_queries[0].dtype),
        ],
        compiler_params=limit(12),
        cost_estimate=cost(2 * 10**10, 2 * sum(part.size for part in caches), multiplies // HEAD_SIZE),
        name="attend",
    )(routing, lengths, *caches, *queries, *far_queries)


def join_kernel(count, samples, rows, *refs):
    message_refs, (out_ref, scaling, flat) = refs[:count], refs[-3:]
    groups = (message_refs[0].shape[0] - STAT_ROWS) // rows
    prompts = max(1, groups // KEY_VALUE_HEADS)
    heads = rows // samples
    tp_index = lax.axis_index("tp")
    levels = []
    for ref in message_refs:
        lines = ref[groups * rows :].astype(jnp.float32)[0:8]
        levels.append(lines + pltpu.roll(lines, 8 - prompts, 0) + pltpu.roll(lines, 8 - 2 * prompts, 0))
    summit = functools.reduce(jnp.maximum, levels)
    scales = [jnp.exp(level - summit) for level in levels]
    total = functools.reduce(jnp.add, scales)
    for n, scale in enumerate(scales):
        scaling[n] = (scale / total).T
    for inner in range(groups):
        if groups % KEY_VALUE_HEADS:
            first = (tp_index * groups + inner) % KEY_VALUE_HEADS * rows
            part = pl.ds(pl.multiple_of(first, rows), rows)
        else:
            part = pl.ds(inner % KEY_VALUE_HEADS * rows, rows)
        prompt = inner // KEY_VALUE_HEADS
        terms = [
            ref[inner * rows : (inner + 1) * rows].astype(jnp.float32) * scaling[n, part, prompt : prompt + 1]
            for n, ref in enumerate(message_refs)
        ]
        joined = functools.reduce(jnp.add, terms)
        for head in range(heads):
            block = joined[head * samples : (head + 1) * samples]
            if len(flat.shape) == 2:
                row = prompt * samples
                column = (inner % KEY_VALUE_HEADS * heads + head) * HEAD_SIZE
                flat[row : row + samples, column : column + HEAD_SIZE] = block
            else:
                flat[inner, :, head * HEAD_SIZE : (head + 1) * HEAD_SIZE] = block
    out_ref[...] = flat[...].astype(jnp.bfloat16)


def join(messages, others, samples, heads):
    rows = heads * samples
    groups = (messages[0].shape[0] - STAT_ROWS) // rows
    width = rows // samples * HEAD_SIZE
    if groups % KEY_VALUE_HEADS == 0:
        shape = (groups // KEY_VALUE_HEADS * samples, KEY_VALUE_HEADS * width)
    else:
        shape = (groups, samples, width)
    count = len(messages)
    return pl.pallas_call(
        functools.partial(join_kernel, count, samples, rows),
        out_shape=jax.ShapeDtypeStruct(shape, jnp.bfloat16),
        in_specs=[VMEM] * count + [ANY] * len(others),
        out_specs=VMEM,
        scratch_shapes=[
            pltpu.VMEM((count, KEY_VALUE_HEADS * rows, 8), jnp.float32),
            pltpu.VMEM(shape, jnp.float32),
        ],
        compiler_params=limit(8),
        cost_estimate=cost(4 * count * messages[0].size, 2 * count * messages[0].size),
        name="join",
    )(*messages, *others)


def fetch_kernel(first, weight_ref, *refs):
    out_ref, sem = refs[-2:]
    copies = []
    step = out_ref.shape[0] // sem.shape[0]
    for n in range(sem.shape[0]):
        rows = weight_ref.at[pl.ds(first + n * step, step)]
        copies.append(pltpu.make_async_copy(rows, out_ref.at[pl.ds(n * step, step)], sem.at[n]))
        copies[-1].start()
    for copy in copies:
        copy.wait()


def fetch(weight, others, number, count):
    size = weight.shape[0] // count
    return pl.pallas_call(
        functools.partial(fetch_kernel, number * size),
        out_shape=jax.ShapeDtypeStruct((size,) + weight.shape[1:], weight.dtype),
        in_specs=[HBM] + [ANY] * len(others),
        out_specs=VMEM,
        scratch_shapes=[pltpu.SemaphoreType.DMA((8,))],
        compiler_params=limit(24),
        cost_estimate=cost(0, 4 * weight.size // count),
        name="fetch",
    )(in_hbm(weight), *others)


def project_kernel(count, tile, skipped, *refs):
    refs = refs[skipped:]
    part_refs, weight_refs, out_ref = refs[:count], refs[count:-1], refs[-1]
    tp_index = lax.axis_index("tp")
    prompts, samples, width = out_ref.shape
    share = prompts // count
    left = jnp.concatenate([ref[...].astype(jnp.float32) for ref in part_refs], axis=0).astype(jnp.bfloat16)
    size = weight_refs[0].shape[0]
    for first in range(0, width, tile):
        result = functools.reduce(
            jnp.add,
            [
                jnp.dot(
                    left[:, n * size : (n + 1) * size],
                    ref[:, first : first + tile],
                    preferred_element_type=jnp.float32,
                )
                for n, ref in enumerate(weight_refs)
            ],
        )
        for offset in range(count):
            for n in range(share):
                row = (offset * share + n) * samples
                block = result[row : row + samples].astype(out_ref.dtype)
                out_ref[(tp_index ^ offset) * share + n, :, first : first + tile] = block


def project(parts, weights, others, samples):
    count = len(parts)
    depth, width = weights[0].shape
    depth *= len(weights)
    total = count * parts[0].shape[0]
    return pl.pallas_call(
        functools.partial(project_kernel, count, min(256, width), len(others)),
        out_shape=jax.ShapeDtypeStruct((total // samples, samples, width), jnp.bfloat16),
        in_specs=[ANY] * len(others) + [VMEM] * (count + len(weights)),
        out_specs=VMEM,
        compiler_params=limit(24),
        cost_estimate=cost(2 * total * depth * width, 2 * depth * width),
        name="project",
    )(*others, *parts, *weights)


def body(prompt_key_values, queries, routing, lengths, out_weight):
    section_count = lax.axis_size("sec")
    tp_count = lax.axis_size("tp")
    slot_count, samples, query_width = queries.shape[1:]
    routing = routing.reshape(-1)

    whole = 2 * CAP
    near = [(offset, 0, whole) for offset in range(2)]
    head, tail = [(2, 0, 1)], [(2, 1, whole - 1)]
    far = tail + [(offset, 0, whole) for offset in range(3, section_count - 1)]
    far += [(section_count - 1, 0, whole - 1), (section_count - 1, whole - 1, 1)]

    def across(parts, pieces):
        return [swap(part, "sec", piece[0]) for part, piece in zip(parts, pieces)]

    head_caches, far_queries = pack_head(
        routing, prompt_key_values, queries, head[0], section_count, tp_count
    )
    head_parts = across(head_caches, head)
    far_queries = [swap(part, "sec", n + 2) for n, part in enumerate(far_queries)]
    far_caches, query_parts = first_pack(
        routing, prompt_key_values, queries, head_caches, far, section_count
    )
    far_parts = across(far_caches[:-1], far[:-1])
    query_parts = [swap(part, "sec", offset) for offset, part in enumerate(query_parts)]
    merged = merge(far_queries, head_parts)
    far_queries = spread(merged, "tp")
    near_caches = pack(routing, prompt_key_values, [merged, query_parts[1]], near, section_count, 10**10)
    near_parts = across(near_caches, near)
    caches, pieces = [*head_caches, *far_caches, *near_caches], head + far + near

    messages = attend(routing, lengths, caches, pieces, query_parts, far_queries)
    partials = [swap(part, "tp", offset) for offset, part in enumerate(messages)]
    held_weight = [fetch(out_weight, [messages[0], *near_parts[1:]], 0, 2)]
    held_cache = place([], [], near_parts + head_parts, near + head, slot_count)
    share = join(partials, [in_hbm(held_cache), *held_weight, *far_parts[:-1]], samples, query_width // HEAD_SIZE // KEY_VALUE_HEADS)
    far_parts += across(gate(far_caches[-1:], [share]), far[-1:])
    shares = spread(share, "tp")
    held_weight.append(fetch(out_weight, [share], 1, 2))
    if share.ndim == 3:
        attended = jnp.stack(shares)[jnp.arange(tp_count) ^ lax.axis_index("tp")]
        attended = attended.reshape(REQ_GRP, KEY_VALUE_HEADS, samples, -1).transpose(0, 2, 1, 3)
        attended = attended.reshape(REQ_GRP * samples, query_width)
        layer_out = jnp.dot(attended, out_weight, preferred_element_type=jnp.float32)
        layer_out = layer_out.astype(jnp.bfloat16).reshape(REQ_GRP, samples, -1)
    else:
        layer_out = project(shares, held_weight, far_parts[:-2], samples)

    held_cache = place([held_cache], [share], far_parts[:-2], far[:-2], slot_count)
    for part, piece in zip(far_parts[-2:], far[-2:]):
        held_cache = place([held_cache, layer_out], [], [part], [piece], slot_count)
    held_cache = held_cache.reshape((1, slot_count) + prompt_key_values.shape[1:])
    return (layer_out, held_cache)


def solution(mesh):
    placed = (
        P(("rep", "sec"), None, "tp", None),
        P(("rep", "sec"), None, None, None),
        P("rep", None),
        P("rep"),
        P(None, "tp"),
    )
    return jax.shard_map(
        body,
        mesh=mesh,
        in_specs=placed,
        out_specs=(P(("rep", "sec"), None, "tp"), P(("rep", "sec"), None, None, "tp", None)),
        check_vma=False,
    )
```

```python
import functools

import jax
import jax.numpy as jnp
from jax import lax
from jax.experimental import pallas as pl
from jax.experimental.pallas import tpu as pltpu
from jax.sharding import PartitionSpec as P

HEAD_SIZE = 128
KEY_VALUE_HEADS = 4
REQ_GRP = 8
CAP = 2
HIDDEN = -1e30
STAT_ROWS = 16

ANY = pl.BlockSpec(memory_space=pl.ANY)
HBM = pl.BlockSpec(memory_space=pltpu.HBM)
VMEM = pl.BlockSpec(memory_space=pltpu.VMEM)
SMEM = pl.BlockSpec(memory_space=pltpu.SMEM)


def limit(mebibytes):
    return pltpu.CompilerParams(vmem_limit_bytes=mebibytes << 20)


def cost(flops, bytes_accessed, transcendentals=0):
    return pl.CostEstimate(flops=flops, bytes_accessed=bytes_accessed, transcendentals=transcendentals)


def swap(value, axis, offset):
    if offset == 0:
        return value
    count = lax.axis_size(axis)
    return lax.ppermute(value, axis, [(i, i ^ offset) for i in range(count)])


def spread(value, axis):
    return [swap(value, axis, offset) for offset in range(lax.axis_size(axis))]


def own_targets(routing_ref, section):
    return [routing_ref[section * REQ_GRP + i] for i in range(REQ_GRP)]


def slot_row(targets, group, order):
    row, before = jnp.int32(0), jnp.int32(0)
    for i, target in enumerate(targets):
        here = target == group
        row = jnp.where(here & (before == order), i, row)
        before = before + here.astype(jnp.int32)
    return row, before > order


def halves_of(pieces):
    return [
        (n, place, offset, first + place)
        for n, (offset, first, count) in enumerate(pieces)
        for place in range(count)
    ]


def start_packing(pieces, section_count, routing_ref, cache_ref, out_refs, sem):
    section = lax.axis_index("sec")
    full = section_count * CAP == REQ_GRP
    targets = own_targets(routing_ref, section)
    halves = halves_of(pieces)
    slots = {(offset, half // 2) for _, _, offset, half in halves}
    rows = {slot: slot_row(targets, section ^ slot[0], slot[1]) for slot in sorted(slots)}

    def copy(n, place, offset, half):
        row, _ = rows[offset, half // 2]
        return pltpu.make_async_copy(
            cache_ref.at[row, half % 2], out_refs[n].at[place], sem.at[offset * 2 * CAP + half]
        )

    for n, place, offset, half in halves:
        if full:
            copy(n, place, offset, half).start()
        else:
            _, filled = rows[offset, half // 2]

            @pl.when(filled)
            def _():
                copy(n, place, offset, half).start()

            @pl.when(jnp.logical_not(filled))
            def _():
                out_refs[n][place] = jnp.zeros_like(out_refs[n][place])

    def finish():
        for n, place, offset, half in halves:
            if full:
                copy(n, place, offset, half).wait()
            else:
                pl.when(rows[offset, half // 2][1])(copy(n, place, offset, half).wait)

    return finish


def start_queries(query_ref, out_refs, offsets, sem):
    section = lax.axis_index("sec")
    copies = []
    for n, (offset, out_ref) in enumerate(zip(offsets, out_refs)):
        width = out_ref.shape[2]
        columns = pl.ds(pl.multiple_of(lax.axis_index("tp") * width, width) if offset > 1 else 0, width)
        part = query_ref.at[0, pl.ds((section ^ offset) * CAP, CAP), :, columns]
        copies.append(pltpu.make_async_copy(part, out_ref, sem.at[n]))
        copies[-1].start()
    return copies


def query_shapes(queries, offsets, tp_count):
    samples, width = queries.shape[2:]
    widths = [width if offset < 2 else width // tp_count for offset in offsets]
    return [jax.ShapeDtypeStruct((CAP, samples, one), queries.dtype) for one in widths]


def head_kernel(piece, offsets, full, routing_ref, cache_ref, query_ref, *refs):
    out_ref, query_out, (routed, held, routing_sem, sem, query_sem) = refs[0], refs[1:-5], refs[-5:]
    offset, half, _ = piece
    section = lax.axis_index("sec")
    copies = [pltpu.make_async_copy(routing_ref, routed, routing_sem)]
    for i in range(REQ_GRP - CAP + 1 if full and half < 2 else REQ_GRP):
        copies.append(pltpu.make_async_copy(cache_ref.at[i, half % 2], held.at[i], sem.at[i]))
    for copy in copies:
        copy.start()
    query_copies = start_queries(query_ref, query_out, offsets, query_sem)
    copies[0].wait()
    row, filled = slot_row(own_targets(routed, section), section ^ offset, half // 2)
    for copy in copies[1:] + query_copies:
        copy.wait()
    block = min(32, held.shape[1])
    for first in range(0, held.shape[1], block):
        chosen = held[row, first : first + block]
        out_ref[0, first : first + block] = chosen if full else jnp.where(filled, chosen, jnp.zeros_like(chosen))


def pack_head(routing, cache, queries, piece, section_count, tp_count):
    shape = cache.shape[2:]
    offsets = range(1, section_count)
    shapes = [jax.ShapeDtypeStruct((1,) + shape, cache.dtype)] + query_shapes(queries, offsets, tp_count)
    head, *parts = pl.pallas_call(
        functools.partial(head_kernel, piece, offsets, section_count * CAP == REQ_GRP),
        out_shape=shapes,
        in_specs=[HBM, HBM, HBM],
        out_specs=[VMEM] * len(shapes),
        scratch_shapes=[
            pltpu.SMEM(routing.shape, jnp.int32),
            pltpu.VMEM((REQ_GRP,) + shape, cache.dtype),
            pltpu.SemaphoreType.DMA,
            pltpu.SemaphoreType.DMA((REQ_GRP,)),
            pltpu.SemaphoreType.DMA((section_count,)),
        ],
        compiler_params=limit(16),
        cost_estimate=cost(0, cache.size),
        name="pack_head",
    )(in_hbm(routing), in_hbm(cache), in_hbm(queries))
    return [head], parts


def first_pack_kernel(pieces, section_count, routing_ref, cache_ref, query_ref, *refs):
    refs, (sem, query_sem) = refs[:-2], refs[-2:]
    query_out, cache_out = refs[-1:], refs[-1 - len(pieces) : -1]
    query_copies = start_queries(query_ref, query_out, range(1), query_sem)
    start_packing(pieces, section_count, routing_ref, cache_ref, cache_out, sem)()
    for copy in query_copies:
        copy.wait()


def pack_kernel(pieces, section_count, routing_ref, cache_ref, *refs):
    cache_out, sem = refs[-1 - len(pieces) : -1], refs[-1]
    start_packing(pieces, section_count, routing_ref, cache_ref, cache_out, sem)()


def merge_kernel(count, *refs):
    for n in range(count):
        refs[-1][n] = refs[n][...]


def merge(parts, others):
    shape = (len(parts),) + parts[0].shape
    return pl.pallas_call(
        functools.partial(merge_kernel, len(parts)),
        out_shape=jax.ShapeDtypeStruct(shape, parts[0].dtype),
        in_specs=[VMEM] * len(parts) + [ANY] * len(others),
        out_specs=VMEM,
        compiler_params=limit(8),
        cost_estimate=cost(3 * 10**9, 8 * len(parts) * parts[0].size),
        name="merge",
    )(*parts, *others)


def in_hbm(value):
    return pltpu.with_memory_space_constraint(value, pltpu.HBM)


def first_pack(routing, cache, queries, others, pieces, section_count):
    shapes = [jax.ShapeDtypeStruct((count,) + cache.shape[2:], cache.dtype) for _, _, count in pieces]
    shapes += query_shapes(queries, range(1), 1)
    parts = pl.pallas_call(
        functools.partial(first_pack_kernel, pieces, section_count),
        out_shape=shapes,
        in_specs=[SMEM, HBM, HBM] + [ANY] * len(others),
        out_specs=[VMEM] * len(shapes),
        scratch_shapes=[
            pltpu.SemaphoreType.DMA((section_count * CAP * 2,)),
            pltpu.SemaphoreType.DMA((2,)),
        ],
        compiler_params=limit(16),
        cost_estimate=cost(0, 4 * sum(shape.size for shape in shapes)),
        name="first_pack",
    )(routing, in_hbm(cache), in_hbm(queries), *others)
    return parts[: len(pieces)], parts[len(pieces) :]


def pack(routing, cache, others, pieces, section_count, flops=0):
    shapes = [jax.ShapeDtypeStruct((count,) + cache.shape[2:], cache.dtype) for _, _, count in pieces]
    return pl.pallas_call(
        functools.partial(pack_kernel, pieces, section_count),
        out_shape=shapes,
        in_specs=[SMEM, HBM] + [ANY] * len(others),
        out_specs=[VMEM] * len(shapes),
        scratch_shapes=[
            pltpu.SemaphoreType.DMA((section_count * CAP * 2,)),
        ],
        compiler_params=limit(16),
        cost_estimate=cost(flops, 4 * sum(shape.size for shape in shapes)),
        name="pack",
    )(routing, in_hbm(cache), *others)


def gate_kernel(*refs):
    pass


def gate(values, others):
    count = len(values)
    return pl.pallas_call(
        gate_kernel,
        out_shape=[jax.ShapeDtypeStruct(value.shape, value.dtype) for value in values],
        in_specs=[ANY] * (count + len(others)),
        out_specs=[ANY] * count,
        input_output_aliases={n: n for n in range(count)},
        compiler_params=limit(1),
        cost_estimate=cost(0, 0),
        name="gate",
    )(*values, *others)


def place_kernel(pieces, *refs):
    count = len(pieces)
    part_refs, out_ref, sem = refs[-2 - count : -2], refs[-2], refs[-1]
    section = lax.axis_index("sec")
    copies = []
    for n, (offset, first, size) in enumerate(pieces):
        for place in range(size):
            half = out_ref.at[0, (section ^ offset) * 2 * CAP + first + place]
            copies.append(pltpu.make_async_copy(part_refs[n].at[place], half, sem.at[len(copies)]))
            copies[-1].start()
    for copy in copies:
        copy.wait()


def place(given, others, parts, pieces, slot_count):
    part = parts[0]
    return pl.pallas_call(
        functools.partial(place_kernel, pieces),
        out_shape=jax.ShapeDtypeStruct((1, 2 * slot_count) + part.shape[1:], part.dtype),
        in_specs=[HBM] * len(given) + [ANY] * len(others) + [VMEM] * len(parts),
        out_specs=HBM,
        scratch_shapes=[pltpu.SemaphoreType.DMA((sum(len(part) for part in parts),))],
        input_output_aliases={0: 0} if given else {},
        compiler_params=limit(8),
        cost_estimate=cost(0, 4 * sum(piece.size for piece in parts)),
        name="place",
    )(*[in_hbm(value) for value in given], *others, *parts)


def attend_kernel(pieces, section_count, tp_count, routing_ref, lengths_ref, *refs):
    cache_refs, refs = refs[: len(pieces)], refs[len(pieces) :]
    query_refs, far_refs = refs[:2], refs[2 : 2 + tp_count]
    message_refs = refs[2 + tp_count : 2 + 2 * tp_count]
    messages, stats, stacked, far_queries = refs[2 + 2 * tp_count :]
    section = lax.axis_index("sec")
    tp_index = lax.axis_index("tp")
    local = cache_refs[0].shape[1]
    groups, rows, _ = messages.shape[1:]
    span = KEY_VALUE_HEADS * rows
    prompts = max(1, groups // KEY_VALUE_HEADS)
    full = section_count * CAP == REQ_GRP
    targets = own_targets(routing_ref, section)
    samples = query_refs[0].shape[1]
    for offset, far_ref in enumerate(far_refs):
        far_queries[tp_index ^ offset] = far_ref[...]
    position = lax.broadcasted_iota(jnp.int32, (local, span), 0) + tp_index * local
    owner = lax.broadcasted_iota(jnp.int32, (HEAD_SIZE, span), 1) // rows

    held = {(offset, half): cache_refs[n].at[place] for n, place, offset, half in halves_of(pieces)}

    def prompt(offset, order):
        keys_ref, values_ref = held[offset, 2 * order], held[offset, 2 * order + 1]
        row, _ = slot_row(targets, section ^ offset, order)
        visible = position < lengths_ref[section * REQ_GRP + row]
        slot = offset * CAP + order
        for head in range(span // samples):
            first, part = head * HEAD_SIZE, far_queries.shape[-1]
            if offset < 2:
                values = query_refs[offset][order, :, first : first + HEAD_SIZE]
            else:
                inner = first % part
                values = far_queries[first // part, offset - 2, order, :, inner : inner + HEAD_SIZE]
            stacked[slot, head * samples : (head + 1) * samples] = values.astype(jnp.float32)
        query = stacked[slot].T.astype(jnp.bfloat16)
        query = [jnp.where(owner == k, query, jnp.zeros_like(query)) for k in range(KEY_VALUE_HEADS)]
        score = jnp.dot(
            keys_ref[...], jnp.concatenate(query, axis=0), preferred_element_type=jnp.float32
        ) * HEAD_SIZE ** (-0.5)
        score = jnp.where(visible, score, HIDDEN)
        peak = jnp.max(score, axis=0, keepdims=True)
        weight = jnp.where(visible, jnp.exp(score - peak), 0.0)
        total = jnp.sum(weight, axis=0, keepdims=True)
        some = total > 0.0
        safe = jnp.where(some, total, 1.0)
        stats[0, pl.ds(row, 1)] = jnp.where(some, peak + jnp.log(safe), HIDDEN)
        weight = (weight * (1.0 / safe)).T.astype(jnp.bfloat16)
        for k in range(KEY_VALUE_HEADS):
            mixed = jnp.dot(
                weight[k * rows : (k + 1) * rows],
                values_ref[:, k * HEAD_SIZE : (k + 1) * HEAD_SIZE],
                preferred_element_type=jnp.float32,
            )
            group = row * KEY_VALUE_HEADS + k
            messages[group // groups, group % groups] = mixed.astype(jnp.bfloat16)

    for offset, half in held:
        if half % 2 == 0:
            one = functools.partial(prompt, offset, half // 2)
            if full:
                one()
            else:
                pl.when(slot_row(targets, section ^ offset, half // 2)[1])(one)

    level = stats[0]
    high = level.astype(jnp.bfloat16).astype(jnp.float32)
    rest = level - high
    middle = rest.astype(jnp.bfloat16).astype(jnp.float32)
    stats[0], stats[1], stats[2] = high, middle, rest - middle
    for offset, message_ref in enumerate(message_refs):
        device = tp_index ^ offset
        for inner in range(groups):
            message_ref[inner * rows : (inner + 1) * rows] = messages[device, inner]
        first = device * groups // KEY_VALUE_HEADS
        lines = [stats[part, pl.ds(first + n, 1)] for part in range(3) for n in range(prompts)]
        lines.append(jnp.zeros((STAT_ROWS - 3 * prompts, span), jnp.float32))
        message_ref[groups * rows :] = jnp.concatenate(lines, axis=0).astype(jnp.bfloat16)


def attend(routing, lengths, caches, pieces, queries, far_queries):
    section_count = len(far_queries[0]) + 2
    tp_count = len(far_queries)
    samples, width = queries[0].shape[1:]
    span = width // HEAD_SIZE * samples
    rows = span // KEY_VALUE_HEADS
    groups = REQ_GRP * KEY_VALUE_HEADS // tp_count
    multiplies = REQ_GRP * span * HEAD_SIZE * caches[0].shape[1]
    return pl.pallas_call(
        functools.partial(attend_kernel, pieces, section_count, tp_count),
        out_shape=[jax.ShapeDtypeStruct((groups * rows + STAT_ROWS, HEAD_SIZE), jnp.bfloat16)] * tp_count,
        in_specs=[SMEM, SMEM] + [VMEM] * (len(caches) + len(queries) + tp_count),
        out_specs=[VMEM] * tp_count,
        scratch_shapes=[
            pltpu.VMEM((tp_count, groups, rows, HEAD_SIZE), jnp.bfloat16),
            pltpu.VMEM((3, REQ_GRP, span), jnp.float32),
            pltpu.VMEM((section_count * CAP, span, HEAD_SIZE), jnp.float32),
            pltpu.VMEM((tp_count,) + far_queries[0].shape, far_queries[0].dtype),
        ],
        compiler_params=limit(12),
        cost_estimate=cost(2 * 10**10, 2 * sum(part.size for part in caches), multiplies // HEAD_SIZE),
        name="attend",
    )(routing, lengths, *caches, *queries, *far_queries)


def join_kernel(count, samples, rows, *refs):
    message_refs, (out_ref, scaling, flat) = refs[:count], refs[-3:]
    groups = (message_refs[0].shape[0] - STAT_ROWS) // rows
    prompts = max(1, groups // KEY_VALUE_HEADS)
    heads = rows // samples
    tp_index = lax.axis_index("tp")
    levels = []
    for ref in message_refs:
        lines = ref[groups * rows :].astype(jnp.float32)[0:8]
        levels.append(lines + pltpu.roll(lines, 8 - prompts, 0) + pltpu.roll(lines, 8 - 2 * prompts, 0))
    summit = functools.reduce(jnp.maximum, levels)
    scales = [jnp.exp(level - summit) for level in levels]
    total = functools.reduce(jnp.add, scales)
    for n, scale in enumerate(scales):
        scaling[n] = (scale / total).T
    for inner in range(groups):
        if groups % KEY_VALUE_HEADS:
            first = (tp_index * groups + inner) % KEY_VALUE_HEADS * rows
            part = pl.ds(pl.multiple_of(first, rows), rows)
        else:
            part = pl.ds(inner % KEY_VALUE_HEADS * rows, rows)
        prompt = inner // KEY_VALUE_HEADS
        terms = [
            ref[inner * rows : (inner + 1) * rows].astype(jnp.float32) * scaling[n, part, prompt : prompt + 1]
            for n, ref in enumerate(message_refs)
        ]
        joined = functools.reduce(jnp.add, terms)
        for head in range(heads):
            block = joined[head * samples : (head + 1) * samples]
            if len(flat.shape) == 2:
                row = prompt * samples
                column = (inner % KEY_VALUE_HEADS * heads + head) * HEAD_SIZE
                flat[row : row + samples, column : column + HEAD_SIZE] = block
            else:
                flat[inner, :, head * HEAD_SIZE : (head + 1) * HEAD_SIZE] = block
    out_ref[...] = flat[...].astype(jnp.bfloat16)


def join(messages, others, samples, heads):
    rows = heads * samples
    groups = (messages[0].shape[0] - STAT_ROWS) // rows
    width = rows // samples * HEAD_SIZE
    if groups % KEY_VALUE_HEADS == 0:
        shape = (groups // KEY_VALUE_HEADS * samples, KEY_VALUE_HEADS * width)
    else:
        shape = (groups, samples, width)
    count = len(messages)
    return pl.pallas_call(
        functools.partial(join_kernel, count, samples, rows),
        out_shape=jax.ShapeDtypeStruct(shape, jnp.bfloat16),
        in_specs=[VMEM] * count + [ANY] * len(others),
        out_specs=VMEM,
        scratch_shapes=[
            pltpu.VMEM((count, KEY_VALUE_HEADS * rows, 8), jnp.float32),
            pltpu.VMEM(shape, jnp.float32),
        ],
        compiler_params=limit(8),
        cost_estimate=cost(4 * count * messages[0].size, 2 * count * messages[0].size),
        name="join",
    )(*messages, *others)


def fetch_kernel(first, weight_ref, *refs):
    out_ref, sem = refs[-2:]
    copies = []
    step = out_ref.shape[0] // sem.shape[0]
    for n in range(sem.shape[0]):
        rows = weight_ref.at[pl.ds(first + n * step, step)]
        copies.append(pltpu.make_async_copy(rows, out_ref.at[pl.ds(n * step, step)], sem.at[n]))
        copies[-1].start()
    for copy in copies:
        copy.wait()


def fetch(weight, others, number, count):
    size = weight.shape[0] // count
    return pl.pallas_call(
        functools.partial(fetch_kernel, number * size),
        out_shape=jax.ShapeDtypeStruct((size,) + weight.shape[1:], weight.dtype),
        in_specs=[HBM] + [ANY] * len(others),
        out_specs=VMEM,
        scratch_shapes=[pltpu.SemaphoreType.DMA((8,))],
        compiler_params=limit(24),
        cost_estimate=cost(0, 4 * weight.size // count),
        name="fetch",
    )(in_hbm(weight), *others)


def project_kernel(count, tile, skipped, *refs):
    refs = refs[skipped:]
    part_refs, weight_refs, out_ref = refs[:count], refs[count:-1], refs[-1]
    tp_index = lax.axis_index("tp")
    prompts, samples, width = out_ref.shape
    share = prompts // count
    left = jnp.concatenate([ref[...].astype(jnp.float32) for ref in part_refs], axis=0).astype(jnp.bfloat16)
    size = weight_refs[0].shape[0]
    for first in range(0, width, tile):
        result = functools.reduce(
            jnp.add,
            [
                jnp.dot(
                    left[:, n * size : (n + 1) * size],
                    ref[:, first : first + tile],
                    preferred_element_type=jnp.float32,
                )
                for n, ref in enumerate(weight_refs)
            ],
        )
        for offset in range(count):
            for n in range(share):
                row = (offset * share + n) * samples
                block = result[row : row + samples].astype(out_ref.dtype)
                out_ref[(tp_index ^ offset) * share + n, :, first : first + tile] = block


def project(parts, weights, others, samples):
    count = len(parts)
    depth, width = weights[0].shape
    depth *= len(weights)
    total = count * parts[0].shape[0]
    return pl.pallas_call(
        functools.partial(project_kernel, count, min(256, width), len(others)),
        out_shape=jax.ShapeDtypeStruct((total // samples, samples, width), jnp.bfloat16),
        in_specs=[ANY] * len(others) + [VMEM] * (count + len(weights)),
        out_specs=VMEM,
        compiler_params=limit(24),
        cost_estimate=cost(2 * total * depth * width, 2 * depth * width),
        name="project",
    )(*others, *parts, *weights)


def body(prompt_key_values, queries, routing, lengths, out_weight):
    section_count = lax.axis_size("sec")
    tp_count = lax.axis_size("tp")
    slot_count, samples, query_width = queries.shape[1:]
    routing = routing.reshape(-1)

    whole = 2 * CAP
    near = [(offset, 0, whole) for offset in range(2)]
    head, tail = [(2, 0, 1)], [(2, 1, whole - 1)]
    far = tail + [(offset, 0, whole) for offset in range(3, section_count - 1)]
    far += [(section_count - 1, 0, whole - 1), (section_count - 1, whole - 1, 1)]

    def across(parts, pieces):
        return [swap(part, "sec", piece[0]) for part, piece in zip(parts, pieces)]

    head_caches, (near_query, *far_queries) = pack_head(
        routing, prompt_key_values, queries, head[0], section_count, tp_count
    )
    head_parts = across(head_caches, head)
    near_query = swap(near_query, "sec", 1)
    far_queries = [swap(part, "sec", n + 2) for n, part in enumerate(far_queries)]
    far_caches, query_parts = first_pack(
        routing, prompt_key_values, queries, head_caches, far, section_count
    )
    far_parts = across(far_caches[:-1], far[:-1])
    query_parts = [*query_parts, near_query]
    merged = merge(far_queries, [*head_parts, near_query])
    far_queries = spread(merged, "tp")
    near_caches = pack(routing, prompt_key_values, [merged], near, section_count, 10**10)
    near_parts = across(near_caches, near)
    caches, pieces = [*head_caches, *far_caches, *near_caches], head + far + near

    messages = attend(routing, lengths, caches, pieces, query_parts, far_queries)
    partials = [swap(part, "tp", offset) for offset, part in enumerate(messages)]
    held_weight = [fetch(out_weight, [messages[0], *near_parts[1:]], 0, 2)]
    held_cache = place([], [], near_parts + head_parts, near + head, slot_count)
    share = join(partials, [in_hbm(held_cache), *held_weight, *far_parts[:-1]], samples, query_width // HEAD_SIZE // KEY_VALUE_HEADS)
    far_parts += across(gate(far_caches[-1:], [share]), far[-1:])
    shares = spread(share, "tp")
    held_weight.append(fetch(out_weight, [share], 1, 2))
    if share.ndim == 3:
        attended = jnp.stack(shares)[jnp.arange(tp_count) ^ lax.axis_index("tp")]
        attended = attended.reshape(REQ_GRP, KEY_VALUE_HEADS, samples, -1).transpose(0, 2, 1, 3)
        attended = attended.reshape(REQ_GRP * samples, query_width)
        layer_out = jnp.dot(attended, out_weight, preferred_element_type=jnp.float32)
        layer_out = layer_out.astype(jnp.bfloat16).reshape(REQ_GRP, samples, -1)
    else:
        layer_out = project(shares, held_weight, far_parts[:-2], samples)

    held_cache = place([held_cache], [share], far_parts[:-2], far[:-2], slot_count)
    for part, piece in zip(far_parts[-2:], far[-2:]):
        held_cache = place([held_cache, layer_out], [], [part], [piece], slot_count)
    held_cache = held_cache.reshape((1, slot_count) + prompt_key_values.shape[1:])
    return (layer_out, held_cache)


def solution(mesh):
    placed = (
        P(("rep", "sec"), None, "tp", None),
        P(("rep", "sec"), None, None, None),
        P("rep", None),
        P("rep"),
        P(None, "tp"),
    )
    return jax.shard_map(
        body,
        mesh=mesh,
        in_specs=placed,
        out_specs=(P(("rep", "sec"), None, "tp"), P(("rep", "sec"), None, None, "tp", None)),
        check_vma=False,
    )
```

```python
import functools

import jax
import jax.numpy as jnp
from jax import lax
from jax.experimental import pallas as pl
from jax.experimental.pallas import tpu as pltpu
from jax.sharding import PartitionSpec as P

HEAD_SIZE = 128
KEY_VALUE_HEADS = 4
REQ_GRP = 8
CAP = 2
HIDDEN = -1e30
STAT_ROWS = 16

ANY = pl.BlockSpec(memory_space=pl.ANY)
HBM = pl.BlockSpec(memory_space=pltpu.HBM)
VMEM = pl.BlockSpec(memory_space=pltpu.VMEM)
SMEM = pl.BlockSpec(memory_space=pltpu.SMEM)


def limit(mebibytes):
    return pltpu.CompilerParams(vmem_limit_bytes=mebibytes << 20)


def cost(flops, bytes_accessed, transcendentals=0):
    return pl.CostEstimate(flops=flops, bytes_accessed=bytes_accessed, transcendentals=transcendentals)


def swap(value, axis, offset):
    if offset == 0:
        return value
    count = lax.axis_size(axis)
    return lax.ppermute(value, axis, [(i, i ^ offset) for i in range(count)])


def spread(value, axis):
    return [swap(value, axis, offset) for offset in range(lax.axis_size(axis))]


def own_targets(routing_ref, section):
    return [routing_ref[section * REQ_GRP + i] for i in range(REQ_GRP)]


def slot_row(targets, group, order):
    row, before = jnp.int32(0), jnp.int32(0)
    for i, target in enumerate(targets):
        here = target == group
        row = jnp.where(here & (before == order), i, row)
        before = before + here.astype(jnp.int32)
    return row, before > order


def halves_of(pieces):
    return [
        (n, place, offset, first + place)
        for n, (offset, first, count) in enumerate(pieces)
        for place in range(count)
    ]


def start_packing(pieces, section_count, routing_ref, cache_ref, out_refs, sem):
    section = lax.axis_index("sec")
    full = section_count * CAP == REQ_GRP
    targets = own_targets(routing_ref, section)
    halves = halves_of(pieces)
    slots = {(offset, half // 2) for _, _, offset, half in halves}
    rows = {slot: slot_row(targets, section ^ slot[0], slot[1]) for slot in sorted(slots)}

    def copy(n, place, offset, half):
        row, _ = rows[offset, half // 2]
        return pltpu.make_async_copy(
            cache_ref.at[row, half % 2], out_refs[n].at[place], sem.at[offset * 2 * CAP + half]
        )

    for n, place, offset, half in halves:
        if full:
            copy(n, place, offset, half).start()
        else:
            _, filled = rows[offset, half // 2]

            @pl.when(filled)
            def _():
                copy(n, place, offset, half).start()

            @pl.when(jnp.logical_not(filled))
            def _():
                out_refs[n][place] = jnp.zeros_like(out_refs[n][place])

    def finish():
        for n, place, offset, half in halves:
            if full:
                copy(n, place, offset, half).wait()
            else:
                pl.when(rows[offset, half // 2][1])(copy(n, place, offset, half).wait)

    return finish


def start_queries(query_ref, out_refs, offsets, sem):
    section = lax.axis_index("sec")
    copies = []
    for n, (offset, out_ref) in enumerate(zip(offsets, out_refs)):
        width = out_ref.shape[2]
        columns = pl.ds(pl.multiple_of(lax.axis_index("tp") * width, width) if offset > 1 else 0, width)
        part = query_ref.at[0, pl.ds((section ^ offset) * CAP, CAP), :, columns]
        copies.append(pltpu.make_async_copy(part, out_ref, sem.at[n]))
        copies[-1].start()
    return copies


def query_shapes(queries, offsets, tp_count):
    samples, width = queries.shape[2:]
    widths = [width if offset < 2 else width // tp_count for offset in offsets]
    return [jax.ShapeDtypeStruct((CAP, samples, one), queries.dtype) for one in widths]


def head_kernel(piece, offsets, full, routing_ref, cache_ref, query_ref, *refs):
    out_ref, query_out, (routed, held, routing_sem, sem, query_sem) = refs[0], refs[1:-5], refs[-5:]
    offset, half, _ = piece
    section = lax.axis_index("sec")
    copies = [pltpu.make_async_copy(routing_ref, routed, routing_sem)]
    for i in range(REQ_GRP - CAP + 1 if full and half < 2 else REQ_GRP):
        copies.append(pltpu.make_async_copy(cache_ref.at[i, half % 2], held.at[i], sem.at[i]))
    for copy in copies:
        copy.start()
    query_copies = start_queries(query_ref, query_out, offsets, query_sem)
    copies[0].wait()
    row, filled = slot_row(own_targets(routed, section), section ^ offset, half // 2)
    for copy in copies[1:] + query_copies:
        copy.wait()
    block = min(32, held.shape[1])
    for first in range(0, held.shape[1], block):
        chosen = held[row, first : first + block]
        out_ref[0, first : first + block] = chosen if full else jnp.where(filled, chosen, jnp.zeros_like(chosen))


def pack_head(routing, cache, queries, piece, section_count, tp_count):
    shape = cache.shape[2:]
    offsets = range(2, section_count)
    shapes = [jax.ShapeDtypeStruct((1,) + shape, cache.dtype)] + query_shapes(queries, offsets, tp_count)
    head, *parts = pl.pallas_call(
        functools.partial(head_kernel, piece, offsets, section_count * CAP == REQ_GRP),
        out_shape=shapes,
        in_specs=[HBM, HBM, HBM],
        out_specs=[VMEM] * len(shapes),
        scratch_shapes=[
            pltpu.SMEM(routing.shape, jnp.int32),
            pltpu.VMEM((REQ_GRP,) + shape, cache.dtype),
            pltpu.SemaphoreType.DMA,
            pltpu.SemaphoreType.DMA((REQ_GRP,)),
            pltpu.SemaphoreType.DMA((section_count,)),
        ],
        compiler_params=limit(16),
        cost_estimate=cost(0, cache.size),
        name="pack_head",
    )(in_hbm(routing), in_hbm(cache), in_hbm(queries))
    return [head], parts


def first_pack_kernel(pieces, section_count, routing_ref, cache_ref, query_ref, *refs):
    refs, (sem, query_sem) = refs[:-2], refs[-2:]
    query_out, cache_out = refs[-2:], refs[-2 - len(pieces) : -2]
    query_copies = start_queries(query_ref, query_out, range(2), query_sem)
    start_packing(pieces, section_count, routing_ref, cache_ref, cache_out, sem)()
    for copy in query_copies:
        copy.wait()


def pack_kernel(pieces, section_count, routing_ref, cache_ref, *refs):
    cache_out, sem = refs[-1 - len(pieces) : -1], refs[-1]
    start_packing(pieces, section_count, routing_ref, cache_ref, cache_out, sem)()


def merge_kernel(count, *refs):
    for n in range(count):
        refs[-1][n] = refs[n][...]


def merge(parts, others):
    shape = (len(parts),) + parts[0].shape
    return pl.pallas_call(
        functools.partial(merge_kernel, len(parts)),
        out_shape=jax.ShapeDtypeStruct(shape, parts[0].dtype),
        in_specs=[VMEM] * len(parts) + [ANY] * len(others),
        out_specs=VMEM,
        compiler_params=limit(8),
        cost_estimate=cost(3 * 10**9, 8 * len(parts) * parts[0].size),
        name="merge",
    )(*parts, *others)


def in_hbm(value):
    return pltpu.with_memory_space_constraint(value, pltpu.HBM)


def first_pack(routing, cache, queries, others, pieces, section_count):
    shapes = [jax.ShapeDtypeStruct((count,) + cache.shape[2:], cache.dtype) for _, _, count in pieces]
    shapes += query_shapes(queries, range(2), 1)
    parts = pl.pallas_call(
        functools.partial(first_pack_kernel, pieces, section_count),
        out_shape=shapes,
        in_specs=[SMEM, HBM, HBM] + [ANY] * len(others),
        out_specs=[VMEM] * len(shapes),
        scratch_shapes=[
            pltpu.SemaphoreType.DMA((section_count * CAP * 2,)),
            pltpu.SemaphoreType.DMA((2,)),
        ],
        compiler_params=limit(16),
        cost_estimate=cost(0, 4 * sum(shape.size for shape in shapes)),
        name="first_pack",
    )(routing, in_hbm(cache), in_hbm(queries), *others)
    return parts[: len(pieces)], parts[len(pieces) :]


def pack(routing, cache, others, pieces, section_count, flops=0):
    shapes = [jax.ShapeDtypeStruct((count,) + cache.shape[2:], cache.dtype) for _, _, count in pieces]
    return pl.pallas_call(
        functools.partial(pack_kernel, pieces, section_count),
        out_shape=shapes,
        in_specs=[SMEM, HBM] + [ANY] * len(others),
        out_specs=[VMEM] * len(shapes),
        scratch_shapes=[
            pltpu.SemaphoreType.DMA((section_count * CAP * 2,)),
        ],
        compiler_params=limit(16),
        cost_estimate=cost(flops, 4 * sum(shape.size for shape in shapes)),
        name="pack",
    )(routing, in_hbm(cache), *others)


def gate_kernel(*refs):
    pass


def gate(values, others):
    count = len(values)
    return pl.pallas_call(
        gate_kernel,
        out_shape=[jax.ShapeDtypeStruct(value.shape, value.dtype) for value in values],
        in_specs=[ANY] * (count + len(others)),
        out_specs=[ANY] * count,
        input_output_aliases={n: n for n in range(count)},
        compiler_params=limit(1),
        cost_estimate=cost(0, 0),
        name="gate",
    )(*values, *others)


def place_kernel(pieces, *refs):
    count = len(pieces)
    part_refs, out_ref, sem = refs[-2 - count : -2], refs[-2], refs[-1]
    section = lax.axis_index("sec")
    copies = []
    for n, (offset, first, size) in enumerate(pieces):
        for place in range(size):
            half = out_ref.at[0, (section ^ offset) * 2 * CAP + first + place]
            copies.append(pltpu.make_async_copy(part_refs[n].at[place], half, sem.at[len(copies)]))
            copies[-1].start()
    for copy in copies:
        copy.wait()


def place(given, others, parts, pieces, slot_count):
    part = parts[0]
    return pl.pallas_call(
        functools.partial(place_kernel, pieces),
        out_shape=jax.ShapeDtypeStruct((1, 2 * slot_count) + part.shape[1:], part.dtype),
        in_specs=[HBM] * len(given) + [ANY] * len(others) + [VMEM] * len(parts),
        out_specs=HBM,
        scratch_shapes=[pltpu.SemaphoreType.DMA((sum(len(part) for part in parts),))],
        input_output_aliases={0: 0} if given else {},
        compiler_params=limit(8),
        cost_estimate=cost(0, 4 * sum(piece.size for piece in parts)),
        name="place",
    )(*[in_hbm(value) for value in given], *others, *parts)


def attend_kernel(pieces, section_count, tp_count, routing_ref, lengths_ref, *refs):
    cache_refs, refs = refs[: len(pieces)], refs[len(pieces) :]
    query_refs, far_refs = refs[:2], refs[2 : 2 + tp_count]
    message_refs = refs[2 + tp_count : 2 + 2 * tp_count]
    messages, stats, stacked, far_queries = refs[2 + 2 * tp_count :]
    section = lax.axis_index("sec")
    tp_index = lax.axis_index("tp")
    local = cache_refs[0].shape[1]
    groups, rows, _ = messages.shape[1:]
    span = KEY_VALUE_HEADS * rows
    prompts = max(1, groups // KEY_VALUE_HEADS)
    full = section_count * CAP == REQ_GRP
    targets = own_targets(routing_ref, section)
    samples = query_refs[0].shape[1]
    for offset, far_ref in enumerate(far_refs):
        far_queries[tp_index ^ offset] = far_ref[...]
    position = lax.broadcasted_iota(jnp.int32, (local, span), 0) + tp_index * local
    owner = lax.broadcasted_iota(jnp.int32, (HEAD_SIZE, span), 1) // rows

    held = {(offset, half): cache_refs[n].at[place] for n, place, offset, half in halves_of(pieces)}

    def prompt(offset, order):
        keys_ref, values_ref = held[offset, 2 * order], held[offset, 2 * order + 1]
        row, _ = slot_row(targets, section ^ offset, order)
        visible = position < lengths_ref[section * REQ_GRP + row]
        slot = offset * CAP + order
        for head in range(span // samples):
            first, part = head * HEAD_SIZE, far_queries.shape[-1]
            if offset < 2:
                values = query_refs[offset][order, :, first : first + HEAD_SIZE]
            else:
                inner = first % part
                values = far_queries[first // part, offset - 2, order, :, inner : inner + HEAD_SIZE]
            stacked[slot, head * samples : (head + 1) * samples] = values.astype(jnp.float32)
        query = stacked[slot].T.astype(jnp.bfloat16)
        query = [jnp.where(owner == k, query, jnp.zeros_like(query)) for k in range(KEY_VALUE_HEADS)]
        score = jnp.dot(
            keys_ref[...], jnp.concatenate(query, axis=0), preferred_element_type=jnp.float32
        ) * HEAD_SIZE ** (-0.5)
        score = jnp.where(visible, score, HIDDEN)
        peak = jnp.max(score, axis=0, keepdims=True)
        weight = jnp.where(visible, jnp.exp(score - peak), 0.0)
        total = jnp.sum(weight, axis=0, keepdims=True)
        some = total > 0.0
        safe = jnp.where(some, total, 1.0)
        stats[0, pl.ds(row, 1)] = jnp.where(some, peak + jnp.log(safe), HIDDEN)
        weight = (weight * (1.0 / safe)).T.astype(jnp.bfloat16)
        for k in range(KEY_VALUE_HEADS):
            mixed = jnp.dot(
                weight[k * rows : (k + 1) * rows],
                values_ref[:, k * HEAD_SIZE : (k + 1) * HEAD_SIZE],
                preferred_element_type=jnp.float32,
            )
            group = row * KEY_VALUE_HEADS + k
            messages[group // groups, group % groups] = mixed.astype(jnp.bfloat16)

    for offset, half in held:
        if half % 2 == 0:
            one = functools.partial(prompt, offset, half // 2)
            if full:
                one()
            else:
                pl.when(slot_row(targets, section ^ offset, half // 2)[1])(one)

    level = stats[0]
    high = level.astype(jnp.bfloat16).astype(jnp.float32)
    rest = level - high
    middle = rest.astype(jnp.bfloat16).astype(jnp.float32)
    stats[0], stats[1], stats[2] = high, middle, rest - middle
    for offset, message_ref in enumerate(message_refs):
        device = tp_index ^ offset
        for inner in range(groups):
            message_ref[inner * rows : (inner + 1) * rows] = messages[device, inner]
        first = device * groups // KEY_VALUE_HEADS
        lines = [stats[part, pl.ds(first + n, 1)] for part in range(3) for n in range(prompts)]
        lines.append(jnp.zeros((STAT_ROWS - 3 * prompts, span), jnp.float32))
        message_ref[groups * rows :] = jnp.concatenate(lines, axis=0).astype(jnp.bfloat16)


def attend(routing, lengths, caches, pieces, queries, far_queries):
    section_count = len(far_queries[0]) + 2
    tp_count = len(far_queries)
    samples, width = queries[0].shape[1:]
    span = width // HEAD_SIZE * samples
    rows = span // KEY_VALUE_HEADS
    groups = REQ_GRP * KEY_VALUE_HEADS // tp_count
    multiplies = REQ_GRP * span * HEAD_SIZE * caches[0].shape[1]
    return pl.pallas_call(
        functools.partial(attend_kernel, pieces, section_count, tp_count),
        out_shape=[jax.ShapeDtypeStruct((groups * rows + STAT_ROWS, HEAD_SIZE), jnp.bfloat16)] * tp_count,
        in_specs=[SMEM, SMEM] + [VMEM] * (len(caches) + len(queries) + tp_count),
        out_specs=[VMEM] * tp_count,
        scratch_shapes=[
            pltpu.VMEM((tp_count, groups, rows, HEAD_SIZE), jnp.bfloat16),
            pltpu.VMEM((3, REQ_GRP, span), jnp.float32),
            pltpu.VMEM((section_count * CAP, span, HEAD_SIZE), jnp.float32),
            pltpu.VMEM((tp_count,) + far_queries[0].shape, far_queries[0].dtype),
        ],
        compiler_params=limit(12),
        cost_estimate=cost(2 * 10**10, 2 * sum(part.size for part in caches), multiplies // HEAD_SIZE),
        name="attend",
    )(routing, lengths, *caches, *queries, *far_queries)


def join_kernel(count, samples, rows, *refs):
    message_refs, (out_ref, scaling, flat) = refs[:count], refs[-3:]
    groups = (message_refs[0].shape[0] - STAT_ROWS) // rows
    prompts = max(1, groups // KEY_VALUE_HEADS)
    heads = rows // samples
    tp_index = lax.axis_index("tp")
    levels = []
    for ref in message_refs:
        lines = ref[groups * rows :].astype(jnp.float32)[0:8]
        levels.append(lines + pltpu.roll(lines, 8 - prompts, 0) + pltpu.roll(lines, 8 - 2 * prompts, 0))
    summit = functools.reduce(jnp.maximum, levels)
    scales = [jnp.exp(level - summit) for level in levels]
    total = functools.reduce(jnp.add, scales)
    for n, scale in enumerate(scales):
        scaling[n] = (scale / total).T
    for inner in range(groups):
        if groups % KEY_VALUE_HEADS:
            first = (tp_index * groups + inner) % KEY_VALUE_HEADS * rows
            part = pl.ds(pl.multiple_of(first, rows), rows)
        else:
            part = pl.ds(inner % KEY_VALUE_HEADS * rows, rows)
        prompt = inner // KEY_VALUE_HEADS
        terms = [
            ref[inner * rows : (inner + 1) * rows].astype(jnp.float32) * scaling[n, part, prompt : prompt + 1]
            for n, ref in enumerate(message_refs)
        ]
        joined = functools.reduce(jnp.add, terms)
        for head in range(heads):
            block = joined[head * samples : (head + 1) * samples]
            if len(flat.shape) == 2:
                row = prompt * samples
                column = (inner % KEY_VALUE_HEADS * heads + head) * HEAD_SIZE
                flat[row : row + samples, column : column + HEAD_SIZE] = block
            else:
                flat[inner, :, head * HEAD_SIZE : (head + 1) * HEAD_SIZE] = block
    out_ref[...] = flat[...].astype(jnp.bfloat16)


def join(messages, others, samples, heads):
    rows = heads * samples
    groups = (messages[0].shape[0] - STAT_ROWS) // rows
    width = rows // samples * HEAD_SIZE
    if groups % KEY_VALUE_HEADS == 0:
        shape = (groups // KEY_VALUE_HEADS * samples, KEY_VALUE_HEADS * width)
    else:
        shape = (groups, samples, width)
    count = len(messages)
    return pl.pallas_call(
        functools.partial(join_kernel, count, samples, rows),
        out_shape=jax.ShapeDtypeStruct(shape, jnp.bfloat16),
        in_specs=[VMEM] * count + [ANY] * len(others),
        out_specs=VMEM,
        scratch_shapes=[
            pltpu.VMEM((count, KEY_VALUE_HEADS * rows, 8), jnp.float32),
            pltpu.VMEM(shape, jnp.float32),
        ],
        compiler_params=limit(8),
        cost_estimate=cost(4 * count * messages[0].size, 2 * count * messages[0].size),
        name="join",
    )(*messages, *others)


def fetch_kernel(first, weight_ref, *refs):
    out_ref, sem = refs[-2:]
    copies = []
    step = out_ref.shape[0] // sem.shape[0]
    for n in range(sem.shape[0]):
        rows = weight_ref.at[pl.ds(first + n * step, step)]
        copies.append(pltpu.make_async_copy(rows, out_ref.at[pl.ds(n * step, step)], sem.at[n]))
        copies[-1].start()
    for copy in copies:
        copy.wait()


def fetch(weight, others, number, count):
    size = weight.shape[0] // count
    return pl.pallas_call(
        functools.partial(fetch_kernel, number * size),
        out_shape=jax.ShapeDtypeStruct((size,) + weight.shape[1:], weight.dtype),
        in_specs=[HBM] + [ANY] * len(others),
        out_specs=VMEM,
        scratch_shapes=[pltpu.SemaphoreType.DMA((8,))],
        compiler_params=limit(24),
        cost_estimate=cost(0, 4 * weight.size // count),
        name="fetch",
    )(in_hbm(weight), *others)


def project_kernel(count, tile, skipped, *refs):
    refs = refs[skipped:]
    part_refs, weight_refs, out_ref = refs[:count], refs[count:-1], refs[-1]
    tp_index = lax.axis_index("tp")
    prompts, samples, width = out_ref.shape
    share = prompts // count
    left = jnp.concatenate([ref[...].astype(jnp.float32) for ref in part_refs], axis=0).astype(jnp.bfloat16)
    size = weight_refs[0].shape[0]
    for first in range(0, width, tile):
        result = functools.reduce(
            jnp.add,
            [
                jnp.dot(
                    left[:, n * size : (n + 1) * size],
                    ref[:, first : first + tile],
                    preferred_element_type=jnp.float32,
                )
                for n, ref in enumerate(weight_refs)
            ],
        )
        for offset in range(count):
            for n in range(share):
                row = (offset * share + n) * samples
                block = result[row : row + samples].astype(out_ref.dtype)
                out_ref[(tp_index ^ offset) * share + n, :, first : first + tile] = block


def project(parts, weights, others, samples):
    count = len(parts)
    depth, width = weights[0].shape
    depth *= len(weights)
    total = count * parts[0].shape[0]
    return pl.pallas_call(
        functools.partial(project_kernel, count, min(256, width), len(others)),
        out_shape=jax.ShapeDtypeStruct((total // samples, samples, width), jnp.bfloat16),
        in_specs=[ANY] * len(others) + [VMEM] * (count + len(weights)),
        out_specs=VMEM,
        compiler_params=limit(24),
        cost_estimate=cost(2 * total * depth * width, 2 * depth * width),
        name="project",
    )(*others, *parts, *weights)


def body(prompt_key_values, queries, routing, lengths, out_weight):
    section_count = lax.axis_size("sec")
    tp_count = lax.axis_size("tp")
    slot_count, samples, query_width = queries.shape[1:]
    routing = routing.reshape(-1)

    whole = 2 * CAP
    near = [(offset, 0, whole) for offset in range(2)]
    head, tail = [(2, 0, 1)], [(2, 1, whole - 1)]
    far = tail + [(offset, 0, whole) for offset in range(3, section_count - 1)]
    far += [(section_count - 1, 0, whole - 1), (section_count - 1, whole - 1, 1)]

    def across(parts, pieces):
        return [swap(part, "sec", piece[0]) for part, piece in zip(parts, pieces)]

    head_caches, far_queries = pack_head(
        routing, prompt_key_values, queries, head[0], section_count, tp_count
    )
    head_parts = across(head_caches, head)
    far_queries = [swap(part, "sec", n + 2) for n, part in enumerate(far_queries)]
    far_caches, query_parts = first_pack(
        routing, prompt_key_values, queries, head_caches, far, section_count
    )
    far_parts = across(far_caches[:-1], far[:-1])
    query_parts = [swap(part, "sec", offset) for offset, part in enumerate(query_parts)]
    merged = merge(far_queries, head_parts)
    far_queries = spread(merged, "tp")
    near_caches = pack(routing, prompt_key_values, [merged, query_parts[1]], near, section_count, 10**10)
    near_parts = across(near_caches, near)
    caches, pieces = [*head_caches, *far_caches, *near_caches], head + far + near

    messages = attend(routing, lengths, caches, pieces, query_parts, far_queries)
    partials = [swap(part, "tp", offset) for offset, part in enumerate(messages)]
    held_weight = [fetch(out_weight, [messages[0], *near_parts[1:]], 0, 2)]
    held_cache = place([], [], near_parts + head_parts, near + head, slot_count)
    share = join(partials, [in_hbm(held_cache), *held_weight, *far_parts[:-1]], samples, query_width // HEAD_SIZE // KEY_VALUE_HEADS)
    far_parts += across(gate(far_caches[-1:], [share]), far[-1:])
    shares = spread(share, "tp")
    held_weight.append(fetch(out_weight, [share], 1, 2))
    if share.ndim == 3:
        attended = jnp.stack(shares)[jnp.arange(tp_count) ^ lax.axis_index("tp")]
        attended = attended.reshape(REQ_GRP, KEY_VALUE_HEADS, samples, -1).transpose(0, 2, 1, 3)
        attended = attended.reshape(REQ_GRP * samples, query_width)
        layer_out = jnp.dot(attended, out_weight, preferred_element_type=jnp.float32)
        layer_out = layer_out.astype(jnp.bfloat16).reshape(REQ_GRP, samples, -1)
    else:
        layer_out = project(shares, held_weight, far_parts[:-2], samples)

    held_cache = place([held_cache], [share], far_parts[:-2], far[:-2], slot_count)
    held_cache = place([held_cache, layer_out], [], far_parts[-2:-1], far[-2:-1], slot_count)
    held_cache = place([held_cache], [], far_parts[-1:], far[-1:], slot_count)
    held_cache = held_cache.reshape((1, slot_count) + prompt_key_values.shape[1:])
    return (layer_out, held_cache)


def solution(mesh):
    placed = (
        P(("rep", "sec"), None, "tp", None),
        P(("rep", "sec"), None, None, None),
        P("rep", None),
        P("rep"),
        P(None, "tp"),
    )
    return jax.shard_map(
        body,
        mesh=mesh,
        in_specs=placed,
        out_specs=(P(("rep", "sec"), None, "tp"), P(("rep", "sec"), None, None, "tp", None)),
        check_vma=False,
    )
```

```python
import functools

import jax
import jax.numpy as jnp
from jax import lax
from jax.experimental import pallas as pl
from jax.experimental.pallas import tpu as pltpu
from jax.sharding import PartitionSpec as P

HEAD_SIZE = 128
KEY_VALUE_HEADS = 4
REQ_GRP = 8
CAP = 2
HIDDEN = -1e30
STAT_ROWS = 16
EARLY_ROWS = 6

ANY = pl.BlockSpec(memory_space=pl.ANY)
HBM = pl.BlockSpec(memory_space=pltpu.HBM)
VMEM = pl.BlockSpec(memory_space=pltpu.VMEM)
SMEM = pl.BlockSpec(memory_space=pltpu.SMEM)


def limit(mebibytes):
    return pltpu.CompilerParams(vmem_limit_bytes=mebibytes << 20)


def cost(flops, bytes_accessed, transcendentals=0):
    return pl.CostEstimate(flops=flops, bytes_accessed=bytes_accessed, transcendentals=transcendentals)


def swap(value, axis, offset):
    if offset == 0:
        return value
    count = lax.axis_size(axis)
    return lax.ppermute(value, axis, [(i, i ^ offset) for i in range(count)])


def spread(value, axis):
    return [swap(value, axis, offset) for offset in range(lax.axis_size(axis))]


def own_targets(routing_ref, section):
    return [routing_ref[section * REQ_GRP + i] for i in range(REQ_GRP)]


def slot_row(targets, group, order):
    row, before = jnp.int32(0), jnp.int32(0)
    for i, target in enumerate(targets):
        here = target == group
        row = jnp.where(here & (before == order), i, row)
        before = before + here.astype(jnp.int32)
    return row, before > order


def halves_of(pieces):
    return [
        (n, place, offset, first + place)
        for n, (offset, first, count) in enumerate(pieces)
        for place in range(count)
    ]


def start_packing(pieces, section_count, routing_ref, cache_ref, out_refs, sem):
    section = lax.axis_index("sec")
    full = section_count * CAP == REQ_GRP
    targets = own_targets(routing_ref, section)
    halves = halves_of(pieces)
    slots = {(offset, half // 2) for _, _, offset, half in halves}
    rows = {slot: slot_row(targets, section ^ slot[0], slot[1]) for slot in sorted(slots)}

    def copy(n, place, offset, half):
        row, _ = rows[offset, half // 2]
        return pltpu.make_async_copy(
            cache_ref.at[row, half % 2], out_refs[n].at[place], sem.at[offset * 2 * CAP + half]
        )

    for n, place, offset, half in halves:
        if full:
            copy(n, place, offset, half).start()
        else:
            _, filled = rows[offset, half // 2]

            @pl.when(filled)
            def _():
                copy(n, place, offset, half).start()

            @pl.when(jnp.logical_not(filled))
            def _():
                out_refs[n][place] = jnp.zeros_like(out_refs[n][place])

    def finish():
        for n, place, offset, half in halves:
            if full:
                copy(n, place, offset, half).wait()
            else:
                pl.when(rows[offset, half // 2][1])(copy(n, place, offset, half).wait)

    return finish


def start_queries(query_ref, out_refs, offsets, sem):
    section = lax.axis_index("sec")
    copies = []
    for n, (offset, out_ref) in enumerate(zip(offsets, out_refs)):
        width = out_ref.shape[2]
        columns = pl.ds(pl.multiple_of(lax.axis_index("tp") * width, width) if offset > 1 else 0, width)
        part = query_ref.at[0, pl.ds((section ^ offset) * CAP, CAP), :, columns]
        copies.append(pltpu.make_async_copy(part, out_ref, sem.at[n]))
        copies[-1].start()
    return copies


def query_shapes(queries, offsets, tp_count):
    samples, width = queries.shape[2:]
    widths = [width if offset < 2 else width // tp_count for offset in offsets]
    return [jax.ShapeDtypeStruct((CAP, samples, one), queries.dtype) for one in widths]


def head_kernel(piece, offsets, full, routing_ref, cache_ref, query_ref, *refs):
    out_ref, query_out, (routed, held, routing_sem, sem, query_sem) = refs[0], refs[1:-5], refs[-5:]
    offset, half, _ = piece
    section = lax.axis_index("sec")
    copies = [pltpu.make_async_copy(routing_ref, routed, routing_sem)]
    for i in range(EARLY_ROWS):
        copies.append(pltpu.make_async_copy(cache_ref.at[i, half % 2], held.at[i], sem.at[i]))
    for copy in copies:
        copy.start()
    query_copies = start_queries(query_ref, query_out, offsets, query_sem)
    copies[0].wait()
    row, filled = slot_row(own_targets(routed, section), section ^ offset, half // 2)
    wanted = pltpu.make_async_copy(cache_ref.at[row, half % 2], held.at[row], sem.at[row])
    pl.when(row >= EARLY_ROWS)(wanted.start)
    wanted.wait()
    block = min(32, held.shape[1])
    for first in range(0, held.shape[1], block):
        chosen = held[row, first : first + block]
        out_ref[0, first : first + block] = chosen if full else jnp.where(filled, chosen, jnp.zeros_like(chosen))
    for i, copy in enumerate(copies[1:]):
        pl.when(i != row)(copy.wait)
    for copy in query_copies:
        copy.wait()


def pack_head(routing, cache, queries, piece, section_count, tp_count):
    shape = cache.shape[2:]
    offsets = range(2, section_count)
    shapes = [jax.ShapeDtypeStruct((1,) + shape, cache.dtype)] + query_shapes(queries, offsets, tp_count)
    head, *parts = pl.pallas_call(
        functools.partial(head_kernel, piece, offsets, section_count * CAP == REQ_GRP),
        out_shape=shapes,
        in_specs=[HBM, HBM, HBM],
        out_specs=[VMEM] * len(shapes),
        scratch_shapes=[
            pltpu.SMEM(routing.shape, jnp.int32),
            pltpu.VMEM((REQ_GRP,) + shape, cache.dtype),
            pltpu.SemaphoreType.DMA,
            pltpu.SemaphoreType.DMA((REQ_GRP,)),
            pltpu.SemaphoreType.DMA((section_count,)),
        ],
        compiler_params=limit(16),
        cost_estimate=cost(0, cache.size),
        name="pack_head",
    )(in_hbm(routing), in_hbm(cache), in_hbm(queries))
    return [head], parts


def first_pack_kernel(pieces, section_count, routing_ref, cache_ref, query_ref, *refs):
    refs, (sem, query_sem) = refs[:-2], refs[-2:]
    query_out, cache_out = refs[-2:], refs[-2 - len(pieces) : -2]
    query_copies = start_queries(query_ref, query_out, range(2), query_sem)
    start_packing(pieces, section_count, routing_ref, cache_ref, cache_out, sem)()
    for copy in query_copies:
        copy.wait()


def pack_kernel(pieces, section_count, routing_ref, cache_ref, *refs):
    cache_out, sem = refs[-1 - len(pieces) : -1], refs[-1]
    start_packing(pieces, section_count, routing_ref, cache_ref, cache_out, sem)()


def merge_kernel(count, *refs):
    for n in range(count):
        refs[-1][n] = refs[n][...]


def merge(parts, others):
    shape = (len(parts),) + parts[0].shape
    return pl.pallas_call(
        functools.partial(merge_kernel, len(parts)),
        out_shape=jax.ShapeDtypeStruct(shape, parts[0].dtype),
        in_specs=[VMEM] * len(parts) + [ANY] * len(others),
        out_specs=VMEM,
        compiler_params=limit(8),
        cost_estimate=cost(3 * 10**9, 8 * len(parts) * parts[0].size),
        name="merge",
    )(*parts, *others)


def in_hbm(value):
    return pltpu.with_memory_space_constraint(value, pltpu.HBM)


def first_pack(routing, cache, queries, others, pieces, section_count):
    shapes = [jax.ShapeDtypeStruct((count,) + cache.shape[2:], cache.dtype) for _, _, count in pieces]
    shapes += query_shapes(queries, range(2), 1)
    parts = pl.pallas_call(
        functools.partial(first_pack_kernel, pieces, section_count),
        out_shape=shapes,
        in_specs=[SMEM, HBM, HBM] + [ANY] * len(others),
        out_specs=[VMEM] * len(shapes),
        scratch_shapes=[
            pltpu.SemaphoreType.DMA((section_count * CAP * 2,)),
            pltpu.SemaphoreType.DMA((2,)),
        ],
        compiler_params=limit(16),
        cost_estimate=cost(0, 4 * sum(shape.size for shape in shapes)),
        name="first_pack",
    )(routing, in_hbm(cache), in_hbm(queries), *others)
    return parts[: len(pieces)], parts[len(pieces) :]


def pack(routing, cache, others, pieces, section_count, flops=0):
    shapes = [jax.ShapeDtypeStruct((count,) + cache.shape[2:], cache.dtype) for _, _, count in pieces]
    return pl.pallas_call(
        functools.partial(pack_kernel, pieces, section_count),
        out_shape=shapes,
        in_specs=[SMEM, HBM] + [ANY] * len(others),
        out_specs=[VMEM] * len(shapes),
        scratch_shapes=[
            pltpu.SemaphoreType.DMA((section_count * CAP * 2,)),
        ],
        compiler_params=limit(16),
        cost_estimate=cost(flops, 4 * sum(shape.size for shape in shapes)),
        name="pack",
    )(routing, in_hbm(cache), *others)


def gate_kernel(*refs):
    pass


def gate(values, others):
    count = len(values)
    return pl.pallas_call(
        gate_kernel,
        out_shape=[jax.ShapeDtypeStruct(value.shape, value.dtype) for value in values],
        in_specs=[ANY] * (count + len(others)),
        out_specs=[ANY] * count,
        input_output_aliases={n: n for n in range(count)},
        compiler_params=limit(1),
        cost_estimate=cost(0, 0),
        name="gate",
    )(*values, *others)


def place_kernel(pieces, *refs):
    count = len(pieces)
    part_refs, out_ref, sem = refs[-2 - count : -2], refs[-2], refs[-1]
    section = lax.axis_index("sec")
    copies = []
    for n, (offset, first, size) in enumerate(pieces):
        for place in range(size):
            half = out_ref.at[0, (section ^ offset) * 2 * CAP + first + place]
            copies.append(pltpu.make_async_copy(part_refs[n].at[place], half, sem.at[len(copies)]))
            copies[-1].start()
    for copy in copies:
        copy.wait()


def place(given, others, parts, pieces, slot_count):
    part = parts[0]
    return pl.pallas_call(
        functools.partial(place_kernel, pieces),
        out_shape=jax.ShapeDtypeStruct((1, 2 * slot_count) + part.shape[1:], part.dtype),
        in_specs=[HBM] * len(given) + [ANY] * len(others) + [VMEM] * len(parts),
        out_specs=HBM,
        scratch_shapes=[pltpu.SemaphoreType.DMA((sum(len(part) for part in parts),))],
        input_output_aliases={0: 0} if given else {},
        compiler_params=limit(8),
        cost_estimate=cost(0, 4 * sum(piece.size for piece in parts)),
        name="place",
    )(*[in_hbm(value) for value in given], *others, *parts)


def attend_kernel(pieces, section_count, tp_count, routing_ref, lengths_ref, *refs):
    cache_refs, refs = refs[: len(pieces)], refs[len(pieces) :]
    query_refs, far_refs = refs[:2], refs[2 : 2 + tp_count]
    message_refs = refs[2 + tp_count : 2 + 2 * tp_count]
    messages, stats, stacked, far_queries = refs[2 + 2 * tp_count :]
    section = lax.axis_index("sec")
    tp_index = lax.axis_index("tp")
    local = cache_refs[0].shape[1]
    groups, rows, _ = messages.shape[1:]
    span = KEY_VALUE_HEADS * rows
    prompts = max(1, groups // KEY_VALUE_HEADS)
    full = section_count * CAP == REQ_GRP
    targets = own_targets(routing_ref, section)
    samples = query_refs[0].shape[1]
    for offset, far_ref in enumerate(far_refs):
        far_queries[tp_index ^ offset] = far_ref[...]
    position = lax.broadcasted_iota(jnp.int32, (local, span), 0) + tp_index * local
    owner = lax.broadcasted_iota(jnp.int32, (HEAD_SIZE, span), 1) // rows

    held = {(offset, half): cache_refs[n].at[place] for n, place, offset, half in halves_of(pieces)}

    def prompt(offset, order):
        keys_ref, values_ref = held[offset, 2 * order], held[offset, 2 * order + 1]
        row, _ = slot_row(targets, section ^ offset, order)
        visible = position < lengths_ref[section * REQ_GRP + row]
        slot = offset * CAP + order
        for head in range(span // samples):
            first, part = head * HEAD_SIZE, far_queries.shape[-1]
            if offset < 2:
                values = query_refs[offset][order, :, first : first + HEAD_SIZE]
            else:
                inner = first % part
                values = far_queries[first // part, offset - 2, order, :, inner : inner + HEAD_SIZE]
            stacked[slot, head * samples : (head + 1) * samples] = values.astype(jnp.float32)
        query = stacked[slot].T.astype(jnp.bfloat16)
        query = [jnp.where(owner == k, query, jnp.zeros_like(query)) for k in range(KEY_VALUE_HEADS)]
        score = jnp.dot(
            keys_ref[...], jnp.concatenate(query, axis=0), preferred_element_type=jnp.float32
        ) * HEAD_SIZE ** (-0.5)
        score = jnp.where(visible, score, HIDDEN)
        peak = jnp.max(score, axis=0, keepdims=True)
        weight = jnp.where(visible, jnp.exp(score - peak), 0.0)
        total = jnp.sum(weight, axis=0, keepdims=True)
        some = total > 0.0
        safe = jnp.where(some, total, 1.0)
        stats[0, pl.ds(row, 1)] = jnp.where(some, peak + jnp.log(safe), HIDDEN)
        weight = (weight * (1.0 / safe)).T.astype(jnp.bfloat16)
        for k in range(KEY_VALUE_HEADS):
            mixed = jnp.dot(
                weight[k * rows : (k + 1) * rows],
                values_ref[:, k * HEAD_SIZE : (k + 1) * HEAD_SIZE],
                preferred_element_type=jnp.float32,
            )
            group = row * KEY_VALUE_HEADS + k
            messages[group // groups, group % groups] = mixed.astype(jnp.bfloat16)

    for offset, half in held:
        if half % 2 == 0:
            one = functools.partial(prompt, offset, half // 2)
            if full:
                one()
            else:
                pl.when(slot_row(targets, section ^ offset, half // 2)[1])(one)

    level = stats[0]
    high = level.astype(jnp.bfloat16).astype(jnp.float32)
    rest = level - high
    middle = rest.astype(jnp.bfloat16).astype(jnp.float32)
    stats[0], stats[1], stats[2] = high, middle, rest - middle
    for offset, message_ref in enumerate(message_refs):
        device = tp_index ^ offset
        for inner in range(groups):
            message_ref[inner * rows : (inner + 1) * rows] = messages[device, inner]
        first = device * groups // KEY_VALUE_HEADS
        lines = [stats[part, pl.ds(first + n, 1)] for part in range(3) for n in range(prompts)]
        lines.append(jnp.zeros((STAT_ROWS - 3 * prompts, span), jnp.float32))
        message_ref[groups * rows :] = jnp.concatenate(lines, axis=0).astype(jnp.bfloat16)


def attend(routing, lengths, caches, pieces, queries, far_queries):
    section_count = len(far_queries[0]) + 2
    tp_count = len(far_queries)
    samples, width = queries[0].shape[1:]
    span = width // HEAD_SIZE * samples
    rows = span // KEY_VALUE_HEADS
    groups = REQ_GRP * KEY_VALUE_HEADS // tp_count
    multiplies = REQ_GRP * span * HEAD_SIZE * caches[0].shape[1]
    return pl.pallas_call(
        functools.partial(attend_kernel, pieces, section_count, tp_count),
        out_shape=[jax.ShapeDtypeStruct((groups * rows + STAT_ROWS, HEAD_SIZE), jnp.bfloat16)] * tp_count,
        in_specs=[SMEM, SMEM] + [VMEM] * (len(caches) + len(queries) + tp_count),
        out_specs=[VMEM] * tp_count,
        scratch_shapes=[
            pltpu.VMEM((tp_count, groups, rows, HEAD_SIZE), jnp.bfloat16),
            pltpu.VMEM((3, REQ_GRP, span), jnp.float32),
            pltpu.VMEM((section_count * CAP, span, HEAD_SIZE), jnp.float32),
            pltpu.VMEM((tp_count,) + far_queries[0].shape, far_queries[0].dtype),
        ],
        compiler_params=limit(12),
        cost_estimate=cost(2 * 10**10, 2 * sum(part.size for part in caches), multiplies // HEAD_SIZE),
        name="attend",
    )(routing, lengths, *caches, *queries, *far_queries)


def join_kernel(count, samples, rows, *refs):
    message_refs, (out_ref, scaling, flat) = refs[:count], refs[-3:]
    groups = (message_refs[0].shape[0] - STAT_ROWS) // rows
    prompts = max(1, groups // KEY_VALUE_HEADS)
    heads = rows // samples
    tp_index = lax.axis_index("tp")
    levels = []
    for ref in message_refs:
        lines = ref[groups * rows :].astype(jnp.float32)[0:8]
        levels.append(lines + pltpu.roll(lines, 8 - prompts, 0) + pltpu.roll(lines, 8 - 2 * prompts, 0))
    summit = functools.reduce(jnp.maximum, levels)
    scales = [jnp.exp(level - summit) for level in levels]
    total = functools.reduce(jnp.add, scales)
    for n, scale in enumerate(scales):
        scaling[n] = (scale / total).T
    for inner in range(groups):
        if groups % KEY_VALUE_HEADS:
            first = (tp_index * groups + inner) % KEY_VALUE_HEADS * rows
            part = pl.ds(pl.multiple_of(first, rows), rows)
        else:
            part = pl.ds(inner % KEY_VALUE_HEADS * rows, rows)
        prompt = inner // KEY_VALUE_HEADS
        terms = [
            ref[inner * rows : (inner + 1) * rows].astype(jnp.float32) * scaling[n, part, prompt : prompt + 1]
            for n, ref in enumerate(message_refs)
        ]
        joined = functools.reduce(jnp.add, terms)
        for head in range(heads):
            block = joined[head * samples : (head + 1) * samples]
            if len(flat.shape) == 2:
                row = prompt * samples
                column = (inner % KEY_VALUE_HEADS * heads + head) * HEAD_SIZE
                flat[row : row + samples, column : column + HEAD_SIZE] = block
            else:
                flat[inner, :, head * HEAD_SIZE : (head + 1) * HEAD_SIZE] = block
    out_ref[...] = flat[...].astype(jnp.bfloat16)


def join(messages, others, samples, heads):
    rows = heads * samples
    groups = (messages[0].shape[0] - STAT_ROWS) // rows
    width = rows // samples * HEAD_SIZE
    if groups % KEY_VALUE_HEADS == 0:
        shape = (groups // KEY_VALUE_HEADS * samples, KEY_VALUE_HEADS * width)
    else:
        shape = (groups, samples, width)
    count = len(messages)
    return pl.pallas_call(
        functools.partial(join_kernel, count, samples, rows),
        out_shape=jax.ShapeDtypeStruct(shape, jnp.bfloat16),
        in_specs=[VMEM] * count + [ANY] * len(others),
        out_specs=VMEM,
        scratch_shapes=[
            pltpu.VMEM((count, KEY_VALUE_HEADS * rows, 8), jnp.float32),
            pltpu.VMEM(shape, jnp.float32),
        ],
        compiler_params=limit(8),
        cost_estimate=cost(4 * count * messages[0].size, 2 * count * messages[0].size),
        name="join",
    )(*messages, *others)


def fetch_kernel(first, weight_ref, *refs):
    out_ref, sem = refs[-2:]
    copies = []
    step = out_ref.shape[0] // sem.shape[0]
    for n in range(sem.shape[0]):
        rows = weight_ref.at[pl.ds(first + n * step, step)]
        copies.append(pltpu.make_async_copy(rows, out_ref.at[pl.ds(n * step, step)], sem.at[n]))
        copies[-1].start()
    for copy in copies:
        copy.wait()


def fetch(weight, others, number, count):
    size = weight.shape[0] // count
    return pl.pallas_call(
        functools.partial(fetch_kernel, number * size),
        out_shape=jax.ShapeDtypeStruct((size,) + weight.shape[1:], weight.dtype),
        in_specs=[HBM] + [ANY] * len(others),
        out_specs=VMEM,
        scratch_shapes=[pltpu.SemaphoreType.DMA((8,))],
        compiler_params=limit(24),
        cost_estimate=cost(0, 4 * weight.size // count),
        name="fetch",
    )(in_hbm(weight), *others)


def project_kernel(count, tile, skipped, *refs):
    refs = refs[skipped:]
    part_refs, weight_refs, out_ref = refs[:count], refs[count:-1], refs[-1]
    tp_index = lax.axis_index("tp")
    prompts, samples, width = out_ref.shape
    share = prompts // count
    left = jnp.concatenate([ref[...].astype(jnp.float32) for ref in part_refs], axis=0).astype(jnp.bfloat16)
    size = weight_refs[0].shape[0]
    for first in range(0, width, tile):
        result = functools.reduce(
            jnp.add,
            [
                jnp.dot(
                    left[:, n * size : (n + 1) * size],
                    ref[:, first : first + tile],
                    preferred_element_type=jnp.float32,
                )
                for n, ref in enumerate(weight_refs)
            ],
        )
        for offset in range(count):
            for n in range(share):
                row = (offset * share + n) * samples
                block = result[row : row + samples].astype(out_ref.dtype)
                out_ref[(tp_index ^ offset) * share + n, :, first : first + tile] = block


def project(parts, weights, others, samples):
    count = len(parts)
    depth, width = weights[0].shape
    depth *= len(weights)
    total = count * parts[0].shape[0]
    return pl.pallas_call(
        functools.partial(project_kernel, count, min(256, width), len(others)),
        out_shape=jax.ShapeDtypeStruct((total // samples, samples, width), jnp.bfloat16),
        in_specs=[ANY] * len(others) + [VMEM] * (count + len(weights)),
        out_specs=VMEM,
        compiler_params=limit(24),
        cost_estimate=cost(2 * total * depth * width, 2 * depth * width),
        name="project",
    )(*others, *parts, *weights)


def body(prompt_key_values, queries, routing, lengths, out_weight):
    section_count = lax.axis_size("sec")
    tp_count = lax.axis_size("tp")
    slot_count, samples, query_width = queries.shape[1:]
    routing = routing.reshape(-1)

    whole = 2 * CAP
    near = [(offset, 0, whole) for offset in range(2)]
    head, tail = [(2, 0, 1)], [(2, 1, whole - 1)]
    far = tail + [(offset, 0, whole) for offset in range(3, section_count - 1)]
    far += [(section_count - 1, 0, whole - 1), (section_count - 1, whole - 1, 1)]

    def across(parts, pieces):
        return [swap(part, "sec", piece[0]) for part, piece in zip(parts, pieces)]

    head_caches, far_queries = pack_head(
        routing, prompt_key_values, queries, head[0], section_count, tp_count
    )
    head_parts = across(head_caches, head)
    far_queries = [swap(part, "sec", n + 2) for n, part in enumerate(far_queries)]
    far_caches, query_parts = first_pack(
        routing, prompt_key_values, queries, head_caches, far, section_count
    )
    far_parts = across(far_caches[:-1], far[:-1])
    query_parts = [swap(part, "sec", offset) for offset, part in enumerate(query_parts)]
    merged = merge(far_queries, head_parts)
    far_queries = spread(merged, "tp")
    near_caches = pack(routing, prompt_key_values, [merged, query_parts[1]], near, section_count, 10**10)
    near_parts = across(near_caches, near)
    caches, pieces = [*head_caches, *far_caches, *near_caches], head + far + near

    messages = attend(routing, lengths, caches, pieces, query_parts, far_queries)
    partials = [swap(part, "tp", offset) for offset, part in enumerate(messages)]
    held_weight = [fetch(out_weight, [messages[0], *near_parts[1:]], 0, 2)]
    held_cache = place([], [], near_parts + head_parts, near + head, slot_count)
    share = join(partials, [in_hbm(held_cache), *held_weight, *far_parts[:-1]], samples, query_width // HEAD_SIZE // KEY_VALUE_HEADS)
    far_parts += across(gate(far_caches[-1:], [share]), far[-1:])
    shares = spread(share, "tp")
    held_weight.append(fetch(out_weight, [share], 1, 2))
    if share.ndim == 3:
        attended = jnp.stack(shares)[jnp.arange(tp_count) ^ lax.axis_index("tp")]
        attended = attended.reshape(REQ_GRP, KEY_VALUE_HEADS, samples, -1).transpose(0, 2, 1, 3)
        attended = attended.reshape(REQ_GRP * samples, query_width)
        layer_out = jnp.dot(attended, out_weight, preferred_element_type=jnp.float32)
        layer_out = layer_out.astype(jnp.bfloat16).reshape(REQ_GRP, samples, -1)
    else:
        layer_out = project(shares, held_weight, far_parts[:-2], samples)

    held_cache = place([held_cache], [share], far_parts[:-2], far[:-2], slot_count)
    for part, piece in zip(far_parts[-2:], far[-2:]):
        held_cache = place([held_cache, layer_out], [], [part], [piece], slot_count)
    held_cache = held_cache.reshape((1, slot_count) + prompt_key_values.shape[1:])
    return (layer_out, held_cache)


def solution(mesh):
    placed = (
        P(("rep", "sec"), None, "tp", None),
        P(("rep", "sec"), None, None, None),
        P("rep", None),
        P("rep"),
        P(None, "tp"),
    )
    return jax.shard_map(
        body,
        mesh=mesh,
        in_specs=placed,
        out_specs=(P(("rep", "sec"), None, "tp"), P(("rep", "sec"), None, None, "tp", None)),
        check_vma=False,
    )
```
